32 devices in a mesh: section: 2 (over core), ctx: 4 (over y, x), shard: 4 (over z).
Axes of the slice: x: 2, y: 2, z: 4, core: 2. Of those that a mesh axis runs over, the one named last changes fastest.
Arguments:
- tokens: int32 [8, 2048], P('shard', 'ctx'), may hold values from 0 to 51199
- lengths: int32 [8], P('shard'), may hold values from 1024 to 2048, as said below
- end_ids: int32 [8], P('shard'), may hold values from 0 to 51199
- pairs: int32 [4, 2], replicated, may hold values from 0 to 7, as said below
- layer_master: float32 [2, 14204928], P('section', ('ctx', 'shard'))
- layer_first: float32 [2, 14204928], P('section', ('ctx', 'shard'))
- layer_second: float32 [2, 14204928], P('section', ('ctx', 'shard'))
- table_master: float32 [1088, 55296], P(('section', 'ctx'), 'shard'), may hold values from -3 to 3
- table_first: float32 [1088, 55296], P(('section', 'ctx'), 'shard')
- table_second: float32 [1088, 55296], P(('section', 'ctx'), 'shard')
- vector_master: float32 [11, 1088], replicated
- vector_first: float32 [11, 1088], replicated
- vector_second: float32 [11, 1088], replicated
Outputs:
- loss_sum: float32 [], replicated
- grad_norm: float32 [], replicated
- layer_master_new: float32 [2, 14204928], P('section', ('ctx', 'shard'))
- layer_first_new: float32 [2, 14204928], P('section', ('ctx', 'shard'))
- layer_second_new: float32 [2, 14204928], P('section', ('ctx', 'shard'))
- table_master_new: float32 [1088, 55296], P(('section', 'ctx'), 'shard')
- table_first_new: float32 [1088, 55296], P(('section', 'ctx'), 'shard')
- table_second_new: float32 [1088, 55296], P(('section', 'ctx'), 'shard')
- vector_master_new: float32 [11, 1088], replicated
- vector_first_new: float32 [11, 1088], replicated
- vector_second_new: float32 [11, 1088], replicated
The draws below stay inside these ranges and needn't reach their ends.
Inputs may be any that keep to these rules, and one draw needn't show every extreme that they name: lengths run from 1024 to 2048; in each aligned group of 2 sequences one or more are 2048 long. `pairs`: every sequence stands in exactly one pair.
All inputs are finite; a program needn't handle non-finite values.
Results may differ from the reference program's by a relative error of at most 0.024.
Values may be sent and summed in bfloat16 or wider, within the bound.
No kernel may reach another device: no remote copies, remote signals or barrier semaphores. Data moves between devices by JAX's collectives and lax.ppermute only.
A program may use at most 768 MiB of HBM per device.

```python
import jax
import jax.numpy as jnp
from jax import lax

D = 1088
HEADS = 17
HD = 64
FF = 4352
VOCAB = 51200
SLOTS = 2048
MICRO = 2
STEP = 10
NVEC = 11
SEQS = 8
PAIRS = 4
LAYER = 14204928
TROWS = 55296
NPARAM = 88583872


def grad_scale():
    return 0.02 * NPARAM ** (-0.5)


def first_moment(key, shape, factor):
    return (jax.random.normal(key, shape) * 0.111 * grad_scale() * factor).astype(jnp.float32)


def second_moment(key, shape, factor):
    spread = jax.random.uniform(key, shape, minval=1.0, maxval=4.0)
    base = grad_scale() * factor
    return (spread * 0.0526 * base * base).astype(jnp.float32)


def draw_lengths(key, part):
    key = jax.random.fold_in(key, 3)
    key_len, key_full = jax.random.split(key)
    drawn = jax.random.randint(key_len, (SEQS,), SLOTS // 2, SLOTS + 1)
    full_at = jax.random.randint(key_full, (SEQS // MICRO,), 0, MICRO)
    hit = jnp.arange(SEQS) % MICRO == jnp.repeat(full_at, MICRO)
    return jnp.where(hit, SLOTS, drawn).astype(jnp.int32)


def draw_pairs(key, part):
    key = jax.random.fold_in(key, 5)
    order = jax.random.permutation(key, SEQS)
    return order.reshape(PAIRS, 2).astype(jnp.int32)


def draw_layer_master(key, part):
    key = jax.random.fold_in(key, 7)
    index_all = jnp.arange(LAYER)
    first = 3 * D * D
    second = first + D * D
    third = second + D * FF
    scale_row = jnp.where(index_all < first, D ** (-0.5), jnp.where(index_all < second, (SLOTS / 16.0) ** 0.5 * D ** (-0.5), jnp.where(index_all < third, D ** (-0.5), FF ** (-0.5))))
    base = jax.random.normal(key, (2, LAYER))
    return (base * scale_row[None, :]).astype(jnp.float32)


def draw_layer_first(key, part):
    key = jax.random.fold_in(key, 11)
    return first_moment(key, (2, LAYER), 1.0)


def draw_layer_second(key, part):
    key = jax.random.fold_in(key, 13)
    return second_moment(key, (2, LAYER), 4.0)


def draw_table_first(key, part):
    key = jax.random.fold_in(key, 17)
    return first_moment(key, (D, TROWS), 0.5)


def draw_table_second(key, part):
    key = jax.random.fold_in(key, 19)
    return second_moment(key, (D, TROWS), 0.5)


def draw_vector_master(key, part):
    key = jax.random.fold_in(key, 23)
    key_gain, key_bias = jax.random.split(key)
    column = jnp.arange(D) / D
    row_kind = jnp.arange(NVEC) % 2
    gains = (0.5 + column)[None, :] * jax.random.uniform(key_gain, (NVEC, D), minval=0.8, maxval=1.25)
    biases = jax.random.normal(key_bias, (NVEC, D)) * 0.3
    head_row = jax.random.normal(key_bias, (NVEC, D))
    values = jnp.where(row_kind[:, None] == 0, gains, biases)
    values = jnp.where((jnp.arange(NVEC) == NVEC - 1)[:, None], head_row, values)
    return values.astype(jnp.float32)


def draw_vector_first(key, part):
    key = jax.random.fold_in(key, 29)
    return first_moment(key, (NVEC, D), 5.0)


def draw_vector_second(key, part):
    key = jax.random.fold_in(key, 31)
    return second_moment(key, (NVEC, D), 5.0)


def set_ends(result, stream_key, smallest, high):
    extent = result.shape
    index_at = [jax.random.randint(jax.random.fold_in(stream_key, axis), (), 0, extent[axis]) for axis in range(len(extent))]
    result = result.at[tuple(index_at)].set(smallest)
    longest = extent.index(max(extent))
    index_at[longest] = (index_at[longest] + 1) % extent[longest]
    return result.at[tuple(index_at)].set(high)


def shard_levels(stream_key, extent, shards, least, top_value):
    def one(position, shards_of):
        steps = jax.random.uniform(jax.random.fold_in(jax.random.fold_in(stream_key, 6), position), (shards_of,), jnp.float32, least / len(shards), top_value / len(shards))
        return jnp.repeat(jnp.exp(steps), extent[position] // shards_of).reshape((-1,) + (1,) * (len(extent) - position - 1))

    gain = one(*shards[0])
    for cut in shards[1:]:
        gain = gain * one(*cut)
    return gain


def gaussian(key, extent, scale, bound, cuts=(), held_as=jnp.bfloat16):
    values = jax.random.normal(key, extent, jnp.float32) * scale
    if len(cuts) > 0:
        values = shard_levels(key, extent, cuts, -0.22, 0.18) * values
    return jnp.clip(values, min=-bound, max=bound).astype(held_as)


def setup_inputs(seed: int = 0) -> dict:
    splits = jax.random.split(jax.random.key(seed), 14)
    tokens = set_ends(jax.random.randint(splits[0], (SEQS, SLOTS), 0, VOCAB), jax.random.fold_in(splits[0], 1), 0, VOCAB - 1).astype(jnp.int32)
    lengths = draw_lengths(jax.random.fold_in(splits[13], 71), 0)
    end_ids = set_ends(jax.random.randint(splits[2], (SEQS,), 0, VOCAB), jax.random.fold_in(splits[2], 1), 0, VOCAB - 1).astype(jnp.int32)
    pairs = draw_pairs(jax.random.fold_in(splits[13], 71), 0)
    layer_master = draw_layer_master(jax.random.fold_in(splits[13], 71), 0)
    layer_first = draw_layer_first(jax.random.fold_in(splits[13], 71), 0)
    layer_second = draw_layer_second(jax.random.fold_in(splits[13], 71), 0)
    table_master = gaussian(splits[7], (D, TROWS), 0.5, 3.0, ((0, 8), (1, 4)), jnp.float32)
    table_first = draw_table_first(jax.random.fold_in(splits[13], 71), 0)
    table_second = draw_table_second(jax.random.fold_in(splits[13], 71), 0)
    vector_master = draw_vector_master(jax.random.fold_in(splits[13], 71), 0)
    vector_first = draw_vector_first(jax.random.fold_in(splits[13], 71), 0)
    vector_second = draw_vector_second(jax.random.fold_in(splits[13], 71), 0)
    return dict(tokens=tokens, lengths=lengths, end_ids=end_ids, pairs=pairs, layer_master=layer_master, layer_first=layer_first, layer_second=layer_second, table_master=table_master, table_first=table_first, table_second=table_second, vector_master=vector_master, vector_first=vector_first, vector_second=vector_second)


@jax.custom_vjp
def low(v):
    return lax.optimization_barrier(v.astype(jnp.bfloat16)).astype(jnp.float32)

@jax.custom_vjp
def low_back(v):
    return v

def low_keep(v):
    return (low(v), None)

def low_pass(kept, grad):
    return (grad,)

def back_keep(v):
    return (v, None)

def back_low(kept, grad):
    return (low(grad),)
low.defvjp(low_keep, low_pass)
low_back.defvjp(back_keep, back_low)
HIGH = lax.Precision.HIGHEST
CLIP_LIMIT = 0.02

def layer_norm(values, gain_vec, bias_vec):
    row_mean = lax.optimization_barrier(jnp.mean(values, -1, keepdims=True))
    centred = values - row_mean
    variance = lax.optimization_barrier(jnp.mean(centred * centred, -1, keepdims=True))
    return centred * lax.rsqrt(variance + 1e-05) * gain_vec + bias_vec

def gelu_tanh(values):
    return 0.5 * values * (1.0 + jnp.tanh(0.7978845608 * (values + 0.044715 * values * values * values)))

def softplus(values):
    return jnp.maximum(values, 0.0) + jnp.log1p(jnp.exp(-jnp.abs(values)))

def unpack(flat):
    first = 3 * D * D
    second = first + D * D
    third = second + D * FF
    return (flat[:first].reshape(D, 3 * D), flat[first:second].reshape(D, D), flat[second:third].reshape(D, FF), flat[third:].reshape(FF, D))

def attention(qkv, length):
    queries = qkv[:, :D].reshape(SLOTS, HEADS, HD)
    keys = qkv[:, D:2 * D].reshape(SLOTS, HEADS, HD)
    values = qkv[:, 2 * D:].reshape(SLOTS, HEADS, HD)
    block_rows = min(512, SLOTS)
    key_pos = jnp.arange(SLOTS, dtype=jnp.int32)

    def one_block(start):
        query_blk = lax.dynamic_slice_in_dim(queries, start, block_rows, 0)
        query_pos = start + jnp.arange(block_rows, dtype=jnp.int32)
        scores = jnp.einsum('qhd,khd->hqk', query_blk, keys, precision=HIGH) * 0.125
        scores = low_back(scores)
        mask = (key_pos[None, :] <= query_pos[:, None]) & (key_pos[None, :] < length)
        scores = jnp.where(mask[None], scores, -1e+30)
        top_val = lax.optimization_barrier(jnp.max(scores, -1, keepdims=True))
        expo = jnp.exp(scores - top_val)
        probs = low(expo / lax.optimization_barrier(jnp.sum(expo, -1, keepdims=True)))
        return jnp.einsum('hqk,khd->qhd', probs, values, precision=HIGH)
    starts = (jnp.arange(SLOTS // block_rows) * block_rows).astype(jnp.int32)
    outs = lax.map(jax.checkpoint(one_block), starts)
    return outs.reshape(SLOTS, D)

def layer_apply(values, flat, vecs, length):
    w_qkv, w_out, w_up, w_down = unpack(flat)
    hidden1 = low(layer_norm(values, vecs[0], vecs[1]))
    qkv = low(low_back(jnp.dot(hidden1, w_qkv, precision=HIGH)))
    attended = low(low_back(attention(qkv, length)))
    middle = values + low_back(jnp.dot(attended, w_out, precision=HIGH))
    hidden2 = low(layer_norm(middle, vecs[2], vecs[3]))
    up_val = low_back(jnp.dot(hidden2, w_up, precision=HIGH))
    gated = low(gelu_tanh(up_val))
    return middle + low_back(jnp.dot(gated, w_down, precision=HIGH))

def score_one(flat_pair, table_low, vectors, ids, length, end_id):
    embedded = table_low[ids] + table_low[VOCAB + jnp.arange(SLOTS, dtype=jnp.int32)]
    embedded = low_back(embedded)
    first_out = layer_apply(embedded, flat_pair[0], vectors[0:4], length)
    first_out = low(low_back(first_out))
    last_out = layer_apply(first_out, flat_pair[1], vectors[4:8], length)
    last_row = lax.dynamic_index_in_dim(last_out, length - 1, 0, keepdims=False)
    normed = layer_norm(last_row, vectors[8], vectors[9])
    end_row = low_back(table_low[end_id])
    return jnp.sum(normed * (end_row + vectors[10])) * D ** (-0.5)

def adam_update(weight, first, second, grad, rate, decay):
    first = 0.9 * first + 0.1 * grad
    second = 0.95 * second + 0.05 * grad * grad
    first_hat = first / (1.0 - 0.9 ** STEP)
    second_hat = second / (1.0 - 0.95 ** STEP)
    weight = weight - rate * (first_hat / (jnp.sqrt(second_hat) + 1e-08) + decay * weight)
    return (weight, first, second)

def reference(tokens, lengths, end_ids, pairs, layer_master, layer_first, layer_second, table_master, table_first, table_second, vector_master, vector_first, vector_second):

    def loss_of(layer_w, table_w, vector_w):
        flat_pair = low(layer_w)
        table_low = low(table_w).T

        def per_seq(carry, item):
            ids, length, end_id = item
            return (carry, jax.checkpoint(score_one)(flat_pair, table_low, vector_w, ids, length, end_id))
        _, scores = lax.scan(per_seq, jnp.zeros((), jnp.float32), (tokens, lengths, end_ids))
        margin = scores[pairs[:, 1]] - scores[pairs[:, 0]]
        return jnp.sum(softplus(margin))
    loss_sum, pullback = jax.vjp(loss_of, layer_master, table_master, vector_master)
    grad_layer, grad_table, grad_vector = pullback(jnp.ones_like(loss_sum))
    squares = jnp.sum(grad_layer * grad_layer) + jnp.sum(grad_table * grad_table) + jnp.sum(grad_vector * grad_vector)
    grad_norm = jnp.sqrt(squares)
    factor = CLIP_LIMIT / jnp.maximum(grad_norm, CLIP_LIMIT)
    layer_new = adam_update(layer_master, layer_first, layer_second, grad_layer * factor, 0.4, 0.1)
    table_new = adam_update(table_master, table_first, table_second, grad_table * factor, 0.5, 0.1)
    vector_new = adam_update(vector_master, vector_first, vector_second, grad_vector * factor, 0.7, 0.0)
    return (loss_sum, grad_norm, layer_new[0], layer_new[1], layer_new[2], table_new[0], table_new[1], table_new[2], vector_new[0], vector_new[1], vector_new[2])
```

```python
import functools

import jax
import jax.numpy as jnp
from jax import lax
from jax.experimental import pallas as pl
from jax.experimental.pallas import tpu as pltpu
from jax.sharding import PartitionSpec as P

D = 1088
HEADS = 17
HD = 64
FF = 4352
VOCAB = 51200
MICRO = 2
STEP = 10
CLIP_LIMIT = 0.02
ALL = ("section", "ctx", "shard")

LANES = 128
PAIRS_OF_HEADS = (HEADS + 1) // 2
WIDE = PAIRS_OF_HEADS * LANES
N_UP = FF // D
U_OUT = 3 * D
U_UP = U_OUT + D
U_DOWN = U_UP + FF
UNITS = U_DOWN + FF

BF = jnp.bfloat16
F32 = jnp.float32
VMEM_BIG = 56 * 1024 * 1024


def params(limit=VMEM_BIG):
    return pltpu.CompilerParams(vmem_limit_bytes=limit)


def dot(a, b, contract=((1,), (0,))):
    return lax.dot_general(a, b, (contract, ((), ())), preferred_element_type=F32)


NT = ((1,), (1,))
TN = ((0,), (0,))


def swap(x, axis, bit):
    size = lax.axis_size(axis)
    return lax.ppermute(x, axis, [(i, i ^ bit) for i in range(size)])


def gather_axis(x, axis):
    size = lax.axis_size(axis)
    me = lax.axis_index(axis)
    x = x[None]
    bit = 1
    while bit < size:
        other = swap(x, axis, bit)
        lower = (me & bit) == 0
        x = jnp.where(lower, jnp.concatenate([x, other]), jnp.concatenate([other, x]))
        bit *= 2
    return x


def sum_axis(x, axis, first=1, last=None):
    size = lax.axis_size(axis) if last is None else last
    bit = first
    while bit < size:
        x = x + swap(x, axis, bit)
        bit *= 2
    return x


def lookup_kernel(rows, n_blocks, ids, meta, table, out, ends, owned, counts, tab, buf):
    step = pl.program_id(0)
    columns, entries = table.shape
    n_ends = ends.shape[0]

    @pl.when(step == 0)
    def _():
        def turn(i, _):
            at = pl.multiple_of(i * 256, 256)
            part = table[:, pl.ds(at, 256)].astype(BF).astype(F32)
            tab[pl.ds(at, 256), :] = part.T
            return 0

        lax.fori_loop(0, entries // 256, turn, 0)
        tab[pl.ds(entries, 8), :] = jnp.zeros((8, columns), F32)
        for n in range(n_ends):
            ends[pl.ds(n, 1), :] = tab[pl.ds(ids[n_blocks * rows + n], 1), :]

    base = step * rows

    def pick(i, count):
        row = ids[base + i]
        buf[pl.ds(i, 1), :] = tab[pl.ds(row, 1), :]
        owned[base + count] = i
        return count + (row < entries).astype(jnp.int32)

    counts[step] = lax.fori_loop(0, rows, pick, jnp.int32(0), unroll=8)

    @pl.when(meta[0] == 1)
    def _():
        half = rows // 2
        group = meta[4 + step]
        for j in range(2):
            block = group if j == 0 else 2 * meta[1] - 1 - group
            at = pl.multiple_of(meta[2] + block * half, 8)
            buf[pl.ds(j * half, half), :] += tab[pl.ds(at, half), :]

    out[0] = buf[...].T.astype(BF)


def lookup(ids, meta, table, n_blocks, rows, n_ends):
    columns, entries = table.shape
    grid_spec = pltpu.PrefetchScalarGridSpec(
        num_scalar_prefetch=2,
        grid=(n_blocks,),
        in_specs=[pl.BlockSpec((columns, entries), lambda i, *_: (0, 0))],
        out_specs=[
            pl.BlockSpec((1, columns, rows), lambda i, *_: (i, 0, 0)),
            pl.BlockSpec((n_ends, columns), lambda i, *_: (0, 0)),
            pl.BlockSpec(memory_space=pltpu.SMEM),
            pl.BlockSpec(memory_space=pltpu.SMEM),
        ],
        scratch_shapes=[pltpu.VMEM((entries + 8, columns), F32), pltpu.VMEM((rows, columns), F32)],
    )
    return pl.pallas_call(
        functools.partial(lookup_kernel, rows, n_blocks),
        grid_spec=grid_spec,
        out_shape=[
            jax.ShapeDtypeStruct((n_blocks, columns, rows), BF),
            jax.ShapeDtypeStruct((n_ends, columns), F32),
            jax.ShapeDtypeStruct((n_blocks * rows,), jnp.int32),
            jax.ShapeDtypeStruct((n_blocks,), jnp.int32),
        ],
        compiler_params=params(),
        name="lookup",
    )(ids, meta, table)


def scatter_kernel(rows, n_blocks, ids, meta, owned, counts, grads, ends, out, acc, buf):
    step = pl.program_id(0)
    columns, entries = out.shape
    n_ends = ends.shape[0]

    @pl.when(step == 0)
    def _():
        def clear(i, _):
            acc[pl.ds(pl.multiple_of(i * 256, 256), 256), :] = jnp.zeros((256, columns), F32)
            return 0

        lax.fori_loop(0, entries // 256, clear, 0)
        for n in range(n_ends):
            at = pl.ds(ids[n_blocks * rows + n], 1)
            acc[at, :] += ends[pl.ds(n, 1), :]

    buf[...] = grads[0].astype(F32).T
    base = step * rows

    def add(t, _):
        i = owned[base + t]
        at = pl.ds(ids[base + i], 1)
        acc[at, :] += buf[pl.ds(i, 1), :]
        return 0

    lax.fori_loop(0, counts[step], add, 0)

    @pl.when(meta[0] == 1)
    def _():
        half = rows // 2
        group = meta[4 + step]
        for j in range(2):
            block = group if j == 0 else 2 * meta[1] - 1 - group
            at = pl.multiple_of(meta[2] + block * half, 8)
            acc[pl.ds(at, half), :] += buf[pl.ds(j * half, half), :]

    @pl.when(step == n_blocks - 1)
    def _():
        def turn(i, _):
            at = pl.multiple_of(i * 256, 256)
            out[:, pl.ds(at, 256)] = acc[pl.ds(at, 256), :].T
            return 0

        lax.fori_loop(0, entries // 256, turn, 0)


def scatter(ids, meta, owned, counts, grads, ends, entries):
    n_blocks, columns, rows = grads.shape
    n_ends = ends.shape[0]
    grid_spec = pltpu.PrefetchScalarGridSpec(
        num_scalar_prefetch=4,
        grid=(n_blocks,),
        in_specs=[
            pl.BlockSpec((1, columns, rows), lambda i, *_: (i, 0, 0)),
            pl.BlockSpec((n_ends, columns), lambda i, *_: (0, 0)),
        ],
        out_specs=pl.BlockSpec((columns, entries), lambda i, *_: (0, 0)),
        scratch_shapes=[pltpu.VMEM((entries + 8, columns), F32), pltpu.VMEM((rows, columns), F32)],
    )
    return pl.pallas_call(
        functools.partial(scatter_kernel, rows, n_blocks),
        grid_spec=grid_spec,
        out_shape=jax.ShapeDtypeStruct((columns, entries), F32),
        compiler_params=params(),
        name="scatter",
    )(ids, meta, owned, counts, grads, ends)


def tile_cuts():
    return [(t * LANES, min(LANES, D - t * LANES)) for t in range(PAIRS_OF_HEADS)]


def split_kernel(count, rb, width, u, out, scr):
    for t, (at, size) in enumerate(tile_cuts()):
        part = u[:, pl.ds(at, size)].astype(F32)
        if size < LANES:
            part = jnp.concatenate([part, jnp.zeros((rb * count, LANES - size), F32)], axis=1)
        scr[t] = part
        for j in range(count):
            picked = scr[t, pl.ds(j, rb, stride=count), :].astype(BF)
            take = min(LANES, width - at)
            out[j, :, pl.ds(at, take)] = picked[:, :take]


def split_units(u, first, count, width=D):
    rb = 64
    return pl.pallas_call(
        functools.partial(split_kernel, count, rb, width),
        grid=(D // rb,),
        in_specs=[pl.BlockSpec((rb * count, D), lambda i: (i + first // (rb * count), 0))],
        out_specs=pl.BlockSpec((count, rb, width), lambda i: (0, i, 0)),
        out_shape=jax.ShapeDtypeStruct((count, D, width), BF),
        scratch_shapes=[pltpu.VMEM((PAIRS_OF_HEADS, rb * count, LANES), F32)],
        compiler_params=params(),
        name="split_units",
    )(u)


def merge_kernel(count, rb, *refs):
    parts, out, scr = refs[:count], refs[count], refs[count + 1]
    for t, (at, size) in enumerate(tile_cuts()):
        for j in range(count):
            part = parts[j][:, pl.ds(at, size)].astype(F32)
            if size < LANES:
                part = jnp.concatenate([part, jnp.zeros((rb, LANES - size), F32)], axis=1)
            scr[t, pl.ds(j, rb, stride=count), :] = part
        out[:, pl.ds(at, size)] = scr[t][:, :size].astype(BF)


def merge_units(parts):
    rb, count = 64, len(parts)
    return pl.pallas_call(
        functools.partial(merge_kernel, count, rb),
        grid=(D // rb,),
        in_specs=[pl.BlockSpec((rb, p.shape[1]), lambda i: (i, 0)) for p in parts],
        out_specs=pl.BlockSpec((rb * count, D), lambda i: (i, 0)),
        out_shape=jax.ShapeDtypeStruct((count * D, D), BF),
        scratch_shapes=[pltpu.VMEM((PAIRS_OF_HEADS, rb * count, LANES), F32)],
        compiler_params=params(),
        name="merge_units",
    )(*parts)


def chunk_plan(n):
    plan = [(0, "ll", True), (0, "hl", False), (0, "hh", True)]
    for p in range(1, n):
        plan += [(p, "hl", False), (p, "sel", False)]
    return plan


def chunk_offsets(meta, n, hb, p, kind):
    own = meta[0]
    piece = meta[2 + p]
    if kind == "ll":
        return 0, p * 2 * hb, own * hb, piece * hb, True
    if kind == "hl":
        return hb, p * 2 * hb, (2 * n - 1 - own) * hb, piece * hb, False
    if kind == "hh":
        return hb, p * 2 * hb + hb, (2 * n - 1 - own) * hb, (2 * n - 1 - piece) * hb, False
    low = piece < own
    q_off = pl.multiple_of(jnp.where(low, 0, hb), hb)
    k_off = pl.multiple_of(p * 2 * hb + jnp.where(low, 0, hb), hb)
    key_pos = jnp.where(low, piece, 2 * n - 1 - piece) * hb
    return q_off, k_off, None, key_pos, low


def chunk_scores(keys, queries, meta, diagonal, kind, q_pos, k_pos, hb):
    s = dot(keys, queries, NT)
    if diagonal:
        ki = lax.broadcasted_iota(jnp.int32, (hb, hb), 0)
        qi = lax.broadcasted_iota(jnp.int32, (hb, hb), 1)
        keep = (ki <= qi) & (ki + k_pos < meta[1])
        s = jnp.where(keep, s, -1e30)
    elif kind == "sel":
        ki = lax.broadcasted_iota(jnp.int32, (hb, hb), 0)
        s = jnp.where(ki < meta[1] - k_pos, s, -1e30)
    return s


def attend_kernel(n, hb, meta, q_ref, k_ref, v_ref, o_ref, lse_ref, vt_ref):
    keys = 2 * hb * n
    for i in range(keys // hb):
        vt_ref[i] = v_ref[pl.ds(i * hb, hb), :].astype(F32).T.astype(BF)
    lane = lax.broadcasted_iota(jnp.int32, (1, LANES), 1)
    plan = chunk_plan(n)
    outs = []
    for head in range(2):
        own_lanes = (lane // HD) == head
        info, scores = [], []
        tops = [jnp.full((1, hb), -3e38, F32), jnp.full((1, hb), -3e38, F32)]
        for p, kind, diagonal in plan:
            q_off, k_off, q_pos, k_pos, low = chunk_offsets(meta, n, hb, p, kind)
            queries = jnp.where(own_lanes, q_ref[pl.ds(q_off, hb), :], 0)
            s = chunk_scores(k_ref[pl.ds(k_off, hb), :], queries, meta, diagonal, kind, q_pos, k_pos, hb)
            top = jnp.max(s, axis=0, keepdims=True)
            if low is True:
                tops[0] = jnp.maximum(tops[0], top)
            elif low is False:
                tops[1] = jnp.maximum(tops[1], top)
            else:
                tops[0] = jnp.maximum(tops[0], jnp.where(low, top, -3e38))
                tops[1] = jnp.maximum(tops[1], jnp.where(low, -3e38, top))
            info.append((k_off, low))
            scores.append(s)
        sums = [jnp.zeros((1, hb), F32), jnp.zeros((1, hb), F32)]
        accs = [jnp.zeros((HD, hb), F32), jnp.zeros((HD, hb), F32)]
        for (k_off, low), s in zip(info, scores):
            if low is True or low is False:
                top = tops[0] if low else tops[1]
            else:
                top = jnp.where(low, tops[0], tops[1])
            e = jnp.exp(s - top)
            total = jnp.sum(e, axis=0, keepdims=True)
            got = dot(vt_ref[k_off // hb, pl.ds(head * HD, HD), :], e.astype(BF))
            if low is True or low is False:
                sums[1 - low] += total
                accs[1 - low] += got
            else:
                sums[0] += jnp.where(low, total, 0.0)
                sums[1] += jnp.where(low, 0.0, total)
                accs[0] += jnp.where(low, got, 0.0)
                accs[1] += jnp.where(low, 0.0, got)
        outs.append([accs[i] / sums[i] for i in range(2)])
        for i in range(2):
            lse_ref[0, pl.ds(head, 1), pl.ds(i * hb, hb)] = tops[i] + jnp.log(sums[i])
    for i in range(2):
        both = jnp.concatenate([outs[0][i], outs[1][i]], axis=0)
        o_ref[pl.ds(i * hb, hb), :] = both.T.astype(BF)


def attend(meta, q, k, v, n):
    rows = q.shape[0]
    keys = k.shape[0]
    grid_spec = pltpu.PrefetchScalarGridSpec(
        num_scalar_prefetch=1,
        grid=(PAIRS_OF_HEADS,),
        in_specs=[
            pl.BlockSpec((rows, LANES), lambda p, *_: (0, p)),
            pl.BlockSpec((keys, LANES), lambda p, *_: (0, p)),
            pl.BlockSpec((keys, LANES), lambda p, *_: (0, p)),
        ],
        out_specs=[
            pl.BlockSpec((rows, LANES), lambda p, *_: (0, p)),
            pl.BlockSpec((1, 8, rows), lambda p, *_: (p, 0, 0)),
        ],
        scratch_shapes=[pltpu.VMEM((2 * n, LANES, rows // 2), BF)],
    )
    return pl.pallas_call(
        functools.partial(attend_kernel, n, rows // 2),
        grid_spec=grid_spec,
        out_shape=[
            jax.ShapeDtypeStruct((rows, WIDE), BF),
            jax.ShapeDtypeStruct((PAIRS_OF_HEADS, 8, rows), F32),
        ],
        compiler_params=params(),
        name="attend",
    )(meta, q, k, v)


def attend_back_kernel(n, hb, meta, q_ref, k_ref, v_ref, o_ref, do_ref, lse_ref, dq_ref, dk_ref, dv_ref, kt_ref, dk_acc, dv_acc):
    keys = 2 * hb * n
    for i in range(keys // hb):
        kt_ref[i] = k_ref[pl.ds(i * hb, hb), :].astype(F32).T.astype(BF)
    dk_acc[...] = jnp.zeros_like(dk_acc)
    dv_acc[...] = jnp.zeros_like(dv_acc)
    lane = lax.broadcasted_iota(jnp.int32, (1, LANES), 1)
    plan = chunk_plan(n)
    prods = []
    for i in range(2):
        part = pl.ds(i * hb, hb)
        prods.append((o_ref[part, :].astype(F32) * do_ref[part, :].astype(F32)).T)
    dqs = []
    for head in range(2):
        own_lanes = (lane // HD) == head
        deltas = [jnp.sum(prods[i][head * HD : (head + 1) * HD, :], axis=0, keepdims=True) for i in range(2)]
        lses = [lse_ref[0, pl.ds(head, 1), pl.ds(i * hb, hb)] for i in range(2)]
        accs = [jnp.zeros((HD, hb), F32), jnp.zeros((HD, hb), F32)]
        for p, kind, diagonal in plan:
            q_off, k_off, q_pos, k_pos, low = chunk_offsets(meta, n, hb, p, kind)
            q_at, k_at = pl.ds(q_off, hb), pl.ds(k_off, hb)
            queries = jnp.where(own_lanes, q_ref[q_at, :], 0)
            d_out = jnp.where(own_lanes, do_ref[q_at, :], 0)
            s = chunk_scores(k_ref[k_at, :], queries, meta, diagonal, kind, q_pos, k_pos, hb)
            if low is True or low is False:
                lse, delta = lses[1 - low], deltas[1 - low]
            else:
                lse, delta = jnp.where(low, lses[0], lses[1]), jnp.where(low, deltas[0], deltas[1])
            prob = jnp.exp(s - lse)
            d_prob = dot(v_ref[k_at, :], d_out, NT)
            d_score = (prob * (d_prob - delta)).astype(BF)
            dv_acc[k_at, :] += dot(prob.astype(BF), d_out)
            dk_acc[k_at, :] += dot(d_score, queries)
            got = dot(kt_ref[k_off // hb, pl.ds(head * HD, HD), :], d_score)
            if low is True or low is False:
                accs[1 - low] += got
            else:
                accs[0] += jnp.where(low, got, 0.0)
                accs[1] += jnp.where(low, 0.0, got)
        dqs.append(accs)
    for i in range(2):
        both = jnp.concatenate([dqs[0][i], dqs[1][i]], axis=0) * 0.125
        dq_ref[pl.ds(i * hb, hb), :] = both.T.astype(BF)
    dk_ref[...] = dk_acc[...].astype(BF)
    dv_ref[...] = dv_acc[...].astype(BF)


def attend_back(meta, q, k, v, o, d_o, lse, n):
    rows = q.shape[0]
    keys = k.shape[0]
    row_spec = pl.BlockSpec((rows, LANES), lambda p, *_: (0, p))
    key_spec = pl.BlockSpec((keys, LANES), lambda p, *_: (0, p))
    grid_spec = pltpu.PrefetchScalarGridSpec(
        num_scalar_prefetch=1,
        grid=(PAIRS_OF_HEADS,),
        in_specs=[row_spec, key_spec, key_spec, row_spec, row_spec, pl.BlockSpec((1, 8, rows), lambda p, *_: (p, 0, 0))],
        out_specs=[row_spec, key_spec, key_spec],
        scratch_shapes=[pltpu.VMEM((2 * n, LANES, rows // 2), BF), pltpu.VMEM((keys, LANES), F32), pltpu.VMEM((keys, LANES), F32)],
    )
    return pl.pallas_call(
        functools.partial(attend_back_kernel, n, rows // 2),
        grid_spec=grid_spec,
        out_shape=[
            jax.ShapeDtypeStruct((rows, WIDE), BF),
            jax.ShapeDtypeStruct((keys, WIDE), BF),
            jax.ShapeDtypeStruct((keys, WIDE), BF),
        ],
        compiler_params=params(),
        name="attend_back",
    )(meta, q, k, v, o, d_o, lse)


def layer_norm(values, gain_vec, bias_vec):
    row_mean = jnp.mean(values, -1, keepdims=True)
    centred = values - row_mean
    variance = jnp.mean(centred * centred, -1, keepdims=True)
    return centred * lax.rsqrt(variance + 1e-05) * gain_vec + bias_vec


def gelu_tanh(values):
    return 0.5 * values * (1.0 + jnp.tanh(0.7978845608 * (values + 0.044715 * values * values * values)))


def softplus(values):
    return jnp.maximum(values, 0.0) + jnp.log1p(jnp.exp(-jnp.abs(values)))


def adam_update(weight, first, second, grad, rate, decay):
    first = 0.9 * first + 0.1 * grad
    second = 0.95 * second + 0.05 * grad * grad
    first_hat = first / (1.0 - 0.9**STEP)
    second_hat = second / (1.0 - 0.95**STEP)
    weight = weight - rate * (first_hat / (jnp.sqrt(second_hat) + 1e-08) + decay * weight)
    return (weight, first, second)


def pieces_of(x, half):
    got = [x]
    bit = 1
    while bit < half:
        got += [swap(y, "ctx", bit) for y in got]
        bit *= 2
    own = jnp.concatenate(got)
    return jnp.concatenate([own, swap(own, "section", 1)])


def sum_pieces(x, half):
    rows = x.shape[0] // (2 * half)
    near = x.shape[0] // 2
    x = x[:near].astype(F32) + swap(x[near:], "section", 1).astype(F32)
    bit = half // 2
    while bit >= 1:
        keep, send = x[: bit * rows], x[bit * rows : 2 * bit * rows]
        x = keep + swap(send.astype(BF), "ctx", bit).astype(F32)
        bit //= 2
    return x


def layer_weights(units):
    w_qkv = split_units(units, 0, 3, WIDE)
    w_out = units[U_OUT:U_UP]
    w_up = split_units(units, U_UP, N_UP)
    w_down = units[U_DOWN:].reshape(N_UP, D, D)
    return w_qkv, w_out, w_up, w_down


def layer_forward(values, meta, n, weights, vecs):
    w_qkv, w_out, w_up, w_down = weights
    hidden1 = layer_norm(values, vecs[0], vecs[1]).astype(BF)
    keys = pieces_of(dot(hidden1, w_qkv[1]).astype(BF), n // 2)
    vals = pieces_of(dot(hidden1, w_qkv[2]).astype(BF), n // 2)
    queries = dot(hidden1, w_qkv[0]).astype(BF) * jnp.asarray(0.125, BF)
    attended, lse = attend(meta, queries, keys, vals, n)
    middle = values + dot(attended[:, :D], w_out)
    hidden2 = layer_norm(middle, vecs[2], vecs[3]).astype(BF)
    ups = [dot(hidden2, w_up[j]) for j in range(N_UP)]
    gated = [gelu_tanh(u).astype(BF) for u in ups]
    result = middle
    for j in range(N_UP):
        result = result + dot(gated[j], w_down[j])
    return result, (values, hidden1, queries, keys, vals, attended, lse, middle, hidden2, ups, gated)


def layer_backward(saved, grad_out, meta, n, weights, vecs):
    values, hidden1, queries, keys, vals, attended, lse, middle, hidden2, ups, gated = saved
    w_qkv, w_out, w_up, w_down = weights
    grad_ffn = grad_out.astype(BF)
    grad_down = [dot(gated[j], grad_ffn, TN).astype(BF) for j in range(N_UP)]
    grad_ups = []
    for j in range(N_UP):
        _, back = jax.vjp(gelu_tanh, ups[j])
        grad_ups.append(back(dot(grad_ffn, w_down[j], NT))[0].astype(BF))
    grad_up = [dot(hidden2, grad_ups[j], TN).astype(BF) for j in range(N_UP)]
    grad_hidden2 = sum(dot(grad_ups[j], w_up[j], NT) for j in range(N_UP))
    _, norm_back2 = jax.vjp(layer_norm, middle, vecs[2], vecs[3])
    grad_norm2, grad_gain2, grad_bias2 = norm_back2(grad_hidden2)
    grad_middle = grad_out + grad_norm2
    grad_branch = grad_middle.astype(BF)
    grad_outw = dot(attended[:, :D], grad_branch, TN).astype(BF)
    grad_att = dot(grad_branch, jnp.pad(w_out, ((0, WIDE - D), (0, 0))), NT).astype(BF)
    grad_q, part_k, part_v = attend_back(meta, queries, keys, vals, attended, grad_att, lse, n)
    grad_k = sum_pieces(part_k, n // 2).astype(BF)
    grad_v = sum_pieces(part_v, n // 2).astype(BF)
    grad_qkv = [grad_q, grad_k, grad_v]
    grad_qkvw = [dot(hidden1, g, TN).astype(BF) for g in grad_qkv]
    grad_hidden1 = sum(dot(g, w_qkv[j], NT) for j, g in enumerate(grad_qkv))
    _, norm_back1 = jax.vjp(layer_norm, values, vecs[0], vecs[1])
    grad_norm1, grad_gain1, grad_bias1 = norm_back1(grad_hidden1)
    grad_input = grad_middle + grad_norm1
    units = jnp.concatenate([merge_units(grad_qkvw), grad_outw, merge_units(grad_up), *grad_down])
    return grad_input, units, [grad_gain1, grad_bias1, grad_gain2, grad_bias2]


def shards(
    tokens,
    lengths,
    end_ids,
    pairs,
    layer_master,
    layer_first,
    layer_second,
    table_master,
    table_first,
    table_second,
    vector_master,
    vector_first,
    vector_second,
):
    rows = tokens.shape[1]
    s_at = lax.axis_index("section")
    c_at = lax.axis_index("ctx")
    z_at = lax.axis_index("shard")
    n_section = lax.axis_size("section")
    n = lax.axis_size("ctx")
    n_shard = lax.axis_size("shard")
    half = n // 2
    hb = rows // 2
    n_dest = n_section * n
    n_seq = MICRO * n_shard
    columns, entries = table_master.shape
    is_first = s_at == 0
    seq_in = c_at // half
    seq_at = z_at * MICRO + seq_in
    group = (c_at % half) * 2 + s_at

    chunk = layer_master.reshape(-1, D).astype(BF)
    cut = chunk.shape[0] // 2
    got = swap(jnp.where(is_first, chunk[cut:], chunk[:cut]), "section", 1)
    piece0 = jnp.where(is_first, chunk[:cut], got)
    piece1 = jnp.where(is_first, got, chunk[cut:])
    order = ("ctx", "shard", "section")
    units0 = lax.all_gather(piece0, order, axis=0, tiled=True)

    own_ids = jnp.concatenate([tokens, end_ids[:, None]], axis=1)
    all_ids = gather_axis(gather_axis(own_ids, "ctx"), "shard")
    natural = all_ids[..., :rows].transpose(0, 2, 1, 3).reshape(n_shard, MICRO, 2 * n, hb)
    zig = jnp.stack([natural[:, :, :n], natural[:, :, n:][:, :, ::-1]], axis=3)
    zig = zig.reshape(n_shard, MICRO, half, 2, rows).transpose(0, 3, 1, 2, 4)
    end_all = all_ids[:, 0, :, rows].reshape(n_seq)
    ids = jnp.concatenate([zig.reshape(-1), end_all]) - z_at * entries
    ids = jnp.where((ids >= 0) & (ids < entries), ids, entries)
    n_blocks = n_shard * n_dest
    dest = jnp.arange(n_blocks, dtype=jnp.int32) % n_dest
    groups = (dest % n % half) * 2 + dest // n
    assert VOCAB >= (n_shard - 1) * entries
    meta_emb = jnp.concatenate(
        [
            jnp.stack([(z_at == n_shard - 1).astype(jnp.int32), jnp.int32(n), jnp.int32(VOCAB - (n_shard - 1) * entries), jnp.int32(0)]),
            groups,
        ]
    )
    picked, end_part, owned, counts = lookup(ids, meta_emb, table_master, n_blocks, rows, n_seq)
    summed = lax.psum_scatter(picked.reshape(n_shard, n_dest, columns, rows), "shard", scatter_dimension=0, tiled=True)
    routed = lax.all_to_all(summed.reshape(n_dest, columns, rows), ("section", "ctx"), split_axis=0, concat_axis=0, tiled=True)
    embedded = routed.reshape(D, rows).T.astype(F32)
    column_at = (s_at * n + c_at) * columns
    end_rows = lax.psum(lax.dynamic_update_slice(jnp.zeros((n_seq, D), F32), end_part, (0, column_at)), ALL)
    end_row = lax.dynamic_slice_in_dim(end_rows, seq_at, 1, 0)

    piece1, _ = lax.optimization_barrier((piece1, units0[:8]))
    units1 = lax.all_gather(piece1, order, axis=0, tiled=True)

    length = lax.dynamic_slice_in_dim(lengths, seq_in, 1, 0)[0]
    others = [group ^ (2 * cb + sb) for sb in range(2) for cb in range(half)]
    meta = jnp.stack([group, length] + others).astype(jnp.int32)
    span = jnp.arange(hb, dtype=jnp.int32)
    positions = jnp.concatenate([group * hb + span, (2 * n - 1 - group) * hb + span])

    weights0 = layer_weights(units0)
    weights1 = layer_weights(units1)
    vecs0, vecs1 = vector_master[0:4], vector_master[4:8]
    out0, saved0 = layer_forward(embedded, meta, n, weights0, vecs0)
    x1 = out0.astype(BF).astype(F32)
    final, saved1 = layer_forward(x1, meta, n, weights1, vecs1)

    def score_terms(final_rows, end_vals, gain_vec, bias_vec, head_vec):
        normed = layer_norm(final_rows, gain_vec, bias_vec)
        per_row = jnp.sum(normed * (end_vals + head_vec), -1)
        return jnp.sum(jnp.where(positions == length - 1, per_row, 0.0)) * D ** (-0.5)

    partial, score_back = jax.vjp(score_terms, final, end_row, vector_master[8], vector_master[9], vector_master[10])
    scores = jnp.where(jnp.arange(n_seq) == seq_at, partial, 0.0)
    scores = sum_axis(sum_axis(sum_axis(scores[None], "section"), "ctx"), "shard")[0]

    def pair_loss(score_vals):
        return jnp.sum(softplus(score_vals[pairs[:, 1]] - score_vals[pairs[:, 0]]))

    loss_sum, loss_back = jax.vjp(pair_loss, scores)
    grad_scores = loss_back(jnp.ones_like(loss_sum))[0]
    grad_own = lax.dynamic_slice_in_dim(grad_scores, seq_at, 1, 0)[0]
    grad_final, grad_end, grad_gainf, grad_biasf, grad_head = score_back(grad_own)

    grad_x1, grads1, vec1 = layer_backward(saved1, grad_final, meta, n, weights1, vecs1)
    grad_x1 = grad_x1.astype(BF).astype(F32)
    grad_x0, grads0, vec0 = layer_backward(saved0, grad_x1, meta, n, weights0, vecs0)

    by_owner = grad_x0.astype(BF).T.reshape(n_dest, columns, rows)
    back = lax.all_to_all(by_owner, ("section", "ctx"), split_axis=0, concat_axis=0, tiled=True)
    every = lax.all_gather(back, "shard", axis=0, tiled=True)
    end_mine = jnp.where((jnp.arange(n_seq) == seq_at)[:, None], grad_end, 0.0)
    zero = jnp.zeros((D,), F32)
    vec_full = jnp.stack(vec0 + vec1 + [grad_gainf, grad_biasf, grad_head])
    vector_grad, end_grads = lax.psum((vec_full, end_mine), ALL)
    end_grads = lax.dynamic_slice(end_grads.astype(BF).astype(F32), (0, column_at), (n_seq, columns))
    table_grad = scatter(ids, meta_emb, owned, counts, every, end_grads, entries)

    own0 = lax.psum_scatter(grads0, order, scatter_dimension=0, tiled=True)
    own1 = lax.psum_scatter(grads1, order, scatter_dimension=0, tiled=True)
    got = swap(jnp.where(is_first, own1, own0), "section", 1)
    layer_grad = jnp.where(is_first, jnp.concatenate([own0, got]), jnp.concatenate([got, own1])).astype(F32)
    layer_grad = layer_grad.reshape(layer_master.shape)

    squares = (jnp.sum(layer_grad * layer_grad) + jnp.sum(table_grad * table_grad)).reshape(1, 1)
    squares = sum_axis(sum_axis(sum_axis(squares, "section"), "ctx"), "shard")[0, 0]
    grad_norm = jnp.sqrt(squares + jnp.sum(vector_grad * vector_grad))
    factor = CLIP_LIMIT / jnp.maximum(grad_norm, CLIP_LIMIT)
    layer_new = adam_update(layer_master, layer_first, layer_second, layer_grad * factor, 0.4, 0.1)
    table_new = adam_update(table_master, table_first, table_second, table_grad * factor, 0.5, 0.1)
    vector_new = adam_update(vector_master, vector_first, vector_second, vector_grad * factor, 0.7, 0.0)
    return (loss_sum, grad_norm, *layer_new, *table_new, *vector_new)


def solution(mesh):
    in_specs = (
        P("shard", "ctx"),
        P("shard"),
        P("shard"),
        P(),
        P("section", ("ctx", "shard")),
        P("section", ("ctx", "shard")),
        P("section", ("ctx", "shard")),
        P(("section", "ctx"), "shard"),
        P(("section", "ctx"), "shard"),
        P(("section", "ctx"), "shard"),
        P(),
        P(),
        P(),
    )
    out_specs = (
        P(),
        P(),
        P("section", ("ctx", "shard")),
        P("section", ("ctx", "shard")),
        P("section", ("ctx", "shard")),
        P(("section", "ctx"), "shard"),
        P(("section", "ctx"), "shard"),
        P(("section", "ctx"), "shard"),
        P(),
        P(),
        P(),
    )
    return jax.shard_map(shards, mesh=mesh, in_specs=in_specs, out_specs=out_specs, check_vma=False)
```

```python
import functools

import jax
import jax.numpy as jnp
from jax import lax
from jax.experimental import pallas as pl
from jax.experimental.pallas import tpu as pltpu
from jax.sharding import PartitionSpec as P

D = 1088
HEADS = 17
HD = 64
FF = 4352
VOCAB = 51200
MICRO = 2
STEP = 10
CLIP_LIMIT = 0.02
ALL = ("section", "ctx", "shard")

LANES = 128
PAIRS_OF_HEADS = (HEADS + 1) // 2
WIDE = PAIRS_OF_HEADS * LANES
N_UP = FF // D
U_OUT = 3 * D
U_UP = U_OUT + D
U_DOWN = U_UP + FF
UNITS = U_DOWN + FF

BF = jnp.bfloat16
F32 = jnp.float32
VMEM_BIG = 56 * 1024 * 1024


def params(limit=VMEM_BIG):
    return pltpu.CompilerParams(vmem_limit_bytes=limit)


def cost(microseconds):
    return pl.CostEstimate(flops=0, bytes_accessed=int(microseconds * 3.0e6), transcendentals=0)


def dot(a, b, contract=((1,), (0,))):
    return lax.dot_general(a, b, (contract, ((), ())), preferred_element_type=F32)


NT = ((1,), (1,))
TN = ((0,), (0,))


def split2(x):
    top = lax.reduce_precision(x, 8, 7)
    return jnp.concatenate([top, x - top]).astype(BF)


def dot2(x, w, contract=((1,), (0,))):
    y = dot(split2(x), w, contract)
    return y[: x.shape[0]] + y[x.shape[0] :]


def swap(x, axis, bit):
    size = lax.axis_size(axis)
    return lax.ppermute(x, axis, [(i, i ^ bit) for i in range(size)])


def gather_axis(x, axis):
    size = lax.axis_size(axis)
    me = lax.axis_index(axis)
    x = x[None]
    bit = 1
    while bit < size:
        other = swap(x, axis, bit)
        lower = (me & bit) == 0
        x = jnp.where(lower, jnp.concatenate([x, other]), jnp.concatenate([other, x]))
        bit *= 2
    return x


def sum_axis(x, axis, first=1, last=None):
    size = lax.axis_size(axis) if last is None else last
    bit = first
    while bit < size:
        x = x + swap(x, axis, bit)
        bit *= 2
    return x


def group_reduce(x, combine, half):
    def step(x, axis, bit):
        other = swap(x, axis, bit)
        lower = (lax.axis_index(axis) & bit) == 0
        return combine(jnp.where(lower, x, other), jnp.where(lower, other, x))

    x = step(x, "section", 1)
    bit = 1
    while bit < half:
        x = step(x, "ctx", bit)
        bit *= 2
    return x


def sum_all(x):
    return sum_axis(sum_axis(sum_axis(x, "section"), "ctx"), "shard")


def rows_kernel(pairs, x, out, scr):
    lane = lax.broadcasted_iota(jnp.int32, (1, LANES), 1)
    step = 2 * D // LANES
    even, odd = pl.ds(0, pairs, stride=2), pl.ds(1, pairs, stride=2)
    flat_row = lambda t: x[pl.ds(t, pairs, stride=step), :]
    for t in range(PAIRS_OF_HEADS):
        scr[t, even, :] = flat_row(t)
    before = pltpu.roll(flat_row(step // 2), HD, 1)
    for t in range(PAIRS_OF_HEADS - 1):
        after = pltpu.roll(flat_row(step // 2 + 1 + t), HD, 1)
        scr[t, odd, :] = jnp.where(lane < HD, before, after)
        before = after
    scr[PAIRS_OF_HEADS - 1, odd, :] = before
    for t, (at, size) in enumerate(tile_cuts()):
        out[:, pl.ds(at, size)] = scr[t][:, :size].astype(BF)


def chunk_rows(flat):
    units = flat.size // D
    return pl.pallas_call(
        functools.partial(rows_kernel, units // 2),
        out_shape=jax.ShapeDtypeStruct((units, D), BF),
        scratch_shapes=[pltpu.VMEM((PAIRS_OF_HEADS, units, LANES), F32)],
        compiler_params=params(),
        cost_estimate=cost(6),
        name="chunk_rows",
    )(flat.reshape(-1, LANES))


def small_block():
    return lax.axis_size("ctx") == 4 and lax.axis_size("shard") == 4 and lax.axis_size("section") == 2


def shift(x, axis, by):
    size = lax.axis_size(axis)
    return lax.ppermute(x, axis, [(i, (i + by) % size) for i in range(size)])


ARRIVALS = ((0,), (1, 3), (2,))
OVERLAP = 16


def place_kernel(rows, at, *refs):
    ins, out, held, sems_in, sems_out = refs[: 2 * len(ARRIVALS)], refs[-4], refs[-3], refs[-2], refs[-1]
    s, c, z = at[0], at[1], at[2]
    short = rows - OVERLAP
    pieces = []
    for g, distances in enumerate(ARRIVALS):
        for other in range(2):
            for e in range(4):
                for i, d in enumerate(distances):
                    chunk = (c ^ e) * 4 + lax.rem(z + 4 - d, 4)
                    pieces.append((ins[2 * g + other].at[e, i], chunk, other))

    def arrive(k):
        return pltpu.make_async_copy(pieces[k][0], held.at[k], sems_in.at[k])

    def leave(k, act):
        _, chunk, other = pieces[k]

        @pl.when(s == other)
        def _():
            act(pltpu.make_async_copy(held.at[k], out.at[chunk, pl.ds(0, rows)], sems_out.at[k]))

        @pl.when(s != other)
        def _():
            act(pltpu.make_async_copy(held.at[k, pl.ds(OVERLAP, short)], out.at[chunk, pl.ds(rows, short)], sems_out.at[k]))

    for k in range(len(pieces)):
        arrive(k).start()
    for k in range(len(pieces)):
        arrive(k).wait()
        leave(k, lambda copy: copy.start())
    for k in range(len(pieces)):
        leave(k, lambda copy: copy.wait())


def by_links(own):
    return swap(own, "ctx", 1), swap(own, "ctx", 2)


def first_moves(piece):
    return shift(piece, "shard", 1), shift(piece, "shard", 3), *by_links(piece[None])


def second_moves(piece, near, far):
    return shift(piece, "shard", 2), *by_links(jnp.stack([near, far]))


def gather_half(piece, first, second):
    rows = piece.shape[0]
    cut = rows // 2
    near, far, *own_links = first
    opposite, *near_links = second
    arrived = {0: piece, 1: near, 3: far, 2: opposite}
    parts = []
    for distances, links in zip(ARRIVALS, (own_links, near_links, None)):
        own = jnp.stack([arrived[d] for d in distances])
        by_x, by_y = by_links(own) if links is None else links
        corner = jnp.concatenate([swap(by_x[:, :cut], "ctx", 2), swap(by_y[:, cut:], "ctx", 1)], axis=1)
        parts.append(jnp.stack([own, by_x, by_y, corner]))
    return parts


def place_units(parts):
    rows = parts[0].shape[2]
    at = jnp.stack([lax.axis_index(a) for a in ALL]).astype(jnp.int32)
    grid_spec = pltpu.PrefetchScalarGridSpec(
        num_scalar_prefetch=1,
        grid=(1,),
        in_specs=[pl.BlockSpec(memory_space=pl.ANY)] * len(parts),
        out_specs=pl.BlockSpec(memory_space=pl.ANY),
        scratch_shapes=[pltpu.VMEM((32, rows, D), BF), pltpu.SemaphoreType.DMA((32,)), pltpu.SemaphoreType.DMA((32,))],
    )
    whole = pl.pallas_call(
        functools.partial(place_kernel, rows),
        grid_spec=grid_spec,
        out_shape=jax.ShapeDtypeStruct((16, 2 * rows - OVERLAP, D), BF),
        compiler_params=params(),
        cost_estimate=cost(16),
        name="place",
    )(at, *parts)
    return whole.reshape(UNITS, D)


def add_low(x, y):
    return (x.astype(F32) + y.astype(F32)).astype(BF)


BLOCK = 136


def fold_cores(region):
    s = lax.axis_index("section")
    blocks = region.reshape(-1, 2, BLOCK, D)
    pick = lambda i: lax.dynamic_index_in_dim(blocks, i, 1, keepdims=False)
    return add_low(pick(s), swap(pick(1 - s), "section", 1))


def one_way(x, bit, sends):
    return lax.ppermute(x, "ctx", [(i, i ^ bit) for i in range(4) if sends(i)])


def three_first(one, two, both, p):
    has_p = (lax.axis_index("ctx") & p) != 0
    return swap(jnp.where(has_p, two, one), "ctx", p), one_way(both, p, lambda i: not i & p)


def three_second(one, two, both, came, came_both, p, q):
    c = lax.axis_index("ctx")
    has_p, has_q = (c & p) != 0, (c & q) != 0
    single = add_low(jnp.where(has_p, one, two), came)
    both = add_low(both, came_both)
    sent = jnp.where(has_p & ~has_q, both, single)
    came = one_way(sent, q, lambda i: not i & q or i & p)
    return add_low(jnp.where(has_p & has_q, both, single), came)


def fold_one(x, p, q):
    x = add_low(x, one_way(x, p, lambda i: i & p))
    return add_low(x, one_way(x, q, lambda i: i & q and not i & p))


def rest_first(rest):
    x = rest.reshape(3, 4, -1, BLOCK, D)
    return *three_first(x[0, :2], x[1, :2], x[2, :2], 1), *three_first(x[1, 2:], x[0, 2:], x[2, 2:], 2)


def rest_second(rest, came):
    x = rest.reshape(3, 4, -1, BLOCK, D)
    first = three_second(x[0, :2], x[1, :2], x[2, :2], came[0], came[1], 1, 2)
    second = three_second(x[1, 2:], x[0, 2:], x[2, 2:], came[2], came[3], 2, 1)
    return jnp.concatenate([first, second])


def fold_qkv(qkv):
    x = qkv.reshape(4, -1, BLOCK, D)
    return jnp.concatenate([fold_one(x[:2], 1, 2), fold_one(x[2:], 2, 1)])


def along_shard(x):
    z = lax.axis_index("shard")
    pick = lambda i: lax.dynamic_index_in_dim(x, lax.rem(i, 4), 0, keepdims=False)
    return [pick(z)] + [shift(pick(z + d), "shard", d) for d in (1, 3, 2)]


def finish_units(terms):
    mine = sum(t.astype(F32) for t in terms)
    other = swap(mine.astype(BF), "section", 1).astype(F32)
    return jnp.stack([mine, other], axis=1).reshape(-1, D)


SHIFT = 10
UNROLL = 8


def owned_rows(ids, entries):
    rows = ids.shape[1]
    assert rows < (1 << SHIFT)
    owned = ids < entries
    place = jnp.cumsum(owned.astype(jnp.int32), axis=1) - 1
    packed = jnp.arange(rows, dtype=jnp.int32)[None, :] + (ids << SHIFT)
    slots = jnp.arange(rows, dtype=jnp.int32)
    hit = (place[:, None, :] == slots[None, :, None]) & owned[:, None, :]
    listed = jnp.sum(jnp.where(hit, packed[:, None, :], 0), axis=2)
    count = jnp.sum(owned.astype(jnp.int32), axis=1)
    listed = jnp.where(slots[None, :] < count[:, None], listed, rows + (entries << SHIFT))
    return listed.reshape(-1), count


def for_owned(listed, counts, step, rows, body):
    def some(t, _):
        for u in range(UNROLL):
            packed = listed[step * rows + t * UNROLL + u]
            body(pl.ds(packed & ((1 << SHIFT) - 1), 1), pl.ds(packed >> SHIFT, 1))
        return 0

    lax.fori_loop(0, (counts[step] + UNROLL - 1) // UNROLL, some, 0)


def lookup_kernel(rows, listed, counts, end_ids, meta, table, out, ends, tab, buf):
    step = pl.program_id(0)
    columns, entries = table.shape

    @pl.when(step == 0)
    def _():
        def turn(i, _):
            at = pl.multiple_of(i * 256, 256)
            tab[pl.ds(at, 256), :] = table[:, pl.ds(at, 256)].astype(BF).astype(F32).T
            return 0

        lax.fori_loop(0, entries // 256, turn, 0)
        tab[pl.ds(entries, 8), :] = jnp.zeros((8, columns), F32)
        for n in range(ends.shape[0]):
            ends[pl.ds(n, 1), :] = tab[pl.ds(end_ids[n], 1), :]

    buf[...] = jnp.zeros_like(buf)

    def pick(place, entry):
        buf[place, :] = tab[entry, :]

    for_owned(listed, counts, step, rows, pick)

    @pl.when(meta[0] == 1)
    def _():
        half = rows // 2
        group = meta[4 + step]
        for j in range(2):
            block = group if j == 0 else 2 * meta[1] - 1 - group
            at = pl.multiple_of(meta[2] + block * half, 8)
            buf[pl.ds(j * half, half), :] += tab[pl.ds(at, half), :]

    out[0] = buf[pl.ds(0, rows), :].T.astype(BF)


def lookup(listed, counts, end_ids, meta, table, n_blocks, rows):
    columns, entries = table.shape
    n_ends = end_ids.shape[0]
    grid_spec = pltpu.PrefetchScalarGridSpec(
        num_scalar_prefetch=4,
        grid=(n_blocks,),
        in_specs=[pl.BlockSpec((columns, entries), lambda i, *_: (0, 0))],
        out_specs=[
            pl.BlockSpec((1, columns, rows), lambda i, *_: (i, 0, 0)),
            pl.BlockSpec((n_ends, columns), lambda i, *_: (0, 0)),
        ],
        scratch_shapes=[pltpu.VMEM((entries + 8, columns), F32), pltpu.VMEM((rows + 8, columns), F32)],
    )
    return pl.pallas_call(
        functools.partial(lookup_kernel, rows),
        grid_spec=grid_spec,
        out_shape=[
            jax.ShapeDtypeStruct((n_blocks, columns, rows), BF),
            jax.ShapeDtypeStruct((n_ends, columns), F32),
        ],
        compiler_params=params(),
        cost_estimate=cost(40),
        name="lookup",
    )(listed, counts, end_ids, meta, table)


def scatter_kernel(rows, n_blocks, listed, counts, end_ids, meta, grads, ends, out, acc, buf):
    step = pl.program_id(0)
    columns, entries = out.shape
    n_ends = ends.shape[0]

    @pl.when(step == 0)
    def _():
        def clear(i, _):
            acc[pl.ds(pl.multiple_of(i * 256, 256), 256), :] = jnp.zeros((256, columns), F32)
            return 0

        lax.fori_loop(0, entries // 256, clear, 0)
        for n in range(n_ends):
            at = pl.ds(end_ids[n], 1)
            acc[at, :] += ends[pl.ds(n, 1), :]

    buf[pl.ds(0, rows), :] = grads[0].astype(F32).T

    def add(place, entry):
        acc[entry, :] += buf[place, :]

    for_owned(listed, counts, step, rows, add)

    @pl.when(meta[0] == 1)
    def _():
        half = rows // 2
        group = meta[4 + step]
        for j in range(2):
            block = group if j == 0 else 2 * meta[1] - 1 - group
            at = pl.multiple_of(meta[2] + block * half, 8)
            acc[pl.ds(at, half), :] += buf[pl.ds(j * half, half), :]

    @pl.when(step == n_blocks - 1)
    def _():
        def turn(i, _):
            at = pl.multiple_of(i * 256, 256)
            out[:, pl.ds(at, 256)] = acc[pl.ds(at, 256), :].T
            return 0

        lax.fori_loop(0, entries // 256, turn, 0)


def scatter(listed, counts, end_ids, meta, grads, ends, entries):
    n_blocks, columns, rows = grads.shape
    n_ends = ends.shape[0]
    grid_spec = pltpu.PrefetchScalarGridSpec(
        num_scalar_prefetch=4,
        grid=(n_blocks,),
        in_specs=[
            pl.BlockSpec((1, columns, rows), lambda i, *_: (i, 0, 0)),
            pl.BlockSpec((n_ends, columns), lambda i, *_: (0, 0)),
        ],
        out_specs=pl.BlockSpec((columns, entries), lambda i, *_: (0, 0)),
        scratch_shapes=[pltpu.VMEM((entries + 8, columns), F32), pltpu.VMEM((rows + 8, columns), F32)],
    )
    return pl.pallas_call(
        functools.partial(scatter_kernel, rows, n_blocks),
        grid_spec=grid_spec,
        out_shape=jax.ShapeDtypeStruct((columns, entries), F32),
        compiler_params=params(),
        cost_estimate=cost(42),
        name="scatter",
    )(listed, counts, end_ids, meta, grads, ends)


def tile_cuts():
    return [(t * LANES, min(LANES, D - t * LANES)) for t in range(PAIRS_OF_HEADS)]


def split_kernel(count, rb, width, u, out, scr):
    for t, (at, size) in enumerate(tile_cuts()):
        part = u[:, pl.ds(at, size)].astype(F32)
        if size < LANES:
            part = jnp.concatenate([part, jnp.zeros((rb * count, LANES - size), F32)], axis=1)
        scr[t] = part
        for j in range(count):
            picked = scr[t, pl.ds(j, rb, stride=count), :].astype(BF)
            take = min(LANES, width - at)
            out[j, :, pl.ds(at, take)] = picked[:, :take]


def split_units(u, first, count, width=D):
    rb = 272
    return pl.pallas_call(
        functools.partial(split_kernel, count, rb, width),
        grid=(D // rb,),
        in_specs=[pl.BlockSpec((rb * count, D), lambda i: (i + first // (rb * count), 0))],
        out_specs=pl.BlockSpec((count, rb, width), lambda i: (0, i, 0)),
        out_shape=jax.ShapeDtypeStruct((count, D, width), BF),
        scratch_shapes=[pltpu.VMEM((PAIRS_OF_HEADS, rb * count, LANES), F32)],
        compiler_params=params(),
        cost_estimate=cost(8),
        name="split_units",
    )(u)


def merge_kernel(count, rb, *refs):
    parts, out, scr = refs[:count], refs[count], refs[count + 1]
    for t, (at, size) in enumerate(tile_cuts()):
        for j in range(count):
            part = parts[j][:, pl.ds(at, size)].astype(F32)
            if size < LANES:
                part = jnp.concatenate([part, jnp.zeros((rb, LANES - size), F32)], axis=1)
            scr[t, pl.ds(j, rb, stride=count), :] = part
        out[:, pl.ds(at, size)] = scr[t][:, :size].astype(BF)


def merge_units(parts):
    rb, count = 272, len(parts)
    return pl.pallas_call(
        functools.partial(merge_kernel, count, rb),
        grid=(D // rb,),
        in_specs=[pl.BlockSpec((rb, p.shape[1]), lambda i: (i, 0)) for p in parts],
        out_specs=pl.BlockSpec((rb * count, D), lambda i: (i, 0)),
        out_shape=jax.ShapeDtypeStruct((count * D, D), BF),
        scratch_shapes=[pltpu.VMEM((PAIRS_OF_HEADS, rb * count, LANES), F32)],
        compiler_params=params(),
        cost_estimate=cost(8),
        name="merge_units",
    )(*parts)


def chunk_plan(n):
    plan = [(0, "ll", True), (0, "hl", False), (0, "hh", True)]
    for p in range(1, n):
        plan += [(p, "hl", False), (p, "sel", False)]
    return plan


def chunk_offsets(meta, n, hb, p, kind):
    own = meta[0]
    piece = meta[2 + p]
    if kind == "ll":
        return 0, p * 2 * hb, own * hb, piece * hb, True
    if kind == "hl":
        return hb, p * 2 * hb, (2 * n - 1 - own) * hb, piece * hb, False
    if kind == "hh":
        return hb, p * 2 * hb + hb, (2 * n - 1 - own) * hb, (2 * n - 1 - piece) * hb, False
    low = piece < own
    q_off = pl.multiple_of(jnp.where(low, 0, hb), hb)
    k_off = pl.multiple_of(p * 2 * hb + jnp.where(low, 0, hb), hb)
    key_pos = jnp.where(low, piece, 2 * n - 1 - piece) * hb
    return q_off, k_off, None, key_pos, low


def chunk_scores(keys, queries, meta, diagonal, kind, q_pos, k_pos, hb):
    s = dot(keys, queries, NT)
    if diagonal:
        ki = lax.broadcasted_iota(jnp.int32, (hb, hb), 0)
        qi = lax.broadcasted_iota(jnp.int32, (hb, hb), 1)
        keep = (ki <= qi) & (ki + k_pos < meta[1])
        s = jnp.where(keep, s, -1e30)
    elif kind == "sel":
        ki = lax.broadcasted_iota(jnp.int32, (hb, hb), 0)
        s = jnp.where(ki < meta[1] - k_pos, s, -1e30)
    return s


def attend_kernel(n, hb, meta, q_ref, k_ref, v_ref, o_ref, lse_ref, vt_ref):
    keys = 2 * hb * n
    for i in range(keys // hb):
        vt_ref[i] = v_ref[pl.ds(i * hb, hb), :].astype(F32).T.astype(BF)
    lane = lax.broadcasted_iota(jnp.int32, (1, LANES), 1)
    plan = chunk_plan(n)
    outs = []
    for head in range(2):
        own_lanes = (lane // HD) == head
        info, scores = [], []
        tops = [jnp.full((1, hb), -3e38, F32), jnp.full((1, hb), -3e38, F32)]
        for p, kind, diagonal in plan:
            q_off, k_off, q_pos, k_pos, low = chunk_offsets(meta, n, hb, p, kind)
            queries = jnp.where(own_lanes, q_ref[pl.ds(q_off, hb), :], 0)
            s = chunk_scores(k_ref[pl.ds(k_off, hb), :], queries, meta, diagonal, kind, q_pos, k_pos, hb)
            top = jnp.max(s, axis=0, keepdims=True)
            if low is True:
                tops[0] = jnp.maximum(tops[0], top)
            elif low is False:
                tops[1] = jnp.maximum(tops[1], top)
            else:
                tops[0] = jnp.maximum(tops[0], jnp.where(low, top, -3e38))
                tops[1] = jnp.maximum(tops[1], jnp.where(low, -3e38, top))
            info.append((k_off, low))
            scores.append(s)
        sums = [jnp.zeros((1, hb), F32), jnp.zeros((1, hb), F32)]
        accs = [jnp.zeros((HD, hb), F32), jnp.zeros((HD, hb), F32)]
        for (k_off, low), s in zip(info, scores):
            if low is True or low is False:
                top = tops[0] if low else tops[1]
            else:
                top = jnp.where(low, tops[0], tops[1])
            e = jnp.exp(s - top)
            total = jnp.sum(e, axis=0, keepdims=True)
            got = dot(vt_ref[k_off // hb, pl.ds(head * HD, HD), :], e.astype(BF))
            if low is True or low is False:
                sums[1 - low] += total
                accs[1 - low] += got
            else:
                sums[0] += jnp.where(low, total, 0.0)
                sums[1] += jnp.where(low, 0.0, total)
                accs[0] += jnp.where(low, got, 0.0)
                accs[1] += jnp.where(low, 0.0, got)
        outs.append([accs[i] / sums[i] for i in range(2)])
        for i in range(2):
            lse_ref[0, pl.ds(head, 1), pl.ds(i * hb, hb)] = tops[i] + jnp.log(sums[i])
    for i in range(2):
        both = jnp.concatenate([outs[0][i], outs[1][i]], axis=0)
        o_ref[pl.ds(i * hb, hb), :] = both.T.astype(BF)


def attend(meta, q, k, v, n):
    rows = q.shape[0]
    keys = k.shape[0]
    grid_spec = pltpu.PrefetchScalarGridSpec(
        num_scalar_prefetch=1,
        grid=(PAIRS_OF_HEADS,),
        in_specs=[
            pl.BlockSpec((rows, LANES), lambda p, *_: (0, p)),
            pl.BlockSpec((keys, LANES), lambda p, *_: (0, p)),
            pl.BlockSpec((keys, LANES), lambda p, *_: (0, p)),
        ],
        out_specs=[
            pl.BlockSpec((rows, LANES), lambda p, *_: (0, p)),
            pl.BlockSpec((1, 8, rows), lambda p, *_: (p, 0, 0)),
        ],
        scratch_shapes=[pltpu.VMEM((2 * n, LANES, rows // 2), BF)],
    )
    return pl.pallas_call(
        functools.partial(attend_kernel, n, rows // 2),
        grid_spec=grid_spec,
        out_shape=[
            jax.ShapeDtypeStruct((rows, WIDE), BF),
            jax.ShapeDtypeStruct((PAIRS_OF_HEADS, 8, rows), F32),
        ],
        compiler_params=params(),
        cost_estimate=cost(23),
        name="attend",
    )(meta, q, k, v)


def attend_back_kernel(n, hb, meta, q_ref, k_ref, v_ref, o_ref, do_ref, lse_ref, dq_ref, dk_ref, dv_ref, kt_ref, dk_acc, dv_acc):
    keys = 2 * hb * n
    for i in range(keys // hb):
        kt_ref[i] = k_ref[pl.ds(i * hb, hb), :].astype(F32).T.astype(BF)
    dk_acc[...] = jnp.zeros_like(dk_acc)
    dv_acc[...] = jnp.zeros_like(dv_acc)
    lane = lax.broadcasted_iota(jnp.int32, (1, LANES), 1)
    plan = chunk_plan(n)
    prods = []
    for i in range(2):
        part = pl.ds(i * hb, hb)
        prods.append((o_ref[part, :].astype(F32) * do_ref[part, :].astype(F32)).T)
    dqs = []
    for head in range(2):
        own_lanes = (lane // HD) == head
        deltas = [jnp.sum(prods[i][head * HD : (head + 1) * HD, :], axis=0, keepdims=True) for i in range(2)]
        lses = [lse_ref[0, pl.ds(head, 1), pl.ds(i * hb, hb)] for i in range(2)]
        accs = [jnp.zeros((HD, hb), F32), jnp.zeros((HD, hb), F32)]
        for p, kind, diagonal in plan:
            q_off, k_off, q_pos, k_pos, low = chunk_offsets(meta, n, hb, p, kind)
            q_at, k_at = pl.ds(q_off, hb), pl.ds(k_off, hb)
            queries = jnp.where(own_lanes, q_ref[q_at, :], 0)
            d_out = jnp.where(own_lanes, do_ref[q_at, :], 0)
            s = chunk_scores(k_ref[k_at, :], queries, meta, diagonal, kind, q_pos, k_pos, hb)
            if low is True or low is False:
                lse, delta = lses[1 - low], deltas[1 - low]
            else:
                lse, delta = jnp.where(low, lses[0], lses[1]), jnp.where(low, deltas[0], deltas[1])
            prob = jnp.exp(s - lse)
            d_prob = dot(v_ref[k_at, :], d_out, NT)
            d_score = (prob * (d_prob - delta)).astype(BF)
            dv_acc[k_at, :] += dot(prob.astype(BF), d_out)
            dk_acc[k_at, :] += dot(d_score, queries)
            got = dot(kt_ref[k_off // hb, pl.ds(head * HD, HD), :], d_score)
            if low is True or low is False:
                accs[1 - low] += got
            else:
                accs[0] += jnp.where(low, got, 0.0)
                accs[1] += jnp.where(low, 0.0, got)
        dqs.append(accs)
    for i in range(2):
        both = jnp.concatenate([dqs[0][i], dqs[1][i]], axis=0) * 0.125
        dq_ref[pl.ds(i * hb, hb), :] = both.T.astype(BF)
    dk_ref[...] = dk_acc[...].astype(BF)
    dv_ref[...] = dv_acc[...].astype(BF)


def attend_back(meta, q, k, v, o, d_o, lse, n):
    rows = q.shape[0]
    keys = k.shape[0]
    row_spec = pl.BlockSpec((rows, LANES), lambda p, *_: (0, p))
    key_spec = pl.BlockSpec((keys, LANES), lambda p, *_: (0, p))
    grid_spec = pltpu.PrefetchScalarGridSpec(
        num_scalar_prefetch=1,
        grid=(PAIRS_OF_HEADS,),
        in_specs=[row_spec, key_spec, key_spec, row_spec, row_spec, pl.BlockSpec((1, 8, rows), lambda p, *_: (p, 0, 0))],
        out_specs=[row_spec, key_spec, key_spec],
        scratch_shapes=[pltpu.VMEM((2 * n, LANES, rows // 2), BF), pltpu.VMEM((keys, LANES), F32), pltpu.VMEM((keys, LANES), F32)],
    )
    return pl.pallas_call(
        functools.partial(attend_back_kernel, n, rows // 2),
        grid_spec=grid_spec,
        out_shape=[
            jax.ShapeDtypeStruct((rows, WIDE), BF),
            jax.ShapeDtypeStruct((keys, WIDE), BF),
            jax.ShapeDtypeStruct((keys, WIDE), BF),
        ],
        compiler_params=params(),
        cost_estimate=cost(46),
        name="attend_back",
    )(meta, q, k, v, o, d_o, lse)


def layer_norm(values, gain_vec, bias_vec):
    row_mean = jnp.mean(values, -1, keepdims=True)
    centred = values - row_mean
    variance = jnp.mean(centred * centred, -1, keepdims=True)
    return centred * lax.rsqrt(variance + 1e-05) * gain_vec + bias_vec


def gelu_tanh(values):
    return 0.5 * values * (1.0 + jnp.tanh(0.7978845608 * (values + 0.044715 * values * values * values)))


def softplus(values):
    return jnp.maximum(values, 0.0) + jnp.log1p(jnp.exp(-jnp.abs(values)))


def adam_update(weight, first, second, grad, rate, decay):
    first = 0.9 * first + 0.1 * grad
    second = 0.95 * second + 0.05 * grad * grad
    first_hat = first / (1.0 - 0.9**STEP)
    second_hat = second / (1.0 - 0.95**STEP)
    weight = weight - rate * (first_hat / (jnp.sqrt(second_hat) + 1e-08) + decay * weight)
    return (weight, first, second)


def pieces_of(x, half):
    got = [x]
    bit = 1
    while bit < half:
        got += [swap(y, "ctx", bit) for y in got]
        bit *= 2
    own = jnp.concatenate(got)
    return jnp.concatenate([own, swap(own, "section", 1)])


def sum_pieces(near, far, half):
    rows = near.shape[0] // half
    x = near + swap(far, "section", 1).astype(F32)
    bit = half // 2
    while bit >= 1:
        keep, send = x[: bit * rows], x[bit * rows : 2 * bit * rows]
        x = keep + swap(send.astype(BF), "ctx", bit).astype(F32)
        bit //= 2
    return x


def layer_weights(units):
    w_qkv = split_units(units, 0, 3, WIDE)
    w_out = units[U_OUT:U_UP]
    w_up = split_units(units, U_UP, N_UP)
    w_down = units[U_DOWN:].reshape(N_UP, D, D)
    return w_qkv, w_out, w_up, w_down


def layer_forward(values, hidden1, all_hidden1, meta, n, weights, vecs):
    w_qkv, w_out, w_up, w_down = weights
    keys = dot(all_hidden1, w_qkv[1]).astype(BF)
    vals = dot(all_hidden1, w_qkv[2]).astype(BF)
    queries = dot(hidden1, w_qkv[0]).astype(BF) * jnp.asarray(0.125, BF)
    attended, lse = attend(meta, queries, keys, vals, n)
    middle = values + dot(attended[:, :D], w_out)
    hidden2 = layer_norm(middle, vecs[2], vecs[3]).astype(BF)
    ups = [dot(hidden2, w_up[j]) for j in range(N_UP)]
    gated = [gelu_tanh(u).astype(BF) for u in ups]
    result = middle
    for j in range(N_UP):
        result = result + dot(gated[j], w_down[j])
    return result, (values, all_hidden1, queries, keys, vals, attended, lse, middle, hidden2, ups, gated)


def layer_backward(saved, grad_out, meta, n, weights, vecs, fast):
    values, all_hidden1, queries, keys, vals, attended, lse, middle, hidden2, ups, gated = saved
    w_qkv, w_out, w_up, w_down = weights
    grad_ffn = grad_out.astype(BF)
    grad_down = [dot(gated[j], grad_ffn, TN).astype(BF) for j in range(N_UP)]
    grad_ups = []
    for j in range(N_UP):
        _, back = jax.vjp(gelu_tanh, ups[j])
        grad_ups.append(back(dot(grad_ffn, w_down[j], NT))[0].astype(BF))
    grad_up = merge_units([dot(hidden2, grad_ups[j], TN).astype(BF) for j in range(N_UP)])
    grad_hidden2 = sum(dot(grad_ups[j], w_up[j], NT) for j in range(N_UP))
    _, norm_back2 = jax.vjp(layer_norm, middle, vecs[2], vecs[3])
    grad_norm2, grad_gain2, grad_bias2 = norm_back2(grad_hidden2)
    grad_middle = grad_out + grad_norm2
    grad_branch = grad_middle.astype(BF)
    grad_outw = dot(attended[:, :D], grad_branch, TN).astype(BF)
    grad_att = dot(grad_branch, jnp.pad(w_out, ((0, WIDE - D), (0, 0))), NT).astype(BF)
    if fast:
        rest = jnp.concatenate([fold_cores(grad_outw), fold_cores(grad_up)] + [fold_cores(g) for g in grad_down])
        grad_att, rest = lax.optimization_barrier((grad_att, rest))
        came = rest_first(rest)
    grad_q, part_k, part_v = attend_back(meta, queries, keys, vals, attended, grad_att, lse, n)
    rows, near = grad_q.shape[0], part_k.shape[0] // 2
    def to_hidden1(at):
        return dot(part_k[at], w_qkv[1], NT) + dot(part_v[at], w_qkv[2], NT)

    far = to_hidden1(slice(near, None)).astype(BF)
    if fast:
        far, *came = lax.optimization_barrier((far, *came))
    grad_q, part_k, part_v, far = lax.optimization_barrier((grad_q, part_k, part_v, far))
    close = to_hidden1(slice(0, near))
    close, grad_q, part_k, part_v = lax.optimization_barrier((close, grad_q, part_k, part_v))
    grad_hidden1 = sum_pieces(close, far, n // 2)
    grad_hidden1 = grad_hidden1 + dot(grad_q, w_qkv[0], NT)
    _, norm_back1 = jax.vjp(layer_norm, values, vecs[0], vecs[1])
    grad_norm1, grad_gain1, grad_bias1 = norm_back1(grad_hidden1)
    grad_input = grad_middle + grad_norm1
    pairs_qkv = [(all_hidden1[:rows], grad_q), (all_hidden1, part_k), (all_hidden1, part_v)]
    grad_qkvw = merge_units([dot(h, g, TN).astype(BF) for h, g in pairs_qkv])
    if fast:
        summed = rest_second(rest, came), fold_cores(grad_qkvw)
    else:
        summed = jnp.concatenate([grad_qkvw, grad_outw, grad_up, *grad_down])
    return grad_input, summed, [grad_gain1, grad_bias1, grad_gain2, grad_bias2]


def head_mask():
    head = lax.broadcasted_iota(jnp.int32, (HEADS, D), 0)
    return lax.broadcasted_iota(jnp.int32, (HEADS, D), 1) // HD == head


def last_forward(values, positions, length, half, weights, vecs):
    (w_q, w_k, w_v), w_out, w_up, w_down = weights
    heads = head_mask()
    hidden1 = layer_norm(values, vecs[0], vecs[1]).astype(BF)
    mine = (positions == length - 1)[:, None]
    row = jnp.sum(jnp.where(mine, values, 0.0), axis=0, keepdims=True)
    row = group_reduce(row, jnp.add, half)
    row_h1 = layer_norm(row, vecs[0], vecs[1]).astype(BF)
    query = dot(row_h1, w_q).astype(BF)
    wq = dot(jnp.where(heads, query, 0), w_k, NT) * 0.125
    scores = dot2(wq, hidden1, NT)
    scores = jnp.where((positions < length)[None, :], scores, -1e30)
    top = jnp.max(scores, axis=1, keepdims=True)
    expo = jnp.exp(scores - top)
    total = jnp.sum(expo, axis=1, keepdims=True)
    mixed = dot(expo.astype(BF), hidden1)
    wide = lambda x: jnp.broadcast_to(x, (HEADS, HD))

    def merge(x, y):
        high = jnp.maximum(x[:, D : D + 1], y[:, D : D + 1])
        x = x * jnp.exp(x[:, D : D + 1] - high)
        y = y * jnp.exp(y[:, D : D + 1] - high)
        return jnp.concatenate([x[:, :D] + y[:, :D], wide(high), x[:, D + HD :] + y[:, D + HD :]], axis=1)

    merged = group_reduce(jnp.concatenate([mixed, wide(top), wide(total)], axis=1), merge, half)
    top, total = merged[:, D : D + 1], merged[:, D + HD : D + HD + 1]
    mixed = merged[:, :D] / total
    probs = jnp.exp(scores - top) / total
    att = jnp.sum(jnp.where(heads, dot2(mixed, w_v), 0.0), axis=0, keepdims=True)
    middle = row + dot(att.astype(BF), w_out)
    hidden2 = layer_norm(middle, vecs[2], vecs[3]).astype(BF)
    ups = jnp.concatenate([dot(hidden2, w_up[j]) for j in range(N_UP)], axis=1)
    gated = gelu_tanh(ups).astype(BF)
    result = middle + dot(gated, w_down)
    return result, (values, hidden1, mine, row_h1, query, wq, probs, mixed, att, middle, hidden2, ups, gated)


def last_backward(saved, grad_out, half, weights, vecs):
    values, hidden1, mine, row_h1, query, wq, probs, mixed, att, middle, hidden2, ups, gated = saved
    (w_q, w_k, w_v), w_out, w_up, w_down = weights
    heads = head_mask()
    grad_ffn = grad_out.astype(BF)
    _, back = jax.vjp(gelu_tanh, ups)
    grad_ups = back(dot(grad_ffn, w_down, NT))[0].astype(BF)
    grad_hidden2 = sum(dot(grad_ups[:, j * D : (j + 1) * D], w_up[j], NT) for j in range(N_UP))
    _, norm_back2 = jax.vjp(layer_norm, middle, vecs[2], vecs[3])
    grad_norm2, grad_gain2, grad_bias2 = norm_back2(grad_hidden2)
    grad_middle = grad_out + grad_norm2
    grad_branch = grad_middle.astype(BF)
    grad_att = dot(grad_branch, w_out, NT).astype(BF)
    att_heads = jnp.where(heads, grad_att, 0)
    wv = dot(att_heads, w_v, NT)
    grad_prob = dot2(wv, hidden1, NT)
    delta = jnp.sum(att_heads.astype(F32) * att, axis=1, keepdims=True)
    grad_score = (probs * (grad_prob - delta)).astype(BF)
    summed = group_reduce(dot(grad_score, hidden1), jnp.add, half)
    grad_query = (jnp.sum(jnp.where(heads, dot2(summed, w_k), 0.0), axis=0, keepdims=True) * 0.125).astype(BF)
    low_probs = probs.astype(BF)
    grad_hidden1 = dot(
        jnp.concatenate([grad_score, grad_score, low_probs, low_probs]), jnp.concatenate([split2(wq), split2(wv)]), TN
    )
    grad_hidden1 = grad_hidden1 + jnp.where(mine, dot(grad_query, w_q, NT), 0.0)
    _, norm_back1 = jax.vjp(layer_norm, values, vecs[0], vecs[1])
    grad_norm1, grad_gain1, grad_bias1 = norm_back1(grad_hidden1)
    grad_input = grad_norm1 + jnp.where(mine, grad_middle, 0.0)
    query8 = query * jnp.asarray(0.125, BF)
    factors = [row_h1, grad_query, query8, grad_att, att, grad_branch, hidden2, grad_ffn]
    factors += [grad_ups.reshape(N_UP, D), gated.reshape(N_UP, D), summed, mixed]
    factors = jnp.concatenate([f.astype(BF) for f in factors])
    return grad_input, factors, [grad_gain1, grad_bias1], [grad_gain2, grad_bias2]


def last_gradient(data, chunk_at, n_chunks, size):
    n_seq = data.shape[0]
    heads = head_mask()
    row_h1, grad_query, query8, grad_att, att, grad_branch, hidden2, grad_ffn = [data[:, i] for i in range(8)]
    at = 8
    grad_ups, gated = data[:, at : at + N_UP], data[:, at + N_UP : at + 2 * N_UP]
    at += 2 * N_UP
    summed, mixed = data[:, at : at + HEADS], data[:, at + HEADS : at + 2 * HEADS]

    def by_unit(parts):
        count, width = len(parts), sum(p.shape[0] for p in parts)
        slot = jnp.concatenate([jnp.full((p.shape[0],), j, jnp.int32) for j, p in enumerate(parts)])
        both = jnp.concatenate(parts).T
        spread = jnp.where(slot[None, None, :] == jnp.arange(count)[None, :, None], both[:, None, :], 0)
        return spread.reshape(count * D, width)

    def per_head(x):
        return jnp.where(heads[None], x[:, None, :], 0).reshape(n_seq * HEADS, D)

    left = by_unit([row_h1, summed.reshape(-1, D), mixed.reshape(-1, D)])
    right = jnp.concatenate([grad_query, per_head(query8), per_head(grad_att)])
    first = chunk_at * size
    qkv = dot(lax.dynamic_slice_in_dim(left, jnp.minimum(first, U_OUT - size), size, 0), right)
    lefts = [att.T, by_unit([hidden2] * N_UP), gated.reshape(n_seq, FF).T]
    rights = [grad_branch, grad_ups.transpose(1, 0, 2).reshape(-1, D), grad_ffn]
    width = sum(x.shape[1] for x in lefts)
    columns, before = [], 0
    for x in lefts:
        columns.append(jnp.pad(x, ((0, 0), (before, width - before - x.shape[1]))))
        before += x.shape[1]
    left = jnp.concatenate(columns)
    rest = dot(lax.dynamic_slice_in_dim(left, jnp.maximum(first - U_OUT, 0), size, 0), jnp.concatenate(rights))
    return jnp.where(first < U_OUT, qkv, rest)


def shards(
    tokens,
    lengths,
    end_ids,
    pairs,
    layer_master,
    layer_first,
    layer_second,
    table_master,
    table_first,
    table_second,
    vector_master,
    vector_first,
    vector_second,
):
    rows = tokens.shape[1]
    s_at = lax.axis_index("section")
    c_at = lax.axis_index("ctx")
    z_at = lax.axis_index("shard")
    n_section = lax.axis_size("section")
    n = lax.axis_size("ctx")
    n_shard = lax.axis_size("shard")
    half = n // 2
    hb = rows // 2
    n_dest = n_section * n
    n_seq = MICRO * n_shard
    columns, entries = table_master.shape
    is_first = s_at == 0
    seq_in = c_at // half
    seq_at = z_at * MICRO + seq_in
    group = (c_at % half) * 2 + s_at

    fast = small_block()
    chunk = chunk_rows(layer_master) if fast else layer_master.reshape(-1, D).astype(BF)
    size = chunk.shape[0]
    cut = size // 2
    if fast:
        wide = cut + OVERLAP // 2
        got = swap(jnp.where(is_first, chunk[size - wide :], chunk[:wide]), "section", 1)
        piece0 = jnp.where(is_first, chunk[:wide], got)
        piece1 = jnp.where(is_first, got[:cut], chunk[cut:])
    else:
        got = swap(jnp.where(is_first, chunk[cut:], chunk[:cut]), "section", 1)
        piece0 = jnp.where(is_first, chunk[:cut], got)
        piece1 = jnp.where(is_first, got, chunk[cut:])
    order = ("ctx", "shard", "section")

    own_ids = jnp.concatenate([tokens, end_ids[:, None]], axis=1)
    all_ids = gather_axis(gather_axis(own_ids, "ctx"), "shard")
    natural = all_ids[..., :rows].transpose(0, 2, 1, 3).reshape(n_shard, MICRO, 2 * n, hb)
    zig = jnp.stack([natural[:, :, :n], natural[:, :, n:][:, :, ::-1]], axis=3)
    zig = zig.reshape(n_shard, MICRO, half, 2, rows).transpose(0, 3, 1, 2, 4)
    end_all = all_ids[:, 0, :, rows].reshape(n_seq)
    n_blocks = n_shard * n_dest

    def held(ids):
        ids = ids - z_at * entries
        return jnp.where((ids >= 0) & (ids < entries), ids, entries)

    listed, counts = owned_rows(held(zig.reshape(n_blocks, rows)), entries)
    end_held = held(end_all)
    if fast:
        first = first_moves(piece0)
        listed, piece0, *first = lax.optimization_barrier((listed, piece0, *first))
        second = second_moves(piece0, first[0], first[1])
    else:
        units0 = lax.all_gather(piece0, order, axis=0, tiled=True)
    dest = jnp.arange(n_blocks, dtype=jnp.int32) % n_dest
    groups = (dest % n % half) * 2 + dest // n
    assert VOCAB >= (n_shard - 1) * entries
    meta_emb = jnp.concatenate(
        [
            jnp.stack([(z_at == n_shard - 1).astype(jnp.int32), jnp.int32(n), jnp.int32(VOCAB - (n_shard - 1) * entries), jnp.int32(0)]),
            groups,
        ]
    )
    picked, end_part = lookup(listed, counts, end_held, meta_emb, table_master, n_blocks, rows)
    if fast:
        picked, *second = lax.optimization_barrier((picked, *second))
        halves = gather_half(piece0, first, second)
    summed = lax.psum_scatter(picked.reshape(n_shard, n_dest, columns, rows), "shard", scatter_dimension=0, tiled=True)
    if fast:
        summed, piece1, *halves = lax.optimization_barrier((summed, piece1, *halves))
        parts = [part for mine in halves for part in (mine, swap(mine, "section", 1))]
    routed = lax.all_to_all(summed.reshape(n_dest, columns, rows), ("section", "ctx"), split_axis=0, concat_axis=0, tiled=True)
    embedded = routed.reshape(D, rows).T.astype(F32)
    column_at = (s_at * n + c_at) * columns
    end_rows = sum_all(lax.dynamic_update_slice(jnp.zeros((n_seq, D), F32), end_part, (0, column_at)))
    end_row = lax.dynamic_slice_in_dim(end_rows, seq_at, 1, 0)

    units1 = lax.all_gather(piece1, order, axis=0, tiled=True)

    length = lax.dynamic_slice_in_dim(lengths, seq_in, 1, 0)[0]
    others = [group ^ (2 * cb + sb) for sb in range(2) for cb in range(half)]
    meta = jnp.stack([group, length] + others).astype(jnp.int32)
    span = jnp.arange(hb, dtype=jnp.int32)
    positions = jnp.concatenate([group * hb + span, (2 * n - 1 - group) * hb + span])

    vecs0, vecs1 = vector_master[0:4], vector_master[4:8]
    hidden1 = layer_norm(embedded, vecs0[0], vecs0[1]).astype(BF)
    if fast:
        hidden1, *parts = lax.optimization_barrier((hidden1, *parts))
        units0 = place_units(parts)
    weights0 = layer_weights(units0)
    out0, saved0 = layer_forward(embedded, hidden1, pieces_of(hidden1, half), meta, n, weights0, vecs0)
    x1 = out0.astype(BF).astype(F32)
    x1, units1 = lax.optimization_barrier((x1, units1))
    w_qkv1 = split_units(units1, 0, 3)
    weights1 = ((w_qkv1[0], w_qkv1[1], w_qkv1[2]), units1[U_OUT:U_UP], split_units(units1, U_UP, N_UP), units1[U_DOWN:])
    final, saved1 = last_forward(x1, positions, length, half, weights1, vecs1)

    def score_terms(final_row, end_vals, gain_vec, bias_vec, head_vec):
        normed = layer_norm(final_row, gain_vec, bias_vec)
        return jnp.sum(normed * (end_vals + head_vec)) * D ** (-0.5)

    counted = group == 0
    score, score_back = jax.vjp(score_terms, final, end_row, vector_master[8], vector_master[9], vector_master[10])
    scores = sum_all(jnp.where((jnp.arange(n_seq) == seq_at) & counted, score, 0.0)[None])[0]

    def pair_loss(score_vals):
        return jnp.sum(softplus(score_vals[pairs[:, 1]] - score_vals[pairs[:, 0]]))

    loss_sum, loss_back = jax.vjp(pair_loss, scores)
    grad_scores = loss_back(jnp.ones_like(loss_sum))[0]
    grad_own = lax.dynamic_slice_in_dim(grad_scores, seq_at, 1, 0)[0]
    grad_final, grad_end, *vec_final = score_back(grad_own)

    grad_x1, factors, vec1, vec1_row = last_backward(saved1, grad_final, half, weights1, vecs1)
    factors = jnp.concatenate([factors, grad_end.astype(BF)])
    grad_x1 = grad_x1.astype(BF).astype(F32)
    grad_x0, grads0, vec0 = layer_backward(saved0, grad_x1, meta, n, weights0, vecs0, fast)
    beside = swap(factors, "ctx", half)
    both = jnp.where(seq_in == 0, jnp.stack([factors, beside]), jnp.stack([beside, factors]))
    every_factor = gather_axis(both, "shard").reshape(n_seq, -1, D)

    by_owner = grad_x0.astype(BF).T.reshape(n_dest, columns, rows)
    back = lax.all_to_all(by_owner, ("section", "ctx"), split_axis=0, concat_axis=0, tiled=True)
    if fast:
        back, rest0, qkv0 = lax.optimization_barrier((back, *grads0))
        grads0 = jnp.where(c_at == 0, fold_qkv(qkv0), rest0)
        every = jnp.concatenate([back] + [shift(back, "shard", d) for d in (1, 3, 2)])
        every, every_factor, *vec0 = lax.optimization_barrier((every, every_factor, *vec0))
        near_order = (z_at + 4 - jnp.array((0, 1, 3, 2), jnp.int32)) % 4
        listed = listed.reshape(n_shard, -1)[near_order].reshape(-1)
        counts = counts.reshape(n_shard, -1)[near_order].reshape(-1)
    else:
        every = lax.all_gather(back, "shard", axis=0, tiled=True)
    end_grads = lax.dynamic_slice(every_factor[:, -1].astype(F32), (0, column_at), (n_seq, columns))
    table_grad = scatter(listed, counts, end_held, meta_emb, every, end_grads, entries)
    once = [jnp.where(counted, v, 0.0) for v in vec1_row + vec_final]
    vector_grad = sum_all(jnp.stack(vec0 + vec1 + once))

    own1 = last_gradient(every_factor, c_at * n_shard + z_at, n * n_shard, size)
    if fast:
        terms = along_shard(grads0)
        table_grad, *terms = lax.optimization_barrier((table_grad, *terms))
        own0 = finish_units(terms)
    else:
        own0 = lax.psum_scatter(grads0, order, scatter_dimension=0, tiled=True)
        own0 = jnp.concatenate([own0, swap(own0, "section", 1)]).astype(F32)
    layer_grad = jnp.where(is_first, own0, own1)
    layer_grad = lax.optimization_barrier(layer_grad.reshape(layer_master.shape))

    squares = (jnp.sum(layer_grad * layer_grad) + jnp.sum(table_grad * table_grad)).reshape(1, 1)
    squares = sum_all(squares)[0, 0]
    grad_norm = jnp.sqrt(squares + jnp.sum(vector_grad * vector_grad))
    factor = CLIP_LIMIT / jnp.maximum(grad_norm, CLIP_LIMIT)
    layer_new = adam_update(layer_master, layer_first, layer_second, layer_grad * factor, 0.4, 0.1)
    table_new = adam_update(table_master, table_first, table_second, table_grad * factor, 0.5, 0.1)
    vector_new = adam_update(vector_master, vector_first, vector_second, vector_grad * factor, 0.7, 0.0)
    return (loss_sum, grad_norm, *layer_new, *table_new, *vector_new)


def solution(mesh):
    in_specs = (
        P("shard", "ctx"),
        P("shard"),
        P("shard"),
        P(),
        P("section", ("ctx", "shard")),
        P("section", ("ctx", "shard")),
        P("section", ("ctx", "shard")),
        P(("section", "ctx"), "shard"),
        P(("section", "ctx"), "shard"),
        P(("section", "ctx"), "shard"),
        P(),
        P(),
        P(),
    )
    out_specs = (
        P(),
        P(),
        P("section", ("ctx", "shard")),
        P("section", ("ctx", "shard")),
        P("section", ("ctx", "shard")),
        P(("section", "ctx"), "shard"),
        P(("section", "ctx"), "shard"),
        P(("section", "ctx"), "shard"),
        P(),
        P(),
        P(),
    )
    return jax.shard_map(shards, mesh=mesh, in_specs=in_specs, out_specs=out_specs, check_vma=False)
```

```python
import functools

import jax
import jax.numpy as jnp
from jax import lax
from jax.experimental import pallas as pl
from jax.experimental.pallas import tpu as pltpu
from jax.sharding import PartitionSpec as P

D = 1088
HEADS = 17
HD = 64
FF = 4352
VOCAB = 51200
MICRO = 2
STEP = 10
CLIP_LIMIT = 0.02
ALL = ("section", "ctx", "shard")

LANES = 128
PAIRS_OF_HEADS = (HEADS + 1) // 2
WIDE = PAIRS_OF_HEADS * LANES
N_UP = FF // D
U_OUT = 3 * D
U_UP = U_OUT + D
U_DOWN = U_UP + FF
UNITS = U_DOWN + FF

BF = jnp.bfloat16
F32 = jnp.float32
VMEM_BIG = 56 * 1024 * 1024


def params(limit=VMEM_BIG):
    return pltpu.CompilerParams(vmem_limit_bytes=limit)


def cost(microseconds):
    return pl.CostEstimate(flops=0, bytes_accessed=int(microseconds * 3.0e6), transcendentals=0)


def dot(a, b, contract=((1,), (0,))):
    return lax.dot_general(a, b, (contract, ((), ())), preferred_element_type=F32)


NT = ((1,), (1,))
TN = ((0,), (0,))


def split2(x):
    top = lax.reduce_precision(x, 8, 7)
    return jnp.concatenate([top, x - top]).astype(BF)


def dot2(x, w, contract=((1,), (0,))):
    y = dot(split2(x), w, contract)
    return y[: x.shape[0]] + y[x.shape[0] :]


def swap(x, axis, bit):
    size = lax.axis_size(axis)
    return lax.ppermute(x, axis, [(i, i ^ bit) for i in range(size)])


def gather_axis(x, axis):
    size = lax.axis_size(axis)
    me = lax.axis_index(axis)
    x = x[None]
    bit = 1
    while bit < size:
        other = swap(x, axis, bit)
        lower = (me & bit) == 0
        x = jnp.where(lower, jnp.concatenate([x, other]), jnp.concatenate([other, x]))
        bit *= 2
    return x


def sum_axis(x, axis, first=1, last=None):
    size = lax.axis_size(axis) if last is None else last
    bit = first
    while bit < size:
        x = x + swap(x, axis, bit)
        bit *= 2
    return x


def group_reduce(x, combine, half):
    def step(x, axis, bit):
        other = swap(x, axis, bit)
        lower = (lax.axis_index(axis) & bit) == 0
        return combine(jnp.where(lower, x, other), jnp.where(lower, other, x))

    x = step(x, "section", 1)
    bit = 1
    while bit < half:
        x = step(x, "ctx", bit)
        bit *= 2
    return x


def sum_all(x):
    return sum_axis(sum_axis(sum_axis(x, "section"), "ctx"), "shard")


def sum_direct(x, axis):
    size = lax.axis_size(axis)
    if size > 4:
        return sum_axis(x, axis)
    terms = [x] + [lax.ppermute(x, axis, [(i, (i + d) % size) for i in range(size)]) for d in range(1, size)]
    turned = jnp.stack(terms[::-1] * 2)
    ordered = lax.dynamic_slice_in_dim(turned, size - 1 - lax.axis_index(axis), size, 0)
    total = ordered[0]
    for i in range(1, size):
        total = total + ordered[i]
    return total


def sum_small(x):
    return sum_direct(sum_direct(sum_direct(x, "section"), "ctx"), "shard")


def rows_kernel(pairs, x, out, scr):
    lane = lax.broadcasted_iota(jnp.int32, (1, LANES), 1)
    step = 2 * D // LANES
    even, odd = pl.ds(0, pairs, stride=2), pl.ds(1, pairs, stride=2)
    flat_row = lambda t: x[pl.ds(t, pairs, stride=step), :]
    for t in range(PAIRS_OF_HEADS):
        scr[t, even, :] = flat_row(t)
    before = pltpu.roll(flat_row(step // 2), HD, 1)
    for t in range(PAIRS_OF_HEADS - 1):
        after = pltpu.roll(flat_row(step // 2 + 1 + t), HD, 1)
        scr[t, odd, :] = jnp.where(lane < HD, before, after)
        before = after
    scr[PAIRS_OF_HEADS - 1, odd, :] = before
    for t, (at, size) in enumerate(tile_cuts()):
        out[:, pl.ds(at, size)] = scr[t][:, :size].astype(BF)


def chunk_rows(flat):
    units = flat.size // D
    return pl.pallas_call(
        functools.partial(rows_kernel, units // 2),
        out_shape=jax.ShapeDtypeStruct((units, D), BF),
        scratch_shapes=[pltpu.VMEM((PAIRS_OF_HEADS, units, LANES), F32)],
        compiler_params=params(),
        cost_estimate=cost(6),
        name="chunk_rows",
    )(flat.reshape(-1, LANES))


def small_block():
    return lax.axis_size("ctx") == 4 and lax.axis_size("shard") == 4 and lax.axis_size("section") == 2


def shift(x, axis, by):
    size = lax.axis_size(axis)
    return lax.ppermute(x, axis, [(i, (i + by) % size) for i in range(size)])


ARRIVALS = ((0,), (1, 3), (2,))
OVERLAP = 16


def place_kernel(rows, at, *refs):
    ins, out, held, sems_in, sems_out = refs[: 2 * len(ARRIVALS)], refs[-4], refs[-3], refs[-2], refs[-1]
    s, c, z = at[0], at[1], at[2]
    short = rows - OVERLAP
    pieces = []
    for g, distances in enumerate(ARRIVALS):
        for other in range(2):
            for e in range(4):
                for i, d in enumerate(distances):
                    chunk = (c ^ e) * 4 + lax.rem(z + 4 - d, 4)
                    pieces.append((ins[2 * g + other].at[e, i], chunk, other))

    def arrive(k):
        return pltpu.make_async_copy(pieces[k][0], held.at[k], sems_in.at[k])

    def leave(k, act):
        _, chunk, other = pieces[k]

        @pl.when(s == other)
        def _():
            act(pltpu.make_async_copy(held.at[k], out.at[chunk, pl.ds(0, rows)], sems_out.at[k]))

        @pl.when(s != other)
        def _():
            act(pltpu.make_async_copy(held.at[k, pl.ds(OVERLAP, short)], out.at[chunk, pl.ds(rows, short)], sems_out.at[k]))

    for k in range(len(pieces)):
        arrive(k).start()
    for k in range(len(pieces)):
        arrive(k).wait()
        leave(k, lambda copy: copy.start())
    for k in range(len(pieces)):
        leave(k, lambda copy: copy.wait())


def by_links(own):
    return swap(own, "ctx", 1), swap(own, "ctx", 2)


def first_moves(piece):
    return shift(piece, "shard", 1), shift(piece, "shard", 3), *by_links(piece[None])


def second_moves(piece, near, far):
    return shift(piece, "shard", 2), *by_links(jnp.stack([near, far]))


def gather_half(piece, first, second):
    rows = piece.shape[0]
    cut = rows // 2
    near, far, *own_links = first
    opposite, *near_links = second
    arrived = {0: piece, 1: near, 3: far, 2: opposite}
    parts = []
    for distances, links in zip(ARRIVALS, (own_links, near_links, None)):
        own = jnp.stack([arrived[d] for d in distances])
        by_x, by_y = by_links(own) if links is None else links
        corner = jnp.concatenate([swap(by_x[:, :cut], "ctx", 2), swap(by_y[:, cut:], "ctx", 1)], axis=1)
        parts.append(jnp.stack([own, by_x, by_y, corner]))
    return parts


def place_units(parts):
    rows = parts[0].shape[2]
    at = jnp.stack([lax.axis_index(a) for a in ALL]).astype(jnp.int32)
    grid_spec = pltpu.PrefetchScalarGridSpec(
        num_scalar_prefetch=1,
        grid=(1,),
        in_specs=[pl.BlockSpec(memory_space=pl.ANY)] * len(parts),
        out_specs=pl.BlockSpec(memory_space=pl.ANY),
        scratch_shapes=[pltpu.VMEM((32, rows, D), BF), pltpu.SemaphoreType.DMA((32,)), pltpu.SemaphoreType.DMA((32,))],
    )
    whole = pl.pallas_call(
        functools.partial(place_kernel, rows),
        grid_spec=grid_spec,
        out_shape=jax.ShapeDtypeStruct((16, 2 * rows - OVERLAP, D), BF),
        compiler_params=params(),
        cost_estimate=cost(16),
        name="place",
    )(at, *parts)
    return whole.reshape(UNITS, D)


def add_low(x, y):
    return (x.astype(F32) + y.astype(F32)).astype(BF)


BLOCK = 136


def fold_cores(region):
    s = lax.axis_index("section")
    blocks = region.reshape(-1, 2, BLOCK, D)
    pick = lambda i: lax.dynamic_index_in_dim(blocks, i, 1, keepdims=False)
    return add_low(pick(s), swap(pick(1 - s), "section", 1))


def one_way(x, bit, sends):
    return lax.ppermute(x, "ctx", [(i, i ^ bit) for i in range(4) if sends(i)])


def three_first(one, two, both, p):
    has_p = (lax.axis_index("ctx") & p) != 0
    return swap(jnp.where(has_p, two, one), "ctx", p), one_way(both, p, lambda i: not i & p)


def three_second(one, two, both, came, came_both, p, q):
    c = lax.axis_index("ctx")
    has_p, has_q = (c & p) != 0, (c & q) != 0
    single = add_low(jnp.where(has_p, one, two), came)
    both = add_low(both, came_both)
    sent = jnp.where(has_p & ~has_q, both, single)
    came = one_way(sent, q, lambda i: not i & q or i & p)
    return add_low(jnp.where(has_p & has_q, both, single), came)


def fold_one(x, p, q):
    x = add_low(x, one_way(x, p, lambda i: i & p))
    return add_low(x, one_way(x, q, lambda i: i & q and not i & p))


def rest_first(rest):
    x = rest.reshape(3, 4, -1, BLOCK, D)
    return *three_first(x[0, :2], x[1, :2], x[2, :2], 1), *three_first(x[1, 2:], x[0, 2:], x[2, 2:], 2)


def rest_second(rest, came):
    x = rest.reshape(3, 4, -1, BLOCK, D)
    first = three_second(x[0, :2], x[1, :2], x[2, :2], came[0], came[1], 1, 2)
    second = three_second(x[1, 2:], x[0, 2:], x[2, 2:], came[2], came[3], 2, 1)
    return jnp.concatenate([first, second])


def fold_qkv(qkv):
    x = qkv.reshape(4, -1, BLOCK, D)
    return jnp.concatenate([fold_one(x[:2], 1, 2), fold_one(x[2:], 2, 1)])


def along_shard(x):
    z = lax.axis_index("shard")
    pick = lambda i: lax.dynamic_index_in_dim(x, lax.rem(i, 4), 0, keepdims=False)
    return [pick(z)] + [shift(pick(z + d), "shard", d) for d in (1, 3, 2)]


SHIFT = 10
UNROLL = 8


def owned_rows(ids, entries):
    rows = ids.shape[1]
    assert rows < (1 << SHIFT)
    owned = ids < entries
    place = jnp.cumsum(owned.astype(jnp.int32), axis=1) - 1
    packed = jnp.arange(rows, dtype=jnp.int32)[None, :] + (ids << SHIFT)
    slots = jnp.arange(rows, dtype=jnp.int32)
    hit = (place[:, None, :] == slots[None, :, None]) & owned[:, None, :]
    listed = jnp.sum(jnp.where(hit, packed[:, None, :], 0), axis=2)
    count = jnp.sum(owned.astype(jnp.int32), axis=1)
    listed = jnp.where(slots[None, :] < count[:, None], listed, rows + (entries << SHIFT))
    return listed.reshape(-1), count


def for_owned(listed, counts, step, rows, body):
    def some(t, _):
        for u in range(UNROLL):
            packed = listed[step * rows + t * UNROLL + u]
            body(pl.ds(packed & ((1 << SHIFT) - 1), 1), pl.ds(packed >> SHIFT, 1))
        return 0

    lax.fori_loop(0, (counts[step] + UNROLL - 1) // UNROLL, some, 0)


def lookup_kernel(rows, listed, counts, end_ids, meta, table, out, ends, tab, buf):
    step = pl.program_id(0)
    columns, entries = table.shape

    @pl.when(step == 0)
    def _():
        def turn(i, _):
            at = pl.multiple_of(i * 256, 256)
            tab[pl.ds(at, 256), :] = table[:, pl.ds(at, 256)].astype(BF).astype(F32).T
            return 0

        lax.fori_loop(0, entries // 256, turn, 0)
        tab[pl.ds(entries, 8), :] = jnp.zeros((8, columns), F32)
        for n in range(ends.shape[0]):
            ends[pl.ds(n, 1), :] = tab[pl.ds(end_ids[n], 1), :]

    buf[...] = jnp.zeros_like(buf)

    def pick(place, entry):
        buf[place, :] = tab[entry, :]

    for_owned(listed, counts, step, rows, pick)

    @pl.when(meta[0] == 1)
    def _():
        half = rows // 2
        group = meta[4 + step]
        for j in range(2):
            block = group if j == 0 else 2 * meta[1] - 1 - group
            at = pl.multiple_of(meta[2] + block * half, 8)
            buf[pl.ds(j * half, half), :] += tab[pl.ds(at, half), :]

    out[0] = buf[pl.ds(0, rows), :].T.astype(BF)


def lookup(listed, counts, end_ids, meta, table, n_blocks, rows):
    columns, entries = table.shape
    n_ends = end_ids.shape[0]
    grid_spec = pltpu.PrefetchScalarGridSpec(
        num_scalar_prefetch=4,
        grid=(n_blocks,),
        in_specs=[pl.BlockSpec((columns, entries), lambda i, *_: (0, 0))],
        out_specs=[
            pl.BlockSpec((1, columns, rows), lambda i, *_: (i, 0, 0)),
            pl.BlockSpec((n_ends, columns), lambda i, *_: (0, 0)),
        ],
        scratch_shapes=[pltpu.VMEM((entries + 8, columns), F32), pltpu.VMEM((rows + 8, columns), F32)],
    )
    return pl.pallas_call(
        functools.partial(lookup_kernel, rows),
        grid_spec=grid_spec,
        out_shape=[
            jax.ShapeDtypeStruct((n_blocks, columns, rows), BF),
            jax.ShapeDtypeStruct((n_ends, columns), F32),
        ],
        compiler_params=params(),
        cost_estimate=cost(40),
        name="lookup",
    )(listed, counts, end_ids, meta, table)


def scatter_kernel(rows, n_blocks, listed, counts, end_ids, meta, grads, ends, out, acc, buf):
    step = pl.program_id(0)
    columns, entries = out.shape
    n_ends = ends.shape[0]

    @pl.when(step == 0)
    def _():
        def clear(i, _):
            acc[pl.ds(pl.multiple_of(i * 256, 256), 256), :] = jnp.zeros((256, columns), F32)
            return 0

        lax.fori_loop(0, entries // 256, clear, 0)
        for n in range(n_ends):
            at = pl.ds(end_ids[n], 1)
            acc[at, :] += ends[pl.ds(n, 1), :]

    buf[pl.ds(0, rows), :] = grads[0].astype(F32).T

    def add(place, entry):
        acc[entry, :] += buf[place, :]

    for_owned(listed, counts, step, rows, add)

    @pl.when(meta[0] == 1)
    def _():
        half = rows // 2
        group = meta[4 + step]
        for j in range(2):
            block = group if j == 0 else 2 * meta[1] - 1 - group
            at = pl.multiple_of(meta[2] + block * half, 8)
            acc[pl.ds(at, half), :] += buf[pl.ds(j * half, half), :]

    @pl.when(step == n_blocks - 1)
    def _():
        def turn(i, _):
            at = pl.multiple_of(i * 256, 256)
            out[:, pl.ds(at, 256)] = acc[pl.ds(at, 256), :].T
            return 0

        lax.fori_loop(0, entries // 256, turn, 0)


def scatter(listed, counts, end_ids, meta, grads, ends, entries):
    n_blocks, columns, rows = grads.shape
    n_ends = ends.shape[0]
    grid_spec = pltpu.PrefetchScalarGridSpec(
        num_scalar_prefetch=4,
        grid=(n_blocks,),
        in_specs=[
            pl.BlockSpec((1, columns, rows), lambda i, *_: (i, 0, 0)),
            pl.BlockSpec((n_ends, columns), lambda i, *_: (0, 0)),
        ],
        out_specs=pl.BlockSpec((columns, entries), lambda i, *_: (0, 0)),
        scratch_shapes=[pltpu.VMEM((entries + 8, columns), F32), pltpu.VMEM((rows + 8, columns), F32)],
    )
    return pl.pallas_call(
        functools.partial(scatter_kernel, rows, n_blocks),
        grid_spec=grid_spec,
        out_shape=jax.ShapeDtypeStruct((columns, entries), F32),
        compiler_params=params(),
        cost_estimate=cost(42),
        name="scatter",
    )(listed, counts, end_ids, meta, grads, ends)


def tile_cuts():
    return [(t * LANES, min(LANES, D - t * LANES)) for t in range(PAIRS_OF_HEADS)]


def split_kernel(count, rb, width, u, out, scr):
    for t, (at, size) in enumerate(tile_cuts()):
        part = u[:, pl.ds(at, size)].astype(F32)
        if size < LANES:
            part = jnp.concatenate([part, jnp.zeros((rb * count, LANES - size), F32)], axis=1)
        scr[t] = part
        for j in range(count):
            picked = scr[t, pl.ds(j, rb, stride=count), :].astype(BF)
            take = min(LANES, width - at)
            out[j, :, pl.ds(at, take)] = picked[:, :take]


def join_kernel(count, rb, u, out, scr):
    for t, (at, size) in enumerate(tile_cuts()):
        part = u[:, pl.ds(at, size)].astype(F32)
        if size < LANES:
            part = jnp.concatenate([part, jnp.zeros((rb * count, LANES - size), F32)], axis=1)
        scr[t] = part
        for j in range(count):
            out[:, pl.ds(j * D + at, size)] = scr[t, pl.ds(j, rb, stride=count), :].astype(BF)[:, :size]


def join_units(u, first, count):
    rb = 272
    return pl.pallas_call(
        functools.partial(join_kernel, count, rb),
        grid=(D // rb,),
        in_specs=[pl.BlockSpec((rb * count, D), lambda i: (i + first // (rb * count), 0))],
        out_specs=pl.BlockSpec((rb, count * D), lambda i: (i, 0)),
        out_shape=jax.ShapeDtypeStruct((D, count * D), BF),
        scratch_shapes=[pltpu.VMEM((PAIRS_OF_HEADS, rb * count, LANES), F32)],
        compiler_params=params(),
        cost_estimate=cost(8),
        name="join_units",
    )(u)


def split_units(u, first, count, width=D):
    rb = 272
    return pl.pallas_call(
        functools.partial(split_kernel, count, rb, width),
        grid=(D // rb,),
        in_specs=[pl.BlockSpec((rb * count, D), lambda i: (i + first // (rb * count), 0))],
        out_specs=pl.BlockSpec((count, rb, width), lambda i: (0, i, 0)),
        out_shape=jax.ShapeDtypeStruct((count, D, width), BF),
        scratch_shapes=[pltpu.VMEM((PAIRS_OF_HEADS, rb * count, LANES), F32)],
        compiler_params=params(),
        cost_estimate=cost(8),
        name="split_units",
    )(u)


def merge_kernel(count, rb, starts, *refs):
    parts, out, scr = refs[:-2], refs[-2], refs[-1]
    for t, (at, size) in enumerate(tile_cuts()):
        for j in range(count):
            which, start = starts[j]
            part = parts[which][:, pl.ds(start + at, size)].astype(F32)
            if size < LANES:
                part = jnp.concatenate([part, jnp.zeros((rb, LANES - size), F32)], axis=1)
            scr[t, pl.ds(j, rb, stride=count), :] = part
        out[:, pl.ds(at, size)] = scr[t][:, :size].astype(BF)


def merge_units(parts, starts):
    rb, count = 272, len(starts)
    return pl.pallas_call(
        functools.partial(merge_kernel, count, rb, starts),
        grid=(D // rb,),
        in_specs=[pl.BlockSpec((rb, p.shape[1]), lambda i: (i, 0)) for p in parts],
        out_specs=pl.BlockSpec((rb * count, D), lambda i: (i, 0)),
        out_shape=jax.ShapeDtypeStruct((count * D, D), BF),
        scratch_shapes=[pltpu.VMEM((PAIRS_OF_HEADS, rb * count, LANES), F32)],
        compiler_params=params(),
        cost_estimate=cost(8),
        name="merge_units",
    )(*parts)


def adam_kernel(rate, decay, factor, w, m, v, g, w_out, m_out, v_out):
    w_out[...], m_out[...], v_out[...] = adam_update(w[...], m[...], v[...], g[...] * factor[0], rate, decay)


def adam(factor, weight, first, second, grad, rate, decay, block):
    shape = weight.shape
    grid = tuple(size // b for size, b in zip(shape, block))
    spec = pl.BlockSpec(block, lambda i, j, *_: (i, j))
    return pl.pallas_call(
        functools.partial(adam_kernel, rate, decay),
        grid_spec=pltpu.PrefetchScalarGridSpec(num_scalar_prefetch=1, grid=grid, in_specs=[spec] * 4, out_specs=[spec] * 3),
        out_shape=[jax.ShapeDtypeStruct(shape, F32)] * 3,
        compiler_params=params(),
        cost_estimate=cost(weight.size * 9.0e-6),
        name="adam",
    )(factor.reshape(1), weight, first, second, grad)


def chunk_plan(n):
    plan = [(0, "ll", True), (0, "hl", False), (0, "hh", True)]
    for p in range(1, n):
        plan += [(p, "hl", False), (p, "sel", False)]
    return plan


def chunk_offsets(meta, n, hb, p, kind):
    own = meta[0]
    piece = meta[2 + p]
    if kind == "ll":
        return 0, p * 2 * hb, own * hb, piece * hb, True
    if kind == "hl":
        return hb, p * 2 * hb, (2 * n - 1 - own) * hb, piece * hb, False
    if kind == "hh":
        return hb, p * 2 * hb + hb, (2 * n - 1 - own) * hb, (2 * n - 1 - piece) * hb, False
    low = piece < own
    q_off = pl.multiple_of(jnp.where(low, 0, hb), hb)
    k_off = pl.multiple_of(p * 2 * hb + jnp.where(low, 0, hb), hb)
    key_pos = jnp.where(low, piece, 2 * n - 1 - piece) * hb
    return q_off, k_off, None, key_pos, low


def chunk_scores(keys, queries, meta, diagonal, kind, q_pos, k_pos, hb):
    s = dot(keys, queries, NT)
    if diagonal:
        ki = lax.broadcasted_iota(jnp.int32, (hb, hb), 0)
        qi = lax.broadcasted_iota(jnp.int32, (hb, hb), 1)
        keep = (ki <= qi) & (ki + k_pos < meta[1])
        s = jnp.where(keep, s, -1e30)
    elif kind == "sel":
        ki = lax.broadcasted_iota(jnp.int32, (hb, hb), 0)
        s = jnp.where(ki < meta[1] - k_pos, s, -1e30)
    return s


def attend_kernel(n, hb, meta, q_ref, k_ref, v_ref, o_ref, lse_ref, vt_ref):
    keys = 2 * hb * n
    for i in range(keys // hb):
        vt_ref[i] = v_ref[pl.ds(i * hb, hb), :].astype(F32).T.astype(BF)
    lane = lax.broadcasted_iota(jnp.int32, (1, LANES), 1)
    plan = chunk_plan(n)
    outs = []
    for head in range(2):
        own_lanes = (lane // HD) == head
        info, scores = [], []
        tops = [jnp.full((1, hb), -3e38, F32), jnp.full((1, hb), -3e38, F32)]
        for p, kind, diagonal in plan:
            q_off, k_off, q_pos, k_pos, low = chunk_offsets(meta, n, hb, p, kind)
            queries = jnp.where(own_lanes, q_ref[pl.ds(q_off, hb), :], 0)
            s = chunk_scores(k_ref[pl.ds(k_off, hb), :], queries, meta, diagonal, kind, q_pos, k_pos, hb)
            top = jnp.max(s, axis=0, keepdims=True)
            if low is True:
                tops[0] = jnp.maximum(tops[0], top)
            elif low is False:
                tops[1] = jnp.maximum(tops[1], top)
            else:
                tops[0] = jnp.maximum(tops[0], jnp.where(low, top, -3e38))
                tops[1] = jnp.maximum(tops[1], jnp.where(low, -3e38, top))
            info.append((k_off, low))
            scores.append(s)
        sums = [jnp.zeros((1, hb), F32), jnp.zeros((1, hb), F32)]
        accs = [jnp.zeros((HD, hb), F32), jnp.zeros((HD, hb), F32)]
        for (k_off, low), s in zip(info, scores):
            if low is True or low is False:
                top = tops[0] if low else tops[1]
            else:
                top = jnp.where(low, tops[0], tops[1])
            e = jnp.exp(s - top)
            total = jnp.sum(e, axis=0, keepdims=True)
            got = dot(vt_ref[k_off // hb, pl.ds(head * HD, HD), :], e.astype(BF))
            if low is True or low is False:
                sums[1 - low] += total
                accs[1 - low] += got
            else:
                sums[0] += jnp.where(low, total, 0.0)
                sums[1] += jnp.where(low, 0.0, total)
                accs[0] += jnp.where(low, got, 0.0)
                accs[1] += jnp.where(low, 0.0, got)
        outs.append([accs[i] / sums[i] for i in range(2)])
        for i in range(2):
            lse_ref[0, pl.ds(head, 1), pl.ds(i * hb, hb)] = tops[i] + jnp.log(sums[i])
    for i in range(2):
        both = jnp.concatenate([outs[0][i], outs[1][i]], axis=0)
        o_ref[pl.ds(i * hb, hb), :] = both.T.astype(BF)


def attend(meta, q, k, v, n):
    rows = q.shape[0]
    keys = k.shape[0]
    grid_spec = pltpu.PrefetchScalarGridSpec(
        num_scalar_prefetch=1,
        grid=(PAIRS_OF_HEADS,),
        in_specs=[
            pl.BlockSpec((rows, LANES), lambda p, *_: (0, p)),
            pl.BlockSpec((keys, LANES), lambda p, *_: (0, p)),
            pl.BlockSpec((keys, LANES), lambda p, *_: (0, p)),
        ],
        out_specs=[
            pl.BlockSpec((rows, LANES), lambda p, *_: (0, p)),
            pl.BlockSpec((1, 8, rows), lambda p, *_: (p, 0, 0)),
        ],
        scratch_shapes=[pltpu.VMEM((2 * n, LANES, rows // 2), BF)],
    )
    return pl.pallas_call(
        functools.partial(attend_kernel, n, rows // 2),
        grid_spec=grid_spec,
        out_shape=[
            jax.ShapeDtypeStruct((rows, WIDE), BF),
            jax.ShapeDtypeStruct((PAIRS_OF_HEADS, 8, rows), F32),
        ],
        compiler_params=params(),
        cost_estimate=cost(23),
        name="attend",
    )(meta, q, k, v)


def attend_back_kernel(n, hb, meta, q_ref, k_ref, v_ref, o_ref, do_ref, lse_ref, dq_ref, dk_ref, dv_ref, kt_ref, dk_acc, dv_acc):
    keys = 2 * hb * n
    for i in range(keys // hb):
        kt_ref[i] = k_ref[pl.ds(i * hb, hb), :].astype(F32).T.astype(BF)
    dk_acc[...] = jnp.zeros_like(dk_acc)
    dv_acc[...] = jnp.zeros_like(dv_acc)
    lane = lax.broadcasted_iota(jnp.int32, (1, LANES), 1)
    plan = chunk_plan(n)
    prods = []
    for i in range(2):
        part = pl.ds(i * hb, hb)
        prods.append((o_ref[part, :].astype(F32) * do_ref[part, :].astype(F32)).T)
    dqs = []
    for head in range(2):
        own_lanes = (lane // HD) == head
        deltas = [jnp.sum(prods[i][head * HD : (head + 1) * HD, :], axis=0, keepdims=True) for i in range(2)]
        lses = [lse_ref[0, pl.ds(head, 1), pl.ds(i * hb, hb)] for i in range(2)]
        accs = [jnp.zeros((HD, hb), F32), jnp.zeros((HD, hb), F32)]
        for p, kind, diagonal in plan:
            q_off, k_off, q_pos, k_pos, low = chunk_offsets(meta, n, hb, p, kind)
            q_at, k_at = pl.ds(q_off, hb), pl.ds(k_off, hb)
            queries = jnp.where(own_lanes, q_ref[q_at, :], 0)
            d_out = jnp.where(own_lanes, do_ref[q_at, :], 0)
            s = chunk_scores(k_ref[k_at, :], queries, meta, diagonal, kind, q_pos, k_pos, hb)
            if low is True or low is False:
                lse, delta = lses[1 - low], deltas[1 - low]
            else:
                lse, delta = jnp.where(low, lses[0], lses[1]), jnp.where(low, deltas[0], deltas[1])
            prob = jnp.exp(s - lse)
            d_prob = dot(v_ref[k_at, :], d_out, NT)
            d_score = (prob * (d_prob - delta)).astype(BF)
            dv_acc[k_at, :] += dot(prob.astype(BF), d_out)
            dk_acc[k_at, :] += dot(d_score, queries)
            got = dot(kt_ref[k_off // hb, pl.ds(head * HD, HD), :], d_score)
            if low is True or low is False:
                accs[1 - low] += got
            else:
                accs[0] += jnp.where(low, got, 0.0)
                accs[1] += jnp.where(low, 0.0, got)
        dqs.append(accs)
    for i in range(2):
        both = jnp.concatenate([dqs[0][i], dqs[1][i]], axis=0) * 0.125
        dq_ref[pl.ds(i * hb, hb), :] = both.T.astype(BF)
    dk_ref[...] = dk_acc[...].astype(BF)
    dv_ref[...] = dv_acc[...].astype(BF)


def attend_back(meta, q, k, v, o, d_o, lse, n):
    rows = q.shape[0]
    keys = k.shape[0]
    row_spec = pl.BlockSpec((rows, LANES), lambda p, *_: (0, p))
    key_spec = pl.BlockSpec((keys, LANES), lambda p, *_: (0, p))
    grid_spec = pltpu.PrefetchScalarGridSpec(
        num_scalar_prefetch=1,
        grid=(PAIRS_OF_HEADS,),
        in_specs=[row_spec, key_spec, key_spec, row_spec, row_spec, pl.BlockSpec((1, 8, rows), lambda p, *_: (p, 0, 0))],
        out_specs=[row_spec, key_spec, key_spec],
        scratch_shapes=[pltpu.VMEM((2 * n, LANES, rows // 2), BF), pltpu.VMEM((keys, LANES), F32), pltpu.VMEM((keys, LANES), F32)],
    )
    return pl.pallas_call(
        functools.partial(attend_back_kernel, n, rows // 2),
        grid_spec=grid_spec,
        out_shape=[
            jax.ShapeDtypeStruct((rows, WIDE), BF),
            jax.ShapeDtypeStruct((keys, WIDE), BF),
            jax.ShapeDtypeStruct((keys, WIDE), BF),
        ],
        compiler_params=params(),
        cost_estimate=cost(46),
        name="attend_back",
    )(meta, q, k, v, o, d_o, lse)


def layer_norm(values, gain_vec, bias_vec):
    row_mean = jnp.mean(values, -1, keepdims=True)
    centred = values - row_mean
    variance = jnp.mean(centred * centred, -1, keepdims=True)
    return centred * lax.rsqrt(variance + 1e-05) * gain_vec + bias_vec


def gelu_tanh(values):
    return 0.5 * values * (1.0 + jnp.tanh(0.7978845608 * (values + 0.044715 * values * values * values)))


def softplus(values):
    return jnp.maximum(values, 0.0) + jnp.log1p(jnp.exp(-jnp.abs(values)))


def adam_update(weight, first, second, grad, rate, decay):
    first = 0.9 * first + 0.1 * grad
    second = 0.95 * second + 0.05 * grad * grad
    first_hat = first / (1.0 - 0.9**STEP)
    second_hat = second / (1.0 - 0.95**STEP)
    weight = weight - rate * (first_hat / (jnp.sqrt(second_hat) + 1e-08) + decay * weight)
    return (weight, first, second)


def pieces_by_ctx(x, half):
    got = [x]
    bit = 1
    while bit < half:
        got += [swap(y, "ctx", bit) for y in got]
        bit *= 2
    return got


def pieces_by_section(got):
    own = jnp.concatenate(got)
    return jnp.concatenate([own, swap(own, "section", 1)])


def sum_pieces(near, far, half):
    rows = near.shape[0] // half
    x = near + swap(far, "section", 1).astype(F32)
    bit = half // 2
    while bit >= 1:
        keep, send = x[: bit * rows], x[bit * rows : 2 * bit * rows]
        x = keep + swap(send.astype(BF), "ctx", bit).astype(F32)
        bit //= 2
    return x


def layer_weights(units):
    return split_units(units, 0, 3, WIDE), units[U_OUT:U_UP], join_units(units, U_UP, N_UP), units[U_DOWN:]


def layer_forward(values, hidden1, all_hidden1, meta, n, weights, vecs):
    w_qkv, w_out, w_up, w_down = weights
    keys = dot(all_hidden1, w_qkv[1]).astype(BF)
    vals = dot(all_hidden1, w_qkv[2]).astype(BF)
    queries = dot(hidden1, w_qkv[0]).astype(BF) * jnp.asarray(0.125, BF)
    attended, lse = attend(meta, queries, keys, vals, n)
    middle = values + dot(attended[:, :D], w_out)
    hidden2 = layer_norm(middle, vecs[2], vecs[3]).astype(BF)
    ups = dot(hidden2, w_up)
    gated = gelu_tanh(ups).astype(BF)
    result = middle + dot(gated, w_down)
    return result, (values, all_hidden1, queries, keys, vals, attended, lse, middle, hidden2, ups, gated)


def layer_backward(saved, grad_out, meta, n, weights, vecs, factors, fast):
    values, all_hidden1, queries, keys, vals, attended, lse, middle, hidden2, ups, gated = saved
    w_qkv, w_out, w_up, w_down = weights
    grad_ffn = grad_out.astype(BF)
    grad_down = dot(gated, grad_ffn, TN).astype(BF)
    _, back = jax.vjp(gelu_tanh, ups)
    grad_ups = back(dot(grad_ffn, w_down, NT))[0].astype(BF)
    grad_up = merge_units([dot(hidden2, grad_ups, TN).astype(BF)], [(0, j * D) for j in range(N_UP)])
    grad_hidden2 = dot(grad_ups, w_up, NT)
    _, norm_back2 = jax.vjp(layer_norm, middle, vecs[2], vecs[3])
    grad_norm2, grad_gain2, grad_bias2 = norm_back2(grad_hidden2)
    grad_middle = grad_out + grad_norm2
    grad_branch = grad_middle.astype(BF)
    grad_outw = dot(attended[:, :D], grad_branch, TN).astype(BF)
    grad_att = dot(grad_branch, jnp.pad(w_out, ((0, WIDE - D), (0, 0))), NT).astype(BF)
    if fast:
        rest = jnp.concatenate([fold_cores(grad_outw), fold_cores(grad_up), fold_cores(grad_down)])
        grad_att, rest, factors = lax.optimization_barrier((grad_att, rest, factors))
        came = rest_first(rest)
    grad_q, part_k, part_v = attend_back(meta, queries, keys, vals, attended, grad_att, lse, n)
    rows, near = grad_q.shape[0], part_k.shape[0] // 2
    def to_hidden1(at):
        return dot(part_k[at], w_qkv[1], NT) + dot(part_v[at], w_qkv[2], NT)

    far = to_hidden1(slice(near, None)).astype(BF)
    if fast:
        far, *came = lax.optimization_barrier((far, *came))
    grad_q, part_k, part_v, far = lax.optimization_barrier((grad_q, part_k, part_v, far))
    close = to_hidden1(slice(0, near))
    close, grad_q, part_k, part_v = lax.optimization_barrier((close, grad_q, part_k, part_v))
    grad_hidden1 = sum_pieces(close, far, n // 2)
    grad_hidden1 = grad_hidden1 + dot(grad_q, w_qkv[0], NT)
    _, norm_back1 = jax.vjp(layer_norm, values, vecs[0], vecs[1])
    grad_norm1, grad_gain1, grad_bias1 = norm_back1(grad_hidden1)
    grad_input = grad_middle + grad_norm1
    pairs_qkv = [(all_hidden1[:rows], grad_q), (all_hidden1, part_k), (all_hidden1, part_v)]
    grad_qkvw = merge_units([dot(h, g, TN).astype(BF) for h, g in pairs_qkv], [(j, 0) for j in range(3)])
    if fast:
        summed = rest_second(rest, came), fold_cores(grad_qkvw)
    else:
        summed = jnp.concatenate([grad_qkvw, grad_outw, grad_up, grad_down])
    return grad_input, summed, [grad_gain1, grad_bias1, grad_gain2, grad_bias2], factors


def head_mask():
    head = lax.broadcasted_iota(jnp.int32, (HEADS, D), 0)
    return lax.broadcasted_iota(jnp.int32, (HEADS, D), 1) // HD == head


def last_forward(values, positions, length, half, weights, vecs):
    (w_q, w_k, w_v), w_out, w_up, w_down = weights
    heads = head_mask()
    hidden1 = layer_norm(values, vecs[0], vecs[1]).astype(BF)
    mine = (positions == length - 1)[:, None]
    row = jnp.sum(jnp.where(mine, values, 0.0), axis=0, keepdims=True)
    row = group_reduce(row, jnp.add, half)
    row_h1 = layer_norm(row, vecs[0], vecs[1]).astype(BF)
    query = dot(row_h1, w_q).astype(BF)
    wq = dot(jnp.where(heads, query, 0), w_k, NT) * 0.125
    scores = dot2(wq, hidden1, NT)
    scores = jnp.where((positions < length)[None, :], scores, -1e30)
    top = jnp.max(scores, axis=1, keepdims=True)
    expo = jnp.exp(scores - top)
    total = jnp.sum(expo, axis=1, keepdims=True)
    mixed = dot(expo.astype(BF), hidden1)
    wide = lambda x: jnp.broadcast_to(x, (HEADS, HD))

    def merge(x, y):
        high = jnp.maximum(x[:, D : D + 1], y[:, D : D + 1])
        x = x * jnp.exp(x[:, D : D + 1] - high)
        y = y * jnp.exp(y[:, D : D + 1] - high)
        return jnp.concatenate([x[:, :D] + y[:, :D], wide(high), x[:, D + HD :] + y[:, D + HD :]], axis=1)

    merged = group_reduce(jnp.concatenate([mixed, wide(top), wide(total)], axis=1), merge, half)
    top, total = merged[:, D : D + 1], merged[:, D + HD : D + HD + 1]
    mixed = merged[:, :D] / total
    probs = jnp.exp(scores - top) / total
    att = jnp.sum(jnp.where(heads, dot2(mixed, w_v), 0.0), axis=0, keepdims=True)
    middle = row + dot(att.astype(BF), w_out)
    hidden2 = layer_norm(middle, vecs[2], vecs[3]).astype(BF)
    ups = dot(hidden2, w_up)
    gated = gelu_tanh(ups).astype(BF)
    result = middle + dot(gated, w_down)
    return result, (values, hidden1, mine, row_h1, query, wq, probs, mixed, att, middle, hidden2, ups, gated)


def last_backward(saved, grad_out, half, weights, vecs):
    values, hidden1, mine, row_h1, query, wq, probs, mixed, att, middle, hidden2, ups, gated = saved
    (w_q, w_k, w_v), w_out, w_up, w_down = weights
    heads = head_mask()
    grad_ffn = grad_out.astype(BF)
    _, back = jax.vjp(gelu_tanh, ups)
    grad_ups = back(dot(grad_ffn, w_down, NT))[0].astype(BF)
    grad_hidden2 = dot(grad_ups, w_up, NT)
    _, norm_back2 = jax.vjp(layer_norm, middle, vecs[2], vecs[3])
    grad_norm2, grad_gain2, grad_bias2 = norm_back2(grad_hidden2)
    grad_middle = grad_out + grad_norm2
    grad_branch = grad_middle.astype(BF)
    grad_att = dot(grad_branch, w_out, NT).astype(BF)
    att_heads = jnp.where(heads, grad_att, 0)
    wv = dot(att_heads, w_v, NT)
    grad_prob = dot2(wv, hidden1, NT)
    delta = jnp.sum(att_heads.astype(F32) * att, axis=1, keepdims=True)
    grad_score = (probs * (grad_prob - delta)).astype(BF)
    summed = group_reduce(dot(grad_score, hidden1), jnp.add, half)
    grad_query = (jnp.sum(jnp.where(heads, dot2(summed, w_k), 0.0), axis=0, keepdims=True) * 0.125).astype(BF)
    low_probs = probs.astype(BF)
    grad_hidden1 = dot(
        jnp.concatenate([grad_score, grad_score, low_probs, low_probs]), jnp.concatenate([split2(wq), split2(wv)]), TN
    )
    grad_hidden1 = grad_hidden1 + jnp.where(mine, dot(grad_query, w_q, NT), 0.0)
    _, norm_back1 = jax.vjp(layer_norm, values, vecs[0], vecs[1])
    grad_norm1, grad_gain1, grad_bias1 = norm_back1(grad_hidden1)
    grad_input = grad_norm1 + jnp.where(mine, grad_middle, 0.0)
    query8 = query * jnp.asarray(0.125, BF)
    factors = [row_h1, grad_query, query8, grad_att, att, grad_branch, hidden2, grad_ffn]
    factors += [grad_ups.reshape(N_UP, D), gated.reshape(N_UP, D), summed, mixed]
    factors = jnp.concatenate([f.astype(BF) for f in factors])
    return grad_input, factors, [grad_gain1, grad_bias1], [grad_gain2, grad_bias2]


def last_gradient(data, chunk_at, n_chunks, size):
    n_seq = data.shape[0]
    heads = head_mask()
    row_h1, grad_query, query8, grad_att, att, grad_branch, hidden2, grad_ffn = [data[:, i] for i in range(8)]
    at = 8
    grad_ups, gated = data[:, at : at + N_UP], data[:, at + N_UP : at + 2 * N_UP]
    at += 2 * N_UP
    summed, mixed = data[:, at : at + HEADS], data[:, at + HEADS : at + 2 * HEADS]

    def by_unit(parts):
        count, width = len(parts), sum(p.shape[0] for p in parts)
        slot = jnp.concatenate([jnp.full((p.shape[0],), j, jnp.int32) for j, p in enumerate(parts)])
        both = jnp.concatenate(parts).T
        spread = jnp.where(slot[None, None, :] == jnp.arange(count)[None, :, None], both[:, None, :], 0)
        return spread.reshape(count * D, width)

    def per_head(x):
        return jnp.where(heads[None], x[:, None, :], 0).reshape(n_seq * HEADS, D)

    left = by_unit([row_h1, summed.reshape(-1, D), mixed.reshape(-1, D)])
    right = jnp.concatenate([grad_query, per_head(query8), per_head(grad_att)])
    first = chunk_at * size
    qkv = dot(lax.dynamic_slice_in_dim(left, jnp.minimum(first, U_OUT - size), size, 0), right)
    lefts = [att.T, by_unit([hidden2] * N_UP), gated.reshape(n_seq, FF).T]
    rights = [grad_branch, grad_ups.transpose(1, 0, 2).reshape(-1, D), grad_ffn]
    width = sum(x.shape[1] for x in lefts)
    columns, before = [], 0
    for x in lefts:
        columns.append(jnp.pad(x, ((0, 0), (before, width - before - x.shape[1]))))
        before += x.shape[1]
    left = jnp.concatenate(columns)
    rest = dot(lax.dynamic_slice_in_dim(left, jnp.maximum(first - U_OUT, 0), size, 0), jnp.concatenate(rights))
    return jnp.where(first < U_OUT, qkv, rest)


def shards(
    tokens,
    lengths,
    end_ids,
    pairs,
    layer_master,
    layer_first,
    layer_second,
    table_master,
    table_first,
    table_second,
    vector_master,
    vector_first,
    vector_second,
):
    rows = tokens.shape[1]
    s_at = lax.axis_index("section")
    c_at = lax.axis_index("ctx")
    z_at = lax.axis_index("shard")
    n_section = lax.axis_size("section")
    n = lax.axis_size("ctx")
    n_shard = lax.axis_size("shard")
    half = n // 2
    hb = rows // 2
    n_dest = n_section * n
    n_seq = MICRO * n_shard
    columns, entries = table_master.shape
    is_first = s_at == 0
    seq_in = c_at // half
    seq_at = z_at * MICRO + seq_in
    group = (c_at % half) * 2 + s_at

    fast = small_block()
    chunk = chunk_rows(layer_master) if fast else layer_master.reshape(-1, D).astype(BF)
    size = chunk.shape[0]
    cut = size // 2
    if fast:
        wide = cut + OVERLAP // 2
        got = swap(jnp.where(is_first, chunk[size - wide :], chunk[:wide]), "section", 1)
        piece0 = jnp.where(is_first, chunk[:wide], got)
        piece1 = jnp.where(is_first, got[:cut], chunk[cut:])
    else:
        got = swap(jnp.where(is_first, chunk[cut:], chunk[:cut]), "section", 1)
        piece0 = jnp.where(is_first, chunk[:cut], got)
        piece1 = jnp.where(is_first, got, chunk[cut:])
    order = ("ctx", "shard", "section")

    own_ids = jnp.concatenate([tokens, end_ids[:, None]], axis=1)
    all_ids = gather_axis(gather_axis(own_ids, "ctx"), "shard")
    natural = all_ids[..., :rows].transpose(0, 2, 1, 3).reshape(n_shard, MICRO, 2 * n, hb)
    zig = jnp.stack([natural[:, :, :n], natural[:, :, n:][:, :, ::-1]], axis=3)
    zig = zig.reshape(n_shard, MICRO, half, 2, rows).transpose(0, 3, 1, 2, 4)
    end_all = all_ids[:, 0, :, rows].reshape(n_seq)
    n_blocks = n_shard * n_dest

    def held(ids):
        ids = ids - z_at * entries
        return jnp.where((ids >= 0) & (ids < entries), ids, entries)

    listed, counts = owned_rows(held(zig.reshape(n_blocks, rows)), entries)
    end_held = held(end_all)
    if fast:
        first = first_moves(piece0)
        listed, piece0, *first = lax.optimization_barrier((listed, piece0, *first))
        second = second_moves(piece0, first[0], first[1])
    else:
        units0 = lax.all_gather(piece0, order, axis=0, tiled=True)
    dest = jnp.arange(n_blocks, dtype=jnp.int32) % n_dest
    groups = (dest % n % half) * 2 + dest // n
    assert VOCAB >= (n_shard - 1) * entries
    meta_emb = jnp.concatenate(
        [
            jnp.stack([(z_at == n_shard - 1).astype(jnp.int32), jnp.int32(n), jnp.int32(VOCAB - (n_shard - 1) * entries), jnp.int32(0)]),
            groups,
        ]
    )
    picked, end_part = lookup(listed, counts, end_held, meta_emb, table_master, n_blocks, rows)
    if fast:
        picked, *second = lax.optimization_barrier((picked, *second))
        halves = gather_half(piece0, first, second)
    column_at = (s_at * n + c_at) * columns
    end_rows = sum_all(lax.dynamic_update_slice(jnp.zeros((n_seq, D), F32), end_part, (0, column_at)))
    summed = lax.psum_scatter(picked.reshape(n_shard, n_dest, columns, rows), "shard", scatter_dimension=0, tiled=True)
    if fast:
        summed, piece1, end_rows, *halves = lax.optimization_barrier((summed, piece1, end_rows, *halves))
        parts = [part for mine in halves for part in (mine, swap(mine, "section", 1))]
    routed = lax.all_to_all(summed.reshape(n_dest, columns, rows), ("section", "ctx"), split_axis=0, concat_axis=0, tiled=True)
    embedded = routed.reshape(D, rows).T.astype(F32)
    end_row = lax.dynamic_slice_in_dim(end_rows, seq_at, 1, 0)
    units1 = lax.all_gather(piece1, order, axis=0, tiled=True)

    length = lax.dynamic_slice_in_dim(lengths, seq_in, 1, 0)[0]
    others = [group ^ (2 * cb + sb) for sb in range(2) for cb in range(half)]
    meta = jnp.stack([group, length] + others).astype(jnp.int32)
    span = jnp.arange(hb, dtype=jnp.int32)
    positions = jnp.concatenate([group * hb + span, (2 * n - 1 - group) * hb + span])

    vecs0, vecs1 = vector_master[0:4], vector_master[4:8]
    hidden1 = layer_norm(embedded, vecs0[0], vecs0[1]).astype(BF)
    if fast:
        hidden1, *parts = lax.optimization_barrier((hidden1, *parts))
        units0 = place_units(parts)
    weights0 = layer_weights(units0)
    others = pieces_by_ctx(hidden1, half)[1:]
    *others, w_qkv0, w_up0 = lax.optimization_barrier((*others, weights0[0], weights0[2]))
    weights0 = (w_qkv0, weights0[1], w_up0, weights0[3])
    out0, saved0 = layer_forward(embedded, hidden1, pieces_by_section([hidden1, *others]), meta, n, weights0, vecs0)
    x1 = out0.astype(BF).astype(F32)
    x1, units1 = lax.optimization_barrier((x1, units1))
    w_qkv1 = split_units(units1, 0, 3)
    weights1 = ((w_qkv1[0], w_qkv1[1], w_qkv1[2]), units1[U_OUT:U_UP], join_units(units1, U_UP, N_UP), units1[U_DOWN:])
    final, saved1 = last_forward(x1, positions, length, half, weights1, vecs1)

    def score_terms(final_row, end_vals, gain_vec, bias_vec, head_vec):
        normed = layer_norm(final_row, gain_vec, bias_vec)
        return jnp.sum(normed * (end_vals + head_vec)) * D ** (-0.5)

    counted = group == 0
    score, score_back = jax.vjp(score_terms, final, end_row, vector_master[8], vector_master[9], vector_master[10])
    scores = sum_small(jnp.where((jnp.arange(n_seq) == seq_at) & counted, score, 0.0)[None])[0]

    def pair_loss(score_vals):
        return jnp.sum(softplus(score_vals[pairs[:, 1]] - score_vals[pairs[:, 0]]))

    loss_sum, loss_back = jax.vjp(pair_loss, scores)
    grad_scores = loss_back(jnp.ones_like(loss_sum))[0]
    grad_own = lax.dynamic_slice_in_dim(grad_scores, seq_at, 1, 0)[0]
    grad_final, grad_end, *vec_final = score_back(grad_own)

    grad_x1, factors, vec1, vec1_row = last_backward(saved1, grad_final, half, weights1, vecs1)
    factors = jnp.concatenate([factors, grad_end.astype(BF)])
    grad_x1 = grad_x1.astype(BF).astype(F32)
    beside = swap(factors, "ctx", half)
    both = jnp.where(seq_in == 0, jnp.stack([factors, beside]), jnp.stack([beside, factors]))
    every_factor = gather_axis(both, "shard").reshape(n_seq, -1, D)
    grad_x0, grads0, vec0, every_factor = layer_backward(saved0, grad_x1, meta, n, weights0, vecs0, every_factor, fast)

    by_owner = grad_x0.astype(BF).T.reshape(n_dest, columns, rows)
    back = lax.all_to_all(by_owner, ("section", "ctx"), split_axis=0, concat_axis=0, tiled=True)
    if fast:
        back, rest0, qkv0 = lax.optimization_barrier((back, *grads0))
        grads0 = jnp.where(c_at == 0, fold_qkv(qkv0), rest0)
        every = jnp.concatenate([back] + [shift(back, "shard", d) for d in (1, 3, 2)])
        every, every_factor, grads0, *vec0 = lax.optimization_barrier((every, every_factor, grads0, *vec0))
        near_order = (z_at + 4 - jnp.array((0, 1, 3, 2), jnp.int32)) % 4
        listed = listed.reshape(n_shard, -1)[near_order].reshape(-1)
        counts = counts.reshape(n_shard, -1)[near_order].reshape(-1)
    else:
        every = lax.all_gather(back, "shard", axis=0, tiled=True)
    end_grads = lax.dynamic_slice(every_factor[:, -1].astype(F32), (0, column_at), (n_seq, columns))
    table_grad = scatter(listed, counts, end_held, meta_emb, every, end_grads, entries)
    once = [jnp.where(counted, v, 0.0) for v in vec1_row + vec_final]
    vector_grad = sum_all(jnp.stack(vec0 + vec1 + once))

    own1 = last_gradient(every_factor, c_at * n_shard + z_at, n * n_shard, size)
    squares = jnp.sum(table_grad * table_grad) + jnp.where(is_first, 0.0, jnp.sum(own1 * own1))
    if fast:
        terms = along_shard(grads0)
        table_grad, own1, squares, vector_grad, *terms = lax.optimization_barrier(
            (table_grad, own1, squares, vector_grad, *terms)
        )
        mine = sum(t.astype(F32) for t in terms)
    else:
        mine = lax.psum_scatter(grads0, order, scatter_dimension=0, tiled=True).astype(F32)
    squares = squares + jnp.sum(mine * mine)
    other = swap(mine.astype(BF), "section", 1).astype(F32)
    own0 = jnp.stack([mine, other], axis=1).reshape(size, D) if fast else jnp.concatenate([mine, other])
    layer_grad = jnp.where(is_first, own0, own1).reshape(-1, LANES)

    squares = sum_small(squares.reshape(1, 1))[0, 0]
    grad_norm = jnp.sqrt(squares + jnp.sum(vector_grad * vector_grad))
    layer_grad, grad_norm = lax.optimization_barrier((layer_grad, grad_norm))
    factor = CLIP_LIMIT / jnp.maximum(grad_norm, CLIP_LIMIT)
    flat = [x.reshape(-1, LANES) for x in (layer_master, layer_first, layer_second)]
    flat_rows = flat[0].shape[0]
    block_rows = max(b for b in range(1, 1025) if flat_rows % b == 0 and (b % 8 == 0 or b == flat_rows))
    table_cols = max(b for b in range(LANES, 1537, LANES) if entries % b == 0)
    layer_new = adam(factor, *flat, layer_grad, 0.4, 0.1, (block_rows, LANES))
    layer_new = [x.reshape(layer_master.shape) for x in layer_new]
    table_new = adam(factor, table_master, table_first, table_second, table_grad, 0.5, 0.1, (columns, table_cols))
    vector_new = adam_update(vector_master, vector_first, vector_second, vector_grad * factor, 0.7, 0.0)
    return (loss_sum, grad_norm, *layer_new, *table_new, *vector_new)


def solution(mesh):
    in_specs = (
        P("shard", "ctx"),
        P("shard"),
        P("shard"),
        P(),
        P("section", ("ctx", "shard")),
        P("section", ("ctx", "shard")),
        P("section", ("ctx", "shard")),
        P(("section", "ctx"), "shard"),
        P(("section", "ctx"), "shard"),
        P(("section", "ctx"), "shard"),
        P(),
        P(),
        P(),
    )
    out_specs = (
        P(),
        P(),
        P("section", ("ctx", "shard")),
        P("section", ("ctx", "shard")),
        P("section", ("ctx", "shard")),
        P(("section", "ctx"), "shard"),
        P(("section", "ctx"), "shard"),
        P(("section", "ctx"), "shard"),
        P(),
        P(),
        P(),
    )
    return jax.shard_map(shards, mesh=mesh, in_specs=in_specs, out_specs=out_specs, check_vma=False)
```

```python
import functools

import jax
import jax.numpy as jnp
from jax import lax
from jax.experimental import pallas as pl
from jax.experimental.layout import Layout, with_layout_constraint
from jax.experimental.pallas import tpu as pltpu
from jax.sharding import PartitionSpec as P

D = 1088
HEADS = 17
HD = 64
FF = 4352
VOCAB = 51200
MICRO = 2
STEP = 10
CLIP_LIMIT = 0.02
ALL = ("section", "ctx", "shard")

LANES = 128
PAIRS_OF_HEADS = (HEADS + 1) // 2
WIDE = PAIRS_OF_HEADS * LANES
N_UP = FF // D
U_OUT = 3 * D
U_UP = U_OUT + D
U_DOWN = U_UP + FF
UNITS = U_DOWN + FF

BF = jnp.bfloat16
F32 = jnp.float32
VMEM_BIG = 56 * 1024 * 1024


def params(limit=VMEM_BIG):
    return pltpu.CompilerParams(vmem_limit_bytes=limit)


def cost(microseconds):
    return pl.CostEstimate(flops=0, bytes_accessed=int(microseconds * 3.0e6), transcendentals=0)


def dot(a, b, contract=((1,), (0,))):
    return lax.dot_general(a, b, (contract, ((), ())), preferred_element_type=F32)


NT = ((1,), (1,))
TN = ((0,), (0,))


def split2(x):
    top = lax.reduce_precision(x, 8, 7)
    return jnp.concatenate([top, x - top]).astype(BF)


def dot2(x, w, contract=((1,), (0,))):
    y = dot(split2(x), w, contract)
    return y[: x.shape[0]] + y[x.shape[0] :]


def swap(x, axis, bit):
    size = lax.axis_size(axis)
    return lax.ppermute(x, axis, [(i, i ^ bit) for i in range(size)])


def gather_axis(x, axis):
    size = lax.axis_size(axis)
    me = lax.axis_index(axis)
    x = x[None]
    bit = 1
    while bit < size:
        other = swap(x, axis, bit)
        lower = (me & bit) == 0
        x = jnp.where(lower, jnp.concatenate([x, other]), jnp.concatenate([other, x]))
        bit *= 2
    return x


def sum_axis(x, axis, first=1, last=None):
    size = lax.axis_size(axis) if last is None else last
    bit = first
    while bit < size:
        x = x + swap(x, axis, bit)
        bit *= 2
    return x


def group_reduce(x, combine, half):
    def step(x, axis, bit):
        other = swap(x, axis, bit)
        lower = (lax.axis_index(axis) & bit) == 0
        return combine(jnp.where(lower, x, other), jnp.where(lower, other, x))

    x = step(x, "section", 1)
    bit = 1
    while bit < half:
        x = step(x, "ctx", bit)
        bit *= 2
    return x


def sum_all(x):
    return sum_axis(sum_axis(sum_axis(x, "section"), "ctx"), "shard")


def sum_direct(x, axis):
    if lax.axis_size(axis) != 4:
        return sum_axis(x, axis)
    one, two, three = [lax.ppermute(x, axis, [(i, (i + d) % 4) for i in range(4)]) for d in (1, 2, 3)]
    return (x + two) + (one + three)


def sum_small(x):
    return sum_direct(sum_direct(sum_direct(x, "section"), "ctx"), "shard")


def rows_kernel(pairs, x, out, scr):
    lane = lax.broadcasted_iota(jnp.int32, (1, LANES), 1)
    step = 2 * D // LANES
    even, odd = pl.ds(0, pairs, stride=2), pl.ds(1, pairs, stride=2)
    flat_row = lambda t: x[pl.ds(t, pairs, stride=step), :]
    for t in range(PAIRS_OF_HEADS):
        scr[t, even, :] = flat_row(t)
    before = pltpu.roll(flat_row(step // 2), HD, 1)
    for t in range(PAIRS_OF_HEADS - 1):
        after = pltpu.roll(flat_row(step // 2 + 1 + t), HD, 1)
        scr[t, odd, :] = jnp.where(lane < HD, before, after)
        before = after
    scr[PAIRS_OF_HEADS - 1, odd, :] = before
    for t, (at, size) in enumerate(tile_cuts()):
        out[:, pl.ds(at, size)] = scr[t][:, :size].astype(BF)


def chunk_rows(flat):
    units = flat.size // D
    return pl.pallas_call(
        functools.partial(rows_kernel, units // 2),
        out_shape=jax.ShapeDtypeStruct((units, D), BF),
        scratch_shapes=[pltpu.VMEM((PAIRS_OF_HEADS, units, LANES), F32)],
        compiler_params=params(),
        cost_estimate=cost(6),
        name="chunk_rows",
    )(flat.reshape(-1, LANES))


def small_block():
    return lax.axis_size("ctx") == 4 and lax.axis_size("shard") == 4 and lax.axis_size("section") == 2


def shift(x, axis, by):
    size = lax.axis_size(axis)
    return lax.ppermute(x, axis, [(i, (i + by) % size) for i in range(size)])


ARRIVALS = ((0,), (1, 3), (2,))
OVERLAP = 16


def place_kernel(rows, at, *refs):
    ins, out, held, sems_in, sems_out = refs[: 2 * len(ARRIVALS)], refs[-4], refs[-3], refs[-2], refs[-1]
    s, c, z = at[0], at[1], at[2]
    short = rows - OVERLAP
    pieces = []
    for g, distances in enumerate(ARRIVALS):
        for other in range(2):
            for e in range(4):
                for i, d in enumerate(distances):
                    chunk = (c ^ e) * 4 + lax.rem(z + 4 - d, 4)
                    pieces.append((ins[2 * g + other].at[e, i], chunk, other))

    def arrive(k):
        return pltpu.make_async_copy(pieces[k][0], held.at[k], sems_in.at[k])

    def leave(k, act):
        _, chunk, other = pieces[k]

        @pl.when(s == other)
        def _():
            act(pltpu.make_async_copy(held.at[k], out.at[chunk, pl.ds(0, rows)], sems_out.at[k]))

        @pl.when(s != other)
        def _():
            act(pltpu.make_async_copy(held.at[k, pl.ds(OVERLAP, short)], out.at[chunk, pl.ds(rows, short)], sems_out.at[k]))

    for k in range(len(pieces)):
        arrive(k).start()
    for k in range(len(pieces)):
        arrive(k).wait()
        leave(k, lambda copy: copy.start())
    for k in range(len(pieces)):
        leave(k, lambda copy: copy.wait())


def by_links(own):
    return swap(own, "ctx", 1), swap(own, "ctx", 2)


def first_moves(piece):
    return shift(piece, "shard", 1), shift(piece, "shard", 3), *by_links(piece[None])


def second_moves(piece, near, far):
    return shift(piece, "shard", 2), *by_links(jnp.stack([near, far]))


def corner_of(by_x, by_y):
    cut = by_x.shape[1] // 2
    return jnp.concatenate([swap(by_x[:, :cut], "ctx", 2), swap(by_y[:, cut:], "ctx", 1)], axis=1)


def gather_half(piece, first, second):
    near, far, *own_links = first
    opposite, *near_links = second
    arrived = {0: piece, 1: near, 3: far, 2: opposite}
    parts = []
    for distances, links in zip(ARRIVALS, (own_links, near_links, None)):
        own = jnp.stack([arrived[d] for d in distances])
        by_x, by_y = by_links(own) if links is None else links
        corner = corner_of(by_x, by_y)
        parts.append(jnp.stack([own, by_x, by_y, corner]))
    return parts


def place_units(parts):
    rows = parts[0].shape[2]
    at = jnp.stack([lax.axis_index(a) for a in ALL]).astype(jnp.int32)
    grid_spec = pltpu.PrefetchScalarGridSpec(
        num_scalar_prefetch=1,
        grid=(1,),
        in_specs=[pl.BlockSpec(memory_space=pl.ANY)] * len(parts),
        out_specs=pl.BlockSpec(memory_space=pl.ANY),
        scratch_shapes=[pltpu.VMEM((32, rows, D), BF), pltpu.SemaphoreType.DMA((32,)), pltpu.SemaphoreType.DMA((32,))],
    )
    whole = pl.pallas_call(
        functools.partial(place_kernel, rows),
        grid_spec=grid_spec,
        out_shape=jax.ShapeDtypeStruct((16, 2 * rows - OVERLAP, D), BF),
        compiler_params=params(),
        cost_estimate=cost(16),
        name="place",
    )(at, *parts)
    return whole.reshape(UNITS, D)


def add_low(x, y):
    return (x.astype(F32) + y.astype(F32)).astype(BF)


BLOCK = 136
QUARTER = 104


def core_blocks(region):
    s = lax.axis_index("section")
    blocks = region.reshape(-1, 2, BLOCK, D)
    pick = lambda i: lax.dynamic_index_in_dim(blocks, i, 1, keepdims=False)
    return pick(s), pick(1 - s)


def fold_cores(region):
    mine, other = core_blocks(region)
    return add_low(mine, swap(other, "section", 1))


def one_way(x, bit, sends):
    return lax.ppermute(x, "ctx", [(i, i ^ bit) for i in range(4) if sends(i)])


def three_first(one, two, both, p):
    has_p = (lax.axis_index("ctx") & p) != 0
    return swap(jnp.where(has_p, two, one), "ctx", p), one_way(both, p, lambda i: not i & p)


def three_second(one, two, both, came, came_both, p, q):
    c = lax.axis_index("ctx")
    has_p, has_q = (c & p) != 0, (c & q) != 0
    single = add_low(jnp.where(has_p, one, two), came)
    both = add_low(both, came_both)
    sent = jnp.where(has_p & ~has_q, both, single)
    came = one_way(sent, q, lambda i: not i & q or i & p)
    return add_low(jnp.where(has_p & has_q, both, single), came)


def rest_first(rest):
    x = rest.reshape(3, 4, -1, BLOCK, D)
    return *three_first(x[0, :2], x[1, :2], x[2, :2], 1), *three_first(x[1, 2:], x[0, 2:], x[2, 2:], 2)


def rest_second(rest, came):
    x = rest.reshape(3, 4, -1, BLOCK, D)
    first = three_second(x[0, :2], x[1, :2], x[2, :2], came[0], came[1], 1, 2)
    second = three_second(x[1, 2:], x[0, 2:], x[2, 2:], came[2], came[3], 2, 1)
    return jnp.concatenate([first, second])


def fold_half(v, axis, bit):
    mine = (lax.axis_index("ctx") // bit) & 1
    pick = lambda i: lax.dynamic_index_in_dim(v, i, axis, keepdims=True)
    return add_low(pick(mine), swap(pick(1 - mine), "ctx", bit))


def qkv_first(qkv):
    x = qkv.reshape(4, -1, D)
    x = jnp.pad(x, ((0, 0), (0, 4 * QUARTER - x.shape[1]), (0, 0))).reshape(4, 2, 2, QUARTER, D)
    return fold_half(x[:2], 2, 1), fold_half(x[2:], 1, 2)


def qkv_second(first, second):
    return jnp.concatenate([fold_half(first, 1, 2), fold_half(second, 2, 1)])[:, 0, 0]


def collect_qkv(quarter):
    low = quarter.astype(BF)
    others = [lax.ppermute(low, "ctx", [(i, 0)]).astype(F32) for i in (1, 2, 3)]
    return jnp.concatenate([quarter, *others])


def shard_chunk(x, by):
    return lax.dynamic_index_in_dim(x, lax.rem(lax.axis_index("shard") + by, 4), 0, keepdims=False)


def along_shard(x, distances):
    return [shift(shard_chunk(x, d), "shard", d) for d in distances]


SHIFT = 10
UNROLL = 8


def owned_rows(ids, entries):
    rows = ids.shape[1]
    assert rows < (1 << SHIFT)
    owned = ids < entries
    place = jnp.cumsum(owned.astype(jnp.int32), axis=1) - 1
    packed = jnp.arange(rows, dtype=jnp.int32)[None, :] + (ids << SHIFT)
    slots = jnp.arange(rows, dtype=jnp.int32)
    hit = (place[:, None, :] == slots[None, :, None]) & owned[:, None, :]
    listed = jnp.sum(jnp.where(hit, packed[:, None, :], 0), axis=2)
    count = jnp.sum(owned.astype(jnp.int32), axis=1)
    listed = jnp.where(slots[None, :] < count[:, None], listed, rows + (entries << SHIFT))
    return listed.reshape(-1), count


def for_owned(listed, counts, step, rows, body):
    def some(t, _):
        for u in range(UNROLL):
            packed = listed[step * rows + t * UNROLL + u]
            body(pl.ds(packed & ((1 << SHIFT) - 1), 1), pl.ds(packed >> SHIFT, 1))
        return 0

    lax.fori_loop(0, (counts[step] + UNROLL - 1) // UNROLL, some, 0)


def lookup_kernel(rows, listed, counts, end_ids, meta, table, out, ends, tab, buf):
    step = pl.program_id(0)
    columns, entries = table.shape

    @pl.when(step == 0)
    def _():
        def turn(i, _):
            at = pl.multiple_of(i * 256, 256)
            tab[pl.ds(at, 256), :] = table[:, pl.ds(at, 256)].astype(BF).astype(F32).T
            return 0

        lax.fori_loop(0, entries // 256, turn, 0)
        tab[pl.ds(entries, 8), :] = jnp.zeros((8, columns), F32)
        for n in range(ends.shape[0]):
            ends[pl.ds(n, 1), :] = tab[pl.ds(end_ids[n], 1), :]

    buf[...] = jnp.zeros_like(buf)

    def pick(place, entry):
        buf[place, :] = tab[entry, :]

    for_owned(listed, counts, step, rows, pick)

    @pl.when(meta[0] == 1)
    def _():
        half = rows // 2
        group = meta[4 + step]
        for j in range(2):
            block = group if j == 0 else 2 * meta[1] - 1 - group
            at = pl.multiple_of(meta[2] + block * half, 8)
            buf[pl.ds(j * half, half), :] += tab[pl.ds(at, half), :]

    out[0] = buf[pl.ds(0, rows), :].T.astype(BF)


def lookup(listed, counts, end_ids, meta, table, n_blocks, rows):
    columns, entries = table.shape
    n_ends = end_ids.shape[0]
    grid_spec = pltpu.PrefetchScalarGridSpec(
        num_scalar_prefetch=4,
        grid=(n_blocks,),
        in_specs=[pl.BlockSpec((columns, entries), lambda i, *_: (0, 0))],
        out_specs=[
            pl.BlockSpec((1, columns, rows), lambda i, *_: (i, 0, 0)),
            pl.BlockSpec((n_ends, columns), lambda i, *_: (0, 0)),
        ],
        scratch_shapes=[pltpu.VMEM((entries + 8, columns), F32), pltpu.VMEM((rows + 8, columns), F32)],
    )
    return pl.pallas_call(
        functools.partial(lookup_kernel, rows),
        grid_spec=grid_spec,
        out_shape=[
            jax.ShapeDtypeStruct((n_blocks, columns, rows), BF),
            jax.ShapeDtypeStruct((n_ends, columns), F32),
        ],
        compiler_params=params(),
        cost_estimate=cost(40),
        name="lookup",
    )(listed, counts, end_ids, meta, table)


def scatter_kernel(rows, n_blocks, listed, counts, end_ids, meta, grads, ends, out, acc, buf):
    step = pl.program_id(0)
    columns, entries = out.shape
    n_ends = ends.shape[0]

    @pl.when(step == 0)
    def _():
        def clear(i, _):
            acc[pl.ds(pl.multiple_of(i * 256, 256), 256), :] = jnp.zeros((256, columns), F32)
            return 0

        lax.fori_loop(0, entries // 256, clear, 0)
        for n in range(n_ends):
            at = pl.ds(end_ids[n], 1)
            acc[at, :] += ends[pl.ds(n, 1), :]

    buf[pl.ds(0, rows), :] = grads[0].astype(F32).T

    def add(place, entry):
        acc[entry, :] += buf[place, :]

    for_owned(listed, counts, step, rows, add)

    @pl.when(meta[0] == 1)
    def _():
        half = rows // 2
        group = meta[4 + step]
        for j in range(2):
            block = group if j == 0 else 2 * meta[1] - 1 - group
            at = pl.multiple_of(meta[2] + block * half, 8)
            acc[pl.ds(at, half), :] += buf[pl.ds(j * half, half), :]

    @pl.when(step == n_blocks - 1)
    def _():
        def turn(i, _):
            at = pl.multiple_of(i * 256, 256)
            out[:, pl.ds(at, 256)] = acc[pl.ds(at, 256), :].T
            return 0

        lax.fori_loop(0, entries // 256, turn, 0)


def scatter(listed, counts, end_ids, meta, grads, ends, entries):
    n_blocks, columns, rows = grads.shape
    n_ends = ends.shape[0]
    grid_spec = pltpu.PrefetchScalarGridSpec(
        num_scalar_prefetch=4,
        grid=(n_blocks,),
        in_specs=[
            pl.BlockSpec((1, columns, rows), lambda i, *_: (i, 0, 0)),
            pl.BlockSpec((n_ends, columns), lambda i, *_: (0, 0)),
        ],
        out_specs=pl.BlockSpec((columns, entries), lambda i, *_: (0, 0)),
        scratch_shapes=[pltpu.VMEM((entries + 8, columns), F32), pltpu.VMEM((rows + 8, columns), F32)],
    )
    return pl.pallas_call(
        functools.partial(scatter_kernel, rows, n_blocks),
        grid_spec=grid_spec,
        out_shape=jax.ShapeDtypeStruct((columns, entries), F32),
        compiler_params=params(),
        cost_estimate=cost(42),
        name="scatter",
    )(listed, counts, end_ids, meta, grads, ends)


def tile_cuts():
    return [(t * LANES, min(LANES, D - t * LANES)) for t in range(PAIRS_OF_HEADS)]


def split_kernel(count, rb, width, u, out, scr):
    for t, (at, size) in enumerate(tile_cuts()):
        part = u[:, pl.ds(at, size)].astype(F32)
        if size < LANES:
            part = jnp.concatenate([part, jnp.zeros((rb * count, LANES - size), F32)], axis=1)
        scr[t] = part
        for j in range(count):
            picked = scr[t, pl.ds(j, rb, stride=count), :].astype(BF)
            take = min(LANES, width - at)
            out[j, :, pl.ds(at, take)] = picked[:, :take]


def join_kernel(count, rb, u, out, scr):
    for t, (at, size) in enumerate(tile_cuts()):
        part = u[:, pl.ds(at, size)].astype(F32)
        if size < LANES:
            part = jnp.concatenate([part, jnp.zeros((rb * count, LANES - size), F32)], axis=1)
        scr[t] = part
        for j in range(count):
            out[:, pl.ds(j * D + at, size)] = scr[t, pl.ds(j, rb, stride=count), :].astype(BF)[:, :size]


def join_units(u, first, count):
    rb = 272
    return pl.pallas_call(
        functools.partial(join_kernel, count, rb),
        grid=(D // rb,),
        in_specs=[pl.BlockSpec((rb * count, D), lambda i: (i + first // (rb * count), 0))],
        out_specs=pl.BlockSpec((rb, count * D), lambda i: (i, 0)),
        out_shape=jax.ShapeDtypeStruct((D, count * D), BF),
        scratch_shapes=[pltpu.VMEM((PAIRS_OF_HEADS, rb * count, LANES), F32)],
        compiler_params=params(),
        cost_estimate=cost(8),
        name="join_units",
    )(u)


def split_units(u, first, count, width=D):
    rb = 272
    return pl.pallas_call(
        functools.partial(split_kernel, count, rb, width),
        grid=(D // rb,),
        in_specs=[pl.BlockSpec((rb * count, D), lambda i: (i + first // (rb * count), 0))],
        out_specs=pl.BlockSpec((count, rb, width), lambda i: (0, i, 0)),
        out_shape=jax.ShapeDtypeStruct((count, D, width), BF),
        scratch_shapes=[pltpu.VMEM((PAIRS_OF_HEADS, rb * count, LANES), F32)],
        compiler_params=params(),
        cost_estimate=cost(8),
        name="split_units",
    )(u)


def merge_kernel(count, rb, starts, *refs):
    parts, out, scr = refs[:-2], refs[-2], refs[-1]
    for t, (at, size) in enumerate(tile_cuts()):
        for j in range(count):
            which, start = starts[j]
            part = parts[which][:, pl.ds(start + at, size)].astype(F32)
            if size < LANES:
                part = jnp.concatenate([part, jnp.zeros((rb, LANES - size), F32)], axis=1)
            scr[t, pl.ds(j, rb, stride=count), :] = part
        out[:, pl.ds(at, size)] = scr[t][:, :size].astype(BF)


def merge_units(parts, starts):
    rb, count = 272, len(starts)
    return pl.pallas_call(
        functools.partial(merge_kernel, count, rb, starts),
        grid=(D // rb,),
        in_specs=[pl.BlockSpec((rb, p.shape[1]), lambda i: (i, 0)) for p in parts],
        out_specs=pl.BlockSpec((rb * count, D), lambda i: (i, 0)),
        out_shape=jax.ShapeDtypeStruct((count * D, D), BF),
        scratch_shapes=[pltpu.VMEM((PAIRS_OF_HEADS, rb * count, LANES), F32)],
        compiler_params=params(),
        cost_estimate=cost(8),
        name="merge_units",
    )(*parts)


def adam_kernel(rate, decay, factor, w, m, v, g, w_out, m_out, v_out):
    w_out[...], m_out[...], v_out[...] = adam_update(w[...], m[...], v[...], g[...] * factor[0], rate, decay)


def adam(factor, weight, first, second, grad, rate, decay, block):
    shape = weight.shape
    grid = tuple(size // b for size, b in zip(shape, block))
    spec = pl.BlockSpec(block, lambda i, j, *_: (i, j))
    return pl.pallas_call(
        functools.partial(adam_kernel, rate, decay),
        grid_spec=pltpu.PrefetchScalarGridSpec(num_scalar_prefetch=1, grid=grid, in_specs=[spec] * 4, out_specs=[spec] * 3),
        out_shape=[jax.ShapeDtypeStruct(shape, F32)] * 3,
        compiler_params=params(),
        cost_estimate=cost(weight.size * 9.0e-6),
        name="adam",
    )(factor.reshape(1), weight, first, second, grad)


def chunk_plan(n):
    plan = [(0, "ll", True), (0, "hl", False), (0, "hh", True)]
    for p in range(1, n):
        plan += [(p, "hl", False), (p, "sel", False)]
    return plan


def chunk_offsets(meta, n, hb, p, kind):
    own = meta[0]
    piece = meta[2 + p]
    if kind == "ll":
        return 0, p * 2 * hb, own * hb, piece * hb, True
    if kind == "hl":
        return hb, p * 2 * hb, (2 * n - 1 - own) * hb, piece * hb, False
    if kind == "hh":
        return hb, p * 2 * hb + hb, (2 * n - 1 - own) * hb, (2 * n - 1 - piece) * hb, False
    low = piece < own
    q_off = pl.multiple_of(jnp.where(low, 0, hb), hb)
    k_off = pl.multiple_of(p * 2 * hb + jnp.where(low, 0, hb), hb)
    key_pos = jnp.where(low, piece, 2 * n - 1 - piece) * hb
    return q_off, k_off, None, key_pos, low


def chunk_scores(keys, queries, meta, diagonal, kind, q_pos, k_pos, hb):
    s = dot(keys, queries, NT)
    if diagonal:
        ki = lax.broadcasted_iota(jnp.int32, (hb, hb), 0)
        qi = lax.broadcasted_iota(jnp.int32, (hb, hb), 1)
        keep = (ki <= qi) & (ki + k_pos < meta[1])
        s = jnp.where(keep, s, -1e30)
    elif kind == "sel":
        ki = lax.broadcasted_iota(jnp.int32, (hb, hb), 0)
        s = jnp.where(ki < meta[1] - k_pos, s, -1e30)
    return s


def attend_kernel(n, hb, meta, q_ref, k_ref, v_ref, o_ref, lse_ref, vt_ref):
    keys = 2 * hb * n
    for i in range(keys // hb):
        vt_ref[i] = v_ref[pl.ds(i * hb, hb), :].astype(F32).T.astype(BF)
    lane = lax.broadcasted_iota(jnp.int32, (1, LANES), 1)
    plan = chunk_plan(n)
    outs = []
    for head in range(2):
        own_lanes = (lane // HD) == head
        info, scores = [], []
        tops = [jnp.full((1, hb), -3e38, F32), jnp.full((1, hb), -3e38, F32)]
        for p, kind, diagonal in plan:
            q_off, k_off, q_pos, k_pos, low = chunk_offsets(meta, n, hb, p, kind)
            queries = jnp.where(own_lanes, q_ref[pl.ds(q_off, hb), :], 0)
            s = chunk_scores(k_ref[pl.ds(k_off, hb), :], queries, meta, diagonal, kind, q_pos, k_pos, hb)
            top = jnp.max(s, axis=0, keepdims=True)
            if low is True:
                tops[0] = jnp.maximum(tops[0], top)
            elif low is False:
                tops[1] = jnp.maximum(tops[1], top)
            else:
                tops[0] = jnp.maximum(tops[0], jnp.where(low, top, -3e38))
                tops[1] = jnp.maximum(tops[1], jnp.where(low, -3e38, top))
            info.append((k_off, low))
            scores.append(s)
        sums = [jnp.zeros((1, hb), F32), jnp.zeros((1, hb), F32)]
        accs = [jnp.zeros((HD, hb), F32), jnp.zeros((HD, hb), F32)]
        for (k_off, low), s in zip(info, scores):
            if low is True or low is False:
                top = tops[0] if low else tops[1]
            else:
                top = jnp.where(low, tops[0], tops[1])
            e = jnp.exp(s - top)
            total = jnp.sum(e, axis=0, keepdims=True)
            got = dot(vt_ref[k_off // hb, pl.ds(head * HD, HD), :], e.astype(BF))
            if low is True or low is False:
                sums[1 - low] += total
                accs[1 - low] += got
            else:
                sums[0] += jnp.where(low, total, 0.0)
                sums[1] += jnp.where(low, 0.0, total)
                accs[0] += jnp.where(low, got, 0.0)
                accs[1] += jnp.where(low, 0.0, got)
        outs.append([accs[i] / sums[i] for i in range(2)])
        for i in range(2):
            lse_ref[0, pl.ds(head, 1), pl.ds(i * hb, hb)] = tops[i] + jnp.log(sums[i])
    for i in range(2):
        both = jnp.concatenate([outs[0][i], outs[1][i]], axis=0)
        o_ref[pl.ds(i * hb, hb), :] = both.T.astype(BF)


def attend(meta, q, k, v, n):
    rows = q.shape[0]
    keys = k.shape[0]
    grid_spec = pltpu.PrefetchScalarGridSpec(
        num_scalar_prefetch=1,
        grid=(PAIRS_OF_HEADS,),
        in_specs=[
            pl.BlockSpec((rows, LANES), lambda p, *_: (0, p)),
            pl.BlockSpec((keys, LANES), lambda p, *_: (0, p)),
            pl.BlockSpec((keys, LANES), lambda p, *_: (0, p)),
        ],
        out_specs=[
            pl.BlockSpec((rows, LANES), lambda p, *_: (0, p)),
            pl.BlockSpec((1, 8, rows), lambda p, *_: (p, 0, 0)),
        ],
        scratch_shapes=[pltpu.VMEM((2 * n, LANES, rows // 2), BF)],
    )
    return pl.pallas_call(
        functools.partial(attend_kernel, n, rows // 2),
        grid_spec=grid_spec,
        out_shape=[
            jax.ShapeDtypeStruct((rows, WIDE), BF),
            jax.ShapeDtypeStruct((PAIRS_OF_HEADS, 8, rows), F32),
        ],
        compiler_params=params(),
        cost_estimate=cost(23),
        name="attend",
    )(meta, q, k, v)


def attend_back_kernel(n, hb, meta, q_ref, k_ref, v_ref, o_ref, do_ref, lse_ref, dq_ref, dk_ref, dv_ref, kt_ref, dk_acc, dv_acc):
    keys = 2 * hb * n
    for i in range(keys // hb):
        kt_ref[i] = k_ref[pl.ds(i * hb, hb), :].astype(F32).T.astype(BF)
    dk_acc[...] = jnp.zeros_like(dk_acc)
    dv_acc[...] = jnp.zeros_like(dv_acc)
    lane = lax.broadcasted_iota(jnp.int32, (1, LANES), 1)
    plan = chunk_plan(n)
    prods = []
    for i in range(2):
        part = pl.ds(i * hb, hb)
        prods.append((o_ref[part, :].astype(F32) * do_ref[part, :].astype(F32)).T)
    dqs = []
    for head in range(2):
        own_lanes = (lane // HD) == head
        deltas = [jnp.sum(prods[i][head * HD : (head + 1) * HD, :], axis=0, keepdims=True) for i in range(2)]
        lses = [lse_ref[0, pl.ds(head, 1), pl.ds(i * hb, hb)] for i in range(2)]
        accs = [jnp.zeros((HD, hb), F32), jnp.zeros((HD, hb), F32)]
        for p, kind, diagonal in plan:
            q_off, k_off, q_pos, k_pos, low = chunk_offsets(meta, n, hb, p, kind)
            q_at, k_at = pl.ds(q_off, hb), pl.ds(k_off, hb)
            queries = jnp.where(own_lanes, q_ref[q_at, :], 0)
            d_out = jnp.where(own_lanes, do_ref[q_at, :], 0)
            s = chunk_scores(k_ref[k_at, :], queries, meta, diagonal, kind, q_pos, k_pos, hb)
            if low is True or low is False:
                lse, delta = lses[1 - low], deltas[1 - low]
            else:
                lse, delta = jnp.where(low, lses[0], lses[1]), jnp.where(low, deltas[0], deltas[1])
            prob = jnp.exp(s - lse)
            d_prob = dot(v_ref[k_at, :], d_out, NT)
            d_score = (prob * (d_prob - delta)).astype(BF)
            dv_acc[k_at, :] += dot(prob.astype(BF), d_out)
            dk_acc[k_at, :] += dot(d_score, queries)
            got = dot(kt_ref[k_off // hb, pl.ds(head * HD, HD), :], d_score)
            if low is True or low is False:
                accs[1 - low] += got
            else:
                accs[0] += jnp.where(low, got, 0.0)
                accs[1] += jnp.where(low, 0.0, got)
        dqs.append(accs)
    for i in range(2):
        both = jnp.concatenate([dqs[0][i], dqs[1][i]], axis=0) * 0.125
        dq_ref[pl.ds(i * hb, hb), :] = both.T.astype(BF)
    dk_ref[...] = dk_acc[...].astype(BF)
    dv_ref[...] = dv_acc[...].astype(BF)


def attend_back(meta, q, k, v, o, d_o, lse, n):
    rows = q.shape[0]
    keys = k.shape[0]
    row_spec = pl.BlockSpec((rows, LANES), lambda p, *_: (0, p))
    key_spec = pl.BlockSpec((keys, LANES), lambda p, *_: (0, p))
    grid_spec = pltpu.PrefetchScalarGridSpec(
        num_scalar_prefetch=1,
        grid=(PAIRS_OF_HEADS,),
        in_specs=[row_spec, key_spec, key_spec, row_spec, row_spec, pl.BlockSpec((1, 8, rows), lambda p, *_: (p, 0, 0))],
        out_specs=[row_spec, key_spec, key_spec],
        scratch_shapes=[pltpu.VMEM((2 * n, LANES, rows // 2), BF), pltpu.VMEM((keys, LANES), F32), pltpu.VMEM((keys, LANES), F32)],
    )
    return pl.pallas_call(
        functools.partial(attend_back_kernel, n, rows // 2),
        grid_spec=grid_spec,
        out_shape=[
            jax.ShapeDtypeStruct((rows, WIDE), BF),
            jax.ShapeDtypeStruct((keys, WIDE), BF),
            jax.ShapeDtypeStruct((keys, WIDE), BF),
        ],
        compiler_params=params(),
        cost_estimate=cost(46),
        name="attend_back",
    )(meta, q, k, v, o, d_o, lse)


def by_rows(x):
    return with_layout_constraint(x, Layout(major_to_minor=tuple(range(x.ndim))))


def layer_norm(values, gain_vec, bias_vec):
    row_mean = jnp.mean(values, -1, keepdims=True)
    centred = values - row_mean
    variance = jnp.mean(centred * centred, -1, keepdims=True)
    return centred * lax.rsqrt(variance + 1e-05) * gain_vec + bias_vec


def gelu_tanh(values):
    return 0.5 * values * (1.0 + jnp.tanh(0.7978845608 * (values + 0.044715 * values * values * values)))


def softplus(values):
    return jnp.maximum(values, 0.0) + jnp.log1p(jnp.exp(-jnp.abs(values)))


def adam_update(weight, first, second, grad, rate, decay):
    first = 0.9 * first + 0.1 * grad
    second = 0.95 * second + 0.05 * grad * grad
    first_hat = first / (1.0 - 0.9**STEP)
    second_hat = second / (1.0 - 0.95**STEP)
    weight = weight - rate * (first_hat / (jnp.sqrt(second_hat) + 1e-08) + decay * weight)
    return (weight, first, second)


def pieces_by_ctx(x, half):
    got = [x]
    bit = 1
    while bit < half:
        got += [swap(y, "ctx", bit) for y in got]
        bit *= 2
    return got


def pieces_by_section(got):
    own = jnp.concatenate(got)
    return jnp.concatenate([own, swap(own, "section", 1)])


def sum_pieces(near, far, half):
    rows = near.shape[0] // half
    x = near + swap(far, "section", 1).astype(F32)
    bit = half // 2
    while bit >= 1:
        keep, send = x[: bit * rows], x[bit * rows : 2 * bit * rows]
        x = keep + swap(send.astype(BF), "ctx", bit).astype(F32)
        bit //= 2
    return x


def layer_weights(units):
    return split_units(units, 0, 3, WIDE), units[U_OUT:U_UP], join_units(units, U_UP, N_UP), units[U_DOWN:]


def layer_forward(values, hidden1, all_hidden1, meta, n, weights, vecs):
    w_qkv, w_out, w_up, w_down = weights
    keys = dot(all_hidden1, w_qkv[1]).astype(BF)
    vals = dot(all_hidden1, w_qkv[2]).astype(BF)
    queries = dot(hidden1, w_qkv[0]).astype(BF) * jnp.asarray(0.125, BF)
    attended, lse = attend(meta, queries, keys, vals, n)
    middle = values + dot(attended[:, :D], w_out)
    hidden2 = layer_norm(middle, vecs[2], vecs[3]).astype(BF)
    ups = dot(hidden2, w_up)
    gated = gelu_tanh(ups).astype(BF)
    result = middle + dot(gated, w_down)
    return result, (values, all_hidden1, queries, keys, vals, attended, lse, middle, hidden2, ups, gated)


def layer_backward(saved, grad_out, meta, n, weights, vecs, factors, fast):
    values, all_hidden1, queries, keys, vals, attended, lse, middle, hidden2, ups, gated = saved
    w_qkv, w_out, w_up, w_down = weights
    grad_ffn = grad_out.astype(BF)
    grad_down = by_rows(dot(gated, grad_ffn, TN).astype(BF))
    if fast:
        mine_down, other_down = core_blocks(grad_down)
        grad_ffn, other_down = lax.optimization_barrier((grad_ffn, other_down))
        came_down = swap(other_down, "section", 1)
    _, back = jax.vjp(gelu_tanh, ups)
    grad_ups = by_rows(back(dot(grad_ffn, w_down, NT))[0].astype(BF))
    grad_up = merge_units([dot(hidden2, grad_ups, TN).astype(BF)], [(0, j * D) for j in range(N_UP)])
    if fast:
        mine_up, other_up = core_blocks(grad_up)
        grad_ups, other_up = lax.optimization_barrier((grad_ups, other_up))
        came_up = swap(other_up, "section", 1)
    grad_hidden2 = dot(grad_ups, w_up, NT)
    _, norm_back2 = jax.vjp(layer_norm, middle, vecs[2], vecs[3])
    grad_norm2, grad_gain2, grad_bias2 = norm_back2(grad_hidden2)
    grad_middle = grad_out + grad_norm2
    grad_branch = grad_middle.astype(BF)
    grad_outw = dot(attended[:, :D], grad_branch, TN).astype(BF)
    grad_att = dot(grad_branch, jnp.pad(w_out, ((0, WIDE - D), (0, 0))), NT).astype(BF)
    if fast:
        rest = jnp.concatenate([fold_cores(grad_outw), add_low(mine_up, came_up), add_low(mine_down, came_down)])
        grad_att, rest, factors = lax.optimization_barrier((grad_att, rest, factors))
        came = rest_first(rest)
    grad_q, part_k, part_v = attend_back(meta, queries, keys, vals, attended, grad_att, lse, n)
    rows, near = grad_q.shape[0], part_k.shape[0] // 2
    def to_hidden1(at):
        return dot(part_k[at], w_qkv[1], NT) + dot(part_v[at], w_qkv[2], NT)

    far = to_hidden1(slice(near, None)).astype(BF)
    if fast:
        far, *came = lax.optimization_barrier((far, *came))
    grad_q, part_k, part_v, far = lax.optimization_barrier((grad_q, part_k, part_v, far))
    close = to_hidden1(slice(0, near))
    grad_hidden1 = sum_pieces(close, far, n // 2)
    grad_hidden1 = grad_hidden1 + dot(grad_q, w_qkv[0], NT)
    _, norm_back1 = jax.vjp(layer_norm, values, vecs[0], vecs[1])
    grad_norm1, grad_gain1, grad_bias1 = norm_back1(grad_hidden1)
    grad_input = (grad_middle + grad_norm1).astype(BF)
    grad_input, grad_q, part_k, part_v = lax.optimization_barrier((grad_input, grad_q, part_k, part_v))
    grad_qk = [dot(h, g, TN).astype(BF) for h, g in ((all_hidden1[:rows], grad_q), (all_hidden1, part_k))]

    def grad_qkvw(part_v):
        return merge_units([*grad_qk, dot(all_hidden1, part_v, TN).astype(BF)], [(j, 0) for j in range(3)])

    if fast:
        rest = rest_second(rest, came)
        summed = (rest, *along_shard(rest, (1, 3))), (part_v, lambda v: fold_cores(grad_qkvw(v)))
    else:
        summed = jnp.concatenate([grad_qkvw(part_v), grad_outw, grad_up, grad_down])
    return grad_input, summed, [grad_gain1, grad_bias1, grad_gain2, grad_bias2], factors


def head_mask():
    head = lax.broadcasted_iota(jnp.int32, (HEADS, D), 0)
    return lax.broadcasted_iota(jnp.int32, (HEADS, D), 1) // HD == head


def last_forward(values, positions, length, half, weights, vecs):
    (w_q, w_k, w_v), w_out, w_up, w_down = weights
    heads = head_mask()
    hidden1 = layer_norm(values, vecs[0], vecs[1]).astype(BF)
    mine = (positions == length - 1)[:, None]
    row = jnp.sum(jnp.where(mine, values, 0.0), axis=0, keepdims=True)
    row = group_reduce(row, jnp.add, half)
    row_h1 = layer_norm(row, vecs[0], vecs[1]).astype(BF)
    query = dot(row_h1, w_q).astype(BF)
    wq = dot(jnp.where(heads, query, 0), w_k, NT) * 0.125
    scores = dot2(wq, hidden1, NT)
    scores = jnp.where((positions < length)[None, :], scores, -1e30)
    top = jnp.max(scores, axis=1, keepdims=True)
    expo = jnp.exp(scores - top)
    total = jnp.sum(expo, axis=1, keepdims=True)
    mixed = dot(expo.astype(BF), hidden1)
    wide = lambda x: jnp.broadcast_to(x, (HEADS, HD))

    def merge(x, y):
        high = jnp.maximum(x[:, D : D + 1], y[:, D : D + 1])
        x = x * jnp.exp(x[:, D : D + 1] - high)
        y = y * jnp.exp(y[:, D : D + 1] - high)
        return jnp.concatenate([x[:, :D] + y[:, :D], wide(high), x[:, D + HD :] + y[:, D + HD :]], axis=1)

    merged = group_reduce(jnp.concatenate([mixed, wide(top), wide(total)], axis=1), merge, half)
    top, total = merged[:, D : D + 1], merged[:, D + HD : D + HD + 1]
    mixed = merged[:, :D] / total
    probs = jnp.exp(scores - top) / total
    att = jnp.sum(jnp.where(heads, dot2(mixed, w_v), 0.0), axis=0, keepdims=True)
    middle = row + dot(att.astype(BF), w_out)
    hidden2 = layer_norm(middle, vecs[2], vecs[3]).astype(BF)
    ups = dot(hidden2, w_up)
    gated = gelu_tanh(ups).astype(BF)
    result = middle + dot(gated, w_down)
    return result, (values, hidden1, mine, row_h1, query, wq, probs, mixed, att, middle, hidden2, ups, gated)


def last_backward(saved, grad_out, half, weights, vecs):
    values, hidden1, mine, row_h1, query, wq, probs, mixed, att, middle, hidden2, ups, gated = saved
    (w_q, w_k, w_v), w_out, w_up, w_down = weights
    heads = head_mask()
    grad_ffn = grad_out.astype(BF)
    _, back = jax.vjp(gelu_tanh, ups)
    grad_ups = back(dot(grad_ffn, w_down, NT))[0].astype(BF)
    grad_hidden2 = dot(grad_ups, w_up, NT)
    _, norm_back2 = jax.vjp(layer_norm, middle, vecs[2], vecs[3])
    grad_norm2, grad_gain2, grad_bias2 = norm_back2(grad_hidden2)
    grad_middle = grad_out + grad_norm2
    grad_branch = grad_middle.astype(BF)
    grad_att = dot(grad_branch, w_out, NT).astype(BF)
    att_heads = jnp.where(heads, grad_att, 0)
    wv = dot(att_heads, w_v, NT)
    grad_prob = dot2(wv, hidden1, NT)
    delta = jnp.sum(att_heads.astype(F32) * att, axis=1, keepdims=True)
    grad_score = (probs * (grad_prob - delta)).astype(BF)
    summed = group_reduce(dot(grad_score, hidden1), jnp.add, half)
    grad_query = (jnp.sum(jnp.where(heads, dot2(summed, w_k), 0.0), axis=0, keepdims=True) * 0.125).astype(BF)
    low_probs = probs.astype(BF)
    grad_hidden1 = dot(
        jnp.concatenate([grad_score, grad_score, low_probs, low_probs]), jnp.concatenate([split2(wq), split2(wv)]), TN
    )
    grad_hidden1 = grad_hidden1 + jnp.where(mine, dot(grad_query, w_q, NT), 0.0)
    _, norm_back1 = jax.vjp(layer_norm, values, vecs[0], vecs[1])
    grad_norm1, grad_gain1, grad_bias1 = norm_back1(grad_hidden1)
    grad_input = grad_norm1 + jnp.where(mine, grad_middle, 0.0)
    query8 = query * jnp.asarray(0.125, BF)
    factors = [row_h1, grad_query, query8, grad_att, att, grad_branch, hidden2, grad_ffn]
    factors += [grad_ups.reshape(N_UP, D), gated.reshape(N_UP, D), summed, mixed]
    factors = jnp.concatenate([f.astype(BF) for f in factors])
    return grad_input, factors, [grad_gain1, grad_bias1], [grad_gain2, grad_bias2]


def last_gradient(data, chunk_at, n_chunks, size):
    n_seq = data.shape[0]
    heads = head_mask()
    row_h1, grad_query, query8, grad_att, att, grad_branch, hidden2, grad_ffn = [data[:, i] for i in range(8)]
    at = 8
    grad_ups, gated = data[:, at : at + N_UP], data[:, at + N_UP : at + 2 * N_UP]
    at += 2 * N_UP
    summed, mixed = data[:, at : at + HEADS], data[:, at + HEADS : at + 2 * HEADS]

    def by_unit(parts):
        count, width = len(parts), sum(p.shape[0] for p in parts)
        slot = jnp.concatenate([jnp.full((p.shape[0],), j, jnp.int32) for j, p in enumerate(parts)])
        both = jnp.concatenate(parts).T
        spread = jnp.where(slot[None, None, :] == jnp.arange(count)[None, :, None], both[:, None, :], 0)
        return spread.reshape(count * D, width)

    def per_head(x):
        return jnp.where(heads[None], x[:, None, :], 0).reshape(n_seq * HEADS, D)

    left = by_unit([row_h1, summed.reshape(-1, D), mixed.reshape(-1, D)])
    right = jnp.concatenate([grad_query, per_head(query8), per_head(grad_att)])
    first = chunk_at * size
    qkv = dot(lax.dynamic_slice_in_dim(left, jnp.minimum(first, U_OUT - size), size, 0), right)
    lefts = [att.T, by_unit([hidden2] * N_UP), gated.reshape(n_seq, FF).T]
    rights = [grad_branch, grad_ups.transpose(1, 0, 2).reshape(-1, D), grad_ffn]
    width = sum(x.shape[1] for x in lefts)
    columns, before = [], 0
    for x in lefts:
        columns.append(jnp.pad(x, ((0, 0), (before, width - before - x.shape[1]))))
        before += x.shape[1]
    left = jnp.concatenate(columns)
    rest = dot(lax.dynamic_slice_in_dim(left, jnp.maximum(first - U_OUT, 0), size, 0), jnp.concatenate(rights))
    return jnp.where(first < U_OUT, qkv, rest)


def shards(
    tokens,
    lengths,
    end_ids,
    pairs,
    layer_master,
    layer_first,
    layer_second,
    table_master,
    table_first,
    table_second,
    vector_master,
    vector_first,
    vector_second,
):
    rows = tokens.shape[1]
    s_at = lax.axis_index("section")
    c_at = lax.axis_index("ctx")
    z_at = lax.axis_index("shard")
    n_section = lax.axis_size("section")
    n = lax.axis_size("ctx")
    n_shard = lax.axis_size("shard")
    half = n // 2
    hb = rows // 2
    n_dest = n_section * n
    n_seq = MICRO * n_shard
    columns, entries = table_master.shape
    is_first = s_at == 0
    seq_in = c_at // half
    seq_at = z_at * MICRO + seq_in
    group = (c_at % half) * 2 + s_at

    fast = small_block()
    chunk = chunk_rows(layer_master) if fast else layer_master.reshape(-1, D).astype(BF)
    size = chunk.shape[0]
    cut = size // 2
    if fast:
        wide = cut + OVERLAP // 2
        got = swap(jnp.where(is_first, chunk[size - wide :], chunk[:wide]), "section", 1)
        piece0 = jnp.where(is_first, chunk[:wide], got)
        piece1 = jnp.where(is_first, got[:cut], chunk[cut:])
    else:
        got = swap(jnp.where(is_first, chunk[cut:], chunk[:cut]), "section", 1)
        piece0 = jnp.where(is_first, chunk[:cut], got)
        piece1 = jnp.where(is_first, got, chunk[cut:])
    order = ("ctx", "shard", "section")

    own_ids = jnp.concatenate([tokens, end_ids[:, None]], axis=1)
    all_ids = gather_axis(gather_axis(own_ids, "ctx"), "shard")
    natural = all_ids[..., :rows].transpose(0, 2, 1, 3).reshape(n_shard, MICRO, 2 * n, hb)
    zig = jnp.stack([natural[:, :, :n], natural[:, :, n:][:, :, ::-1]], axis=3)
    zig = zig.reshape(n_shard, MICRO, half, 2, rows).transpose(0, 3, 1, 2, 4)
    end_all = all_ids[:, 0, :, rows].reshape(n_seq)
    n_blocks = n_shard * n_dest

    def held(ids):
        ids = ids - z_at * entries
        return jnp.where((ids >= 0) & (ids < entries), ids, entries)

    listed, counts = owned_rows(held(zig.reshape(n_blocks, rows)), entries)
    end_held = held(end_all)
    if fast:
        first = first_moves(piece0)
        listed, piece0, *first = lax.optimization_barrier((listed, piece0, *first))
        second = second_moves(piece0, first[0], first[1])
    else:
        units0 = lax.all_gather(piece0, order, axis=0, tiled=True)
    dest = jnp.arange(n_blocks, dtype=jnp.int32) % n_dest
    groups = (dest % n % half) * 2 + dest // n
    assert VOCAB >= (n_shard - 1) * entries
    meta_emb = jnp.concatenate(
        [
            jnp.stack([(z_at == n_shard - 1).astype(jnp.int32), jnp.int32(n), jnp.int32(VOCAB - (n_shard - 1) * entries), jnp.int32(0)]),
            groups,
        ]
    )
    picked, end_part = lookup(listed, counts, end_held, meta_emb, table_master, n_blocks, rows)
    if fast:
        picked, *second = lax.optimization_barrier((picked, *second))
        halves = gather_half(piece0, first, second)
    column_at = (s_at * n + c_at) * columns
    end_rows = sum_all(lax.dynamic_update_slice(jnp.zeros((n_seq, D), F32), end_part, (0, column_at)))
    summed = lax.psum_scatter(picked.reshape(n_shard, n_dest, columns, rows), "shard", scatter_dimension=0, tiled=True)
    if fast:
        summed, piece1, end_rows, *halves = lax.optimization_barrier((summed, piece1, end_rows, *halves))
        parts = [part for mine in halves for part in (mine, swap(mine, "section", 1))]
    routed = lax.all_to_all(summed.reshape(n_dest, columns, rows), ("section", "ctx"), split_axis=0, concat_axis=0, tiled=True)
    embedded = routed.reshape(D, rows).T.astype(F32)
    end_row = lax.dynamic_slice_in_dim(end_rows, seq_at, 1, 0)
    units1 = lax.all_gather(piece1, order, axis=0, tiled=True)

    length = lax.dynamic_slice_in_dim(lengths, seq_in, 1, 0)[0]
    others = [group ^ (2 * cb + sb) for sb in range(2) for cb in range(half)]
    meta = jnp.stack([group, length] + others).astype(jnp.int32)
    span = jnp.arange(hb, dtype=jnp.int32)
    positions = jnp.concatenate([group * hb + span, (2 * n - 1 - group) * hb + span])

    vecs0, vecs1 = vector_master[0:4], vector_master[4:8]
    hidden1 = layer_norm(embedded, vecs0[0], vecs0[1]).astype(BF)
    if fast:
        hidden1, *parts = lax.optimization_barrier((hidden1, *parts))
        units0 = place_units(parts)
    weights0 = layer_weights(units0)
    others = pieces_by_ctx(hidden1, half)[1:]
    *others, w_qkv0, w_up0 = lax.optimization_barrier((*others, weights0[0], weights0[2]))
    weights0 = (w_qkv0, weights0[1], w_up0, weights0[3])
    out0, saved0 = layer_forward(embedded, hidden1, pieces_by_section([hidden1, *others]), meta, n, weights0, vecs0)
    x1 = out0.astype(BF).astype(F32)
    x1, units1 = lax.optimization_barrier((x1, units1))
    w_qkv1 = split_units(units1, 0, 3)
    weights1 = ((w_qkv1[0], w_qkv1[1], w_qkv1[2]), units1[U_OUT:U_UP], join_units(units1, U_UP, N_UP), units1[U_DOWN:])
    final, saved1 = last_forward(x1, positions, length, half, weights1, vecs1)

    def score_terms(final_row, end_vals, gain_vec, bias_vec, head_vec):
        normed = layer_norm(final_row, gain_vec, bias_vec)
        return jnp.sum(normed * (end_vals + head_vec)) * D ** (-0.5)

    counted = group == 0
    score, score_back = jax.vjp(score_terms, final, end_row, vector_master[8], vector_master[9], vector_master[10])
    scores = sum_small(jnp.where((jnp.arange(n_seq) == seq_at) & counted, score, 0.0)[None])[0]

    def pair_loss(score_vals):
        return jnp.sum(softplus(score_vals[pairs[:, 1]] - score_vals[pairs[:, 0]]))

    loss_sum, loss_back = jax.vjp(pair_loss, scores)
    grad_scores = loss_back(jnp.ones_like(loss_sum))[0]
    grad_own = lax.dynamic_slice_in_dim(grad_scores, seq_at, 1, 0)[0]
    grad_final, grad_end, *vec_final = score_back(grad_own)

    grad_x1, factors, vec1, vec1_row = last_backward(saved1, grad_final, half, weights1, vecs1)
    factors = jnp.concatenate([factors, grad_end.astype(BF)])
    grad_x1 = grad_x1.astype(BF).astype(F32)
    beside = swap(factors, "ctx", half)
    both = jnp.where(seq_in == 0, jnp.stack([factors, beside]), jnp.stack([beside, factors]))
    every_factor = gather_axis(both, "shard").reshape(n_seq, -1, D)
    grad_x0, grads0, vec0, every_factor = layer_backward(saved0, grad_x1, meta, n, weights0, vecs0, every_factor, fast)

    by_owner = grad_x0.T.reshape(n_dest, columns, rows)
    back = lax.all_to_all(by_owner, ("section", "ctx"), split_axis=0, concat_axis=0, tiled=True)
    if fast:
        (rest, one, three), (part_v, finish_qkv) = grads0
        back, one, three = lax.optimization_barrier((back, one, three))
        every = [back] + [shift(back, "shard", d) for d in (1, 3, 2)]
        every[1], every[2], part_v, every_factor, rest = lax.optimization_barrier(
            (every[1], every[2], part_v, every_factor, rest)
        )
        every_factor, qkv_part = lax.optimization_barrier((every_factor, finish_qkv(part_v)))
        qkv_part = qkv_second(*qkv_first(qkv_part))
        rest_terms = [shard_chunk(rest, 0), one, three] + along_shard(rest, (2,))
        every[3], qkv_part = lax.optimization_barrier((every[3], qkv_part))
        every = jnp.concatenate(every)
        near_order = (z_at + 4 - jnp.array((0, 1, 3, 2), jnp.int32)) % 4
        listed = listed.reshape(n_shard, -1)[near_order].reshape(-1)
        counts = counts.reshape(n_shard, -1)[near_order].reshape(-1)
    else:
        every = lax.all_gather(back, "shard", axis=0, tiled=True)
    end_grads = lax.dynamic_slice(every_factor[:, -1].astype(F32), (0, column_at), (n_seq, columns))
    table_grad = scatter(listed, counts, end_held, meta_emb, every, end_grads, entries)
    once = [jnp.where(counted, v, 0.0) for v in vec1_row + vec_final]
    vector_part = jnp.stack(vec0 + vec1 + once)

    own1 = last_gradient(every_factor, c_at * n_shard + z_at, n * n_shard, size)
    squares = jnp.sum(table_grad * table_grad) + jnp.where(is_first, 0.0, jnp.sum(own1 * own1))
    if fast:
        qkv_terms = [shard_chunk(qkv_part, 0)] + along_shard(qkv_part, (1, 3, 2))
        table_grad, own1, squares, vector_part, *qkv_terms = lax.optimization_barrier(
            (table_grad, own1, squares, vector_part, *qkv_terms)
        )
        mine = sum(t.astype(F32) for t in rest_terms)
        collected = collect_qkv(sum(t.astype(F32) for t in qkv_terms))[: mine.shape[0] * BLOCK]
        mine = jnp.where(c_at == 0, collected.reshape(mine.shape), mine)
    else:
        mine = lax.psum_scatter(grads0, order, scatter_dimension=0, tiled=True).astype(F32)
    squares = squares + jnp.sum(mine * mine)
    other = swap(mine.astype(BF), "section", 1).astype(F32)
    own0 = jnp.stack([mine, other], axis=1).reshape(size, D) if fast else jnp.concatenate([mine, other])
    layer_grad = jnp.where(is_first, own0, own1).reshape(-1, LANES)

    n_vec = vector_part.shape[0]
    totals = sum_small(jnp.concatenate([vector_part, jnp.full((1, D), squares)]))
    vector_grad = totals[:n_vec]
    grad_norm = jnp.sqrt(totals[n_vec, 0] + jnp.sum(vector_grad * vector_grad))
    layer_grad, grad_norm = lax.optimization_barrier((layer_grad, grad_norm))
    factor = CLIP_LIMIT / jnp.maximum(grad_norm, CLIP_LIMIT)
    flat = [x.reshape(-1, LANES) for x in (layer_master, layer_first, layer_second)]
    flat_rows = flat[0].shape[0]
    block_rows = max(b for b in range(1, 2313) if flat_rows % b == 0 and (b % 8 == 0 or b == flat_rows))
    table_cols = max(b for b in range(LANES, 1537, LANES) if entries % b == 0)
    layer_new = adam(factor, *flat, layer_grad, 0.4, 0.1, (block_rows, LANES))
    layer_new = [x.reshape(layer_master.shape) for x in layer_new]
    table_new = adam(factor, table_master, table_first, table_second, table_grad, 0.5, 0.1, (columns, table_cols))
    vector_new = adam_update(vector_master, vector_first, vector_second, vector_grad * factor, 0.7, 0.0)
    return (loss_sum, grad_norm, *layer_new, *table_new, *vector_new)


def solution(mesh):
    in_specs = (
        P("shard", "ctx"),
        P("shard"),
        P("shard"),
        P(),
        P("section", ("ctx", "shard")),
        P("section", ("ctx", "shard")),
        P("section", ("ctx", "shard")),
        P(("section", "ctx"), "shard"),
        P(("section", "ctx"), "shard"),
        P(("section", "ctx"), "shard"),
        P(),
        P(),
        P(),
    )
    out_specs = (
        P(),
        P(),
        P("section", ("ctx", "shard")),
        P("section", ("ctx", "shard")),
        P("section", ("ctx", "shard")),
        P(("section", "ctx"), "shard"),
        P(("section", "ctx"), "shard"),
        P(("section", "ctx"), "shard"),
        P(),
        P(),
        P(),
    )
    return jax.shard_map(shards, mesh=mesh, in_specs=in_specs, out_specs=out_specs, check_vma=False)
```

```python
import functools

import jax
import jax.numpy as jnp
from jax import lax
from jax.experimental import pallas as pl
from jax.experimental.layout import Layout, with_layout_constraint
from jax.experimental.pallas import tpu as pltpu
from jax.sharding import PartitionSpec as P

D = 1088
HEADS = 17
HD = 64
FF = 4352
VOCAB = 51200
MICRO = 2
STEP = 10
CLIP_LIMIT = 0.02
ALL = ("section", "ctx", "shard")

LANES = 128
PAIRS_OF_HEADS = (HEADS + 1) // 2
WIDE = PAIRS_OF_HEADS * LANES
N_UP = FF // D
U_OUT = 3 * D
U_UP = U_OUT + D
U_DOWN = U_UP + FF
UNITS = U_DOWN + FF

BF = jnp.bfloat16
F32 = jnp.float32
VMEM_BIG = 56 * 1024 * 1024


def params(limit=VMEM_BIG):
    return pltpu.CompilerParams(vmem_limit_bytes=limit)


def cost(microseconds):
    return pl.CostEstimate(flops=0, bytes_accessed=int(microseconds * 3.0e6), transcendentals=0)


def dot(a, b, contract=((1,), (0,))):
    return lax.dot_general(a, b, (contract, ((), ())), preferred_element_type=F32)


NT = ((1,), (1,))
TN = ((0,), (0,))


def split2(x):
    top = lax.reduce_precision(x, 8, 7)
    return jnp.concatenate([top, x - top]).astype(BF)


def dot2(x, w, contract=((1,), (0,))):
    y = dot(split2(x), w, contract)
    return y[: x.shape[0]] + y[x.shape[0] :]


def swap(x, axis, bit):
    size = lax.axis_size(axis)
    return lax.ppermute(x, axis, [(i, i ^ bit) for i in range(size)])


def gather_step(x, axis, bit):
    other = swap(x, axis, bit)
    lower = (lax.axis_index(axis) & bit) == 0
    return jnp.where(lower, jnp.concatenate([x, other]), jnp.concatenate([other, x]))


def gather_axis(x, axis):
    x = x[None]
    bit = 1
    while bit < lax.axis_size(axis):
        x = gather_step(x, axis, bit)
        bit *= 2
    return x


def beside(x):
    return gather_step(x[None], "ctx", lax.axis_size("ctx") // 2)


def sum_axis(x, axis, first=1, last=None):
    size = lax.axis_size(axis) if last is None else last
    bit = first
    while bit < size:
        x = x + swap(x, axis, bit)
        bit *= 2
    return x


def group_reduce(x, combine, half):
    def step(x, axis, bit):
        other = swap(x, axis, bit)
        lower = (lax.axis_index(axis) & bit) == 0
        return combine(jnp.where(lower, x, other), jnp.where(lower, other, x))

    x = step(x, "section", 1)
    bit = 1
    while bit < half:
        x = step(x, "ctx", bit)
        bit *= 2
    return x


def sum_all(x):
    return sum_axis(sum_axis(sum_axis(x, "section"), "ctx"), "shard")


def sum_direct(x, axis):
    if lax.axis_size(axis) != 4:
        return sum_axis(x, axis)
    one, two, three = [lax.ppermute(x, axis, [(i, (i + d) % 4) for i in range(4)]) for d in (1, 2, 3)]
    return (x + two) + (one + three)


def sum_small(x):
    return sum_direct(sum_direct(sum_direct(x, "section"), "ctx"), "shard")


def rows_kernel(pairs, x, out, scr):
    lane = lax.broadcasted_iota(jnp.int32, (1, LANES), 1)
    step = 2 * D // LANES
    even, odd = pl.ds(0, pairs, stride=2), pl.ds(1, pairs, stride=2)
    flat_row = lambda t: x[pl.ds(t, pairs, stride=step), :]
    for t in range(PAIRS_OF_HEADS):
        scr[t, even, :] = flat_row(t)
    before = pltpu.roll(flat_row(step // 2), HD, 1)
    for t in range(PAIRS_OF_HEADS - 1):
        after = pltpu.roll(flat_row(step // 2 + 1 + t), HD, 1)
        scr[t, odd, :] = jnp.where(lane < HD, before, after)
        before = after
    scr[PAIRS_OF_HEADS - 1, odd, :] = before
    for t, (at, size) in enumerate(tile_cuts()):
        out[:, pl.ds(at, size)] = scr[t][:, :size].astype(BF)


def chunk_rows(flat):
    units = flat.size // D
    return pl.pallas_call(
        functools.partial(rows_kernel, units // 2),
        out_shape=jax.ShapeDtypeStruct((units, D), BF),
        scratch_shapes=[pltpu.VMEM((PAIRS_OF_HEADS, units, LANES), F32)],
        compiler_params=params(),
        cost_estimate=cost(6),
        name="chunk_rows",
    )(flat.reshape(-1, LANES))


def small_block():
    return lax.axis_size("ctx") == 4 and lax.axis_size("shard") == 4 and lax.axis_size("section") == 2


def shift(x, axis, by):
    size = lax.axis_size(axis)
    return lax.ppermute(x, axis, [(i, (i + by) % size) for i in range(size)])


ARRIVALS = ((0,), (1, 3), (2,))
OVERLAP = 16


def place_kernel(rows, at, *refs):
    ins, out, held, sems_in, sems_out = refs[: 2 * len(ARRIVALS)], refs[-4], refs[-3], refs[-2], refs[-1]
    s, c, z = at[0], at[1], at[2]
    short = rows - OVERLAP
    pieces = []
    for g, distances in enumerate(ARRIVALS):
        for other in range(2):
            for e in range(4):
                for i, d in enumerate(distances):
                    chunk = (c ^ e) * 4 + lax.rem(z + 4 - d, 4)
                    pieces.append((ins[2 * g + other].at[e, i], chunk, other))

    def arrive(k):
        return pltpu.make_async_copy(pieces[k][0], held.at[k], sems_in.at[k])

    def leave(k, act):
        _, chunk, other = pieces[k]

        @pl.when(s == other)
        def _():
            act(pltpu.make_async_copy(held.at[k], out.at[chunk, pl.ds(0, rows)], sems_out.at[k]))

        @pl.when(s != other)
        def _():
            act(pltpu.make_async_copy(held.at[k, pl.ds(OVERLAP, short)], out.at[chunk, pl.ds(rows, short)], sems_out.at[k]))

    for k in range(len(pieces)):
        arrive(k).start()
    for k in range(len(pieces)):
        arrive(k).wait()
        leave(k, lambda copy: copy.start())
    for k in range(len(pieces)):
        leave(k, lambda copy: copy.wait())


def by_links(own):
    return swap(own, "ctx", 1), swap(own, "ctx", 2)


def first_moves(piece):
    return shift(piece, "shard", 1), shift(piece, "shard", 3), *by_links(piece[None])


def second_moves(piece, near, far):
    return shift(piece, "shard", 2), *by_links(jnp.stack([near, far]))


def corner_of(by_x, by_y):
    cut = by_x.shape[1] // 2
    return jnp.concatenate([swap(by_x[:, :cut], "ctx", 2), swap(by_y[:, cut:], "ctx", 1)], axis=1)


def gather_half(piece, first, second):
    near, far, *own_links = first
    opposite, *near_links = second
    arrived = {0: piece, 1: near, 3: far, 2: opposite}
    parts = []
    for distances, links in zip(ARRIVALS, (own_links, near_links, None)):
        own = jnp.stack([arrived[d] for d in distances])
        by_x, by_y = by_links(own) if links is None else links
        corner = corner_of(by_x, by_y)
        parts.append(jnp.stack([own, by_x, by_y, corner]))
    return parts


def place_units(parts):
    rows = parts[0].shape[2]
    at = jnp.stack([lax.axis_index(a) for a in ALL]).astype(jnp.int32)
    grid_spec = pltpu.PrefetchScalarGridSpec(
        num_scalar_prefetch=1,
        grid=(1,),
        in_specs=[pl.BlockSpec(memory_space=pl.ANY)] * len(parts),
        out_specs=pl.BlockSpec(memory_space=pl.ANY),
        scratch_shapes=[pltpu.VMEM((32, rows, D), BF), pltpu.SemaphoreType.DMA((32,)), pltpu.SemaphoreType.DMA((32,))],
    )
    whole = pl.pallas_call(
        functools.partial(place_kernel, rows),
        grid_spec=grid_spec,
        out_shape=jax.ShapeDtypeStruct((16, 2 * rows - OVERLAP, D), BF),
        compiler_params=params(),
        cost_estimate=cost(16),
        name="place",
    )(at, *parts)
    return whole.reshape(UNITS, D)


def add_low(x, y):
    return (x.astype(F32) + y.astype(F32)).astype(BF)


BLOCK = 136
QUARTER = 104


def core_blocks(region):
    s = lax.axis_index("section")
    blocks = region.reshape(-1, 2, BLOCK, D)
    pick = lambda i: lax.dynamic_index_in_dim(blocks, i, 1, keepdims=False)
    return pick(s), pick(1 - s)


def fold_cores(region):
    mine, other = core_blocks(region)
    return add_low(mine, swap(other, "section", 1))


def one_way(x, bit, sends):
    return lax.ppermute(x, "ctx", [(i, i ^ bit) for i in range(4) if sends(i)])


def three_first(one, two, both, p):
    has_p = (lax.axis_index("ctx") & p) != 0
    return swap(jnp.where(has_p, two, one), "ctx", p), one_way(both, p, lambda i: not i & p)


def three_second(one, two, both, came, came_both, p, q):
    c = lax.axis_index("ctx")
    has_p, has_q = (c & p) != 0, (c & q) != 0
    single = add_low(jnp.where(has_p, one, two), came)
    both = add_low(both, came_both)
    sent = jnp.where(has_p & ~has_q, both, single)
    came = one_way(sent, q, lambda i: not i & q or i & p)
    return add_low(jnp.where(has_p & has_q, both, single), came)


def rest_first(rest):
    x = rest.reshape(3, 4, -1, BLOCK, D)
    return *three_first(x[0, :2], x[1, :2], x[2, :2], 1), *three_first(x[1, 2:], x[0, 2:], x[2, 2:], 2)


def rest_second(rest, came):
    x = rest.reshape(3, 4, -1, BLOCK, D)
    first = three_second(x[0, :2], x[1, :2], x[2, :2], came[0], came[1], 1, 2)
    second = three_second(x[1, 2:], x[0, 2:], x[2, 2:], came[2], came[3], 2, 1)
    return jnp.concatenate([first, second])


def fold_half(v, axis, bit):
    mine = (lax.axis_index("ctx") // bit) & 1
    pick = lambda i: lax.dynamic_index_in_dim(v, i, axis, keepdims=True)
    return add_low(pick(mine), swap(pick(1 - mine), "ctx", bit))


def qkv_first(qkv):
    x = qkv.reshape(4, -1, D)
    x = jnp.pad(x, ((0, 0), (0, 4 * QUARTER - x.shape[1]), (0, 0))).reshape(4, 2, 2, QUARTER, D)
    return fold_half(x[:2], 2, 1), fold_half(x[2:], 1, 2)


def qkv_second(first, second):
    return jnp.concatenate([fold_half(first, 1, 2), fold_half(second, 2, 1)])[:, 0, 0]


def collect_qkv(quarter):
    low = quarter.astype(BF)
    others = [lax.ppermute(low, "ctx", [(i, 0)]).astype(F32) for i in (1, 2, 3)]
    return jnp.concatenate([quarter, *others])


def shard_chunk(x, by):
    return lax.dynamic_index_in_dim(x, lax.rem(lax.axis_index("shard") + by, 4), 0, keepdims=False)


def along_shard(x, distances):
    return [shift(shard_chunk(x, d), "shard", d) for d in distances]


SHIFT = 10
UNROLL = 8


def owned_rows(ids, entries):
    rows = ids.shape[1]
    assert rows < (1 << SHIFT)
    owned = ids < entries
    place = jnp.cumsum(owned.astype(jnp.int32), axis=1) - 1
    packed = jnp.arange(rows, dtype=jnp.int32)[None, :] + (ids << SHIFT)
    slots = jnp.arange(rows, dtype=jnp.int32)
    hit = (place[:, None, :] == slots[None, :, None]) & owned[:, None, :]
    listed = jnp.sum(jnp.where(hit, packed[:, None, :], 0), axis=2)
    count = jnp.sum(owned.astype(jnp.int32), axis=1)
    listed = jnp.where(slots[None, :] < count[:, None], listed, rows + (entries << SHIFT))
    return listed.reshape(-1), count


def for_owned(listed, counts, step, rows, body):
    def some(t, _):
        for u in range(UNROLL):
            packed = listed[step * rows + t * UNROLL + u]
            body(pl.ds(packed & ((1 << SHIFT) - 1), 1), pl.ds(packed >> SHIFT, 1))
        return 0

    lax.fori_loop(0, (counts[step] + UNROLL - 1) // UNROLL, some, 0)


def lookup_kernel(rows, listed, counts, end_ids, meta, table, out, ends, tab, buf):
    step = pl.program_id(0)
    columns, entries = table.shape

    @pl.when(step == 0)
    def _():
        def turn(i, _):
            at = pl.multiple_of(i * 256, 256)
            tab[pl.ds(at, 256), :] = table[:, pl.ds(at, 256)].astype(BF).astype(F32).T
            return 0

        lax.fori_loop(0, entries // 256, turn, 0)
        tab[pl.ds(entries, 8), :] = jnp.zeros((8, columns), F32)
        for n in range(ends.shape[0]):
            ends[pl.ds(n, 1), :] = tab[pl.ds(end_ids[n], 1), :]

    buf[...] = jnp.zeros_like(buf)

    def pick(place, entry):
        buf[place, :] = tab[entry, :]

    for_owned(listed, counts, step, rows, pick)

    @pl.when(meta[0] == 1)
    def _():
        half = rows // 2
        group = meta[4 + step]
        for j in range(2):
            block = group if j == 0 else 2 * meta[1] - 1 - group
            at = pl.multiple_of(meta[2] + block * half, 8)
            buf[pl.ds(j * half, half), :] += tab[pl.ds(at, half), :]

    out[0] = buf[pl.ds(0, rows), :].T.astype(BF)


def lookup(listed, counts, end_ids, meta, table, n_blocks, rows):
    columns, entries = table.shape
    n_ends = end_ids.shape[0]
    grid_spec = pltpu.PrefetchScalarGridSpec(
        num_scalar_prefetch=4,
        grid=(n_blocks,),
        in_specs=[pl.BlockSpec((columns, entries), lambda i, *_: (0, 0))],
        out_specs=[
            pl.BlockSpec((1, columns, rows), lambda i, *_: (i, 0, 0)),
            pl.BlockSpec((n_ends, columns), lambda i, *_: (0, 0)),
        ],
        scratch_shapes=[pltpu.VMEM((entries + 8, columns), F32), pltpu.VMEM((rows + 8, columns), F32)],
    )
    return pl.pallas_call(
        functools.partial(lookup_kernel, rows),
        grid_spec=grid_spec,
        out_shape=[
            jax.ShapeDtypeStruct((n_blocks, columns, rows), BF),
            jax.ShapeDtypeStruct((n_ends, columns), F32),
        ],
        compiler_params=params(),
        cost_estimate=cost(40),
        name="lookup",
    )(listed, counts, end_ids, meta, table)


def scatter_kernel(rows, n_blocks, listed, counts, end_ids, meta, grads, ends, out, acc, buf):
    step = pl.program_id(0)
    columns, entries = out.shape
    n_ends = ends.shape[0]

    @pl.when(step == 0)
    def _():
        def clear(i, _):
            acc[pl.ds(pl.multiple_of(i * 256, 256), 256), :] = jnp.zeros((256, columns), F32)
            return 0

        lax.fori_loop(0, entries // 256, clear, 0)
        for n in range(n_ends):
            at = pl.ds(end_ids[n], 1)
            acc[at, :] += ends[pl.ds(n, 1), :]

    buf[pl.ds(0, rows), :] = grads[0].astype(F32).T

    def add(place, entry):
        acc[entry, :] += buf[place, :]

    for_owned(listed, counts, step, rows, add)

    @pl.when(meta[0] == 1)
    def _():
        half = rows // 2
        group = meta[4 + step]
        for j in range(2):
            block = group if j == 0 else 2 * meta[1] - 1 - group
            at = pl.multiple_of(meta[2] + block * half, 8)
            acc[pl.ds(at, half), :] += buf[pl.ds(j * half, half), :]

    @pl.when(step == n_blocks - 1)
    def _():
        def turn(i, _):
            at = pl.multiple_of(i * 256, 256)
            out[:, pl.ds(at, 256)] = acc[pl.ds(at, 256), :].T
            return 0

        lax.fori_loop(0, entries // 256, turn, 0)


def scatter(listed, counts, end_ids, meta, grads, ends, entries):
    n_blocks, columns, rows = grads.shape
    n_ends = ends.shape[0]
    grid_spec = pltpu.PrefetchScalarGridSpec(
        num_scalar_prefetch=4,
        grid=(n_blocks,),
        in_specs=[
            pl.BlockSpec((1, columns, rows), lambda i, *_: (i, 0, 0)),
            pl.BlockSpec((n_ends, columns), lambda i, *_: (0, 0)),
        ],
        out_specs=pl.BlockSpec((columns, entries), lambda i, *_: (0, 0)),
        scratch_shapes=[pltpu.VMEM((entries + 8, columns), F32), pltpu.VMEM((rows + 8, columns), F32)],
    )
    return pl.pallas_call(
        functools.partial(scatter_kernel, rows, n_blocks),
        grid_spec=grid_spec,
        out_shape=jax.ShapeDtypeStruct((columns, entries), F32),
        compiler_params=params(),
        cost_estimate=cost(42),
        name="scatter",
    )(listed, counts, end_ids, meta, grads, ends)


def tile_cuts():
    return [(t * LANES, min(LANES, D - t * LANES)) for t in range(PAIRS_OF_HEADS)]


def split_kernel(count, rb, width, u, out, scr):
    for t, (at, size) in enumerate(tile_cuts()):
        part = u[:, pl.ds(at, size)].astype(F32)
        if size < LANES:
            part = jnp.concatenate([part, jnp.zeros((rb * count, LANES - size), F32)], axis=1)
        scr[t] = part
        for j in range(count):
            picked = scr[t, pl.ds(j, rb, stride=count), :].astype(BF)
            take = min(LANES, width - at)
            out[j, :, pl.ds(at, take)] = picked[:, :take]


def join_kernel(count, rb, u, out, scr):
    for t, (at, size) in enumerate(tile_cuts()):
        part = u[:, pl.ds(at, size)].astype(F32)
        if size < LANES:
            part = jnp.concatenate([part, jnp.zeros((rb * count, LANES - size), F32)], axis=1)
        scr[t] = part
        for j in range(count):
            out[:, pl.ds(j * D + at, size)] = scr[t, pl.ds(j, rb, stride=count), :].astype(BF)[:, :size]


def join_units(u, first, count):
    rb = 272
    return pl.pallas_call(
        functools.partial(join_kernel, count, rb),
        grid=(D // rb,),
        in_specs=[pl.BlockSpec((rb * count, D), lambda i: (i + first // (rb * count), 0))],
        out_specs=pl.BlockSpec((rb, count * D), lambda i: (i, 0)),
        out_shape=jax.ShapeDtypeStruct((D, count * D), BF),
        scratch_shapes=[pltpu.VMEM((PAIRS_OF_HEADS, rb * count, LANES), F32)],
        compiler_params=params(),
        cost_estimate=cost(8),
        name="join_units",
    )(u)


def split_units(u, first, count, width=D):
    rb = 272
    return pl.pallas_call(
        functools.partial(split_kernel, count, rb, width),
        grid=(D // rb,),
        in_specs=[pl.BlockSpec((rb * count, D), lambda i: (i + first // (rb * count), 0))],
        out_specs=pl.BlockSpec((count, rb, width), lambda i: (0, i, 0)),
        out_shape=jax.ShapeDtypeStruct((count, D, width), BF),
        scratch_shapes=[pltpu.VMEM((PAIRS_OF_HEADS, rb * count, LANES), F32)],
        compiler_params=params(),
        cost_estimate=cost(8),
        name="split_units",
    )(u)


def merge_kernel(count, rb, starts, *refs):
    parts, out, scr = refs[:-2], refs[-2], refs[-1]
    for t, (at, size) in enumerate(tile_cuts()):
        for j in range(count):
            which, start = starts[j]
            part = parts[which][:, pl.ds(start + at, size)].astype(F32)
            if size < LANES:
                part = jnp.concatenate([part, jnp.zeros((rb, LANES - size), F32)], axis=1)
            scr[t, pl.ds(j, rb, stride=count), :] = part
        out[:, pl.ds(at, size)] = scr[t][:, :size].astype(BF)


def merge_units(parts, starts):
    rb, count = 272, len(starts)
    return pl.pallas_call(
        functools.partial(merge_kernel, count, rb, starts),
        grid=(D // rb,),
        in_specs=[pl.BlockSpec((rb, p.shape[1]), lambda i: (i, 0)) for p in parts],
        out_specs=pl.BlockSpec((rb * count, D), lambda i: (i, 0)),
        out_shape=jax.ShapeDtypeStruct((count * D, D), BF),
        scratch_shapes=[pltpu.VMEM((PAIRS_OF_HEADS, rb * count, LANES), F32)],
        compiler_params=params(),
        cost_estimate=cost(8),
        name="merge_units",
    )(*parts)


def adam_kernel(rate, decay, factor, w, m, v, g, w_out, m_out, v_out):
    w_out[...], m_out[...], v_out[...] = adam_update(w[...], m[...], v[...], g[...] * factor[0], rate, decay)


def adam(factor, weight, first, second, grad, rate, decay, block):
    shape = weight.shape
    grid = tuple(size // b for size, b in zip(shape, block))
    spec = pl.BlockSpec(block, lambda i, j, *_: (i, j))
    return pl.pallas_call(
        functools.partial(adam_kernel, rate, decay),
        grid_spec=pltpu.PrefetchScalarGridSpec(num_scalar_prefetch=1, grid=grid, in_specs=[spec] * 4, out_specs=[spec] * 3),
        out_shape=[jax.ShapeDtypeStruct(shape, F32)] * 3,
        compiler_params=params(),
        cost_estimate=cost(weight.size * 9.0e-6),
        name="adam",
    )(factor.reshape(1), weight, first, second, grad)


def chunk_plan(n):
    plan = [(0, "ll", True), (0, "hl", False), (0, "hh", True)]
    for p in range(1, n):
        plan += [(p, "hl", False), (p, "sel", False)]
    return plan


def chunk_offsets(meta, n, hb, p, kind):
    own = meta[0]
    piece = meta[2 + p]
    if kind == "ll":
        return 0, p * 2 * hb, own * hb, piece * hb, True
    if kind == "hl":
        return hb, p * 2 * hb, (2 * n - 1 - own) * hb, piece * hb, False
    if kind == "hh":
        return hb, p * 2 * hb + hb, (2 * n - 1 - own) * hb, (2 * n - 1 - piece) * hb, False
    low = piece < own
    q_off = pl.multiple_of(jnp.where(low, 0, hb), hb)
    k_off = pl.multiple_of(p * 2 * hb + jnp.where(low, 0, hb), hb)
    key_pos = jnp.where(low, piece, 2 * n - 1 - piece) * hb
    return q_off, k_off, None, key_pos, low


def chunk_scores(keys, queries, meta, diagonal, kind, q_pos, k_pos, hb):
    s = dot(keys, queries, NT)
    if diagonal:
        ki = lax.broadcasted_iota(jnp.int32, (hb, hb), 0)
        qi = lax.broadcasted_iota(jnp.int32, (hb, hb), 1)
        keep = (ki <= qi) & (ki + k_pos < meta[1])
        s = jnp.where(keep, s, -1e30)
    elif kind == "sel":
        ki = lax.broadcasted_iota(jnp.int32, (hb, hb), 0)
        s = jnp.where(ki < meta[1] - k_pos, s, -1e30)
    return s


def attend_kernel(n, hb, meta, q_ref, k_ref, v_ref, o_ref, lse_ref, vt_ref):
    keys = 2 * hb * n
    for i in range(keys // hb):
        vt_ref[i] = v_ref[pl.ds(i * hb, hb), :].astype(F32).T.astype(BF)
    lane = lax.broadcasted_iota(jnp.int32, (1, LANES), 1)
    plan = chunk_plan(n)
    outs = []
    for head in range(2):
        own_lanes = (lane // HD) == head
        info, scores = [], []
        tops = [jnp.full((1, hb), -3e38, F32), jnp.full((1, hb), -3e38, F32)]
        for p, kind, diagonal in plan:
            q_off, k_off, q_pos, k_pos, low = chunk_offsets(meta, n, hb, p, kind)
            queries = jnp.where(own_lanes, q_ref[pl.ds(q_off, hb), :], 0)
            s = chunk_scores(k_ref[pl.ds(k_off, hb), :], queries, meta, diagonal, kind, q_pos, k_pos, hb)
            top = jnp.max(s, axis=0, keepdims=True)
            if low is True:
                tops[0] = jnp.maximum(tops[0], top)
            elif low is False:
                tops[1] = jnp.maximum(tops[1], top)
            else:
                tops[0] = jnp.maximum(tops[0], jnp.where(low, top, -3e38))
                tops[1] = jnp.maximum(tops[1], jnp.where(low, -3e38, top))
            info.append((k_off, low))
            scores.append(s)
        sums = [jnp.zeros((1, hb), F32), jnp.zeros((1, hb), F32)]
        accs = [jnp.zeros((HD, hb), F32), jnp.zeros((HD, hb), F32)]
        for (k_off, low), s in zip(info, scores):
            if low is True or low is False:
                top = tops[0] if low else tops[1]
            else:
                top = jnp.where(low, tops[0], tops[1])
            e = jnp.exp(s - top)
            total = jnp.sum(e, axis=0, keepdims=True)
            got = dot(vt_ref[k_off // hb, pl.ds(head * HD, HD), :], e.astype(BF))
            if low is True or low is False:
                sums[1 - low] += total
                accs[1 - low] += got
            else:
                sums[0] += jnp.where(low, total, 0.0)
                sums[1] += jnp.where(low, 0.0, total)
                accs[0] += jnp.where(low, got, 0.0)
                accs[1] += jnp.where(low, 0.0, got)
        outs.append([accs[i] / sums[i] for i in range(2)])
        for i in range(2):
            lse_ref[0, pl.ds(head, 1), pl.ds(i * hb, hb)] = tops[i] + jnp.log(sums[i])
    for i in range(2):
        both = jnp.concatenate([outs[0][i], outs[1][i]], axis=0)
        o_ref[pl.ds(i * hb, hb), :] = both.T.astype(BF)


def attend(meta, q, k, v, n):
    rows = q.shape[0]
    keys = k.shape[0]
    grid_spec = pltpu.PrefetchScalarGridSpec(
        num_scalar_prefetch=1,
        grid=(PAIRS_OF_HEADS,),
        in_specs=[
            pl.BlockSpec((rows, LANES), lambda p, *_: (0, p)),
            pl.BlockSpec((keys, LANES), lambda p, *_: (0, p)),
            pl.BlockSpec((keys, LANES), lambda p, *_: (0, p)),
        ],
        out_specs=[
            pl.BlockSpec((rows, LANES), lambda p, *_: (0, p)),
            pl.BlockSpec((1, 8, rows), lambda p, *_: (p, 0, 0)),
        ],
        scratch_shapes=[pltpu.VMEM((2 * n, LANES, rows // 2), BF)],
    )
    return pl.pallas_call(
        functools.partial(attend_kernel, n, rows // 2),
        grid_spec=grid_spec,
        out_shape=[
            jax.ShapeDtypeStruct((rows, WIDE), BF),
            jax.ShapeDtypeStruct((PAIRS_OF_HEADS, 8, rows), F32),
        ],
        compiler_params=params(),
        cost_estimate=cost(23),
        name="attend",
    )(meta, q, k, v)


def attend_back_kernel(n, hb, meta, q_ref, k_ref, v_ref, o_ref, do_ref, lse_ref, dq_ref, dk_ref, dv_ref, kt_ref, dk_acc, dv_acc):
    keys = 2 * hb * n
    for i in range(keys // hb):
        kt_ref[i] = k_ref[pl.ds(i * hb, hb), :].astype(F32).T.astype(BF)
    dk_acc[...] = jnp.zeros_like(dk_acc)
    dv_acc[...] = jnp.zeros_like(dv_acc)
    lane = lax.broadcasted_iota(jnp.int32, (1, LANES), 1)
    plan = chunk_plan(n)
    prods = []
    for i in range(2):
        part = pl.ds(i * hb, hb)
        prods.append((o_ref[part, :].astype(F32) * do_ref[part, :].astype(F32)).T)
    dqs = []
    for head in range(2):
        own_lanes = (lane // HD) == head
        deltas = [jnp.sum(prods[i][head * HD : (head + 1) * HD, :], axis=0, keepdims=True) for i in range(2)]
        lses = [lse_ref[0, pl.ds(head, 1), pl.ds(i * hb, hb)] for i in range(2)]
        accs = [jnp.zeros((HD, hb), F32), jnp.zeros((HD, hb), F32)]
        for p, kind, diagonal in plan:
            q_off, k_off, q_pos, k_pos, low = chunk_offsets(meta, n, hb, p, kind)
            q_at, k_at = pl.ds(q_off, hb), pl.ds(k_off, hb)
            queries = jnp.where(own_lanes, q_ref[q_at, :], 0)
            d_out = jnp.where(own_lanes, do_ref[q_at, :], 0)
            s = chunk_scores(k_ref[k_at, :], queries, meta, diagonal, kind, q_pos, k_pos, hb)
            if low is True or low is False:
                lse, delta = lses[1 - low], deltas[1 - low]
            else:
                lse, delta = jnp.where(low, lses[0], lses[1]), jnp.where(low, deltas[0], deltas[1])
            prob = jnp.exp(s - lse)
            d_prob = dot(v_ref[k_at, :], d_out, NT)
            d_score = (prob * (d_prob - delta)).astype(BF)
            dv_acc[k_at, :] += dot(prob.astype(BF), d_out)
            dk_acc[k_at, :] += dot(d_score, queries)
            got = dot(kt_ref[k_off // hb, pl.ds(head * HD, HD), :], d_score)
            if low is True or low is False:
                accs[1 - low] += got
            else:
                accs[0] += jnp.where(low, got, 0.0)
                accs[1] += jnp.where(low, 0.0, got)
        dqs.append(accs)
    for i in range(2):
        both = jnp.concatenate([dqs[0][i], dqs[1][i]], axis=0) * 0.125
        dq_ref[pl.ds(i * hb, hb), :] = both.T.astype(BF)
    dk_ref[...] = dk_acc[...].astype(BF)
    dv_ref[...] = dv_acc[...].astype(BF)


def attend_back(meta, q, k, v, o, d_o, lse, n):
    rows = q.shape[0]
    keys = k.shape[0]
    row_spec = pl.BlockSpec((rows, LANES), lambda p, *_: (0, p))
    key_spec = pl.BlockSpec((keys, LANES), lambda p, *_: (0, p))
    grid_spec = pltpu.PrefetchScalarGridSpec(
        num_scalar_prefetch=1,
        grid=(PAIRS_OF_HEADS,),
        in_specs=[row_spec, key_spec, key_spec, row_spec, row_spec, pl.BlockSpec((1, 8, rows), lambda p, *_: (p, 0, 0))],
        out_specs=[row_spec, key_spec, key_spec],
        scratch_shapes=[pltpu.VMEM((2 * n, LANES, rows // 2), BF), pltpu.VMEM((keys, LANES), F32), pltpu.VMEM((keys, LANES), F32)],
    )
    return pl.pallas_call(
        functools.partial(attend_back_kernel, n, rows // 2),
        grid_spec=grid_spec,
        out_shape=[
            jax.ShapeDtypeStruct((rows, WIDE), BF),
            jax.ShapeDtypeStruct((keys, WIDE), BF),
            jax.ShapeDtypeStruct((keys, WIDE), BF),
        ],
        compiler_params=params(),
        cost_estimate=cost(46),
        name="attend_back",
    )(meta, q, k, v, o, d_o, lse)


def by_rows(x):
    return with_layout_constraint(x, Layout(major_to_minor=tuple(range(x.ndim))))


def layer_norm(values, gain_vec, bias_vec):
    row_mean = jnp.mean(values, -1, keepdims=True)
    centred = values - row_mean
    variance = jnp.mean(centred * centred, -1, keepdims=True)
    return centred * lax.rsqrt(variance + 1e-05) * gain_vec + bias_vec


def gelu_tanh(values):
    return 0.5 * values * (1.0 + jnp.tanh(0.7978845608 * (values + 0.044715 * values * values * values)))


def softplus(values):
    return jnp.maximum(values, 0.0) + jnp.log1p(jnp.exp(-jnp.abs(values)))


def adam_update(weight, first, second, grad, rate, decay):
    first = 0.9 * first + 0.1 * grad
    second = 0.95 * second + 0.05 * grad * grad
    first_hat = first / (1.0 - 0.9**STEP)
    second_hat = second / (1.0 - 0.95**STEP)
    weight = weight - rate * (first_hat / (jnp.sqrt(second_hat) + 1e-08) + decay * weight)
    return (weight, first, second)


def pieces_by_ctx(x, half):
    got = [x]
    bit = 1
    while bit < half:
        got += [swap(y, "ctx", bit) for y in got]
        bit *= 2
    return got


def pieces_by_section(got):
    own = jnp.concatenate(got)
    return jnp.concatenate([own, swap(own, "section", 1)])


def sum_pieces(x, half):
    rows = x.shape[0] // half
    bit = half // 2
    while bit >= 1:
        keep, send = x[: bit * rows], x[bit * rows : 2 * bit * rows]
        x = keep + swap(send.astype(BF), "ctx", bit).astype(F32)
        bit //= 2
    return x


def layer_weights(units):
    return split_units(units, 0, 3, WIDE), units[U_OUT:U_UP], join_units(units, U_UP, N_UP), units[U_DOWN:]


def layer_forward(values, hidden1, all_hidden1, meta, n, weights, vecs):
    w_qkv, w_out, w_up, w_down = weights
    keys = dot(all_hidden1, w_qkv[1]).astype(BF)
    vals = dot(all_hidden1, w_qkv[2]).astype(BF)
    queries = dot(hidden1, w_qkv[0]).astype(BF) * jnp.asarray(0.125, BF)
    attended, lse = attend(meta, queries, keys, vals, n)
    middle = values + dot(attended[:, :D], w_out)
    hidden2 = layer_norm(middle, vecs[2], vecs[3]).astype(BF)
    ups = dot(hidden2, w_up)
    gated = gelu_tanh(ups).astype(BF)
    result = middle + dot(gated, w_down)
    return result, (values, all_hidden1, queries, keys, vals, attended, lse, middle, hidden2, ups, gated)


def layer_backward(saved, grad_out, meta, n, weights, vecs, factors, fast):
    values, all_hidden1, queries, keys, vals, attended, lse, middle, hidden2, ups, gated = saved
    w_qkv, w_out, w_up, w_down = weights
    grad_ffn = grad_out.astype(BF)
    grad_down = by_rows(dot(gated, grad_ffn, TN).astype(BF))
    if fast:
        mine_down, other_down = core_blocks(grad_down)
        both = beside(factors)
        grad_ffn, other_down, both = lax.optimization_barrier((grad_ffn, other_down, both))
        came_down = swap(other_down, "section", 1)
    _, back = jax.vjp(gelu_tanh, ups)
    grad_ups = by_rows(back(dot(grad_ffn, w_down, NT))[0].astype(BF))
    grad_up = merge_units([dot(hidden2, grad_ups, TN).astype(BF)], [(0, j * D) for j in range(N_UP)])
    if fast:
        mine_up, other_up = core_blocks(grad_up)
        four = gather_step(both[None], "shard", 1)
        grad_ups, other_up, four = lax.optimization_barrier((grad_ups, other_up, four))
        came_up = swap(other_up, "section", 1)
    grad_hidden2 = dot(grad_ups, w_up, NT)
    _, norm_back2 = jax.vjp(layer_norm, middle, vecs[2], vecs[3])
    grad_norm2, grad_gain2, grad_bias2 = norm_back2(grad_hidden2)
    grad_middle = grad_out + grad_norm2
    grad_branch = grad_middle.astype(BF)
    grad_outw = dot(attended[:, :D], grad_branch, TN).astype(BF)
    grad_att = dot(grad_branch, jnp.pad(w_out, ((0, WIDE - D), (0, 0))), NT).astype(BF)
    if fast:
        rest = jnp.concatenate([fold_cores(grad_outw), add_low(mine_up, came_up), add_low(mine_down, came_down)])
        factors = gather_step(four, "shard", 2)
        grad_att, rest, factors = lax.optimization_barrier((grad_att, rest, factors))
        came = rest_first(rest)
    grad_q, part_k, part_v = attend_back(meta, queries, keys, vals, attended, grad_att, lse, n)
    rows, near = grad_q.shape[0], part_k.shape[0] // 2
    def to_hidden1(at):
        return dot(part_k[at], w_qkv[1], NT) + dot(part_v[at], w_qkv[2], NT)

    far = to_hidden1(slice(near, None)).astype(BF)
    grad_q, part_k, part_v, far = lax.optimization_barrier((grad_q, part_k, part_v, far))
    if fast:
        far, *came = lax.optimization_barrier((far, *came))
    close = to_hidden1(slice(0, near)) + swap(far, "section", 1).astype(F32)
    if fast:
        close, *came = lax.optimization_barrier((close, *came))
    grad_hidden1 = sum_pieces(close, n // 2)
    grad_hidden1 = grad_hidden1 + dot(grad_q, w_qkv[0], NT)
    _, norm_back1 = jax.vjp(layer_norm, values, vecs[0], vecs[1])
    grad_norm1, grad_gain1, grad_bias1 = norm_back1(grad_hidden1)
    grad_input = (grad_middle + grad_norm1).astype(BF)
    grad_input, grad_q, part_k, part_v = lax.optimization_barrier((grad_input, grad_q, part_k, part_v))
    grad_qk = [dot(h, g, TN).astype(BF) for h, g in ((all_hidden1[:rows], grad_q), (all_hidden1, part_k))]

    def grad_qkvw(part_v):
        return merge_units([*grad_qk, dot(all_hidden1, part_v, TN).astype(BF)], [(j, 0) for j in range(3)])

    if fast:
        rest = rest_second(rest, came)
        summed = (rest, *along_shard(rest, (1, 3))), (part_v, lambda v: fold_cores(grad_qkvw(v)))
    else:
        summed = jnp.concatenate([grad_qkvw(part_v), grad_outw, grad_up, grad_down])
        factors = gather_axis(beside(factors), "shard")
    return grad_input, summed, [grad_gain1, grad_bias1, grad_gain2, grad_bias2], factors


def head_mask():
    head = lax.broadcasted_iota(jnp.int32, (HEADS, D), 0)
    return lax.broadcasted_iota(jnp.int32, (HEADS, D), 1) // HD == head


def last_forward(values, positions, length, half, weights, vecs):
    (w_q, w_k, w_v), w_out, w_up, w_down = weights
    heads = head_mask()
    hidden1 = layer_norm(values, vecs[0], vecs[1]).astype(BF)
    mine = (positions == length - 1)[:, None]
    row = jnp.sum(jnp.where(mine, values, 0.0), axis=0, keepdims=True)
    row = group_reduce(row, jnp.add, half)
    row_h1 = layer_norm(row, vecs[0], vecs[1]).astype(BF)
    query = dot(row_h1, w_q).astype(BF)
    wq = dot(jnp.where(heads, query, 0), w_k, NT) * 0.125
    scores = dot2(wq, hidden1, NT)
    scores = jnp.where((positions < length)[None, :], scores, -1e30)
    top = jnp.max(scores, axis=1, keepdims=True)
    expo = jnp.exp(scores - top)
    total = jnp.sum(expo, axis=1, keepdims=True)
    mixed = dot(expo.astype(BF), hidden1)
    wide = lambda x: jnp.broadcast_to(x, (HEADS, HD))

    def merge(x, y):
        high = jnp.maximum(x[:, D : D + 1], y[:, D : D + 1])
        x = x * jnp.exp(x[:, D : D + 1] - high)
        y = y * jnp.exp(y[:, D : D + 1] - high)
        return jnp.concatenate([x[:, :D] + y[:, :D], wide(high), x[:, D + HD :] + y[:, D + HD :]], axis=1)

    merged = group_reduce(jnp.concatenate([mixed, wide(top), wide(total)], axis=1), merge, half)
    top, total = merged[:, D : D + 1], merged[:, D + HD : D + HD + 1]
    mixed = merged[:, :D] / total
    probs = jnp.exp(scores - top) / total
    att = jnp.sum(jnp.where(heads, dot2(mixed, w_v), 0.0), axis=0, keepdims=True)
    middle = row + dot(att.astype(BF), w_out)
    hidden2 = layer_norm(middle, vecs[2], vecs[3]).astype(BF)
    ups = dot(hidden2, w_up)
    gated = gelu_tanh(ups).astype(BF)
    result = middle + dot(gated, w_down)
    return result, (values, hidden1, mine, row_h1, query, wq, probs, mixed, att, middle, hidden2, ups, gated)


def last_backward(saved, grad_out, half, weights, vecs):
    values, hidden1, mine, row_h1, query, wq, probs, mixed, att, middle, hidden2, ups, gated = saved
    (w_q, w_k, w_v), w_out, w_up, w_down = weights
    heads = head_mask()
    grad_ffn = grad_out.astype(BF)
    _, back = jax.vjp(gelu_tanh, ups)
    grad_ups = back(dot(grad_ffn, w_down, NT))[0].astype(BF)
    grad_hidden2 = dot(grad_ups, w_up, NT)
    _, norm_back2 = jax.vjp(layer_norm, middle, vecs[2], vecs[3])
    grad_norm2, grad_gain2, grad_bias2 = norm_back2(grad_hidden2)
    grad_middle = grad_out + grad_norm2
    grad_branch = grad_middle.astype(BF)
    grad_att = dot(grad_branch, w_out, NT).astype(BF)
    att_heads = jnp.where(heads, grad_att, 0)
    wv = dot(att_heads, w_v, NT)
    grad_prob = dot2(wv, hidden1, NT)
    delta = jnp.sum(att_heads.astype(F32) * att, axis=1, keepdims=True)
    grad_score = (probs * (grad_prob - delta)).astype(BF)
    summed = group_reduce(dot(grad_score, hidden1), jnp.add, half)
    grad_query = (jnp.sum(jnp.where(heads, dot2(summed, w_k), 0.0), axis=0, keepdims=True) * 0.125).astype(BF)
    low_probs = probs.astype(BF)
    grad_hidden1 = dot(
        jnp.concatenate([grad_score, grad_score, low_probs, low_probs]), jnp.concatenate([split2(wq), split2(wv)]), TN
    )
    grad_hidden1 = grad_hidden1 + jnp.where(mine, dot(grad_query, w_q, NT), 0.0)
    _, norm_back1 = jax.vjp(layer_norm, values, vecs[0], vecs[1])
    grad_norm1, grad_gain1, grad_bias1 = norm_back1(grad_hidden1)
    grad_input = grad_norm1 + jnp.where(mine, grad_middle, 0.0)
    query8 = query * jnp.asarray(0.125, BF)
    factors = [row_h1, grad_query, query8, grad_att, att, grad_branch, hidden2, grad_ffn]
    factors += [grad_ups.reshape(N_UP, D), gated.reshape(N_UP, D), summed, mixed]
    factors = jnp.concatenate([f.astype(BF) for f in factors])
    return grad_input, factors, [grad_gain1, grad_bias1], [grad_gain2, grad_bias2]


def last_gradient(data, chunk_at, n_chunks, size):
    n_seq = data.shape[0]
    heads = head_mask()
    row_h1, grad_query, query8, grad_att, att, grad_branch, hidden2, grad_ffn = [data[:, i] for i in range(8)]
    at = 8
    grad_ups, gated = data[:, at : at + N_UP], data[:, at + N_UP : at + 2 * N_UP]
    at += 2 * N_UP
    summed, mixed = data[:, at : at + HEADS], data[:, at + HEADS : at + 2 * HEADS]

    def by_unit(parts):
        count, width = len(parts), sum(p.shape[0] for p in parts)
        slot = jnp.concatenate([jnp.full((p.shape[0],), j, jnp.int32) for j, p in enumerate(parts)])
        both = jnp.concatenate(parts).T
        spread = jnp.where(slot[None, None, :] == jnp.arange(count)[None, :, None], both[:, None, :], 0)
        return spread.reshape(count * D, width)

    def per_head(x):
        return jnp.where(heads[None], x[:, None, :], 0).reshape(n_seq * HEADS, D)

    left = by_unit([row_h1, summed.reshape(-1, D), mixed.reshape(-1, D)])
    right = jnp.concatenate([grad_query, per_head(query8), per_head(grad_att)])
    first = chunk_at * size
    qkv = dot(lax.dynamic_slice_in_dim(left, jnp.minimum(first, U_OUT - size), size, 0), right)
    lefts = [att.T, by_unit([hidden2] * N_UP), gated.reshape(n_seq, FF).T]
    rights = [grad_branch, grad_ups.transpose(1, 0, 2).reshape(-1, D), grad_ffn]
    width = sum(x.shape[1] for x in lefts)
    columns, before = [], 0
    for x in lefts:
        columns.append(jnp.pad(x, ((0, 0), (before, width - before - x.shape[1]))))
        before += x.shape[1]
    left = jnp.concatenate(columns)
    rest = dot(lax.dynamic_slice_in_dim(left, jnp.maximum(first - U_OUT, 0), size, 0), jnp.concatenate(rights))
    return jnp.where(first < U_OUT, qkv, rest)


def shards(
    tokens,
    lengths,
    end_ids,
    pairs,
    layer_master,
    layer_first,
    layer_second,
    table_master,
    table_first,
    table_second,
    vector_master,
    vector_first,
    vector_second,
):
    rows = tokens.shape[1]
    s_at = lax.axis_index("section")
    c_at = lax.axis_index("ctx")
    z_at = lax.axis_index("shard")
    n_section = lax.axis_size("section")
    n = lax.axis_size("ctx")
    n_shard = lax.axis_size("shard")
    half = n // 2
    hb = rows // 2
    n_dest = n_section * n
    n_seq = MICRO * n_shard
    columns, entries = table_master.shape
    is_first = s_at == 0
    seq_in = c_at // half
    seq_at = z_at * MICRO + seq_in
    group = (c_at % half) * 2 + s_at

    fast = small_block()
    chunk = chunk_rows(layer_master) if fast else layer_master.reshape(-1, D).astype(BF)
    size = chunk.shape[0]
    cut = size // 2
    if fast:
        wide = cut + OVERLAP // 2
        got = swap(jnp.where(is_first, chunk[size - wide :], chunk[:wide]), "section", 1)
        piece0 = jnp.where(is_first, chunk[:wide], got)
        piece1 = jnp.where(is_first, got[:cut], chunk[cut:])
    else:
        got = swap(jnp.where(is_first, chunk[cut:], chunk[:cut]), "section", 1)
        piece0 = jnp.where(is_first, chunk[:cut], got)
        piece1 = jnp.where(is_first, got, chunk[cut:])
    order = ("ctx", "shard", "section")

    own_ids = jnp.concatenate([tokens, end_ids[:, None]], axis=1)
    all_ids = gather_axis(gather_axis(own_ids, "ctx"), "shard")
    natural = all_ids[..., :rows].transpose(0, 2, 1, 3).reshape(n_shard, MICRO, 2 * n, hb)
    zig = jnp.stack([natural[:, :, :n], natural[:, :, n:][:, :, ::-1]], axis=3)
    zig = zig.reshape(n_shard, MICRO, half, 2, rows).transpose(0, 3, 1, 2, 4)
    end_all = all_ids[:, 0, :, rows].reshape(n_seq)
    n_blocks = n_shard * n_dest

    def held(ids):
        ids = ids - z_at * entries
        return jnp.where((ids >= 0) & (ids < entries), ids, entries)

    listed, counts = owned_rows(held(zig.reshape(n_blocks, rows)), entries)
    end_held = held(end_all)
    if fast:
        first = first_moves(piece0)
        listed, piece0, *first = lax.optimization_barrier((listed, piece0, *first))
        second = second_moves(piece0, first[0], first[1])
    else:
        units0 = lax.all_gather(piece0, order, axis=0, tiled=True)
    dest = jnp.arange(n_blocks, dtype=jnp.int32) % n_dest
    groups = (dest % n % half) * 2 + dest // n
    assert VOCAB >= (n_shard - 1) * entries
    meta_emb = jnp.concatenate(
        [
            jnp.stack([(z_at == n_shard - 1).astype(jnp.int32), jnp.int32(n), jnp.int32(VOCAB - (n_shard - 1) * entries), jnp.int32(0)]),
            groups,
        ]
    )
    picked, end_part = lookup(listed, counts, end_held, meta_emb, table_master, n_blocks, rows)
    if fast:
        picked, *second = lax.optimization_barrier((picked, *second))
        halves = gather_half(piece0, first, second)
    column_at = (s_at * n + c_at) * columns
    end_rows = sum_all(lax.dynamic_update_slice(jnp.zeros((n_seq, D), F32), end_part, (0, column_at)))
    summed = lax.psum_scatter(picked.reshape(n_shard, n_dest, columns, rows), "shard", scatter_dimension=0, tiled=True)
    if fast:
        summed, piece1, end_rows, *halves = lax.optimization_barrier((summed, piece1, end_rows, *halves))
        parts = [part for mine in halves for part in (mine, swap(mine, "section", 1))]
    routed = lax.all_to_all(summed.reshape(n_dest, columns, rows), ("section", "ctx"), split_axis=0, concat_axis=0, tiled=True)
    embedded = routed.reshape(D, rows).T.astype(F32)
    end_row = lax.dynamic_slice_in_dim(end_rows, seq_at, 1, 0)
    units1 = lax.all_gather(piece1, order, axis=0, tiled=True)

    length = lax.dynamic_slice_in_dim(lengths, seq_in, 1, 0)[0]
    others = [group ^ (2 * cb + sb) for sb in range(2) for cb in range(half)]
    meta = jnp.stack([group, length] + others).astype(jnp.int32)
    span = jnp.arange(hb, dtype=jnp.int32)
    positions = jnp.concatenate([group * hb + span, (2 * n - 1 - group) * hb + span])

    vecs0, vecs1 = vector_master[0:4], vector_master[4:8]
    hidden1 = layer_norm(embedded, vecs0[0], vecs0[1]).astype(BF)
    if fast:
        hidden1, *parts = lax.optimization_barrier((hidden1, *parts))
        units0 = place_units(parts)
    weights0 = layer_weights(units0)
    others = pieces_by_ctx(hidden1, half)[1:]
    *others, w_qkv0, w_up0 = lax.optimization_barrier((*others, weights0[0], weights0[2]))
    weights0 = (w_qkv0, weights0[1], w_up0, weights0[3])
    out0, saved0 = layer_forward(embedded, hidden1, pieces_by_section([hidden1, *others]), meta, n, weights0, vecs0)
    x1 = out0.astype(BF).astype(F32)
    x1, units1 = lax.optimization_barrier((x1, units1))
    w_qkv1 = split_units(units1, 0, 3)
    weights1 = ((w_qkv1[0], w_qkv1[1], w_qkv1[2]), units1[U_OUT:U_UP], join_units(units1, U_UP, N_UP), units1[U_DOWN:])
    final, saved1 = last_forward(x1, positions, length, half, weights1, vecs1)

    def score_terms(final_row, end_vals, gain_vec, bias_vec, head_vec):
        normed = layer_norm(final_row, gain_vec, bias_vec)
        return jnp.sum(normed * (end_vals + head_vec)) * D ** (-0.5)

    counted = group == 0
    score, score_back = jax.vjp(score_terms, final, end_row, vector_master[8], vector_master[9], vector_master[10])
    scores = sum_small(jnp.where((jnp.arange(n_seq) == seq_at) & counted, score, 0.0)[None])[0]

    def pair_loss(score_vals):
        return jnp.sum(softplus(score_vals[pairs[:, 1]] - score_vals[pairs[:, 0]]))

    loss_sum, loss_back = jax.vjp(pair_loss, scores)
    grad_scores = loss_back(jnp.ones_like(loss_sum))[0]
    grad_own = lax.dynamic_slice_in_dim(grad_scores, seq_at, 1, 0)[0]
    grad_final, grad_end, *vec_final = score_back(grad_own)

    grad_x1, factors, vec1, vec1_row = last_backward(saved1, grad_final, half, weights1, vecs1)
    factors = jnp.concatenate([factors, grad_end.astype(BF)])
    grad_x1 = grad_x1.astype(BF).astype(F32)
    grad_x0, grads0, vec0, every_factor = layer_backward(saved0, grad_x1, meta, n, weights0, vecs0, factors, fast)
    every_factor = every_factor.reshape(n_seq, -1, D)

    by_owner = grad_x0.T.reshape(n_dest, columns, rows)
    back = lax.all_to_all(by_owner, ("section", "ctx"), split_axis=0, concat_axis=0, tiled=True)
    if fast:
        (rest, one, three), (part_v, finish_qkv) = grads0
        every = [back] + [shift(back, "shard", d) for d in (1, 3, 2)]
        every[1], every[2], every_factor, rest = lax.optimization_barrier((every[1], every[2], every_factor, rest))
        qkv_part = qkv_second(*qkv_first(finish_qkv(part_v)))
        rest_terms = [shard_chunk(rest, 0), one, three] + along_shard(rest, (2,))
        every[3], qkv_part = lax.optimization_barrier((every[3], qkv_part))
        every = jnp.concatenate(every)
        near_order = (z_at + 4 - jnp.array((0, 1, 3, 2), jnp.int32)) % 4
        listed = listed.reshape(n_shard, -1)[near_order].reshape(-1)
        counts = counts.reshape(n_shard, -1)[near_order].reshape(-1)
    else:
        every = lax.all_gather(back, "shard", axis=0, tiled=True)
    end_grads = lax.dynamic_slice(every_factor[:, -1].astype(F32), (0, column_at), (n_seq, columns))
    table_grad = scatter(listed, counts, end_held, meta_emb, every, end_grads, entries)
    once = [jnp.where(counted, v, 0.0) for v in vec1_row + vec_final]
    vector_part = jnp.stack(vec0 + vec1 + once)

    own1 = last_gradient(every_factor, c_at * n_shard + z_at, n * n_shard, size)
    squares = jnp.sum(table_grad * table_grad) + jnp.where(is_first, 0.0, jnp.sum(own1 * own1))
    if fast:
        qkv_terms = [shard_chunk(qkv_part, 0)] + along_shard(qkv_part, (1, 3, 2))
        terms = [*rest_terms, *qkv_terms]
        table_grad, own1, squares, vector_part, *terms = lax.optimization_barrier(
            (table_grad, own1, squares, vector_part, *terms)
        )
        rest_terms, qkv_terms = terms[:4], terms[4:]
        mine = sum(t.astype(F32) for t in rest_terms)
        collected = collect_qkv(sum(t.astype(F32) for t in qkv_terms))[: mine.shape[0] * BLOCK]
        mine = jnp.where(c_at == 0, collected.reshape(mine.shape), mine)
    else:
        mine = lax.psum_scatter(grads0, order, scatter_dimension=0, tiled=True).astype(F32)
    squares = squares + jnp.sum(mine * mine)
    other = swap(mine.astype(BF), "section", 1).astype(F32)
    own0 = jnp.stack([mine, other], axis=1).reshape(size, D) if fast else jnp.concatenate([mine, other])
    layer_grad = jnp.where(is_first, own0, own1).reshape(-1, LANES)

    n_vec = vector_part.shape[0]
    totals = sum_small(jnp.concatenate([vector_part, jnp.full((1, D), squares)]))
    vector_grad = totals[:n_vec]
    grad_norm = jnp.sqrt(totals[n_vec, 0] + jnp.sum(vector_grad * vector_grad))
    layer_grad, grad_norm = lax.optimization_barrier((layer_grad, grad_norm))
    factor = CLIP_LIMIT / jnp.maximum(grad_norm, CLIP_LIMIT)
    flat = [x.reshape(-1, LANES) for x in (layer_master, layer_first, layer_second)]
    flat_rows = flat[0].shape[0]
    block_rows = max(b for b in range(1, 2313) if flat_rows % b == 0 and (b % 8 == 0 or b == flat_rows))
    table_cols = max(b for b in range(LANES, 1537, LANES) if entries % b == 0)
    layer_new = adam(factor, *flat, layer_grad, 0.4, 0.1, (block_rows, LANES))
    layer_new = [x.reshape(layer_master.shape) for x in layer_new]
    table_new = adam(factor, table_master, table_first, table_second, table_grad, 0.5, 0.1, (columns, table_cols))
    vector_new = adam_update(vector_master, vector_first, vector_second, vector_grad * factor, 0.7, 0.0)
    return (loss_sum, grad_norm, *layer_new, *table_new, *vector_new)


def solution(mesh):
    in_specs = (
        P("shard", "ctx"),
        P("shard"),
        P("shard"),
        P(),
        P("section", ("ctx", "shard")),
        P("section", ("ctx", "shard")),
        P("section", ("ctx", "shard")),
        P(("section", "ctx"), "shard"),
        P(("section", "ctx"), "shard"),
        P(("section", "ctx"), "shard"),
        P(),
        P(),
        P(),
    )
    out_specs = (
        P(),
        P(),
        P("section", ("ctx", "shard")),
        P("section", ("ctx", "shard")),
        P("section", ("ctx", "shard")),
        P(("section", "ctx"), "shard"),
        P(("section", "ctx"), "shard"),
        P(("section", "ctx"), "shard"),
        P(),
        P(),
        P(),
    )
    return jax.shard_map(shards, mesh=mesh, in_specs=in_specs, out_specs=out_specs, check_vma=False)
```

```python
import functools

import jax
import jax.numpy as jnp
from jax import lax
from jax.experimental import pallas as pl
from jax.experimental.layout import Layout, with_layout_constraint
from jax.experimental.pallas import tpu as pltpu
from jax.sharding import PartitionSpec as P

D = 1088
HEADS = 17
HD = 64
FF = 4352
VOCAB = 51200
MICRO = 2
STEP = 10
CLIP_LIMIT = 0.02
ALL = ("section", "ctx", "shard")

LANES = 128
PAIRS_OF_HEADS = (HEADS + 1) // 2
WIDE = PAIRS_OF_HEADS * LANES
N_UP = FF // D
U_OUT = 3 * D
U_UP = U_OUT + D
U_DOWN = U_UP + FF
UNITS = U_DOWN + FF

BF = jnp.bfloat16
F32 = jnp.float32
VMEM_BIG = 56 * 1024 * 1024


def params(limit=VMEM_BIG):
    return pltpu.CompilerParams(vmem_limit_bytes=limit)


def cost(microseconds):
    return pl.CostEstimate(flops=0, bytes_accessed=int(microseconds * 3.0e6), transcendentals=0)


def dot(a, b, contract=((1,), (0,))):
    return lax.dot_general(a, b, (contract, ((), ())), preferred_element_type=F32)


NT = ((1,), (1,))
TN = ((0,), (0,))


def split2(x):
    top = lax.reduce_precision(x, 8, 7)
    return jnp.concatenate([top, x - top]).astype(BF)


def dot2(x, w, contract=((1,), (0,))):
    y = dot(split2(x), w, contract)
    return y[: x.shape[0]] + y[x.shape[0] :]


def swap(x, axis, bit):
    size = lax.axis_size(axis)
    return lax.ppermute(x, axis, [(i, i ^ bit) for i in range(size)])


def gather_step(x, axis, bit):
    other = swap(x, axis, bit)
    lower = (lax.axis_index(axis) & bit) == 0
    return jnp.where(lower, jnp.concatenate([x, other]), jnp.concatenate([other, x]))


def gather_axis(x, axis):
    x = x[None]
    bit = 1
    while bit < lax.axis_size(axis):
        x = gather_step(x, axis, bit)
        bit *= 2
    return x


def beside(x):
    return gather_step(x[None], "ctx", lax.axis_size("ctx") // 2)


def sum_axis(x, axis, first=1, last=None):
    size = lax.axis_size(axis) if last is None else last
    bit = first
    while bit < size:
        x = x + swap(x, axis, bit)
        bit *= 2
    return x


def group_reduce(x, combine, half):
    def step(x, axis, bit):
        other = swap(x, axis, bit)
        lower = (lax.axis_index(axis) & bit) == 0
        return combine(jnp.where(lower, x, other), jnp.where(lower, other, x))

    x = step(x, "section", 1)
    bit = 1
    while bit < half:
        x = step(x, "ctx", bit)
        bit *= 2
    return x


def sum_all(x):
    return sum_axis(sum_axis(sum_axis(x, "section"), "ctx"), "shard")


def sum_direct(x, axis):
    if lax.axis_size(axis) != 4:
        return sum_axis(x, axis)
    one, two, three = [lax.ppermute(x, axis, [(i, (i + d) % 4) for i in range(4)]) for d in (1, 2, 3)]
    return (x + two) + (one + three)


def sum_small(x):
    return sum_direct(sum_direct(sum_direct(x, "section"), "ctx"), "shard")


def rows_kernel(pairs, x, out, scr):
    lane = lax.broadcasted_iota(jnp.int32, (1, LANES), 1)
    step = 2 * D // LANES
    even, odd = pl.ds(0, pairs, stride=2), pl.ds(1, pairs, stride=2)
    flat_row = lambda t: x[pl.ds(t, pairs, stride=step), :]
    for t in range(PAIRS_OF_HEADS):
        scr[t, even, :] = flat_row(t)
    before = pltpu.roll(flat_row(step // 2), HD, 1)
    for t in range(PAIRS_OF_HEADS - 1):
        after = pltpu.roll(flat_row(step // 2 + 1 + t), HD, 1)
        scr[t, odd, :] = jnp.where(lane < HD, before, after)
        before = after
    scr[PAIRS_OF_HEADS - 1, odd, :] = before
    for t, (at, size) in enumerate(tile_cuts()):
        out[:, pl.ds(at, size)] = scr[t][:, :size].astype(BF)


def chunk_rows(flat):
    units = flat.size // D
    return pl.pallas_call(
        functools.partial(rows_kernel, units // 2),
        out_shape=jax.ShapeDtypeStruct((units, D), BF),
        scratch_shapes=[pltpu.VMEM((PAIRS_OF_HEADS, units, LANES), F32)],
        compiler_params=params(),
        cost_estimate=cost(6),
        name="chunk_rows",
    )(flat.reshape(-1, LANES))


def small_block():
    return lax.axis_size("ctx") == 4 and lax.axis_size("shard") == 4 and lax.axis_size("section") == 2


def shift(x, axis, by):
    size = lax.axis_size(axis)
    return lax.ppermute(x, axis, [(i, (i + by) % size) for i in range(size)])


ARRIVALS = ((0,), (1, 3), (2,))
OVERLAP = 16


def place_kernel(rows, at, *refs):
    ins, out, held, sems_in, sems_out = refs[: 2 * len(ARRIVALS)], refs[-4], refs[-3], refs[-2], refs[-1]
    s, c, z = at[0], at[1], at[2]
    short = rows - OVERLAP
    pieces = []
    for g, distances in enumerate(ARRIVALS):
        for other in range(2):
            for e in range(4):
                for i, d in enumerate(distances):
                    chunk = (c ^ e) * 4 + lax.rem(z + 4 - d, 4)
                    pieces.append((ins[2 * g + other].at[e, i], chunk, other))

    def arrive(k):
        return pltpu.make_async_copy(pieces[k][0], held.at[k], sems_in.at[k])

    def leave(k, act):
        _, chunk, other = pieces[k]

        @pl.when(s == other)
        def _():
            act(pltpu.make_async_copy(held.at[k], out.at[chunk, pl.ds(0, rows)], sems_out.at[k]))

        @pl.when(s != other)
        def _():
            act(pltpu.make_async_copy(held.at[k, pl.ds(OVERLAP, short)], out.at[chunk, pl.ds(rows, short)], sems_out.at[k]))

    for k in range(len(pieces)):
        arrive(k).start()
    for k in range(len(pieces)):
        arrive(k).wait()
        leave(k, lambda copy: copy.start())
    for k in range(len(pieces)):
        leave(k, lambda copy: copy.wait())


def by_links(own):
    return swap(own, "ctx", 1), swap(own, "ctx", 2)


def first_moves(piece):
    return shift(piece, "shard", 1), shift(piece, "shard", 3), *by_links(piece[None])


def second_moves(piece, near, far):
    return shift(piece, "shard", 2), *by_links(jnp.stack([near, far]))


def corner_of(by_x, by_y):
    cut = by_x.shape[1] // 2
    return jnp.concatenate([swap(by_x[:, :cut], "ctx", 2), swap(by_y[:, cut:], "ctx", 1)], axis=1)


def gather_half(piece, first, second):
    near, far, *own_links = first
    opposite, *near_links = second
    arrived = {0: piece, 1: near, 3: far, 2: opposite}
    parts = []
    for distances, links in zip(ARRIVALS, (own_links, near_links, None)):
        own = jnp.stack([arrived[d] for d in distances])
        by_x, by_y = by_links(own) if links is None else links
        corner = corner_of(by_x, by_y)
        parts.append(jnp.stack([own, by_x, by_y, corner]))
    return parts


def place_units(parts):
    rows = parts[0].shape[2]
    at = jnp.stack([lax.axis_index(a) for a in ALL]).astype(jnp.int32)
    grid_spec = pltpu.PrefetchScalarGridSpec(
        num_scalar_prefetch=1,
        grid=(1,),
        in_specs=[pl.BlockSpec(memory_space=pl.ANY)] * len(parts),
        out_specs=pl.BlockSpec(memory_space=pl.ANY),
        scratch_shapes=[pltpu.VMEM((32, rows, D), BF), pltpu.SemaphoreType.DMA((32,)), pltpu.SemaphoreType.DMA((32,))],
    )
    whole = pl.pallas_call(
        functools.partial(place_kernel, rows),
        grid_spec=grid_spec,
        out_shape=jax.ShapeDtypeStruct((16, 2 * rows - OVERLAP, D), BF),
        compiler_params=params(),
        cost_estimate=cost(16),
        name="place",
    )(at, *parts)
    return whole.reshape(UNITS, D)


def add_low(x, y):
    return (x.astype(F32) + y.astype(F32)).astype(BF)


BLOCK = 136
QUARTER = 104


def core_blocks(region):
    s = lax.axis_index("section")
    blocks = region.reshape(-1, 2, BLOCK, D)
    pick = lambda i: lax.dynamic_index_in_dim(blocks, i, 1, keepdims=False)
    return pick(s), pick(1 - s)


def fold_cores(region):
    mine, other = core_blocks(region)
    return add_low(mine, swap(other, "section", 1))


def one_way(x, bit, sends):
    return lax.ppermute(x, "ctx", [(i, i ^ bit) for i in range(4) if sends(i)])


def three_first(one, two, both, p):
    has_p = (lax.axis_index("ctx") & p) != 0
    return swap(jnp.where(has_p, two, one), "ctx", p), one_way(both, p, lambda i: not i & p)


def three_second(one, two, both, came, came_both, p, q):
    c = lax.axis_index("ctx")
    has_p, has_q = (c & p) != 0, (c & q) != 0
    single = add_low(jnp.where(has_p, one, two), came)
    both = add_low(both, came_both)
    sent = jnp.where(has_p & ~has_q, both, single)
    came = one_way(sent, q, lambda i: not i & q or i & p)
    return add_low(jnp.where(has_p & has_q, both, single), came)


def rest_first(rest):
    x = rest.reshape(3, 4, -1, BLOCK, D)
    return *three_first(x[0, :2], x[1, :2], x[2, :2], 1), *three_first(x[1, 2:], x[0, 2:], x[2, 2:], 2)


def rest_second(rest, came):
    x = rest.reshape(3, 4, -1, BLOCK, D)
    first = three_second(x[0, :2], x[1, :2], x[2, :2], came[0], came[1], 1, 2)
    second = three_second(x[1, 2:], x[0, 2:], x[2, 2:], came[2], came[3], 2, 1)
    return jnp.concatenate([first, second])


def fold_half(v, axis, bit):
    mine = (lax.axis_index("ctx") // bit) & 1
    pick = lambda i: lax.dynamic_index_in_dim(v, i, axis, keepdims=True)
    return add_low(pick(mine), swap(pick(1 - mine), "ctx", bit))


def qkv_first(qkv):
    x = qkv.reshape(4, -1, D)
    x = jnp.pad(x, ((0, 0), (0, 4 * QUARTER - x.shape[1]), (0, 0))).reshape(4, 2, 2, QUARTER, D)
    return fold_half(x[:2], 2, 1), fold_half(x[2:], 1, 2)


def qkv_second(first, second):
    return jnp.concatenate([fold_half(first, 1, 2), fold_half(second, 2, 1)])[:, 0, 0]


def collect_qkv(quarter):
    low = quarter.astype(BF)
    others = [lax.ppermute(low, "ctx", [(i, 0)]).astype(F32) for i in (1, 2, 3)]
    return jnp.concatenate([quarter, *others])


def shard_chunk(x, by):
    return lax.dynamic_index_in_dim(x, lax.rem(lax.axis_index("shard") + by, 4), 0, keepdims=False)


def along_shard_first(x):
    return shift(shard_chunk(x, 2), "shard", 1)


def along_shard(x, passing):
    through = add_low(shard_chunk(x, 1), passing)
    return [shard_chunk(x, 0), shift(shard_chunk(x, 3), "shard", 3), shift(through, "shard", 1)]


SHIFT = 10
UNROLL = 8


def owned_rows(ids, entries):
    rows = ids.shape[1]
    assert rows < (1 << SHIFT)
    owned = ids < entries
    place = jnp.cumsum(owned.astype(jnp.int32), axis=1) - 1
    packed = jnp.arange(rows, dtype=jnp.int32)[None, :] + (ids << SHIFT)
    slots = jnp.arange(rows, dtype=jnp.int32)
    hit = (place[:, None, :] == slots[None, :, None]) & owned[:, None, :]
    listed = jnp.sum(jnp.where(hit, packed[:, None, :], 0), axis=2)
    count = jnp.sum(owned.astype(jnp.int32), axis=1)
    listed = jnp.where(slots[None, :] < count[:, None], listed, rows + (entries << SHIFT))
    return listed.reshape(-1), count


def for_owned(listed, counts, step, rows, body):
    def some(t, _):
        for u in range(UNROLL):
            packed = listed[step * rows + t * UNROLL + u]
            body(pl.ds(packed & ((1 << SHIFT) - 1), 1), pl.ds(packed >> SHIFT, 1))
        return 0

    lax.fori_loop(0, (counts[step] + UNROLL - 1) // UNROLL, some, 0)


def lookup_kernel(rows, listed, counts, end_ids, meta, table, out, ends, tab, buf):
    step = pl.program_id(0)
    columns, entries = table.shape

    @pl.when(step == 0)
    def _():
        def turn(i, _):
            at = pl.multiple_of(i * 256, 256)
            tab[pl.ds(at, 256), :] = table[:, pl.ds(at, 256)].astype(BF).astype(F32).T
            return 0

        lax.fori_loop(0, entries // 256, turn, 0)
        tab[pl.ds(entries, 8), :] = jnp.zeros((8, columns), F32)
        for n in range(ends.shape[0]):
            ends[pl.ds(n, 1), :] = tab[pl.ds(end_ids[n], 1), :]

    buf[...] = jnp.zeros_like(buf)

    def pick(place, entry):
        buf[place, :] = tab[entry, :]

    for_owned(listed, counts, step, rows, pick)

    @pl.when(meta[0] == 1)
    def _():
        half = rows // 2
        group = meta[4 + step]
        for j in range(2):
            block = group if j == 0 else 2 * meta[1] - 1 - group
            at = pl.multiple_of(meta[2] + block * half, 8)
            buf[pl.ds(j * half, half), :] += tab[pl.ds(at, half), :]

    out[0] = buf[pl.ds(0, rows), :].T.astype(BF)


def lookup(listed, counts, end_ids, meta, table, n_blocks, rows):
    columns, entries = table.shape
    n_ends = end_ids.shape[0]
    grid_spec = pltpu.PrefetchScalarGridSpec(
        num_scalar_prefetch=4,
        grid=(n_blocks,),
        in_specs=[pl.BlockSpec((columns, entries), lambda i, *_: (0, 0))],
        out_specs=[
            pl.BlockSpec((1, columns, rows), lambda i, *_: (i, 0, 0)),
            pl.BlockSpec((n_ends, columns), lambda i, *_: (0, 0)),
        ],
        scratch_shapes=[pltpu.VMEM((entries + 8, columns), F32), pltpu.VMEM((rows + 8, columns), F32)],
    )
    return pl.pallas_call(
        functools.partial(lookup_kernel, rows),
        grid_spec=grid_spec,
        out_shape=[
            jax.ShapeDtypeStruct((n_blocks, columns, rows), BF),
            jax.ShapeDtypeStruct((n_ends, columns), F32),
        ],
        compiler_params=params(),
        cost_estimate=cost(40),
        name="lookup",
    )(listed, counts, end_ids, meta, table)


def scatter_kernel(rows, n_blocks, listed, counts, end_ids, meta, grads, ends, out, acc, buf):
    step = pl.program_id(0)
    columns, entries = out.shape
    n_ends = ends.shape[0]

    @pl.when(step == 0)
    def _():
        def clear(i, _):
            acc[pl.ds(pl.multiple_of(i * 256, 256), 256), :] = jnp.zeros((256, columns), F32)
            return 0

        lax.fori_loop(0, entries // 256, clear, 0)
        for n in range(n_ends):
            at = pl.ds(end_ids[n], 1)
            acc[at, :] += ends[pl.ds(n, 1), :]

    buf[pl.ds(0, rows), :] = grads[0].astype(F32).T

    def add(place, entry):
        acc[entry, :] += buf[place, :]

    for_owned(listed, counts, step, rows, add)

    @pl.when(meta[0] == 1)
    def _():
        half = rows // 2
        group = meta[4 + step]
        for j in range(2):
            block = group if j == 0 else 2 * meta[1] - 1 - group
            at = pl.multiple_of(meta[2] + block * half, 8)
            acc[pl.ds(at, half), :] += buf[pl.ds(j * half, half), :]

    @pl.when(step == n_blocks - 1)
    def _():
        def turn(i, _):
            at = pl.multiple_of(i * 256, 256)
            out[:, pl.ds(at, 256)] = acc[pl.ds(at, 256), :].T
            return 0

        lax.fori_loop(0, entries // 256, turn, 0)


def scatter(listed, counts, end_ids, meta, grads, ends, entries):
    n_blocks, columns, rows = grads.shape
    n_ends = ends.shape[0]
    grid_spec = pltpu.PrefetchScalarGridSpec(
        num_scalar_prefetch=4,
        grid=(n_blocks,),
        in_specs=[
            pl.BlockSpec((1, columns, rows), lambda i, *_: (i, 0, 0)),
            pl.BlockSpec((n_ends, columns), lambda i, *_: (0, 0)),
        ],
        out_specs=pl.BlockSpec((columns, entries), lambda i, *_: (0, 0)),
        scratch_shapes=[pltpu.VMEM((entries + 8, columns), F32), pltpu.VMEM((rows + 8, columns), F32)],
    )
    return pl.pallas_call(
        functools.partial(scatter_kernel, rows, n_blocks),
        grid_spec=grid_spec,
        out_shape=jax.ShapeDtypeStruct((columns, entries), F32),
        compiler_params=params(),
        cost_estimate=cost(42),
        name="scatter",
    )(listed, counts, end_ids, meta, grads, ends)


def tile_cuts():
    return [(t * LANES, min(LANES, D - t * LANES)) for t in range(PAIRS_OF_HEADS)]


def split_kernel(count, rb, width, u, out, scr):
    for t, (at, size) in enumerate(tile_cuts()):
        part = u[:, pl.ds(at, size)].astype(F32)
        if size < LANES:
            part = jnp.concatenate([part, jnp.zeros((rb * count, LANES - size), F32)], axis=1)
        scr[t] = part
        for j in range(count):
            picked = scr[t, pl.ds(j, rb, stride=count), :].astype(BF)
            take = min(LANES, width - at)
            out[j, :, pl.ds(at, take)] = picked[:, :take]


def join_kernel(count, rb, u, out, scr):
    for t, (at, size) in enumerate(tile_cuts()):
        part = u[:, pl.ds(at, size)].astype(F32)
        if size < LANES:
            part = jnp.concatenate([part, jnp.zeros((rb * count, LANES - size), F32)], axis=1)
        scr[t] = part
        for j in range(count):
            out[:, pl.ds(j * D + at, size)] = scr[t, pl.ds(j, rb, stride=count), :].astype(BF)[:, :size]


def join_units(u, first, count):
    rb = 272
    return pl.pallas_call(
        functools.partial(join_kernel, count, rb),
        grid=(D // rb,),
        in_specs=[pl.BlockSpec((rb * count, D), lambda i: (i + first // (rb * count), 0))],
        out_specs=pl.BlockSpec((rb, count * D), lambda i: (i, 0)),
        out_shape=jax.ShapeDtypeStruct((D, count * D), BF),
        scratch_shapes=[pltpu.VMEM((PAIRS_OF_HEADS, rb * count, LANES), F32)],
        compiler_params=params(),
        cost_estimate=cost(8),
        name="join_units",
    )(u)


def split_units(u, first, count, width=D):
    rb = 272
    return pl.pallas_call(
        functools.partial(split_kernel, count, rb, width),
        grid=(D // rb,),
        in_specs=[pl.BlockSpec((rb * count, D), lambda i: (i + first // (rb * count), 0))],
        out_specs=pl.BlockSpec((count, rb, width), lambda i: (0, i, 0)),
        out_shape=jax.ShapeDtypeStruct((count, D, width), BF),
        scratch_shapes=[pltpu.VMEM((PAIRS_OF_HEADS, rb * count, LANES), F32)],
        compiler_params=params(),
        cost_estimate=cost(8),
        name="split_units",
    )(u)


def merge_kernel(count, rb, starts, *refs):
    parts, out, scr = refs[:-2], refs[-2], refs[-1]
    for t, (at, size) in enumerate(tile_cuts()):
        for j in range(count):
            which, start = starts[j]
            part = parts[which][:, pl.ds(start + at, size)].astype(F32)
            if size < LANES:
                part = jnp.concatenate([part, jnp.zeros((rb, LANES - size), F32)], axis=1)
            scr[t, pl.ds(j, rb, stride=count), :] = part
        out[:, pl.ds(at, size)] = scr[t][:, :size].astype(BF)


def merge_units(parts, starts):
    rb, count = 272, len(starts)
    return pl.pallas_call(
        functools.partial(merge_kernel, count, rb, starts),
        grid=(D // rb,),
        in_specs=[pl.BlockSpec((rb, p.shape[1]), lambda i: (i, 0)) for p in parts],
        out_specs=pl.BlockSpec((rb * count, D), lambda i: (i, 0)),
        out_shape=jax.ShapeDtypeStruct((count * D, D), BF),
        scratch_shapes=[pltpu.VMEM((PAIRS_OF_HEADS, rb * count, LANES), F32)],
        compiler_params=params(),
        cost_estimate=cost(8),
        name="merge_units",
    )(*parts)


def merge_apart_kernel(count, rb, starts, core, *refs):
    parts, mine, other, scr = refs[:-3], refs[-3], refs[-2], refs[-1]
    for t, (at, size) in enumerate(tile_cuts()):
        for j in range(count):
            which, start = starts[j]
            part = parts[which][:, pl.ds(start + at, size)].astype(F32)
            if size < LANES:
                part = jnp.concatenate([part, jnp.zeros((rb, LANES - size), F32)], axis=1)
            scr[t, pl.ds(j, rb, stride=count), :] = part
        for block in range(rb * count // (2 * BLOCK)):
            for out, which in ((mine, core[0]), (other, 1 - core[0])):
                first = pl.multiple_of(2 * BLOCK * block + BLOCK * which, 8)
                out[block, :, pl.ds(at, size)] = scr[t, pl.ds(first, BLOCK), :][:, :size].astype(BF)


def merge_apart(parts, starts):
    rb, count = 272, len(starts)
    blocks = rb * count // (2 * BLOCK)
    out_spec = pl.BlockSpec((blocks, BLOCK, D), lambda i, *_: (i, 0, 0))
    grid_spec = pltpu.PrefetchScalarGridSpec(
        num_scalar_prefetch=1,
        grid=(D // rb,),
        in_specs=[pl.BlockSpec((rb, p.shape[1]), lambda i, *_: (i, 0)) for p in parts],
        out_specs=[out_spec, out_spec],
        scratch_shapes=[pltpu.VMEM((PAIRS_OF_HEADS, rb * count, LANES), F32)],
    )
    return pl.pallas_call(
        functools.partial(merge_apart_kernel, count, rb, starts),
        grid_spec=grid_spec,
        out_shape=[jax.ShapeDtypeStruct((D // rb * blocks, BLOCK, D), BF)] * 2,
        compiler_params=params(),
        cost_estimate=cost(8),
        name="merge_apart",
    )(lax.axis_index("section").reshape(1), *parts)


def adam_kernel(rate, decay, factor, w, m, v, g, w_out, m_out, v_out):
    w_out[...], m_out[...], v_out[...] = adam_update(w[...], m[...], v[...], g[...] * factor[0], rate, decay)


def adam(factor, weight, first, second, grad, rate, decay, block):
    shape = weight.shape
    grid = tuple(size // b for size, b in zip(shape, block))
    spec = pl.BlockSpec(block, lambda i, j, *_: (i, j))
    return pl.pallas_call(
        functools.partial(adam_kernel, rate, decay),
        grid_spec=pltpu.PrefetchScalarGridSpec(num_scalar_prefetch=1, grid=grid, in_specs=[spec] * 4, out_specs=[spec] * 3),
        out_shape=[jax.ShapeDtypeStruct(shape, F32)] * 3,
        compiler_params=params(),
        cost_estimate=cost(weight.size * 9.0e-6),
        name="adam",
    )(factor.reshape(1), weight, first, second, grad)


def chunk_plan(n):
    plan = [(0, "ll", True), (0, "hl", False), (0, "hh", True)]
    for p in range(1, n):
        plan += [(p, "hl", False), (p, "sel", False)]
    return plan


def chunk_offsets(meta, n, hb, p, kind):
    own = meta[0]
    piece = meta[2 + p]
    if kind == "ll":
        return 0, p * 2 * hb, own * hb, piece * hb, True
    if kind == "hl":
        return hb, p * 2 * hb, (2 * n - 1 - own) * hb, piece * hb, False
    if kind == "hh":
        return hb, p * 2 * hb + hb, (2 * n - 1 - own) * hb, (2 * n - 1 - piece) * hb, False
    low = piece < own
    q_off = pl.multiple_of(jnp.where(low, 0, hb), hb)
    k_off = pl.multiple_of(p * 2 * hb + jnp.where(low, 0, hb), hb)
    key_pos = jnp.where(low, piece, 2 * n - 1 - piece) * hb
    return q_off, k_off, None, key_pos, low


def chunk_scores(keys, queries, meta, diagonal, kind, q_pos, k_pos, hb):
    s = dot(keys, queries, NT)
    if diagonal:
        ki = lax.broadcasted_iota(jnp.int32, (hb, hb), 0)
        qi = lax.broadcasted_iota(jnp.int32, (hb, hb), 1)
        keep = (ki <= qi) & (ki + k_pos < meta[1])
        s = jnp.where(keep, s, -1e30)
    elif kind == "sel":
        ki = lax.broadcasted_iota(jnp.int32, (hb, hb), 0)
        s = jnp.where(ki < meta[1] - k_pos, s, -1e30)
    return s


def attend_kernel(n, hb, meta, q_ref, k_ref, v_ref, o_ref, lse_ref, vt_ref):
    keys = 2 * hb * n
    for i in range(keys // hb):
        vt_ref[i] = v_ref[pl.ds(i * hb, hb), :].astype(F32).T.astype(BF)
    lane = lax.broadcasted_iota(jnp.int32, (1, LANES), 1)
    plan = chunk_plan(n)
    outs = []
    for head in range(2):
        own_lanes = (lane // HD) == head
        info, scores = [], []
        tops = [jnp.full((1, hb), -3e38, F32), jnp.full((1, hb), -3e38, F32)]
        for p, kind, diagonal in plan:
            q_off, k_off, q_pos, k_pos, low = chunk_offsets(meta, n, hb, p, kind)
            queries = jnp.where(own_lanes, q_ref[pl.ds(q_off, hb), :], 0)
            s = chunk_scores(k_ref[pl.ds(k_off, hb), :], queries, meta, diagonal, kind, q_pos, k_pos, hb)
            top = jnp.max(s, axis=0, keepdims=True)
            if low is True:
                tops[0] = jnp.maximum(tops[0], top)
            elif low is False:
                tops[1] = jnp.maximum(tops[1], top)
            else:
                tops[0] = jnp.maximum(tops[0], jnp.where(low, top, -3e38))
                tops[1] = jnp.maximum(tops[1], jnp.where(low, -3e38, top))
            info.append((k_off, low))
            scores.append(s)
        sums = [jnp.zeros((1, hb), F32), jnp.zeros((1, hb), F32)]
        accs = [jnp.zeros((HD, hb), F32), jnp.zeros((HD, hb), F32)]
        for (k_off, low), s in zip(info, scores):
            if low is True or low is False:
                top = tops[0] if low else tops[1]
            else:
                top = jnp.where(low, tops[0], tops[1])
            e = jnp.exp(s - top)
            total = jnp.sum(e, axis=0, keepdims=True)
            got = dot(vt_ref[k_off // hb, pl.ds(head * HD, HD), :], e.astype(BF))
            if low is True or low is False:
                sums[1 - low] += total
                accs[1 - low] += got
            else:
                sums[0] += jnp.where(low, total, 0.0)
                sums[1] += jnp.where(low, 0.0, total)
                accs[0] += jnp.where(low, got, 0.0)
                accs[1] += jnp.where(low, 0.0, got)
        outs.append([accs[i] / sums[i] for i in range(2)])
        for i in range(2):
            lse_ref[0, pl.ds(head, 1), pl.ds(i * hb, hb)] = tops[i] + jnp.log(sums[i])
    for i in range(2):
        both = jnp.concatenate([outs[0][i], outs[1][i]], axis=0)
        o_ref[pl.ds(i * hb, hb), :] = both.T.astype(BF)


def attend(meta, q, k, v, n):
    rows = q.shape[0]
    keys = k.shape[0]
    grid_spec = pltpu.PrefetchScalarGridSpec(
        num_scalar_prefetch=1,
        grid=(PAIRS_OF_HEADS,),
        in_specs=[
            pl.BlockSpec((rows, LANES), lambda p, *_: (0, p)),
            pl.BlockSpec((keys, LANES), lambda p, *_: (0, p)),
            pl.BlockSpec((keys, LANES), lambda p, *_: (0, p)),
        ],
        out_specs=[
            pl.BlockSpec((rows, LANES), lambda p, *_: (0, p)),
            pl.BlockSpec((1, 8, rows), lambda p, *_: (p, 0, 0)),
        ],
        scratch_shapes=[pltpu.VMEM((2 * n, LANES, rows // 2), BF)],
    )
    return pl.pallas_call(
        functools.partial(attend_kernel, n, rows // 2),
        grid_spec=grid_spec,
        out_shape=[
            jax.ShapeDtypeStruct((rows, WIDE), BF),
            jax.ShapeDtypeStruct((PAIRS_OF_HEADS, 8, rows), F32),
        ],
        compiler_params=params(),
        cost_estimate=cost(23),
        name="attend",
    )(meta, q, k, v)


def attend_back_kernel(n, hb, meta, q_ref, k_ref, v_ref, o_ref, do_ref, lse_ref, dq_ref, dk_ref, dv_ref, kt_ref, dk_acc, dv_acc):
    keys = 2 * hb * n
    for i in range(keys // hb):
        kt_ref[i] = k_ref[pl.ds(i * hb, hb), :].astype(F32).T.astype(BF)
    dk_acc[...] = jnp.zeros_like(dk_acc)
    dv_acc[...] = jnp.zeros_like(dv_acc)
    lane = lax.broadcasted_iota(jnp.int32, (1, LANES), 1)
    plan = chunk_plan(n)
    prods = []
    for i in range(2):
        part = pl.ds(i * hb, hb)
        prods.append((o_ref[part, :].astype(F32) * do_ref[part, :].astype(F32)).T)
    dqs = []
    for head in range(2):
        own_lanes = (lane // HD) == head
        deltas = [jnp.sum(prods[i][head * HD : (head + 1) * HD, :], axis=0, keepdims=True) for i in range(2)]
        lses = [lse_ref[0, pl.ds(head, 1), pl.ds(i * hb, hb)] for i in range(2)]
        accs = [jnp.zeros((HD, hb), F32), jnp.zeros((HD, hb), F32)]
        for p, kind, diagonal in plan:
            q_off, k_off, q_pos, k_pos, low = chunk_offsets(meta, n, hb, p, kind)
            q_at, k_at = pl.ds(q_off, hb), pl.ds(k_off, hb)
            queries = jnp.where(own_lanes, q_ref[q_at, :], 0)
            d_out = jnp.where(own_lanes, do_ref[q_at, :], 0)
            s = chunk_scores(k_ref[k_at, :], queries, meta, diagonal, kind, q_pos, k_pos, hb)
            if low is True or low is False:
                lse, delta = lses[1 - low], deltas[1 - low]
            else:
                lse, delta = jnp.where(low, lses[0], lses[1]), jnp.where(low, deltas[0], deltas[1])
            prob = jnp.exp(s - lse)
            d_prob = dot(v_ref[k_at, :], d_out, NT)
            d_score = (prob * (d_prob - delta)).astype(BF)
            dv_acc[k_at, :] += dot(prob.astype(BF), d_out)
            dk_acc[k_at, :] += dot(d_score, queries)
            got = dot(kt_ref[k_off // hb, pl.ds(head * HD, HD), :], d_score)
            if low is True or low is False:
                accs[1 - low] += got
            else:
                accs[0] += jnp.where(low, got, 0.0)
                accs[1] += jnp.where(low, 0.0, got)
        dqs.append(accs)
    for i in range(2):
        both = jnp.concatenate([dqs[0][i], dqs[1][i]], axis=0) * 0.125
        dq_ref[pl.ds(i * hb, hb), :] = both.T.astype(BF)
    dk_ref[...] = dk_acc[...].astype(BF)
    dv_ref[...] = dv_acc[...].astype(BF)


def attend_back(meta, q, k, v, o, d_o, lse, n):
    rows = q.shape[0]
    keys = k.shape[0]
    row_spec = pl.BlockSpec((rows, LANES), lambda p, *_: (0, p))
    key_spec = pl.BlockSpec((keys, LANES), lambda p, *_: (0, p))
    grid_spec = pltpu.PrefetchScalarGridSpec(
        num_scalar_prefetch=1,
        grid=(PAIRS_OF_HEADS,),
        in_specs=[row_spec, key_spec, key_spec, row_spec, row_spec, pl.BlockSpec((1, 8, rows), lambda p, *_: (p, 0, 0))],
        out_specs=[row_spec, key_spec, key_spec],
        scratch_shapes=[pltpu.VMEM((2 * n, LANES, rows // 2), BF), pltpu.VMEM((keys, LANES), F32), pltpu.VMEM((keys, LANES), F32)],
    )
    return pl.pallas_call(
        functools.partial(attend_back_kernel, n, rows // 2),
        grid_spec=grid_spec,
        out_shape=[
            jax.ShapeDtypeStruct((rows, WIDE), BF),
            jax.ShapeDtypeStruct((keys, WIDE), BF),
            jax.ShapeDtypeStruct((keys, WIDE), BF),
        ],
        compiler_params=params(),
        cost_estimate=cost(46),
        name="attend_back",
    )(meta, q, k, v, o, d_o, lse)


def by_rows(x):
    return with_layout_constraint(x, Layout(major_to_minor=tuple(range(x.ndim))))


def layer_norm(values, gain_vec, bias_vec):
    row_mean = jnp.mean(values, -1, keepdims=True)
    centred = values - row_mean
    variance = jnp.mean(centred * centred, -1, keepdims=True)
    return centred * lax.rsqrt(variance + 1e-05) * gain_vec + bias_vec


def gelu_tanh(values):
    return 0.5 * values * (1.0 + jnp.tanh(0.7978845608 * (values + 0.044715 * values * values * values)))


def softplus(values):
    return jnp.maximum(values, 0.0) + jnp.log1p(jnp.exp(-jnp.abs(values)))


def adam_update(weight, first, second, grad, rate, decay):
    first = 0.9 * first + 0.1 * grad
    second = 0.95 * second + 0.05 * grad * grad
    first_hat = first / (1.0 - 0.9**STEP)
    second_hat = second / (1.0 - 0.95**STEP)
    weight = weight - rate * (first_hat / (jnp.sqrt(second_hat) + 1e-08) + decay * weight)
    return (weight, first, second)


def pieces_by_ctx(x, half):
    got = [x]
    bit = 1
    while bit < half:
        got += [swap(y, "ctx", bit) for y in got]
        bit *= 2
    return got


def pieces_by_section(got):
    own = jnp.concatenate(got)
    return jnp.concatenate([own, swap(own, "section", 1)])


def sum_pieces(x, half):
    rows = x.shape[0] // half
    bit = half // 2
    while bit >= 1:
        keep, send = x[: bit * rows], x[bit * rows : 2 * bit * rows]
        x = keep + swap(send.astype(BF), "ctx", bit).astype(F32)
        bit //= 2
    return x


def layer_weights(units):
    return split_units(units, 0, 3, WIDE), units[U_OUT:U_UP], join_units(units, U_UP, N_UP), units[U_DOWN:]


def layer_forward(values, hidden1, all_hidden1, meta, n, weights, vecs):
    w_qkv, w_out, w_up, w_down = weights
    keys = dot(all_hidden1, w_qkv[1]).astype(BF)
    vals = dot(all_hidden1, w_qkv[2]).astype(BF)
    queries = dot(hidden1, w_qkv[0]).astype(BF) * jnp.asarray(0.125, BF)
    attended, lse = attend(meta, queries, keys, vals, n)
    middle = values + dot(attended[:, :D], w_out)
    hidden2 = layer_norm(middle, vecs[2], vecs[3]).astype(BF)
    ups = dot(hidden2, w_up)
    gated = gelu_tanh(ups).astype(BF)
    result = middle + dot(gated, w_down)
    return result, (values, all_hidden1, queries, keys, vals, attended, lse, middle, hidden2, ups, gated)


def layer_backward(saved, grad_out, meta, n, weights, vecs, factors, fast):
    values, all_hidden1, queries, keys, vals, attended, lse, middle, hidden2, ups, gated = saved
    w_qkv, w_out, w_up, w_down = weights
    grad_ffn = grad_out.astype(BF)
    grad_down = by_rows(dot(gated, grad_ffn, TN).astype(BF))
    if fast:
        mine_down, other_down = core_blocks(grad_down)
        both = beside(factors)
        grad_ffn, other_down, both = lax.optimization_barrier((grad_ffn, other_down, both))
        came_down = swap(other_down, "section", 1)
    _, back = jax.vjp(gelu_tanh, ups)
    grad_ups = by_rows(back(dot(grad_ffn, w_down, NT))[0].astype(BF))
    grad_up, up_starts = dot(hidden2, grad_ups, TN).astype(BF), [(0, j * D) for j in range(N_UP)]
    if fast:
        mine_up, other_up = merge_apart([grad_up], up_starts)
        four = gather_step(both[None], "shard", 1)
        grad_ups, other_up, four = lax.optimization_barrier((grad_ups, other_up, four))
        came_up = swap(other_up, "section", 1)
    grad_hidden2 = dot(grad_ups, w_up, NT)
    _, norm_back2 = jax.vjp(layer_norm, middle, vecs[2], vecs[3])
    grad_norm2, grad_gain2, grad_bias2 = norm_back2(grad_hidden2)
    grad_middle = grad_out + grad_norm2
    grad_branch = grad_middle.astype(BF)
    grad_outw = dot(attended[:, :D], grad_branch, TN).astype(BF)
    grad_att = dot(grad_branch, jnp.pad(w_out, ((0, WIDE - D), (0, 0))), NT).astype(BF)
    if fast:
        rest = jnp.concatenate([fold_cores(grad_outw), add_low(mine_up, came_up), add_low(mine_down, came_down)])
        grad_att, rest = lax.optimization_barrier((grad_att, rest))
        came = rest_first(rest)
    grad_q, part_k, part_v = attend_back(meta, queries, keys, vals, attended, grad_att, lse, n)
    rows, near = grad_q.shape[0], part_k.shape[0] // 2
    if fast:
        grad_q, four = lax.optimization_barrier((grad_q, four))
        factors = gather_step(four, "shard", 2)
    def to_hidden1(at):
        return dot(part_k[at], w_qkv[1], NT) + dot(part_v[at], w_qkv[2], NT)

    far = to_hidden1(slice(near, None)).astype(BF)
    grad_q, part_k, part_v, far = lax.optimization_barrier((grad_q, part_k, part_v, far))
    if fast:
        far, factors, *came = lax.optimization_barrier((far, factors, *came))
    close = to_hidden1(slice(0, near)) + swap(far, "section", 1).astype(F32)
    if fast:
        close, *came = lax.optimization_barrier((close, *came))
    grad_hidden1 = sum_pieces(close, n // 2)
    grad_hidden1 = grad_hidden1 + dot(grad_q, w_qkv[0], NT)
    _, norm_back1 = jax.vjp(layer_norm, values, vecs[0], vecs[1])
    grad_norm1, grad_gain1, grad_bias1 = norm_back1(grad_hidden1)
    grad_input = (grad_middle + grad_norm1).astype(BF)
    grad_input, grad_q, part_k, part_v = lax.optimization_barrier((grad_input, grad_q, part_k, part_v))
    grad_qk = [dot(h, g, TN).astype(BF) for h, g in ((all_hidden1[:rows], grad_q), (all_hidden1, part_k))]

    def grad_qkvw(part_v):
        parts, starts = [*grad_qk, dot(all_hidden1, part_v, TN).astype(BF)], [(j, 0) for j in range(3)]
        if not fast:
            return merge_units(parts, starts)
        mine, other = merge_apart(parts, starts)
        return add_low(mine, swap(other, "section", 1))

    if fast:
        rest = rest_second(rest, came)
        summed = (rest, along_shard_first(rest)), (part_v, grad_qkvw)
    else:
        summed = jnp.concatenate([grad_qkvw(part_v), grad_outw, merge_units([grad_up], up_starts), grad_down])
        factors = gather_axis(beside(factors), "shard")
    return grad_input, summed, [grad_gain1, grad_bias1, grad_gain2, grad_bias2], factors


def head_mask():
    head = lax.broadcasted_iota(jnp.int32, (HEADS, D), 0)
    return lax.broadcasted_iota(jnp.int32, (HEADS, D), 1) // HD == head


def last_forward(values, positions, length, half, weights, vecs):
    (w_q, w_k, w_v), w_out, w_up, w_down = weights
    heads = head_mask()
    hidden1 = layer_norm(values, vecs[0], vecs[1]).astype(BF)
    mine = (positions == length - 1)[:, None]
    row = jnp.sum(jnp.where(mine, values, 0.0), axis=0, keepdims=True)
    row = group_reduce(row, jnp.add, half)
    row_h1 = layer_norm(row, vecs[0], vecs[1]).astype(BF)
    query = dot(row_h1, w_q).astype(BF)
    wq = dot(jnp.where(heads, query, 0), w_k, NT) * 0.125
    scores = dot2(wq, hidden1, NT)
    scores = jnp.where((positions < length)[None, :], scores, -1e30)
    top = jnp.max(scores, axis=1, keepdims=True)
    expo = jnp.exp(scores - top)
    total = jnp.sum(expo, axis=1, keepdims=True)
    mixed = dot(expo.astype(BF), hidden1)
    wide = lambda x: jnp.broadcast_to(x, (HEADS, HD))

    def merge(x, y):
        high = jnp.maximum(x[:, D : D + 1], y[:, D : D + 1])
        x = x * jnp.exp(x[:, D : D + 1] - high)
        y = y * jnp.exp(y[:, D : D + 1] - high)
        return jnp.concatenate([x[:, :D] + y[:, :D], wide(high), x[:, D + HD :] + y[:, D + HD :]], axis=1)

    merged = group_reduce(jnp.concatenate([mixed, wide(top), wide(total)], axis=1), merge, half)
    top, total = merged[:, D : D + 1], merged[:, D + HD : D + HD + 1]
    mixed = merged[:, :D] / total
    probs = jnp.exp(scores - top) / total
    att = jnp.sum(jnp.where(heads, dot2(mixed, w_v), 0.0), axis=0, keepdims=True)
    middle = row + dot(att.astype(BF), w_out)
    hidden2 = layer_norm(middle, vecs[2], vecs[3]).astype(BF)
    ups = dot(hidden2, w_up)
    gated = gelu_tanh(ups).astype(BF)
    result = middle + dot(gated, w_down)
    return result, (values, hidden1, mine, row_h1, query, wq, probs, mixed, att, middle, hidden2, ups, gated)


def last_backward(saved, grad_out, half, weights, vecs):
    values, hidden1, mine, row_h1, query, wq, probs, mixed, att, middle, hidden2, ups, gated = saved
    (w_q, w_k, w_v), w_out, w_up, w_down = weights
    heads = head_mask()
    grad_ffn = grad_out.astype(BF)
    _, back = jax.vjp(gelu_tanh, ups)
    grad_ups = back(dot(grad_ffn, w_down, NT))[0].astype(BF)
    grad_hidden2 = dot(grad_ups, w_up, NT)
    _, norm_back2 = jax.vjp(layer_norm, middle, vecs[2], vecs[3])
    grad_norm2, grad_gain2, grad_bias2 = norm_back2(grad_hidden2)
    grad_middle = grad_out + grad_norm2
    grad_branch = grad_middle.astype(BF)
    grad_att = dot(grad_branch, w_out, NT).astype(BF)
    att_heads = jnp.where(heads, grad_att, 0)
    wv = dot(att_heads, w_v, NT)
    grad_prob = dot2(wv, hidden1, NT)
    delta = jnp.sum(att_heads.astype(F32) * att, axis=1, keepdims=True)
    grad_score = (probs * (grad_prob - delta)).astype(BF)
    summed = group_reduce(dot(grad_score, hidden1), jnp.add, half)
    grad_query = (jnp.sum(jnp.where(heads, dot2(summed, w_k), 0.0), axis=0, keepdims=True) * 0.125).astype(BF)
    low_probs = probs.astype(BF)
    grad_hidden1 = dot(
        jnp.concatenate([grad_score, grad_score, low_probs, low_probs]), jnp.concatenate([split2(wq), split2(wv)]), TN
    )
    grad_hidden1 = grad_hidden1 + jnp.where(mine, dot(grad_query, w_q, NT), 0.0)
    _, norm_back1 = jax.vjp(layer_norm, values, vecs[0], vecs[1])
    grad_norm1, grad_gain1, grad_bias1 = norm_back1(grad_hidden1)
    grad_input = grad_norm1 + jnp.where(mine, grad_middle, 0.0)
    query8 = query * jnp.asarray(0.125, BF)
    factors = [row_h1, grad_query, query8, grad_att, att, grad_branch, hidden2, grad_ffn]
    factors += [grad_ups.reshape(N_UP, D), gated.reshape(N_UP, D), summed, mixed]
    factors = jnp.concatenate([f.astype(BF) for f in factors])
    return grad_input, factors, [grad_gain1, grad_bias1], [grad_gain2, grad_bias2]


def last_gradient(data, chunk_at, n_chunks, size):
    n_seq = data.shape[0]
    heads = head_mask()
    row_h1, grad_query, query8, grad_att, att, grad_branch, hidden2, grad_ffn = [data[:, i] for i in range(8)]
    at = 8
    grad_ups, gated = data[:, at : at + N_UP], data[:, at + N_UP : at + 2 * N_UP]
    at += 2 * N_UP
    summed, mixed = data[:, at : at + HEADS], data[:, at + HEADS : at + 2 * HEADS]

    def by_unit(parts):
        count, width = len(parts), sum(p.shape[0] for p in parts)
        slot = jnp.concatenate([jnp.full((p.shape[0],), j, jnp.int32) for j, p in enumerate(parts)])
        both = jnp.concatenate(parts).T
        spread = jnp.where(slot[None, None, :] == jnp.arange(count)[None, :, None], both[:, None, :], 0)
        return spread.reshape(count * D, width)

    def per_head(x):
        return jnp.where(heads[None], x[:, None, :], 0).reshape(n_seq * HEADS, D)

    left = by_unit([row_h1, summed.reshape(-1, D), mixed.reshape(-1, D)])
    right = jnp.concatenate([grad_query, per_head(query8), per_head(grad_att)])
    first = chunk_at * size
    qkv = dot(lax.dynamic_slice_in_dim(left, jnp.minimum(first, U_OUT - size), size, 0), right)
    lefts = [att.T, by_unit([hidden2] * N_UP), gated.reshape(n_seq, FF).T]
    rights = [grad_branch, grad_ups.transpose(1, 0, 2).reshape(-1, D), grad_ffn]
    width = sum(x.shape[1] for x in lefts)
    columns, before = [], 0
    for x in lefts:
        columns.append(jnp.pad(x, ((0, 0), (before, width - before - x.shape[1]))))
        before += x.shape[1]
    left = jnp.concatenate(columns)
    rest = dot(lax.dynamic_slice_in_dim(left, jnp.maximum(first - U_OUT, 0), size, 0), jnp.concatenate(rights))
    return jnp.where(first < U_OUT, qkv, rest)


def shards(
    tokens,
    lengths,
    end_ids,
    pairs,
    layer_master,
    layer_first,
    layer_second,
    table_master,
    table_first,
    table_second,
    vector_master,
    vector_first,
    vector_second,
):
    rows = tokens.shape[1]
    s_at = lax.axis_index("section")
    c_at = lax.axis_index("ctx")
    z_at = lax.axis_index("shard")
    n_section = lax.axis_size("section")
    n = lax.axis_size("ctx")
    n_shard = lax.axis_size("shard")
    half = n // 2
    hb = rows // 2
    n_dest = n_section * n
    n_seq = MICRO * n_shard
    columns, entries = table_master.shape
    is_first = s_at == 0
    seq_in = c_at // half
    seq_at = z_at * MICRO + seq_in
    group = (c_at % half) * 2 + s_at

    fast = small_block()
    chunk = chunk_rows(layer_master) if fast else layer_master.reshape(-1, D).astype(BF)
    size = chunk.shape[0]
    cut = size // 2
    if fast:
        wide = cut + OVERLAP // 2
        got = swap(jnp.where(is_first, chunk[size - wide :], chunk[:wide]), "section", 1)
        piece0 = jnp.where(is_first, chunk[:wide], got)
        piece1 = jnp.where(is_first, got[:cut], chunk[cut:])
    else:
        got = swap(jnp.where(is_first, chunk[cut:], chunk[:cut]), "section", 1)
        piece0 = jnp.where(is_first, chunk[:cut], got)
        piece1 = jnp.where(is_first, got, chunk[cut:])
    order = ("ctx", "shard", "section")

    own_ids = jnp.concatenate([tokens, end_ids[:, None]], axis=1)
    all_ids = gather_axis(gather_axis(own_ids, "ctx"), "shard")
    natural = all_ids[..., :rows].transpose(0, 2, 1, 3).reshape(n_shard, MICRO, 2 * n, hb)
    zig = jnp.stack([natural[:, :, :n], natural[:, :, n:][:, :, ::-1]], axis=3)
    zig = zig.reshape(n_shard, MICRO, half, 2, rows).transpose(0, 3, 1, 2, 4)
    end_all = all_ids[:, 0, :, rows].reshape(n_seq)
    n_blocks = n_shard * n_dest

    def held(ids):
        ids = ids - z_at * entries
        return jnp.where((ids >= 0) & (ids < entries), ids, entries)

    listed, counts = owned_rows(held(zig.reshape(n_blocks, rows)), entries)
    end_held = held(end_all)
    if fast:
        first = first_moves(piece0)
        listed, piece0, *first = lax.optimization_barrier((listed, piece0, *first))
        second = second_moves(piece0, first[0], first[1])
    else:
        units0 = lax.all_gather(piece0, order, axis=0, tiled=True)
    dest = jnp.arange(n_blocks, dtype=jnp.int32) % n_dest
    groups = (dest % n % half) * 2 + dest // n
    assert VOCAB >= (n_shard - 1) * entries
    meta_emb = jnp.concatenate(
        [
            jnp.stack([(z_at == n_shard - 1).astype(jnp.int32), jnp.int32(n), jnp.int32(VOCAB - (n_shard - 1) * entries), jnp.int32(0)]),
            groups,
        ]
    )
    picked, end_part = lookup(listed, counts, end_held, meta_emb, table_master, n_blocks, rows)
    if fast:
        picked, *second = lax.optimization_barrier((picked, *second))
        halves = gather_half(piece0, first, second)
    column_at = (s_at * n + c_at) * columns
    end_rows = sum_all(lax.dynamic_update_slice(jnp.zeros((n_seq, D), F32), end_part, (0, column_at)))
    summed = lax.psum_scatter(picked.reshape(n_shard, n_dest, columns, rows), "shard", scatter_dimension=0, tiled=True)
    if fast:
        summed, piece1, end_rows, *halves = lax.optimization_barrier((summed, piece1, end_rows, *halves))
        parts = [part for mine in halves for part in (mine, swap(mine, "section", 1))]
    routed = lax.all_to_all(summed.reshape(n_dest, columns, rows), ("section", "ctx"), split_axis=0, concat_axis=0, tiled=True)
    embedded = routed.reshape(D, rows).T.astype(F32)
    end_row = lax.dynamic_slice_in_dim(end_rows, seq_at, 1, 0)
    units1 = lax.all_gather(piece1, order, axis=0, tiled=True)

    length = lax.dynamic_slice_in_dim(lengths, seq_in, 1, 0)[0]
    others = [group ^ (2 * cb + sb) for sb in range(2) for cb in range(half)]
    meta = jnp.stack([group, length] + others).astype(jnp.int32)
    span = jnp.arange(hb, dtype=jnp.int32)
    positions = jnp.concatenate([group * hb + span, (2 * n - 1 - group) * hb + span])

    vecs0, vecs1 = vector_master[0:4], vector_master[4:8]
    hidden1 = layer_norm(embedded, vecs0[0], vecs0[1]).astype(BF)
    if fast:
        hidden1, *parts = lax.optimization_barrier((hidden1, *parts))
        units0 = place_units(parts)
    weights0 = layer_weights(units0)
    others = pieces_by_ctx(hidden1, half)[1:]
    *others, w_qkv0, w_up0 = lax.optimization_barrier((*others, weights0[0], weights0[2]))
    weights0 = (w_qkv0, weights0[1], w_up0, weights0[3])
    out0, saved0 = layer_forward(embedded, hidden1, pieces_by_section([hidden1, *others]), meta, n, weights0, vecs0)
    x1 = out0.astype(BF).astype(F32)
    x1, units1 = lax.optimization_barrier((x1, units1))
    w_qkv1 = split_units(units1, 0, 3)
    weights1 = ((w_qkv1[0], w_qkv1[1], w_qkv1[2]), units1[U_OUT:U_UP], join_units(units1, U_UP, N_UP), units1[U_DOWN:])
    final, saved1 = last_forward(x1, positions, length, half, weights1, vecs1)

    def score_terms(final_row, end_vals, gain_vec, bias_vec, head_vec):
        normed = layer_norm(final_row, gain_vec, bias_vec)
        return jnp.sum(normed * (end_vals + head_vec)) * D ** (-0.5)

    counted = group == 0
    score, score_back = jax.vjp(score_terms, final, end_row, vector_master[8], vector_master[9], vector_master[10])
    scores = sum_small(jnp.where((jnp.arange(n_seq) == seq_at) & counted, score, 0.0)[None])[0]

    def pair_loss(score_vals):
        return jnp.sum(softplus(score_vals[pairs[:, 1]] - score_vals[pairs[:, 0]]))

    loss_sum, loss_back = jax.vjp(pair_loss, scores)
    grad_scores = loss_back(jnp.ones_like(loss_sum))[0]
    grad_own = lax.dynamic_slice_in_dim(grad_scores, seq_at, 1, 0)[0]
    grad_final, grad_end, *vec_final = score_back(grad_own)

    grad_x1, factors, vec1, vec1_row = last_backward(saved1, grad_final, half, weights1, vecs1)
    factors = jnp.concatenate([factors, grad_end.astype(BF)])
    grad_x1 = grad_x1.astype(BF).astype(F32)
    grad_x0, grads0, vec0, every_factor = layer_backward(saved0, grad_x1, meta, n, weights0, vecs0, factors, fast)
    every_factor = every_factor.reshape(n_seq, -1, D)

    by_owner = grad_x0.T.reshape(n_dest, columns, rows)
    back = lax.all_to_all(by_owner, ("section", "ctx"), split_axis=0, concat_axis=0, tiled=True)
    if fast:
        (rest, passing), (part_v, finish_qkv) = grads0
        every = [back] + [shift(back, "shard", d) for d in (1, 3)]
        every[1], every[2], every_factor, rest, passing = lax.optimization_barrier(
            (every[1], every[2], every_factor, rest, passing)
        )
        every.append(shift(every[1], "shard", 1))
        rest_terms = along_shard(rest, passing)
        qkv_part = qkv_second(*qkv_first(finish_qkv(part_v)))
        every[3], qkv_part = lax.optimization_barrier((every[3], qkv_part))
        every = jnp.concatenate(every)
        near_order = (z_at + 4 - jnp.array((0, 1, 3, 2), jnp.int32)) % 4
        listed = listed.reshape(n_shard, -1)[near_order].reshape(-1)
        counts = counts.reshape(n_shard, -1)[near_order].reshape(-1)
    else:
        every = lax.all_gather(back, "shard", axis=0, tiled=True)
    end_grads = lax.dynamic_slice(every_factor[:, -1].astype(F32), (0, column_at), (n_seq, columns))
    table_grad = scatter(listed, counts, end_held, meta_emb, every, end_grads, entries)
    once = [jnp.where(counted, v, 0.0) for v in vec1_row + vec_final]
    vector_part = jnp.stack(vec0 + vec1 + once)

    own1 = last_gradient(every_factor, c_at * n_shard + z_at, n * n_shard, size)
    squares = jnp.sum(table_grad * table_grad) + jnp.where(is_first, 0.0, jnp.sum(own1 * own1))
    if fast:
        qkv_terms = along_shard(qkv_part, along_shard_first(qkv_part))
        terms = [*rest_terms, *qkv_terms]
        table_grad, own1, squares, vector_part, *terms = lax.optimization_barrier(
            (table_grad, own1, squares, vector_part, *terms)
        )
        rest_terms, qkv_terms = terms[:3], terms[3:]
        mine = sum(t.astype(F32) for t in rest_terms)
        quarter = sum(t.astype(F32) for t in qkv_terms)
        squares = squares + jnp.sum(quarter * quarter) + jnp.where(c_at == 0, 0.0, jnp.sum(mine * mine))
        squares, quarter = lax.optimization_barrier((squares, quarter))
        collected = collect_qkv(quarter)[: mine.shape[0] * BLOCK]
        mine = jnp.where(c_at == 0, collected.reshape(mine.shape), mine)
    else:
        mine = lax.psum_scatter(grads0, order, scatter_dimension=0, tiled=True).astype(F32)
        squares = squares + jnp.sum(mine * mine)
    other = swap(mine.astype(BF), "section", 1).astype(F32)
    own0 = jnp.stack([mine, other], axis=1).reshape(size, D) if fast else jnp.concatenate([mine, other])
    layer_grad = jnp.where(is_first, own0, own1).reshape(-1, LANES)

    n_vec = vector_part.shape[0]
    totals = sum_small(jnp.concatenate([vector_part, jnp.full((1, D), squares)]))
    vector_grad = totals[:n_vec]
    grad_norm = jnp.sqrt(totals[n_vec, 0] + jnp.sum(vector_grad * vector_grad))
    layer_grad, grad_norm = lax.optimization_barrier((layer_grad, grad_norm))
    factor = CLIP_LIMIT / jnp.maximum(grad_norm, CLIP_LIMIT)
    flat = [x.reshape(-1, LANES) for x in (layer_master, layer_first, layer_second)]
    flat_rows = flat[0].shape[0]
    block_rows = max(b for b in range(1, 2313) if flat_rows % b == 0 and (b % 8 == 0 or b == flat_rows))
    table_cols = max(b for b in range(LANES, 1537, LANES) if entries % b == 0)
    layer_new = adam(factor, *flat, layer_grad, 0.4, 0.1, (block_rows, LANES))
    layer_new = [x.reshape(layer_master.shape) for x in layer_new]
    table_new = adam(factor, table_master, table_first, table_second, table_grad, 0.5, 0.1, (columns, table_cols))
    vector_new = adam_update(vector_master, vector_first, vector_second, vector_grad * factor, 0.7, 0.0)
    return (loss_sum, grad_norm, *layer_new, *table_new, *vector_new)


def solution(mesh):
    in_specs = (
        P("shard", "ctx"),
        P("shard"),
        P("shard"),
        P(),
        P("section", ("ctx", "shard")),
        P("section", ("ctx", "shard")),
        P("section", ("ctx", "shard")),
        P(("section", "ctx"), "shard"),
        P(("section", "ctx"), "shard"),
        P(("section", "ctx"), "shard"),
        P(),
        P(),
        P(),
    )
    out_specs = (
        P(),
        P(),
        P("section", ("ctx", "shard")),
        P("section", ("ctx", "shard")),
        P("section", ("ctx", "shard")),
        P(("section", "ctx"), "shard"),
        P(("section", "ctx"), "shard"),
        P(("section", "ctx"), "shard"),
        P(),
        P(),
        P(),
    )
    return jax.shard_map(shards, mesh=mesh, in_specs=in_specs, out_specs=out_specs, check_vma=False)
```

```python
import functools

import jax
import jax.numpy as jnp
from jax import lax
from jax.experimental import pallas as pl
from jax.experimental.layout import Layout, with_layout_constraint
from jax.experimental.pallas import tpu as pltpu
from jax.sharding import PartitionSpec as P

D = 1088
HEADS = 17
HD = 64
FF = 4352
VOCAB = 51200
MICRO = 2
STEP = 10
CLIP_LIMIT = 0.02
ALL = ("section", "ctx", "shard")

LANES = 128
PAIRS_OF_HEADS = (HEADS + 1) // 2
WIDE = PAIRS_OF_HEADS * LANES
N_UP = FF // D
U_OUT = 3 * D
U_UP = U_OUT + D
U_DOWN = U_UP + FF
UNITS = U_DOWN + FF

BF = jnp.bfloat16
F32 = jnp.float32
VMEM_BIG = 56 * 1024 * 1024


def params(limit=VMEM_BIG):
    return pltpu.CompilerParams(vmem_limit_bytes=limit)


def cost(microseconds):
    return pl.CostEstimate(flops=0, bytes_accessed=int(microseconds * 3.0e6), transcendentals=0)


def dot(a, b, contract=((1,), (0,))):
    return lax.dot_general(a, b, (contract, ((), ())), preferred_element_type=F32)


NT = ((1,), (1,))
TN = ((0,), (0,))


def split2(x):
    top = lax.reduce_precision(x, 8, 7)
    return jnp.concatenate([top, x - top]).astype(BF)


def dot2(x, w, contract=((1,), (0,))):
    y = dot(split2(x), w, contract)
    return y[: x.shape[0]] + y[x.shape[0] :]


def swap(x, axis, bit):
    size = lax.axis_size(axis)
    return lax.ppermute(x, axis, [(i, i ^ bit) for i in range(size)])


def gather_step(x, axis, bit):
    other = swap(x, axis, bit)
    lower = (lax.axis_index(axis) & bit) == 0
    return jnp.where(lower, jnp.concatenate([x, other]), jnp.concatenate([other, x]))


def gather_axis(x, axis):
    x = x[None]
    bit = 1
    while bit < lax.axis_size(axis):
        x = gather_step(x, axis, bit)
        bit *= 2
    return x


def beside(x):
    return gather_step(x[None], "ctx", lax.axis_size("ctx") // 2)


def sum_axis(x, axis, first=1, last=None):
    size = lax.axis_size(axis) if last is None else last
    bit = first
    while bit < size:
        x = x + swap(x, axis, bit)
        bit *= 2
    return x


def group_reduce(x, combine, half):
    def step(x, axis, bit):
        other = swap(x, axis, bit)
        lower = (lax.axis_index(axis) & bit) == 0
        return combine(jnp.where(lower, x, other), jnp.where(lower, other, x))

    x = step(x, "section", 1)
    bit = 1
    while bit < half:
        x = step(x, "ctx", bit)
        bit *= 2
    return x


def sum_all(x):
    return sum_axis(sum_axis(sum_axis(x, "section"), "ctx"), "shard")


def sum_direct(x, axis):
    if lax.axis_size(axis) != 4:
        return sum_axis(x, axis)
    one, two, three = [lax.ppermute(x, axis, [(i, (i + d) % 4) for i in range(4)]) for d in (1, 2, 3)]
    return (x + two) + (one + three)


def sum_small(x):
    return sum_direct(sum_direct(sum_direct(x, "section"), "ctx"), "shard")


def rows_kernel(pairs, x, out, scr):
    lane = lax.broadcasted_iota(jnp.int32, (1, LANES), 1)
    step = 2 * D // LANES
    even, odd = pl.ds(0, pairs, stride=2), pl.ds(1, pairs, stride=2)
    flat_row = lambda t: x[pl.ds(t, pairs, stride=step), :]
    for t in range(PAIRS_OF_HEADS):
        scr[t, even, :] = flat_row(t)
    before = pltpu.roll(flat_row(step // 2), HD, 1)
    for t in range(PAIRS_OF_HEADS - 1):
        after = pltpu.roll(flat_row(step // 2 + 1 + t), HD, 1)
        scr[t, odd, :] = jnp.where(lane < HD, before, after)
        before = after
    scr[PAIRS_OF_HEADS - 1, odd, :] = before
    for t, (at, size) in enumerate(tile_cuts()):
        out[:, pl.ds(at, size)] = scr[t][:, :size].astype(BF)


def chunk_rows(flat):
    units = flat.size // D
    return pl.pallas_call(
        functools.partial(rows_kernel, units // 2),
        out_shape=jax.ShapeDtypeStruct((units, D), BF),
        scratch_shapes=[pltpu.VMEM((PAIRS_OF_HEADS, units, LANES), F32)],
        compiler_params=params(),
        cost_estimate=cost(6),
        name="chunk_rows",
    )(flat.reshape(-1, LANES))


def small_block():
    return lax.axis_size("ctx") == 4 and lax.axis_size("shard") == 4 and lax.axis_size("section") == 2


def shift(x, axis, by):
    size = lax.axis_size(axis)
    return lax.ppermute(x, axis, [(i, (i + by) % size) for i in range(size)])


ARRIVALS = ((0,), (1, 3), (2,))
OVERLAP = 16


def place_kernel(rows, at, *refs):
    ins, out, held, sems_in, sems_out = refs[: 2 * len(ARRIVALS)], refs[-4], refs[-3], refs[-2], refs[-1]
    s, c, z = at[0], at[1], at[2]
    short = rows - OVERLAP
    pieces = []
    for g, distances in enumerate(ARRIVALS):
        for other in range(2):
            for e in range(4):
                for i, d in enumerate(distances):
                    chunk = (c ^ e) * 4 + lax.rem(z + 4 - d, 4)
                    pieces.append((ins[2 * g + other].at[e, i], chunk, other))

    def arrive(k):
        return pltpu.make_async_copy(pieces[k][0], held.at[k], sems_in.at[k])

    def leave(k, act):
        _, chunk, other = pieces[k]

        @pl.when(s == other)
        def _():
            act(pltpu.make_async_copy(held.at[k], out.at[chunk, pl.ds(0, rows)], sems_out.at[k]))

        @pl.when(s != other)
        def _():
            act(pltpu.make_async_copy(held.at[k, pl.ds(OVERLAP, short)], out.at[chunk, pl.ds(rows, short)], sems_out.at[k]))

    for k in range(len(pieces)):
        arrive(k).start()
    for k in range(len(pieces)):
        arrive(k).wait()
        leave(k, lambda copy: copy.start())
    for k in range(len(pieces)):
        leave(k, lambda copy: copy.wait())


def by_links(own):
    return swap(own, "ctx", 1), swap(own, "ctx", 2)


def first_moves(piece):
    return shift(piece, "shard", 1), shift(piece, "shard", 3), *by_links(piece[None])


def second_moves(piece, near, far):
    return shift(piece, "shard", 2), *by_links(jnp.stack([near, far]))


def corner_of(by_x, by_y):
    cut = by_x.shape[1] // 2
    return jnp.concatenate([swap(by_x[:, :cut], "ctx", 2), swap(by_y[:, cut:], "ctx", 1)], axis=1)


def gather_half(piece, first, second):
    near, far, *own_links = first
    opposite, *near_links = second
    arrived = {0: piece, 1: near, 3: far, 2: opposite}
    parts = []
    for distances, links in zip(ARRIVALS, (own_links, near_links, None)):
        own = jnp.stack([arrived[d] for d in distances])
        by_x, by_y = by_links(own) if links is None else links
        corner = corner_of(by_x, by_y)
        parts.append(jnp.stack([own, by_x, by_y, corner]))
    return parts


def place_units(parts):
    rows = parts[0].shape[2]
    at = jnp.stack([lax.axis_index(a) for a in ALL]).astype(jnp.int32)
    grid_spec = pltpu.PrefetchScalarGridSpec(
        num_scalar_prefetch=1,
        grid=(1,),
        in_specs=[pl.BlockSpec(memory_space=pl.ANY)] * len(parts),
        out_specs=pl.BlockSpec(memory_space=pl.ANY),
        scratch_shapes=[pltpu.VMEM((32, rows, D), BF), pltpu.SemaphoreType.DMA((32,)), pltpu.SemaphoreType.DMA((32,))],
    )
    whole = pl.pallas_call(
        functools.partial(place_kernel, rows),
        grid_spec=grid_spec,
        out_shape=jax.ShapeDtypeStruct((16, 2 * rows - OVERLAP, D), BF),
        compiler_params=params(),
        cost_estimate=cost(16),
        name="place",
    )(at, *parts)
    return whole.reshape(UNITS, D)


def add_low(x, y):
    return (x.astype(F32) + y.astype(F32)).astype(BF)


BLOCK = 136
QUARTER = 104


def core_blocks(region):
    s = lax.axis_index("section")
    blocks = region.reshape(-1, 2, BLOCK, D)
    pick = lambda i: lax.dynamic_index_in_dim(blocks, i, 1, keepdims=False)
    return pick(s), pick(1 - s)


def fold_cores(region):
    mine, other = core_blocks(region)
    return add_low(mine, swap(other, "section", 1))


def one_way(x, bit, sends):
    return lax.ppermute(x, "ctx", [(i, i ^ bit) for i in range(4) if sends(i)])


def three_first(one, two, both, p):
    has_p = (lax.axis_index("ctx") & p) != 0
    return swap(jnp.where(has_p, two, one), "ctx", p), one_way(both, p, lambda i: not i & p)


def three_second(one, two, both, came, came_both, p, q):
    c = lax.axis_index("ctx")
    has_p, has_q = (c & p) != 0, (c & q) != 0
    single = add_low(jnp.where(has_p, one, two), came)
    both = add_low(both, came_both)
    sent = jnp.where(has_p & ~has_q, both, single)
    came = one_way(sent, q, lambda i: not i & q or i & p)
    return add_low(jnp.where(has_p & has_q, both, single), came)


def rest_first(rest):
    x = rest.reshape(3, 4, -1, BLOCK, D)
    return *three_first(x[0, :2], x[1, :2], x[2, :2], 1), *three_first(x[1, 2:], x[0, 2:], x[2, 2:], 2)


def rest_second(rest, came):
    x = rest.reshape(3, 4, -1, BLOCK, D)
    first = three_second(x[0, :2], x[1, :2], x[2, :2], came[0], came[1], 1, 2)
    second = three_second(x[1, 2:], x[0, 2:], x[2, 2:], came[2], came[3], 2, 1)
    return jnp.concatenate([first, second])


def fold_half(v, axis, bit):
    mine = (lax.axis_index("ctx") // bit) & 1
    pick = lambda i: lax.dynamic_index_in_dim(v, i, axis, keepdims=True)
    return add_low(pick(mine), swap(pick(1 - mine), "ctx", bit))


def qkv_first(qkv):
    x = qkv.reshape(4, -1, D)
    x = jnp.pad(x, ((0, 0), (0, 4 * QUARTER - x.shape[1]), (0, 0))).reshape(4, 2, 2, QUARTER, D)
    return fold_half(x[:2], 2, 1), fold_half(x[2:], 1, 2)


def qkv_second(first, second):
    return jnp.concatenate([fold_half(first, 1, 2), fold_half(second, 2, 1)])[:, 0, 0]


def collect_qkv(quarter):
    low = quarter.astype(BF)
    others = [lax.ppermute(low, "ctx", [(i, 0)]).astype(F32) for i in (1, 2, 3)]
    return jnp.concatenate([quarter, *others])


def shard_chunk(x, by):
    return lax.dynamic_index_in_dim(x, lax.rem(lax.axis_index("shard") + by, 4), 0, keepdims=False)


def along_shard_first(x):
    return shift(shard_chunk(x, 2), "shard", 1)


def along_shard(x, passing):
    through = add_low(shard_chunk(x, 1), passing)
    return [shard_chunk(x, 0), shift(shard_chunk(x, 3), "shard", 3), shift(through, "shard", 1)]


SHIFT = 10
UNROLL = 8


def owned_rows(ids, entries):
    rows = ids.shape[1]
    assert rows < (1 << SHIFT)
    owned = ids < entries
    place = jnp.cumsum(owned.astype(jnp.int32), axis=1) - 1
    packed = jnp.arange(rows, dtype=jnp.int32)[None, :] + (ids << SHIFT)
    slots = jnp.arange(rows, dtype=jnp.int32)
    hit = (place[:, None, :] == slots[None, :, None]) & owned[:, None, :]
    listed = jnp.sum(jnp.where(hit, packed[:, None, :], 0), axis=2)
    count = jnp.sum(owned.astype(jnp.int32), axis=1)
    listed = jnp.where(slots[None, :] < count[:, None], listed, rows + (entries << SHIFT))
    return listed.reshape(-1), count


def for_owned(listed, counts, step, rows, body):
    def some(t, _):
        for u in range(UNROLL):
            packed = listed[step * rows + t * UNROLL + u]
            body(pl.ds(packed & ((1 << SHIFT) - 1), 1), pl.ds(packed >> SHIFT, 1))
        return 0

    lax.fori_loop(0, (counts[step] + UNROLL - 1) // UNROLL, some, 0)


def lookup_kernel(rows, listed, counts, end_ids, meta, table, out, ends, tab, buf):
    step = pl.program_id(0)
    columns, entries = table.shape

    @pl.when(step == 0)
    def _():
        def turn(i, _):
            at = pl.multiple_of(i * 256, 256)
            tab[pl.ds(at, 256), :] = table[:, pl.ds(at, 256)].astype(BF).astype(F32).T
            return 0

        lax.fori_loop(0, entries // 256, turn, 0)
        tab[pl.ds(entries, 8), :] = jnp.zeros((8, columns), F32)
        for n in range(ends.shape[0]):
            ends[pl.ds(n, 1), :] = tab[pl.ds(end_ids[n], 1), :]

    buf[...] = jnp.zeros_like(buf)

    def pick(place, entry):
        buf[place, :] = tab[entry, :]

    for_owned(listed, counts, step, rows, pick)

    @pl.when(meta[0] == 1)
    def _():
        half = rows // 2
        group = meta[4 + step]
        for j in range(2):
            block = group if j == 0 else 2 * meta[1] - 1 - group
            at = pl.multiple_of(meta[2] + block * half, 8)
            buf[pl.ds(j * half, half), :] += tab[pl.ds(at, half), :]

    out[0] = buf[pl.ds(0, rows), :].T.astype(BF)


def lookup(listed, counts, end_ids, meta, table, n_blocks, rows):
    columns, entries = table.shape
    n_ends = end_ids.shape[0]
    grid_spec = pltpu.PrefetchScalarGridSpec(
        num_scalar_prefetch=4,
        grid=(n_blocks,),
        in_specs=[pl.BlockSpec((columns, entries), lambda i, *_: (0, 0))],
        out_specs=[
            pl.BlockSpec((1, columns, rows), lambda i, *_: (i, 0, 0)),
            pl.BlockSpec((n_ends, columns), lambda i, *_: (0, 0)),
        ],
        scratch_shapes=[pltpu.VMEM((entries + 8, columns), F32), pltpu.VMEM((rows + 8, columns), F32)],
    )
    return pl.pallas_call(
        functools.partial(lookup_kernel, rows),
        grid_spec=grid_spec,
        out_shape=[
            jax.ShapeDtypeStruct((n_blocks, columns, rows), BF),
            jax.ShapeDtypeStruct((n_ends, columns), F32),
        ],
        compiler_params=params(),
        cost_estimate=cost(40),
        name="lookup",
    )(listed, counts, end_ids, meta, table)


def scatter_kernel(rows, n_blocks, listed, counts, end_ids, meta, grads, ends, out, squares, acc, buf):
    step = pl.program_id(0)
    columns, entries = out.shape
    n_ends = ends.shape[0]

    @pl.when(step == 0)
    def _():
        def clear(i, _):
            acc[pl.ds(pl.multiple_of(i * 256, 256), 256), :] = jnp.zeros((256, columns), F32)
            return 0

        lax.fori_loop(0, entries // 256, clear, 0)
        for n in range(n_ends):
            at = pl.ds(end_ids[n], 1)
            acc[at, :] += ends[pl.ds(n, 1), :]

    buf[pl.ds(0, rows), :] = grads[0].astype(F32).T

    def add(place, entry):
        acc[entry, :] += buf[place, :]

    for_owned(listed, counts, step, rows, add)

    @pl.when(meta[0] == 1)
    def _():
        half = rows // 2
        group = meta[4 + step]
        for j in range(2):
            block = group if j == 0 else 2 * meta[1] - 1 - group
            at = pl.multiple_of(meta[2] + block * half, 8)
            acc[pl.ds(at, half), :] += buf[pl.ds(j * half, half), :]

    @pl.when(step == n_blocks - 1)
    def _():
        def turn(i, total):
            at = pl.multiple_of(i * 256, 256)
            part = acc[pl.ds(at, 256), :]
            out[:, pl.ds(at, 256)] = part.T
            return total + part * part

        total = lax.fori_loop(0, entries // 256, turn, jnp.zeros((256, columns), F32))
        squares[...] = jnp.sum(total, axis=0, keepdims=True)


def scatter(listed, counts, end_ids, meta, grads, ends, entries):
    n_blocks, columns, rows = grads.shape
    n_ends = ends.shape[0]
    grid_spec = pltpu.PrefetchScalarGridSpec(
        num_scalar_prefetch=4,
        grid=(n_blocks,),
        in_specs=[
            pl.BlockSpec((1, columns, rows), lambda i, *_: (i, 0, 0)),
            pl.BlockSpec((n_ends, columns), lambda i, *_: (0, 0)),
        ],
        out_specs=[
            pl.BlockSpec((columns, entries), lambda i, *_: (0, 0)),
            pl.BlockSpec((1, columns), lambda i, *_: (0, 0)),
        ],
        scratch_shapes=[pltpu.VMEM((entries + 8, columns), F32), pltpu.VMEM((rows + 8, columns), F32)],
    )
    return pl.pallas_call(
        functools.partial(scatter_kernel, rows, n_blocks),
        grid_spec=grid_spec,
        out_shape=[jax.ShapeDtypeStruct((columns, entries), F32), jax.ShapeDtypeStruct((1, columns), F32)],
        compiler_params=params(),
        cost_estimate=cost(42),
        name="scatter",
    )(listed, counts, end_ids, meta, grads, ends)


def tile_cuts():
    return [(t * LANES, min(LANES, D - t * LANES)) for t in range(PAIRS_OF_HEADS)]


def split_kernel(count, rb, width, u, out, scr):
    for t, (at, size) in enumerate(tile_cuts()):
        part = u[:, pl.ds(at, size)].astype(F32)
        if size < LANES:
            part = jnp.concatenate([part, jnp.zeros((rb * count, LANES - size), F32)], axis=1)
        scr[t] = part
        for j in range(count):
            picked = scr[t, pl.ds(j, rb, stride=count), :].astype(BF)
            take = min(LANES, width - at)
            out[j, :, pl.ds(at, take)] = picked[:, :take]


def join_kernel(count, rb, u, out, scr):
    for t, (at, size) in enumerate(tile_cuts()):
        part = u[:, pl.ds(at, size)].astype(F32)
        if size < LANES:
            part = jnp.concatenate([part, jnp.zeros((rb * count, LANES - size), F32)], axis=1)
        scr[t] = part
        for j in range(count):
            out[:, pl.ds(j * D + at, size)] = scr[t, pl.ds(j, rb, stride=count), :].astype(BF)[:, :size]


def join_units(u, first, count):
    rb = 272
    return pl.pallas_call(
        functools.partial(join_kernel, count, rb),
        grid=(D // rb,),
        in_specs=[pl.BlockSpec((rb * count, D), lambda i: (i + first // (rb * count), 0))],
        out_specs=pl.BlockSpec((rb, count * D), lambda i: (i, 0)),
        out_shape=jax.ShapeDtypeStruct((D, count * D), BF),
        scratch_shapes=[pltpu.VMEM((PAIRS_OF_HEADS, rb * count, LANES), F32)],
        compiler_params=params(),
        cost_estimate=cost(8),
        name="join_units",
    )(u)


def split_units(u, first, count, width=D):
    rb = 272
    return pl.pallas_call(
        functools.partial(split_kernel, count, rb, width),
        grid=(D // rb,),
        in_specs=[pl.BlockSpec((rb * count, D), lambda i: (i + first // (rb * count), 0))],
        out_specs=pl.BlockSpec((count, rb, width), lambda i: (0, i, 0)),
        out_shape=jax.ShapeDtypeStruct((count, D, width), BF),
        scratch_shapes=[pltpu.VMEM((PAIRS_OF_HEADS, rb * count, LANES), F32)],
        compiler_params=params(),
        cost_estimate=cost(8),
        name="split_units",
    )(u)


def merge_kernel(count, rb, starts, *refs):
    parts, out, scr = refs[:-2], refs[-2], refs[-1]
    for t, (at, size) in enumerate(tile_cuts()):
        for j in range(count):
            which, start = starts[j]
            part = parts[which][:, pl.ds(start + at, size)].astype(F32)
            if size < LANES:
                part = jnp.concatenate([part, jnp.zeros((rb, LANES - size), F32)], axis=1)
            scr[t, pl.ds(j, rb, stride=count), :] = part
        out[:, pl.ds(at, size)] = scr[t][:, :size].astype(BF)


def merge_units(parts, starts):
    rb, count = 272, len(starts)
    return pl.pallas_call(
        functools.partial(merge_kernel, count, rb, starts),
        grid=(D // rb,),
        in_specs=[pl.BlockSpec((rb, p.shape[1]), lambda i: (i, 0)) for p in parts],
        out_specs=pl.BlockSpec((rb * count, D), lambda i: (i, 0)),
        out_shape=jax.ShapeDtypeStruct((count * D, D), BF),
        scratch_shapes=[pltpu.VMEM((PAIRS_OF_HEADS, rb * count, LANES), F32)],
        compiler_params=params(),
        cost_estimate=cost(8),
        name="merge_units",
    )(*parts)


def merge_apart_kernel(count, rb, starts, core, *refs):
    parts, mine, other, scr = refs[:-3], refs[-3], refs[-2], refs[-1]
    for t, (at, size) in enumerate(tile_cuts()):
        for j in range(count):
            which, start = starts[j]
            part = parts[which][:, pl.ds(start + at, size)].astype(F32)
            if size < LANES:
                part = jnp.concatenate([part, jnp.zeros((rb, LANES - size), F32)], axis=1)
            scr[t, pl.ds(j, rb, stride=count), :] = part
        for block in range(rb * count // (2 * BLOCK)):
            for out, which in ((mine, core[0]), (other, 1 - core[0])):
                first = pl.multiple_of(2 * BLOCK * block + BLOCK * which, 8)
                out[block, :, pl.ds(at, size)] = scr[t, pl.ds(first, BLOCK), :][:, :size].astype(BF)


def merge_apart(parts, starts):
    rb, count = 272, len(starts)
    blocks = rb * count // (2 * BLOCK)
    out_spec = pl.BlockSpec((blocks, BLOCK, D), lambda i, *_: (i, 0, 0))
    grid_spec = pltpu.PrefetchScalarGridSpec(
        num_scalar_prefetch=1,
        grid=(D // rb,),
        in_specs=[pl.BlockSpec((rb, p.shape[1]), lambda i, *_: (i, 0)) for p in parts],
        out_specs=[out_spec, out_spec],
        scratch_shapes=[pltpu.VMEM((PAIRS_OF_HEADS, rb * count, LANES), F32)],
    )
    return pl.pallas_call(
        functools.partial(merge_apart_kernel, count, rb, starts),
        grid_spec=grid_spec,
        out_shape=[jax.ShapeDtypeStruct((D // rb * blocks, BLOCK, D), BF)] * 2,
        compiler_params=params(),
        cost_estimate=cost(8),
        name="merge_apart",
    )(lax.axis_index("section").reshape(1), *parts)


def adam_kernel(rate, decay, factor, w, m, v, g, w_out, m_out, v_out):
    w_out[...], m_out[...], v_out[...] = adam_update(w[...], m[...], v[...], g[...] * factor[0], rate, decay)


def adam(factor, weight, first, second, grad, rate, decay, block):
    shape = weight.shape
    grid = tuple(size // b for size, b in zip(shape, block))
    spec = pl.BlockSpec(block, lambda i, j, *_: (i, j))
    return pl.pallas_call(
        functools.partial(adam_kernel, rate, decay),
        grid_spec=pltpu.PrefetchScalarGridSpec(num_scalar_prefetch=1, grid=grid, in_specs=[spec] * 4, out_specs=[spec] * 3),
        out_shape=[jax.ShapeDtypeStruct(shape, F32)] * 3,
        compiler_params=params(),
        cost_estimate=cost(weight.size * 9.0e-6),
        name="adam",
    )(factor.reshape(1), weight, first, second, grad)


def chunk_plan(n):
    plan = [(0, "ll", True), (0, "hl", False), (0, "hh", True)]
    for p in range(1, n):
        plan += [(p, "hl", False), (p, "sel", False)]
    return plan


def chunk_offsets(meta, n, hb, p, kind):
    own = meta[0]
    piece = meta[2 + p]
    if kind == "ll":
        return 0, p * 2 * hb, own * hb, piece * hb, True
    if kind == "hl":
        return hb, p * 2 * hb, (2 * n - 1 - own) * hb, piece * hb, False
    if kind == "hh":
        return hb, p * 2 * hb + hb, (2 * n - 1 - own) * hb, (2 * n - 1 - piece) * hb, False
    low = piece < own
    q_off = pl.multiple_of(jnp.where(low, 0, hb), hb)
    k_off = pl.multiple_of(p * 2 * hb + jnp.where(low, 0, hb), hb)
    key_pos = jnp.where(low, piece, 2 * n - 1 - piece) * hb
    return q_off, k_off, None, key_pos, low


def chunk_scores(keys, queries, meta, diagonal, kind, q_pos, k_pos, hb):
    s = dot(keys, queries, NT)
    if diagonal:
        ki = lax.broadcasted_iota(jnp.int32, (hb, hb), 0)
        qi = lax.broadcasted_iota(jnp.int32, (hb, hb), 1)
        keep = (ki <= qi) & (ki + k_pos < meta[1])
        s = jnp.where(keep, s, -1e30)
    elif kind == "sel":
        ki = lax.broadcasted_iota(jnp.int32, (hb, hb), 0)
        s = jnp.where(ki < meta[1] - k_pos, s, -1e30)
    return s


def attend_kernel(n, hb, meta, q_ref, k_ref, v_ref, o_ref, lse_ref, vt_ref):
    keys = 2 * hb * n
    for i in range(keys // hb):
        vt_ref[i] = v_ref[pl.ds(i * hb, hb), :].astype(F32).T.astype(BF)
    lane = lax.broadcasted_iota(jnp.int32, (1, LANES), 1)
    plan = chunk_plan(n)
    outs = []
    for head in range(2):
        own_lanes = (lane // HD) == head
        info, scores = [], []
        tops = [jnp.full((1, hb), -3e38, F32), jnp.full((1, hb), -3e38, F32)]
        for p, kind, diagonal in plan:
            q_off, k_off, q_pos, k_pos, low = chunk_offsets(meta, n, hb, p, kind)
            queries = jnp.where(own_lanes, q_ref[pl.ds(q_off, hb), :], 0)
            s = chunk_scores(k_ref[pl.ds(k_off, hb), :], queries, meta, diagonal, kind, q_pos, k_pos, hb)
            top = jnp.max(s, axis=0, keepdims=True)
            if low is True:
                tops[0] = jnp.maximum(tops[0], top)
            elif low is False:
                tops[1] = jnp.maximum(tops[1], top)
            else:
                tops[0] = jnp.maximum(tops[0], jnp.where(low, top, -3e38))
                tops[1] = jnp.maximum(tops[1], jnp.where(low, -3e38, top))
            info.append((k_off, low))
            scores.append(s)
        sums = [jnp.zeros((1, hb), F32), jnp.zeros((1, hb), F32)]
        accs = [jnp.zeros((HD, hb), F32), jnp.zeros((HD, hb), F32)]
        for (k_off, low), s in zip(info, scores):
            if low is True or low is False:
                top = tops[0] if low else tops[1]
            else:
                top = jnp.where(low, tops[0], tops[1])
            e = jnp.exp(s - top)
            total = jnp.sum(e, axis=0, keepdims=True)
            got = dot(vt_ref[k_off // hb, pl.ds(head * HD, HD), :], e.astype(BF))
            if low is True or low is False:
                sums[1 - low] += total
                accs[1 - low] += got
            else:
                sums[0] += jnp.where(low, total, 0.0)
                sums[1] += jnp.where(low, 0.0, total)
                accs[0] += jnp.where(low, got, 0.0)
                accs[1] += jnp.where(low, 0.0, got)
        outs.append([accs[i] / sums[i] for i in range(2)])
        for i in range(2):
            lse_ref[0, pl.ds(head, 1), pl.ds(i * hb, hb)] = tops[i] + jnp.log(sums[i])
    for i in range(2):
        both = jnp.concatenate([outs[0][i], outs[1][i]], axis=0)
        o_ref[pl.ds(i * hb, hb), :] = both.T.astype(BF)


def attend(meta, q, k, v, n):
    rows = q.shape[0]
    keys = k.shape[0]
    grid_spec = pltpu.PrefetchScalarGridSpec(
        num_scalar_prefetch=1,
        grid=(PAIRS_OF_HEADS,),
        in_specs=[
            pl.BlockSpec((rows, LANES), lambda p, *_: (0, p)),
            pl.BlockSpec((keys, LANES), lambda p, *_: (0, p)),
            pl.BlockSpec((keys, LANES), lambda p, *_: (0, p)),
        ],
        out_specs=[
            pl.BlockSpec((rows, LANES), lambda p, *_: (0, p)),
            pl.BlockSpec((1, 8, rows), lambda p, *_: (p, 0, 0)),
        ],
        scratch_shapes=[pltpu.VMEM((2 * n, LANES, rows // 2), BF)],
    )
    return pl.pallas_call(
        functools.partial(attend_kernel, n, rows // 2),
        grid_spec=grid_spec,
        out_shape=[
            jax.ShapeDtypeStruct((rows, WIDE), BF),
            jax.ShapeDtypeStruct((PAIRS_OF_HEADS, 8, rows), F32),
        ],
        compiler_params=params(),
        cost_estimate=cost(23),
        name="attend",
    )(meta, q, k, v)


def attend_back_kernel(n, hb, meta, q_ref, k_ref, v_ref, o_ref, do_ref, lse_ref, dq_ref, dk_ref, dv_ref, kt_ref, dk_acc, dv_acc):
    keys = 2 * hb * n
    for i in range(keys // hb):
        kt_ref[i] = k_ref[pl.ds(i * hb, hb), :].astype(F32).T.astype(BF)
    dk_acc[...] = jnp.zeros_like(dk_acc)
    dv_acc[...] = jnp.zeros_like(dv_acc)
    lane = lax.broadcasted_iota(jnp.int32, (1, LANES), 1)
    plan = chunk_plan(n)
    prods = []
    for i in range(2):
        part = pl.ds(i * hb, hb)
        prods.append((o_ref[part, :].astype(F32) * do_ref[part, :].astype(F32)).T)
    dqs = []
    for head in range(2):
        own_lanes = (lane // HD) == head
        deltas = [jnp.sum(prods[i][head * HD : (head + 1) * HD, :], axis=0, keepdims=True) for i in range(2)]
        lses = [lse_ref[0, pl.ds(head, 1), pl.ds(i * hb, hb)] for i in range(2)]
        accs = [jnp.zeros((HD, hb), F32), jnp.zeros((HD, hb), F32)]
        for p, kind, diagonal in plan:
            q_off, k_off, q_pos, k_pos, low = chunk_offsets(meta, n, hb, p, kind)
            q_at, k_at = pl.ds(q_off, hb), pl.ds(k_off, hb)
            queries = jnp.where(own_lanes, q_ref[q_at, :], 0)
            d_out = jnp.where(own_lanes, do_ref[q_at, :], 0)
            s = chunk_scores(k_ref[k_at, :], queries, meta, diagonal, kind, q_pos, k_pos, hb)
            if low is True or low is False:
                lse, delta = lses[1 - low], deltas[1 - low]
            else:
                lse, delta = jnp.where(low, lses[0], lses[1]), jnp.where(low, deltas[0], deltas[1])
            prob = jnp.exp(s - lse)
            d_prob = dot(v_ref[k_at, :], d_out, NT)
            d_score = (prob * (d_prob - delta)).astype(BF)
            dv_acc[k_at, :] += dot(prob.astype(BF), d_out)
            dk_acc[k_at, :] += dot(d_score, queries)
            got = dot(kt_ref[k_off // hb, pl.ds(head * HD, HD), :], d_score)
            if low is True or low is False:
                accs[1 - low] += got
            else:
                accs[0] += jnp.where(low, got, 0.0)
                accs[1] += jnp.where(low, 0.0, got)
        dqs.append(accs)
    for i in range(2):
        both = jnp.concatenate([dqs[0][i], dqs[1][i]], axis=0) * 0.125
        dq_ref[pl.ds(i * hb, hb), :] = both.T.astype(BF)
    dk_ref[...] = dk_acc[...].astype(BF)
    dv_ref[...] = dv_acc[...].astype(BF)


def attend_back(meta, q, k, v, o, d_o, lse, n):
    rows = q.shape[0]
    keys = k.shape[0]
    row_spec = pl.BlockSpec((rows, LANES), lambda p, *_: (0, p))
    key_spec = pl.BlockSpec((keys, LANES), lambda p, *_: (0, p))
    grid_spec = pltpu.PrefetchScalarGridSpec(
        num_scalar_prefetch=1,
        grid=(PAIRS_OF_HEADS,),
        in_specs=[row_spec, key_spec, key_spec, row_spec, row_spec, pl.BlockSpec((1, 8, rows), lambda p, *_: (p, 0, 0))],
        out_specs=[row_spec, key_spec, key_spec],
        scratch_shapes=[pltpu.VMEM((2 * n, LANES, rows // 2), BF), pltpu.VMEM((keys, LANES), F32), pltpu.VMEM((keys, LANES), F32)],
    )
    return pl.pallas_call(
        functools.partial(attend_back_kernel, n, rows // 2),
        grid_spec=grid_spec,
        out_shape=[
            jax.ShapeDtypeStruct((rows, WIDE), BF),
            jax.ShapeDtypeStruct((keys, WIDE), BF),
            jax.ShapeDtypeStruct((keys, WIDE), BF),
        ],
        compiler_params=params(),
        cost_estimate=cost(46),
        name="attend_back",
    )(meta, q, k, v, o, d_o, lse)


def by_rows(x):
    return with_layout_constraint(x, Layout(major_to_minor=tuple(range(x.ndim))))


def layer_norm(values, gain_vec, bias_vec):
    row_mean = jnp.mean(values, -1, keepdims=True)
    centred = values - row_mean
    variance = jnp.mean(centred * centred, -1, keepdims=True)
    return centred * lax.rsqrt(variance + 1e-05) * gain_vec + bias_vec


def gelu_tanh(values):
    return 0.5 * values * (1.0 + jnp.tanh(0.7978845608 * (values + 0.044715 * values * values * values)))


def softplus(values):
    return jnp.maximum(values, 0.0) + jnp.log1p(jnp.exp(-jnp.abs(values)))


def adam_update(weight, first, second, grad, rate, decay):
    first = 0.9 * first + 0.1 * grad
    second = 0.95 * second + 0.05 * grad * grad
    first_hat = first / (1.0 - 0.9**STEP)
    second_hat = second / (1.0 - 0.95**STEP)
    weight = weight - rate * (first_hat / (jnp.sqrt(second_hat) + 1e-08) + decay * weight)
    return (weight, first, second)


def pieces_by_ctx(x, half):
    got = [x]
    bit = 1
    while bit < half:
        got += [swap(y, "ctx", bit) for y in got]
        bit *= 2
    return got


def pieces_by_section(got):
    own = jnp.concatenate(got)
    return jnp.concatenate([own, swap(own, "section", 1)])


def sum_pieces(x, half):
    rows = x.shape[0] // half
    bit = half // 2
    while bit >= 1:
        keep, send = x[: bit * rows], x[bit * rows : 2 * bit * rows]
        x = keep + swap(send.astype(BF), "ctx", bit).astype(F32)
        bit //= 2
    return x


def layer_weights(units):
    return split_units(units, 0, 3, WIDE), units[U_OUT:U_UP], join_units(units, U_UP, N_UP), units[U_DOWN:]


def layer_forward(values, hidden1, all_hidden1, meta, n, weights, vecs):
    w_qkv, w_out, w_up, w_down = weights
    keys = dot(all_hidden1, w_qkv[1]).astype(BF)
    vals = dot(all_hidden1, w_qkv[2]).astype(BF)
    queries = dot(hidden1, w_qkv[0]).astype(BF) * jnp.asarray(0.125, BF)
    attended, lse = attend(meta, queries, keys, vals, n)
    middle = values + dot(attended[:, :D], w_out)
    hidden2 = layer_norm(middle, vecs[2], vecs[3]).astype(BF)
    ups = dot(hidden2, w_up)
    gated, back = jax.vjp(gelu_tanh, ups)
    gated, slopes = gated.astype(BF), back(jnp.ones_like(ups))[0]
    result = middle + dot(gated, w_down)
    return result, (values, all_hidden1, queries, keys, vals, attended, lse, middle, hidden2, slopes, gated)


def layer_backward(saved, grad_out, meta, n, weights, vecs, factors, fast):
    values, all_hidden1, queries, keys, vals, attended, lse, middle, hidden2, slopes, gated = saved
    w_qkv, w_out, w_up, w_down = weights
    grad_ffn = grad_out.astype(BF)
    grad_down = by_rows(dot(gated, grad_ffn, TN).astype(BF))
    if fast:
        mine_down, other_down = core_blocks(grad_down)
        both = beside(factors)
        grad_ffn, other_down, both = lax.optimization_barrier((grad_ffn, other_down, both))
        came_down = swap(other_down, "section", 1)
    grad_ups = by_rows((slopes * dot(grad_ffn, w_down, NT)).astype(BF))
    grad_up, up_starts = dot(hidden2, grad_ups, TN).astype(BF), [(0, j * D) for j in range(N_UP)]
    if fast:
        mine_up, other_up = merge_apart([grad_up], up_starts)
        four = gather_step(both[None], "shard", 1)
        grad_ups, other_up, four = lax.optimization_barrier((grad_ups, other_up, four))
        came_up = swap(other_up, "section", 1)
    grad_hidden2 = dot(grad_ups, w_up, NT)
    _, norm_back2 = jax.vjp(layer_norm, middle, vecs[2], vecs[3])
    grad_norm2, grad_gain2, grad_bias2 = norm_back2(grad_hidden2)
    grad_middle = grad_out + grad_norm2
    grad_branch = grad_middle.astype(BF)
    grad_outw = dot(attended[:, :D], grad_branch, TN).astype(BF)
    grad_att = dot(grad_branch, jnp.pad(w_out, ((0, WIDE - D), (0, 0))), NT).astype(BF)
    if fast:
        rest = jnp.concatenate([fold_cores(grad_outw), add_low(mine_up, came_up), add_low(mine_down, came_down)])
        grad_att, rest = lax.optimization_barrier((grad_att, rest))
        came = rest_first(rest)
    grad_q, part_k, part_v = attend_back(meta, queries, keys, vals, attended, grad_att, lse, n)
    rows, near = grad_q.shape[0], part_k.shape[0] // 2
    if fast:
        grad_q, four = lax.optimization_barrier((grad_q, four))
        factors = gather_step(four, "shard", 2)
    def to_hidden1(at):
        return dot(part_k[at], w_qkv[1], NT) + dot(part_v[at], w_qkv[2], NT)

    far = to_hidden1(slice(near, None)).astype(BF)
    grad_q, part_k, part_v, far = lax.optimization_barrier((grad_q, part_k, part_v, far))
    if fast:
        far, factors, *came = lax.optimization_barrier((far, factors, *came))
    close = to_hidden1(slice(0, near)) + swap(far, "section", 1).astype(F32)
    if fast:
        close, *came = lax.optimization_barrier((close, *came))
    grad_hidden1 = sum_pieces(close, n // 2)
    grad_hidden1 = grad_hidden1 + dot(grad_q, w_qkv[0], NT)
    _, norm_back1 = jax.vjp(layer_norm, values, vecs[0], vecs[1])
    grad_norm1, grad_gain1, grad_bias1 = norm_back1(grad_hidden1)
    grad_input = (grad_middle + grad_norm1).astype(BF)
    grad_input, grad_q, part_k, part_v = lax.optimization_barrier((grad_input, grad_q, part_k, part_v))
    def grad_qkvw(grads):
        rows_of = (all_hidden1[:rows], all_hidden1, all_hidden1)
        parts, starts = [dot(h, g, TN).astype(BF) for h, g in zip(rows_of, grads)], [(j, 0) for j in range(3)]
        if not fast:
            return merge_units(parts, starts)
        mine, other = merge_apart(parts, starts)
        return add_low(mine, swap(other, "section", 1))

    if fast:
        rest = rest_second(rest, came)
        summed = (rest, along_shard_first(rest)), ((grad_q, part_k, part_v), grad_qkvw)
    else:
        summed = jnp.concatenate([grad_qkvw((grad_q, part_k, part_v)), grad_outw, merge_units([grad_up], up_starts), grad_down])
        factors = gather_axis(beside(factors), "shard")
    return grad_input, summed, [grad_gain1, grad_bias1, grad_gain2, grad_bias2], factors


def head_mask():
    head = lax.broadcasted_iota(jnp.int32, (HEADS, D), 0)
    return lax.broadcasted_iota(jnp.int32, (HEADS, D), 1) // HD == head


def last_forward(values, positions, length, half, weights, vecs):
    (w_q, w_k, w_v), w_out, w_up, w_down = weights
    heads = head_mask()
    hidden1 = layer_norm(values, vecs[0], vecs[1]).astype(BF)
    mine = (positions == length - 1)[:, None]
    row = jnp.sum(jnp.where(mine, values, 0.0), axis=0, keepdims=True)
    row = group_reduce(row, jnp.add, half)
    row_h1 = layer_norm(row, vecs[0], vecs[1]).astype(BF)
    query = dot(row_h1, w_q).astype(BF)
    wq = dot(jnp.where(heads, query, 0), w_k, NT) * 0.125
    scores = dot2(wq, hidden1, NT)
    scores = jnp.where((positions < length)[None, :], scores, -1e30)
    top = jnp.max(scores, axis=1, keepdims=True)
    expo = jnp.exp(scores - top)
    total = jnp.sum(expo, axis=1, keepdims=True)
    mixed = dot(expo.astype(BF), hidden1)
    wide = lambda x: jnp.broadcast_to(x, (HEADS, HD))

    def merge(x, y):
        high = jnp.maximum(x[:, D : D + 1], y[:, D : D + 1])
        x = x * jnp.exp(x[:, D : D + 1] - high)
        y = y * jnp.exp(y[:, D : D + 1] - high)
        return jnp.concatenate([x[:, :D] + y[:, :D], wide(high), x[:, D + HD :] + y[:, D + HD :]], axis=1)

    merged = group_reduce(jnp.concatenate([mixed, wide(top), wide(total)], axis=1), merge, half)
    top, total = merged[:, D : D + 1], merged[:, D + HD : D + HD + 1]
    mixed = merged[:, :D] / total
    probs = jnp.exp(scores - top) / total
    att = jnp.sum(jnp.where(heads, dot2(mixed, w_v), 0.0), axis=0, keepdims=True)
    middle = row + dot(att.astype(BF), w_out)
    hidden2 = layer_norm(middle, vecs[2], vecs[3]).astype(BF)
    ups = dot(hidden2, w_up)
    gated = gelu_tanh(ups).astype(BF)
    result = middle + dot(gated, w_down)
    return result, (values, hidden1, mine, row_h1, query, wq, probs, mixed, att, middle, hidden2, ups, gated)


def last_backward(saved, grad_out, half, weights, vecs):
    values, hidden1, mine, row_h1, query, wq, probs, mixed, att, middle, hidden2, ups, gated = saved
    (w_q, w_k, w_v), w_out, w_up, w_down = weights
    heads = head_mask()
    grad_ffn = grad_out.astype(BF)
    _, back = jax.vjp(gelu_tanh, ups)
    grad_ups = back(dot(grad_ffn, w_down, NT))[0].astype(BF)
    grad_hidden2 = dot(grad_ups, w_up, NT)
    _, norm_back2 = jax.vjp(layer_norm, middle, vecs[2], vecs[3])
    grad_norm2, grad_gain2, grad_bias2 = norm_back2(grad_hidden2)
    grad_middle = grad_out + grad_norm2
    grad_branch = grad_middle.astype(BF)
    grad_att = dot(grad_branch, w_out, NT).astype(BF)
    att_heads = jnp.where(heads, grad_att, 0)
    wv = dot(att_heads, w_v, NT)
    grad_prob = dot2(wv, hidden1, NT)
    delta = jnp.sum(att_heads.astype(F32) * att, axis=1, keepdims=True)
    grad_score = (probs * (grad_prob - delta)).astype(BF)
    summed = group_reduce(dot(grad_score, hidden1), jnp.add, half)
    grad_query = (jnp.sum(jnp.where(heads, dot2(summed, w_k), 0.0), axis=0, keepdims=True) * 0.125).astype(BF)
    low_probs = probs.astype(BF)
    grad_hidden1 = dot(
        jnp.concatenate([grad_score, grad_score, low_probs, low_probs]), jnp.concatenate([split2(wq), split2(wv)]), TN
    )
    grad_hidden1 = grad_hidden1 + jnp.where(mine, dot(grad_query, w_q, NT), 0.0)
    _, norm_back1 = jax.vjp(layer_norm, values, vecs[0], vecs[1])
    grad_norm1, grad_gain1, grad_bias1 = norm_back1(grad_hidden1)
    grad_input = grad_norm1 + jnp.where(mine, grad_middle, 0.0)
    query8 = query * jnp.asarray(0.125, BF)
    factors = [row_h1, grad_query, query8, grad_att, att, grad_branch, hidden2, grad_ffn]
    factors += [grad_ups.reshape(N_UP, D), gated.reshape(N_UP, D), summed, mixed]
    factors = jnp.concatenate([f.astype(BF) for f in factors])
    return grad_input, factors, [grad_gain1, grad_bias1], [grad_gain2, grad_bias2]


def last_gradient(data, chunk_at, n_chunks, size):
    n_seq = data.shape[0]
    heads = head_mask()
    row_h1, grad_query, query8, grad_att, att, grad_branch, hidden2, grad_ffn = [data[:, i] for i in range(8)]
    at = 8
    grad_ups, gated = data[:, at : at + N_UP], data[:, at + N_UP : at + 2 * N_UP]
    at += 2 * N_UP
    summed, mixed = data[:, at : at + HEADS], data[:, at + HEADS : at + 2 * HEADS]

    def by_unit(parts):
        count, width = len(parts), sum(p.shape[0] for p in parts)
        slot = jnp.concatenate([jnp.full((p.shape[0],), j, jnp.int32) for j, p in enumerate(parts)])
        both = jnp.concatenate(parts).T
        spread = jnp.where(slot[None, None, :] == jnp.arange(count)[None, :, None], both[:, None, :], 0)
        return spread.reshape(count * D, width)

    def per_head(x):
        return jnp.where(heads[None], x[:, None, :], 0).reshape(n_seq * HEADS, D)

    left = by_unit([row_h1, summed.reshape(-1, D), mixed.reshape(-1, D)])
    right = jnp.concatenate([grad_query, per_head(query8), per_head(grad_att)])
    first = chunk_at * size
    qkv = dot(lax.dynamic_slice_in_dim(left, jnp.minimum(first, U_OUT - size), size, 0), right)
    lefts = [att.T, by_unit([hidden2] * N_UP), gated.reshape(n_seq, FF).T]
    rights = [grad_branch, grad_ups.transpose(1, 0, 2).reshape(-1, D), grad_ffn]
    width = sum(x.shape[1] for x in lefts)
    columns, before = [], 0
    for x in lefts:
        columns.append(jnp.pad(x, ((0, 0), (before, width - before - x.shape[1]))))
        before += x.shape[1]
    left = jnp.concatenate(columns)
    rest = dot(lax.dynamic_slice_in_dim(left, jnp.maximum(first - U_OUT, 0), size, 0), jnp.concatenate(rights))
    return jnp.where(first < U_OUT, qkv, rest)


def shards(
    tokens,
    lengths,
    end_ids,
    pairs,
    layer_master,
    layer_first,
    layer_second,
    table_master,
    table_first,
    table_second,
    vector_master,
    vector_first,
    vector_second,
):
    rows = tokens.shape[1]
    s_at = lax.axis_index("section")
    c_at = lax.axis_index("ctx")
    z_at = lax.axis_index("shard")
    n_section = lax.axis_size("section")
    n = lax.axis_size("ctx")
    n_shard = lax.axis_size("shard")
    half = n // 2
    hb = rows // 2
    n_dest = n_section * n
    n_seq = MICRO * n_shard
    columns, entries = table_master.shape
    is_first = s_at == 0
    seq_in = c_at // half
    seq_at = z_at * MICRO + seq_in
    group = (c_at % half) * 2 + s_at

    fast = small_block()
    chunk = chunk_rows(layer_master) if fast else layer_master.reshape(-1, D).astype(BF)
    size = chunk.shape[0]
    cut = size // 2
    if fast:
        wide = cut + OVERLAP // 2
        got = swap(jnp.where(is_first, chunk[size - wide :], chunk[:wide]), "section", 1)
        piece0 = jnp.where(is_first, chunk[:wide], got)
        piece1 = jnp.where(is_first, got[:cut], chunk[cut:])
    else:
        got = swap(jnp.where(is_first, chunk[cut:], chunk[:cut]), "section", 1)
        piece0 = jnp.where(is_first, chunk[:cut], got)
        piece1 = jnp.where(is_first, got, chunk[cut:])
    order = ("ctx", "shard", "section")

    own_ids = jnp.concatenate([tokens, end_ids[:, None]], axis=1)
    all_ids = gather_axis(gather_axis(own_ids, "ctx"), "shard")
    natural = all_ids[..., :rows].transpose(0, 2, 1, 3).reshape(n_shard, MICRO, 2 * n, hb)
    zig = jnp.stack([natural[:, :, :n], natural[:, :, n:][:, :, ::-1]], axis=3)
    zig = zig.reshape(n_shard, MICRO, half, 2, rows).transpose(0, 3, 1, 2, 4)
    end_all = all_ids[:, 0, :, rows].reshape(n_seq)
    n_blocks = n_shard * n_dest

    def held(ids):
        ids = ids - z_at * entries
        return jnp.where((ids >= 0) & (ids < entries), ids, entries)

    listed, counts = owned_rows(held(zig.reshape(n_blocks, rows)), entries)
    end_held = held(end_all)
    if fast:
        first = first_moves(piece0)
        listed, piece0, *first = lax.optimization_barrier((listed, piece0, *first))
        second = second_moves(piece0, first[0], first[1])
    else:
        units0 = lax.all_gather(piece0, order, axis=0, tiled=True)
    dest = jnp.arange(n_blocks, dtype=jnp.int32) % n_dest
    groups = (dest % n % half) * 2 + dest // n
    assert VOCAB >= (n_shard - 1) * entries
    meta_emb = jnp.concatenate(
        [
            jnp.stack([(z_at == n_shard - 1).astype(jnp.int32), jnp.int32(n), jnp.int32(VOCAB - (n_shard - 1) * entries), jnp.int32(0)]),
            groups,
        ]
    )
    picked, end_part = lookup(listed, counts, end_held, meta_emb, table_master, n_blocks, rows)
    if fast:
        picked, *second = lax.optimization_barrier((picked, *second))
        halves = gather_half(piece0, first, second)
    column_at = (s_at * n + c_at) * columns
    end_rows = sum_all(lax.dynamic_update_slice(jnp.zeros((n_seq, D), F32), end_part, (0, column_at)))
    summed = lax.psum_scatter(picked.reshape(n_shard, n_dest, columns, rows), "shard", scatter_dimension=0, tiled=True)
    if fast:
        summed, piece1, end_rows, *halves = lax.optimization_barrier((summed, piece1, end_rows, *halves))
        parts = [part for mine in halves for part in (mine, swap(mine, "section", 1))]
    routed = lax.all_to_all(summed.reshape(n_dest, columns, rows), ("section", "ctx"), split_axis=0, concat_axis=0, tiled=True)
    embedded = routed.reshape(D, rows).T.astype(F32)
    end_row = lax.dynamic_slice_in_dim(end_rows, seq_at, 1, 0)
    units1 = lax.all_gather(piece1, order, axis=0, tiled=True)

    length = lax.dynamic_slice_in_dim(lengths, seq_in, 1, 0)[0]
    others = [group ^ (2 * cb + sb) for sb in range(2) for cb in range(half)]
    meta = jnp.stack([group, length] + others).astype(jnp.int32)
    span = jnp.arange(hb, dtype=jnp.int32)
    positions = jnp.concatenate([group * hb + span, (2 * n - 1 - group) * hb + span])

    vecs0, vecs1 = vector_master[0:4], vector_master[4:8]
    hidden1 = layer_norm(embedded, vecs0[0], vecs0[1]).astype(BF)
    if fast:
        hidden1, *parts = lax.optimization_barrier((hidden1, *parts))
        units0 = place_units(parts)
    weights0 = layer_weights(units0)
    others = pieces_by_ctx(hidden1, half)[1:]
    *others, w_qkv0, w_up0 = lax.optimization_barrier((*others, weights0[0], weights0[2]))
    weights0 = (w_qkv0, weights0[1], w_up0, weights0[3])
    out0, saved0 = layer_forward(embedded, hidden1, pieces_by_section([hidden1, *others]), meta, n, weights0, vecs0)
    x1 = out0.astype(BF).astype(F32)
    *saved0, slopes, gated = saved0
    x1, units1, slopes = lax.optimization_barrier((x1, units1, slopes))
    saved0 = (*saved0, slopes, gated)
    w_qkv1 = split_units(units1, 0, 3)
    weights1 = ((w_qkv1[0], w_qkv1[1], w_qkv1[2]), units1[U_OUT:U_UP], join_units(units1, U_UP, N_UP), units1[U_DOWN:])
    final, saved1 = last_forward(x1, positions, length, half, weights1, vecs1)

    def score_terms(final_row, end_vals, gain_vec, bias_vec, head_vec):
        normed = layer_norm(final_row, gain_vec, bias_vec)
        return jnp.sum(normed * (end_vals + head_vec)) * D ** (-0.5)

    counted = group == 0
    score, score_back = jax.vjp(score_terms, final, end_row, vector_master[8], vector_master[9], vector_master[10])
    scores = sum_small(jnp.where((jnp.arange(n_seq) == seq_at) & counted, score, 0.0)[None])[0]

    def pair_loss(score_vals):
        return jnp.sum(softplus(score_vals[pairs[:, 1]] - score_vals[pairs[:, 0]]))

    loss_sum, loss_back = jax.vjp(pair_loss, scores)
    grad_scores = loss_back(jnp.ones_like(loss_sum))[0]
    grad_own = lax.dynamic_slice_in_dim(grad_scores, seq_at, 1, 0)[0]
    grad_final, grad_end, *vec_final = score_back(grad_own)

    grad_x1, factors, vec1, vec1_row = last_backward(saved1, grad_final, half, weights1, vecs1)
    factors = jnp.concatenate([factors, grad_end.astype(BF)])
    grad_x1 = grad_x1.astype(BF).astype(F32)
    grad_x0, grads0, vec0, every_factor = layer_backward(saved0, grad_x1, meta, n, weights0, vecs0, factors, fast)
    every_factor = every_factor.reshape(n_seq, -1, D)

    by_owner = grad_x0.T.reshape(n_dest, columns, rows)
    back = lax.all_to_all(by_owner, ("section", "ctx"), split_axis=0, concat_axis=0, tiled=True)
    if fast:
        (rest, passing), (qkv_grads, finish_qkv) = grads0
        back, *qkv_grads = lax.optimization_barrier((back, *qkv_grads))
        every = [back] + [shift(back, "shard", d) for d in (1, 3)]
        every[1], every[2], rest, passing = lax.optimization_barrier((every[1], every[2], rest, passing))
        every.append(shift(every[1], "shard", 1))
        rest_terms = along_shard(rest, passing)
        every_factor, *qkv_part = lax.optimization_barrier((every_factor, *qkv_first(finish_qkv(qkv_grads))))
        qkv_part = qkv_second(*qkv_part)
        every[3], qkv_part = lax.optimization_barrier((every[3], qkv_part))
        every = jnp.concatenate(every)
        near_order = (z_at + 4 - jnp.array((0, 1, 3, 2), jnp.int32)) % 4
        listed = listed.reshape(n_shard, -1)[near_order].reshape(-1)
        counts = counts.reshape(n_shard, -1)[near_order].reshape(-1)
    else:
        every = lax.all_gather(back, "shard", axis=0, tiled=True)
    end_grads = lax.dynamic_slice(every_factor[:, -1].astype(F32), (0, column_at), (n_seq, columns))
    table_grad, table_squares = scatter(listed, counts, end_held, meta_emb, every, end_grads, entries)
    once = [jnp.where(counted, v, 0.0) for v in vec1_row + vec_final]
    vector_part = jnp.stack(vec0 + vec1 + once)

    own1 = last_gradient(every_factor, c_at * n_shard + z_at, n * n_shard, size)
    squares = jnp.sum(table_squares) + jnp.where(is_first, 0.0, jnp.sum(own1 * own1))
    if fast:
        qkv_terms = along_shard(qkv_part, along_shard_first(qkv_part))
        terms = [*rest_terms, *qkv_terms]
        table_grad, own1, squares, vector_part, *terms = lax.optimization_barrier(
            (table_grad, own1, squares, vector_part, *terms)
        )
        rest_terms, qkv_terms = terms[:3], terms[3:]
        mine = sum(t.astype(F32) for t in rest_terms)
        quarter = sum(t.astype(F32) for t in qkv_terms)
        squares = squares + jnp.sum(quarter * quarter) + jnp.where(c_at == 0, 0.0, jnp.sum(mine * mine))
        squares, quarter = lax.optimization_barrier((squares, quarter))
        collected = collect_qkv(quarter)[: mine.shape[0] * BLOCK]
        mine = jnp.where(c_at == 0, collected.reshape(mine.shape), mine)
    else:
        mine = lax.psum_scatter(grads0, order, scatter_dimension=0, tiled=True).astype(F32)
        squares = squares + jnp.sum(mine * mine)
    other = swap(mine.astype(BF), "section", 1).astype(F32)
    own0 = jnp.stack([mine, other], axis=1).reshape(size, D) if fast else jnp.concatenate([mine, other])
    layer_grad = jnp.where(is_first, own0, own1).reshape(-1, LANES)

    n_vec = vector_part.shape[0]
    totals = sum_small(jnp.concatenate([vector_part, jnp.full((1, D), squares)]))
    vector_grad = totals[:n_vec]
    grad_norm = jnp.sqrt(totals[n_vec, 0] + jnp.sum(vector_grad * vector_grad))
    layer_grad, grad_norm = lax.optimization_barrier((layer_grad, grad_norm))
    factor = CLIP_LIMIT / jnp.maximum(grad_norm, CLIP_LIMIT)
    flat = [x.reshape(-1, LANES) for x in (layer_master, layer_first, layer_second)]
    flat_rows = flat[0].shape[0]
    block_rows = max(b for b in range(1, 2313) if flat_rows % b == 0 and (b % 8 == 0 or b == flat_rows))
    table_cols = max(b for b in range(LANES, 1537, LANES) if entries % b == 0)
    layer_new = adam(factor, *flat, layer_grad, 0.4, 0.1, (block_rows, LANES))
    layer_new = [x.reshape(layer_master.shape) for x in layer_new]
    table_new = adam(factor, table_master, table_first, table_second, table_grad, 0.5, 0.1, (columns, table_cols))
    vector_new = adam_update(vector_master, vector_first, vector_second, vector_grad * factor, 0.7, 0.0)
    return (loss_sum, grad_norm, *layer_new, *table_new, *vector_new)


def solution(mesh):
    in_specs = (
        P("shard", "ctx"),
        P("shard"),
        P("shard"),
        P(),
        P("section", ("ctx", "shard")),
        P("section", ("ctx", "shard")),
        P("section", ("ctx", "shard")),
        P(("section", "ctx"), "shard"),
        P(("section", "ctx"), "shard"),
        P(("section", "ctx"), "shard"),
        P(),
        P(),
        P(),
    )
    out_specs = (
        P(),
        P(),
        P("section", ("ctx", "shard")),
        P("section", ("ctx", "shard")),
        P("section", ("ctx", "shard")),
        P(("section", "ctx"), "shard"),
        P(("section", "ctx"), "shard"),
        P(("section", "ctx"), "shard"),
        P(),
        P(),
        P(),
    )
    return jax.shard_map(shards, mesh=mesh, in_specs=in_specs, out_specs=out_specs, check_vma=False)
```

```python
import functools

import jax
import jax.numpy as jnp
from jax import lax
from jax.experimental import pallas as pl
from jax.experimental.layout import Layout, with_layout_constraint
from jax.experimental.pallas import tpu as pltpu
from jax.sharding import PartitionSpec as P

D = 1088
HEADS = 17
HD = 64
FF = 4352
VOCAB = 51200
MICRO = 2
STEP = 10
CLIP_LIMIT = 0.02
ALL = ("section", "ctx", "shard")

LANES = 128
PAIRS_OF_HEADS = (HEADS + 1) // 2
WIDE = PAIRS_OF_HEADS * LANES
N_UP = FF // D
U_OUT = 3 * D
U_UP = U_OUT + D
U_DOWN = U_UP + FF
UNITS = U_DOWN + FF

BF = jnp.bfloat16
F32 = jnp.float32
VMEM_BIG = 56 * 1024 * 1024


def params(limit=VMEM_BIG):
    return pltpu.CompilerParams(vmem_limit_bytes=limit)


def cost(microseconds):
    return pl.CostEstimate(flops=0, bytes_accessed=int(microseconds * 3.0e6), transcendentals=0)


def dot(a, b, contract=((1,), (0,))):
    return lax.dot_general(a, b, (contract, ((), ())), preferred_element_type=F32)


NT = ((1,), (1,))
TN = ((0,), (0,))


def split2(x):
    top = lax.reduce_precision(x, 8, 7)
    return jnp.concatenate([top, x - top]).astype(BF)


def dot2(x, w, contract=((1,), (0,))):
    y = dot(split2(x), w, contract)
    return y[: x.shape[0]] + y[x.shape[0] :]


def swap(x, axis, bit):
    size = lax.axis_size(axis)
    return lax.ppermute(x, axis, [(i, i ^ bit) for i in range(size)])


def gather_step(x, axis, bit):
    other = swap(x, axis, bit)
    lower = (lax.axis_index(axis) & bit) == 0
    return jnp.where(lower, jnp.concatenate([x, other]), jnp.concatenate([other, x]))


def gather_axis(x, axis):
    x = x[None]
    bit = 1
    while bit < lax.axis_size(axis):
        x = gather_step(x, axis, bit)
        bit *= 2
    return x


def beside(x):
    return gather_step(x[None], "ctx", lax.axis_size("ctx") // 2)


def sum_axis(x, axis, first=1, last=None):
    size = lax.axis_size(axis) if last is None else last
    bit = first
    while bit < size:
        x = x + swap(x, axis, bit)
        bit *= 2
    return x


def group_reduce(x, combine, half):
    def step(x, axis, bit):
        other = swap(x, axis, bit)
        lower = (lax.axis_index(axis) & bit) == 0
        return combine(jnp.where(lower, x, other), jnp.where(lower, other, x))

    x = step(x, "section", 1)
    bit = 1
    while bit < half:
        x = step(x, "ctx", bit)
        bit *= 2
    return x


def sum_all(x):
    return sum_axis(sum_axis(sum_axis(x, "section"), "ctx"), "shard")


def sum_direct(x, axis):
    if lax.axis_size(axis) != 4:
        return sum_axis(x, axis)
    one, two, three = [lax.ppermute(x, axis, [(i, (i + d) % 4) for i in range(4)]) for d in (1, 2, 3)]
    return (x + two) + (one + three)


def sum_small(x):
    return sum_direct(sum_direct(sum_direct(x, "section"), "ctx"), "shard")


def rows_kernel(pairs, x, out, scr):
    lane = lax.broadcasted_iota(jnp.int32, (1, LANES), 1)
    step = 2 * D // LANES
    even, odd = pl.ds(0, pairs, stride=2), pl.ds(1, pairs, stride=2)
    flat_row = lambda t: x[pl.ds(t, pairs, stride=step), :]
    for t in range(PAIRS_OF_HEADS):
        scr[t, even, :] = flat_row(t)
    before = pltpu.roll(flat_row(step // 2), HD, 1)
    for t in range(PAIRS_OF_HEADS - 1):
        after = pltpu.roll(flat_row(step // 2 + 1 + t), HD, 1)
        scr[t, odd, :] = jnp.where(lane < HD, before, after)
        before = after
    scr[PAIRS_OF_HEADS - 1, odd, :] = before
    for t, (at, size) in enumerate(tile_cuts()):
        out[:, pl.ds(at, size)] = scr[t][:, :size].astype(BF)


def chunk_rows(flat):
    units = flat.size // D
    return pl.pallas_call(
        functools.partial(rows_kernel, units // 2),
        out_shape=jax.ShapeDtypeStruct((units, D), BF),
        scratch_shapes=[pltpu.VMEM((PAIRS_OF_HEADS, units, LANES), F32)],
        compiler_params=params(),
        cost_estimate=cost(6),
        name="chunk_rows",
    )(flat.reshape(-1, LANES))


def small_block():
    return lax.axis_size("ctx") == 4 and lax.axis_size("shard") == 4 and lax.axis_size("section") == 2


def shift(x, axis, by):
    size = lax.axis_size(axis)
    return lax.ppermute(x, axis, [(i, (i + by) % size) for i in range(size)])


ARRIVALS = ((0,), (1, 3), (2,))
OVERLAP = 16


def place_kernel(rows, at, *refs):
    ins, out, held, sems_in, sems_out = refs[: 2 * len(ARRIVALS)], refs[-4], refs[-3], refs[-2], refs[-1]
    s, c, z = at[0], at[1], at[2]
    short = rows - OVERLAP
    pieces = []
    for g, distances in enumerate(ARRIVALS):
        for other in range(2):
            for e in range(4):
                for i, d in enumerate(distances):
                    chunk = (c ^ e) * 4 + lax.rem(z + 4 - d, 4)
                    pieces.append((ins[2 * g + other].at[e, i], chunk, other))

    def arrive(k):
        return pltpu.make_async_copy(pieces[k][0], held.at[k], sems_in.at[k])

    def leave(k, act):
        _, chunk, other = pieces[k]

        @pl.when(s == other)
        def _():
            act(pltpu.make_async_copy(held.at[k], out.at[chunk, pl.ds(0, rows)], sems_out.at[k]))

        @pl.when(s != other)
        def _():
            act(pltpu.make_async_copy(held.at[k, pl.ds(OVERLAP, short)], out.at[chunk, pl.ds(rows, short)], sems_out.at[k]))

    for k in range(len(pieces)):
        arrive(k).start()
    for k in range(len(pieces)):
        arrive(k).wait()
        leave(k, lambda copy: copy.start())
    for k in range(len(pieces)):
        leave(k, lambda copy: copy.wait())


def by_links(own):
    return swap(own, "ctx", 1), swap(own, "ctx", 2)


def first_moves(piece):
    return shift(piece, "shard", 1), shift(piece, "shard", 3), *by_links(piece[None])


def second_moves(piece, near, far):
    return shift(piece, "shard", 2), *by_links(jnp.stack([near, far]))


def corner_of(by_x, by_y):
    cut = by_x.shape[1] // 2
    return jnp.concatenate([swap(by_x[:, :cut], "ctx", 2), swap(by_y[:, cut:], "ctx", 1)], axis=1)


def gather_half(piece, first, second, later):
    near, far, *own_links = first
    opposite, *near_links = second
    arrived = {0: piece, 1: near, 3: far, 2: opposite}
    parts = []
    for distances, links in zip(ARRIVALS, (own_links, near_links, None)):
        own = jnp.stack([arrived[d] for d in distances])
        by_x, by_y = by_links(own) if links is None else links
        if links is None:
            by_x, by_y, later = lax.optimization_barrier((by_x, by_y, later))
        corner = corner_of(by_x, by_y)
        parts.append(jnp.stack([own, by_x, by_y, corner]))
    return parts, later


def place_units(parts):
    rows = parts[0].shape[2]
    at = jnp.stack([lax.axis_index(a) for a in ALL]).astype(jnp.int32)
    grid_spec = pltpu.PrefetchScalarGridSpec(
        num_scalar_prefetch=1,
        grid=(1,),
        in_specs=[pl.BlockSpec(memory_space=pl.ANY)] * len(parts),
        out_specs=pl.BlockSpec(memory_space=pl.ANY),
        scratch_shapes=[pltpu.VMEM((32, rows, D), BF), pltpu.SemaphoreType.DMA((32,)), pltpu.SemaphoreType.DMA((32,))],
    )
    whole = pl.pallas_call(
        functools.partial(place_kernel, rows),
        grid_spec=grid_spec,
        out_shape=jax.ShapeDtypeStruct((16, 2 * rows - OVERLAP, D), BF),
        compiler_params=params(),
        cost_estimate=cost(16),
        name="place",
    )(at, *parts)
    return whole.reshape(UNITS, D)


def add_low(x, y):
    return (x.astype(F32) + y.astype(F32)).astype(BF)


BLOCK = 136
QUARTER = 104


def core_blocks(region):
    s = lax.axis_index("section")
    blocks = region.reshape(-1, 2, BLOCK, D)
    pick = lambda i: lax.dynamic_index_in_dim(blocks, i, 1, keepdims=False)
    return pick(s), pick(1 - s)


def fold_cores(region):
    mine, other = core_blocks(region)
    return add_low(mine, swap(other, "section", 1))


def one_way(x, bit, sends):
    return lax.ppermute(x, "ctx", [(i, i ^ bit) for i in range(4) if sends(i)])


def three_first(one, two, both, p):
    has_p = (lax.axis_index("ctx") & p) != 0
    return swap(jnp.where(has_p, two, one), "ctx", p), one_way(both, p, lambda i: not i & p)


def three_second(one, two, both, came, came_both, p, q):
    c = lax.axis_index("ctx")
    has_p, has_q = (c & p) != 0, (c & q) != 0
    single = add_low(jnp.where(has_p, one, two), came)
    both = add_low(both, came_both)
    sent = jnp.where(has_p & ~has_q, both, single)
    came = one_way(sent, q, lambda i: not i & q or i & p)
    return add_low(jnp.where(has_p & has_q, both, single), came)


def rest_first(rest):
    x = rest.reshape(3, 4, -1, BLOCK, D)
    return *three_first(x[0, :2], x[1, :2], x[2, :2], 1), *three_first(x[1, 2:], x[0, 2:], x[2, 2:], 2)


def rest_second(rest, came):
    x = rest.reshape(3, 4, -1, BLOCK, D)
    first = three_second(x[0, :2], x[1, :2], x[2, :2], came[0], came[1], 1, 2)
    second = three_second(x[1, 2:], x[0, 2:], x[2, 2:], came[2], came[3], 2, 1)
    return jnp.concatenate([first, second])


def fold_half(v, axis, bit):
    mine = (lax.axis_index("ctx") // bit) & 1
    pick = lambda i: lax.dynamic_index_in_dim(v, i, axis, keepdims=True)
    return add_low(pick(mine), swap(pick(1 - mine), "ctx", bit))


def qkv_first(qkv):
    x = qkv.reshape(4, -1, D)
    x = jnp.pad(x, ((0, 0), (0, 4 * QUARTER - x.shape[1]), (0, 0))).reshape(4, 2, 2, QUARTER, D)
    return fold_half(x[:2], 2, 1), fold_half(x[2:], 1, 2)


def qkv_second(first, second):
    return jnp.concatenate([fold_half(first, 1, 2), fold_half(second, 2, 1)])[:, 0, 0]


def collect_qkv(quarter):
    low = quarter.astype(BF)
    others = [lax.ppermute(low, "ctx", [(i, 0)]).astype(F32) for i in (1, 2, 3)]
    return jnp.concatenate([quarter, *others])


def shard_chunk(x, by):
    return lax.dynamic_index_in_dim(x, lax.rem(lax.axis_index("shard") + by, 4), 0, keepdims=False)


def along_shard_first(x):
    return shift(shard_chunk(x, 2), "shard", 1)


def along_shard(x, passing):
    through = add_low(shard_chunk(x, 1), passing)
    return [shard_chunk(x, 0), shift(shard_chunk(x, 3), "shard", 3), shift(through, "shard", 1)]


SHIFT = 10
UNROLL = 8


def owned_rows(ids, entries):
    rows = ids.shape[1]
    assert rows < (1 << SHIFT)
    owned = ids < entries
    place = jnp.cumsum(owned.astype(jnp.int32), axis=1) - 1
    packed = jnp.arange(rows, dtype=jnp.int32)[None, :] + (ids << SHIFT)
    slots = jnp.arange(rows, dtype=jnp.int32)
    hit = (place[:, None, :] == slots[None, :, None]) & owned[:, None, :]
    listed = jnp.sum(jnp.where(hit, packed[:, None, :], 0), axis=2)
    count = jnp.sum(owned.astype(jnp.int32), axis=1)
    listed = jnp.where(slots[None, :] < count[:, None], listed, rows + (entries << SHIFT))
    return listed.reshape(-1), count


def for_owned(listed, counts, step, rows, body):
    def some(t, _):
        for u in range(UNROLL):
            packed = listed[step * rows + t * UNROLL + u]
            body(pl.ds(packed & ((1 << SHIFT) - 1), 1), pl.ds(packed >> SHIFT, 1))
        return 0

    lax.fori_loop(0, (counts[step] + UNROLL - 1) // UNROLL, some, 0)


def lookup_kernel(rows, listed, counts, end_ids, meta, table, out, ends, tab, buf):
    step = pl.program_id(0)
    columns, entries = table.shape

    @pl.when(step == 0)
    def _():
        def turn(i, _):
            at = pl.multiple_of(i * 256, 256)
            tab[pl.ds(at, 256), :] = table[:, pl.ds(at, 256)].astype(BF).astype(F32).T
            return 0

        lax.fori_loop(0, entries // 256, turn, 0)
        tab[pl.ds(entries, 8), :] = jnp.zeros((8, columns), F32)
        for n in range(ends.shape[0]):
            ends[pl.ds(n, 1), :] = tab[pl.ds(end_ids[n], 1), :]

    buf[...] = jnp.zeros_like(buf)

    def pick(place, entry):
        buf[place, :] = tab[entry, :]

    for_owned(listed, counts, step, rows, pick)

    @pl.when(meta[0] == 1)
    def _():
        half = rows // 2
        group = meta[4 + step]
        for j in range(2):
            block = group if j == 0 else 2 * meta[1] - 1 - group
            at = pl.multiple_of(meta[2] + block * half, 8)
            buf[pl.ds(j * half, half), :] += tab[pl.ds(at, half), :]

    out[0] = buf[pl.ds(0, rows), :].T.astype(BF)


def lookup(listed, counts, end_ids, meta, table, n_blocks, rows):
    columns, entries = table.shape
    n_ends = end_ids.shape[0]
    grid_spec = pltpu.PrefetchScalarGridSpec(
        num_scalar_prefetch=4,
        grid=(n_blocks,),
        in_specs=[pl.BlockSpec((columns, entries), lambda i, *_: (0, 0))],
        out_specs=[
            pl.BlockSpec((1, columns, rows), lambda i, *_: (i, 0, 0)),
            pl.BlockSpec((n_ends, columns), lambda i, *_: (0, 0)),
        ],
        scratch_shapes=[pltpu.VMEM((entries + 8, columns), F32), pltpu.VMEM((rows + 8, columns), F32)],
    )
    return pl.pallas_call(
        functools.partial(lookup_kernel, rows),
        grid_spec=grid_spec,
        out_shape=[
            jax.ShapeDtypeStruct((n_blocks, columns, rows), BF),
            jax.ShapeDtypeStruct((n_ends, columns), F32),
        ],
        compiler_params=params(),
        cost_estimate=cost(40),
        name="lookup",
    )(listed, counts, end_ids, meta, table)


def scatter_kernel(rows, n_blocks, listed, counts, end_ids, meta, grads, ends, out, squares, acc, buf):
    step = pl.program_id(0)
    columns, entries = out.shape
    n_ends = ends.shape[0]

    @pl.when(step == 0)
    def _():
        def clear(i, _):
            acc[pl.ds(pl.multiple_of(i * 256, 256), 256), :] = jnp.zeros((256, columns), F32)
            return 0

        lax.fori_loop(0, entries // 256, clear, 0)
        for n in range(n_ends):
            at = pl.ds(end_ids[n], 1)
            acc[at, :] += ends[pl.ds(n, 1), :]

    buf[pl.ds(0, rows), :] = grads[0].astype(F32).T

    def add(place, entry):
        acc[entry, :] += buf[place, :]

    for_owned(listed, counts, step, rows, add)

    @pl.when(meta[0] == 1)
    def _():
        half = rows // 2
        group = meta[4 + step]
        for j in range(2):
            block = group if j == 0 else 2 * meta[1] - 1 - group
            at = pl.multiple_of(meta[2] + block * half, 8)
            acc[pl.ds(at, half), :] += buf[pl.ds(j * half, half), :]

    @pl.when(step == n_blocks - 1)
    def _():
        def turn(i, total):
            at = pl.multiple_of(i * 256, 256)
            part = acc[pl.ds(at, 256), :]
            out[:, pl.ds(at, 256)] = part.T
            return total + part * part

        total = lax.fori_loop(0, entries // 256, turn, jnp.zeros((256, columns), F32))
        squares[...] = jnp.sum(total, axis=0, keepdims=True)


def scatter(listed, counts, end_ids, meta, grads, ends, entries):
    n_blocks, columns, rows = grads.shape
    n_ends = ends.shape[0]
    grid_spec = pltpu.PrefetchScalarGridSpec(
        num_scalar_prefetch=4,
        grid=(n_blocks,),
        in_specs=[
            pl.BlockSpec((1, columns, rows), lambda i, *_: (i, 0, 0)),
            pl.BlockSpec((n_ends, columns), lambda i, *_: (0, 0)),
        ],
        out_specs=[
            pl.BlockSpec((columns, entries), lambda i, *_: (0, 0)),
            pl.BlockSpec((1, columns), lambda i, *_: (0, 0)),
        ],
        scratch_shapes=[pltpu.VMEM((entries + 8, columns), F32), pltpu.VMEM((rows + 8, columns), F32)],
    )
    return pl.pallas_call(
        functools.partial(scatter_kernel, rows, n_blocks),
        grid_spec=grid_spec,
        out_shape=[jax.ShapeDtypeStruct((columns, entries), F32), jax.ShapeDtypeStruct((1, columns), F32)],
        compiler_params=params(),
        cost_estimate=cost(42),
        name="scatter",
    )(listed, counts, end_ids, meta, grads, ends)


def tile_cuts():
    return [(t * LANES, min(LANES, D - t * LANES)) for t in range(PAIRS_OF_HEADS)]


def split_kernel(count, rb, width, u, out, scr):
    for t, (at, size) in enumerate(tile_cuts()):
        part = u[:, pl.ds(at, size)].astype(F32)
        if size < LANES:
            part = jnp.concatenate([part, jnp.zeros((rb * count, LANES - size), F32)], axis=1)
        scr[t] = part
        for j in range(count):
            picked = scr[t, pl.ds(j, rb, stride=count), :].astype(BF)
            take = min(LANES, width - at)
            out[j, :, pl.ds(at, take)] = picked[:, :take]


def join_kernel(count, rb, u, out, scr):
    for t, (at, size) in enumerate(tile_cuts()):
        part = u[:, pl.ds(at, size)].astype(F32)
        if size < LANES:
            part = jnp.concatenate([part, jnp.zeros((rb * count, LANES - size), F32)], axis=1)
        scr[t] = part
        for j in range(count):
            out[:, pl.ds(j * D + at, size)] = scr[t, pl.ds(j, rb, stride=count), :].astype(BF)[:, :size]


def join_units(u, first, count):
    rb = 272
    return pl.pallas_call(
        functools.partial(join_kernel, count, rb),
        grid=(D // rb,),
        in_specs=[pl.BlockSpec((rb * count, D), lambda i: (i + first // (rb * count), 0))],
        out_specs=pl.BlockSpec((rb, count * D), lambda i: (i, 0)),
        out_shape=jax.ShapeDtypeStruct((D, count * D), BF),
        scratch_shapes=[pltpu.VMEM((PAIRS_OF_HEADS, rb * count, LANES), F32)],
        compiler_params=params(),
        cost_estimate=cost(8),
        name="join_units",
    )(u)


def split_units(u, first, count, width=D):
    rb = 272
    return pl.pallas_call(
        functools.partial(split_kernel, count, rb, width),
        grid=(D // rb,),
        in_specs=[pl.BlockSpec((rb * count, D), lambda i: (i + first // (rb * count), 0))],
        out_specs=pl.BlockSpec((count, rb, width), lambda i: (0, i, 0)),
        out_shape=jax.ShapeDtypeStruct((count, D, width), BF),
        scratch_shapes=[pltpu.VMEM((PAIRS_OF_HEADS, rb * count, LANES), F32)],
        compiler_params=params(),
        cost_estimate=cost(8),
        name="split_units",
    )(u)


def merge_kernel(count, rb, starts, *refs):
    parts, out, scr = refs[:-2], refs[-2], refs[-1]
    for t, (at, size) in enumerate(tile_cuts()):
        for j in range(count):
            which, start = starts[j]
            part = parts[which][:, pl.ds(start + at, size)].astype(F32)
            if size < LANES:
                part = jnp.concatenate([part, jnp.zeros((rb, LANES - size), F32)], axis=1)
            scr[t, pl.ds(j, rb, stride=count), :] = part
        out[:, pl.ds(at, size)] = scr[t][:, :size].astype(BF)


def merge_units(parts, starts):
    rb, count = 272, len(starts)
    return pl.pallas_call(
        functools.partial(merge_kernel, count, rb, starts),
        grid=(D // rb,),
        in_specs=[pl.BlockSpec((rb, p.shape[1]), lambda i: (i, 0)) for p in parts],
        out_specs=pl.BlockSpec((rb * count, D), lambda i: (i, 0)),
        out_shape=jax.ShapeDtypeStruct((count * D, D), BF),
        scratch_shapes=[pltpu.VMEM((PAIRS_OF_HEADS, rb * count, LANES), F32)],
        compiler_params=params(),
        cost_estimate=cost(8),
        name="merge_units",
    )(*parts)


def merge_apart_kernel(count, rb, starts, core, *refs):
    parts, mine, other, scr = refs[:-3], refs[-3], refs[-2], refs[-1]
    for t, (at, size) in enumerate(tile_cuts()):
        for j in range(count):
            which, start = starts[j]
            part = parts[which][:, pl.ds(start + at, size)].astype(F32)
            if size < LANES:
                part = jnp.concatenate([part, jnp.zeros((rb, LANES - size), F32)], axis=1)
            scr[t, pl.ds(j, rb, stride=count), :] = part
        for block in range(rb * count // (2 * BLOCK)):
            for out, which in ((mine, core[0]), (other, 1 - core[0])):
                first = pl.multiple_of(2 * BLOCK * block + BLOCK * which, 8)
                out[block, :, pl.ds(at, size)] = scr[t, pl.ds(first, BLOCK), :][:, :size].astype(BF)


def merge_apart(parts, starts):
    rb, count = 272, len(starts)
    blocks = rb * count // (2 * BLOCK)
    out_spec = pl.BlockSpec((blocks, BLOCK, D), lambda i, *_: (i, 0, 0))
    grid_spec = pltpu.PrefetchScalarGridSpec(
        num_scalar_prefetch=1,
        grid=(D // rb,),
        in_specs=[pl.BlockSpec((rb, p.shape[1]), lambda i, *_: (i, 0)) for p in parts],
        out_specs=[out_spec, out_spec],
        scratch_shapes=[pltpu.VMEM((PAIRS_OF_HEADS, rb * count, LANES), F32)],
    )
    return pl.pallas_call(
        functools.partial(merge_apart_kernel, count, rb, starts),
        grid_spec=grid_spec,
        out_shape=[jax.ShapeDtypeStruct((D // rb * blocks, BLOCK, D), BF)] * 2,
        compiler_params=params(),
        cost_estimate=cost(8),
        name="merge_apart",
    )(lax.axis_index("section").reshape(1), *parts)


def adam_kernel(rate, decay, factor, w, m, v, g, w_out, m_out, v_out):
    w_out[...], m_out[...], v_out[...] = adam_update(w[...], m[...], v[...], g[...] * factor[0], rate, decay)


def adam(factor, weight, first, second, grad, rate, decay, block):
    shape = weight.shape
    grid = tuple(size // b for size, b in zip(shape, block))
    spec = pl.BlockSpec(block, lambda i, j, *_: (i, j))
    return pl.pallas_call(
        functools.partial(adam_kernel, rate, decay),
        grid_spec=pltpu.PrefetchScalarGridSpec(num_scalar_prefetch=1, grid=grid, in_specs=[spec] * 4, out_specs=[spec] * 3),
        out_shape=[jax.ShapeDtypeStruct(shape, F32)] * 3,
        compiler_params=params(),
        cost_estimate=cost(weight.size * 9.0e-6),
        name="adam",
    )(factor.reshape(1), weight, first, second, grad)


def chunk_plan(n):
    plan = [(0, "ll", True), (0, "hl", False), (0, "hh", True)]
    for p in range(1, n):
        plan += [(p, "hl", False), (p, "sel", False)]
    return plan


def chunk_offsets(meta, n, hb, p, kind):
    own = meta[0]
    piece = meta[2 + p]
    if kind == "ll":
        return 0, p * 2 * hb, own * hb, piece * hb, True
    if kind == "hl":
        return hb, p * 2 * hb, (2 * n - 1 - own) * hb, piece * hb, False
    if kind == "hh":
        return hb, p * 2 * hb + hb, (2 * n - 1 - own) * hb, (2 * n - 1 - piece) * hb, False
    low = piece < own
    q_off = pl.multiple_of(jnp.where(low, 0, hb), hb)
    k_off = pl.multiple_of(p * 2 * hb + jnp.where(low, 0, hb), hb)
    key_pos = jnp.where(low, piece, 2 * n - 1 - piece) * hb
    return q_off, k_off, None, key_pos, low


def chunk_scores(keys, queries, meta, diagonal, kind, q_pos, k_pos, hb):
    s = dot(keys, queries, NT)
    if diagonal:
        ki = lax.broadcasted_iota(jnp.int32, (hb, hb), 0)
        qi = lax.broadcasted_iota(jnp.int32, (hb, hb), 1)
        keep = (ki <= qi) & (ki + k_pos < meta[1])
        s = jnp.where(keep, s, -1e30)
    elif kind == "sel":
        ki = lax.broadcasted_iota(jnp.int32, (hb, hb), 0)
        s = jnp.where(ki < meta[1] - k_pos, s, -1e30)
    return s


def attend_kernel(n, hb, meta, q_ref, k_ref, v_ref, o_ref, lse_ref, vt_ref):
    keys = 2 * hb * n
    for i in range(keys // hb):
        vt_ref[i] = v_ref[pl.ds(i * hb, hb), :].astype(F32).T.astype(BF)
    lane = lax.broadcasted_iota(jnp.int32, (1, LANES), 1)
    plan = chunk_plan(n)
    outs = []
    for head in range(2):
        own_lanes = (lane // HD) == head
        info, scores = [], []
        tops = [jnp.full((1, hb), -3e38, F32), jnp.full((1, hb), -3e38, F32)]
        for p, kind, diagonal in plan:
            q_off, k_off, q_pos, k_pos, low = chunk_offsets(meta, n, hb, p, kind)
            queries = jnp.where(own_lanes, q_ref[pl.ds(q_off, hb), :], 0)
            s = chunk_scores(k_ref[pl.ds(k_off, hb), :], queries, meta, diagonal, kind, q_pos, k_pos, hb)
            top = jnp.max(s, axis=0, keepdims=True)
            if low is True:
                tops[0] = jnp.maximum(tops[0], top)
            elif low is False:
                tops[1] = jnp.maximum(tops[1], top)
            else:
                tops[0] = jnp.maximum(tops[0], jnp.where(low, top, -3e38))
                tops[1] = jnp.maximum(tops[1], jnp.where(low, -3e38, top))
            info.append((k_off, low))
            scores.append(s)
        sums = [jnp.zeros((1, hb), F32), jnp.zeros((1, hb), F32)]
        accs = [jnp.zeros((HD, hb), F32), jnp.zeros((HD, hb), F32)]
        for (k_off, low), s in zip(info, scores):
            if low is True or low is False:
                top = tops[0] if low else tops[1]
            else:
                top = jnp.where(low, tops[0], tops[1])
            e = jnp.exp(s - top)
            total = jnp.sum(e, axis=0, keepdims=True)
            got = dot(vt_ref[k_off // hb, pl.ds(head * HD, HD), :], e.astype(BF))
            if low is True or low is False:
                sums[1 - low] += total
                accs[1 - low] += got
            else:
                sums[0] += jnp.where(low, total, 0.0)
                sums[1] += jnp.where(low, 0.0, total)
                accs[0] += jnp.where(low, got, 0.0)
                accs[1] += jnp.where(low, 0.0, got)
        outs.append([accs[i] / sums[i] for i in range(2)])
        for i in range(2):
            lse_ref[0, pl.ds(head, 1), pl.ds(i * hb, hb)] = tops[i] + jnp.log(sums[i])
    for i in range(2):
        both = jnp.concatenate([outs[0][i], outs[1][i]], axis=0)
        o_ref[pl.ds(i * hb, hb), :] = both.T.astype(BF)


def attend(meta, q, k, v, n):
    rows = q.shape[0]
    keys = k.shape[0]
    grid_spec = pltpu.PrefetchScalarGridSpec(
        num_scalar_prefetch=1,
        grid=(PAIRS_OF_HEADS,),
        in_specs=[
            pl.BlockSpec((rows, LANES), lambda p, *_: (0, p)),
            pl.BlockSpec((keys, LANES), lambda p, *_: (0, p)),
            pl.BlockSpec((keys, LANES), lambda p, *_: (0, p)),
        ],
        out_specs=[
            pl.BlockSpec((rows, LANES), lambda p, *_: (0, p)),
            pl.BlockSpec((1, 8, rows), lambda p, *_: (p, 0, 0)),
        ],
        scratch_shapes=[pltpu.VMEM((2 * n, LANES, rows // 2), BF)],
    )
    return pl.pallas_call(
        functools.partial(attend_kernel, n, rows // 2),
        grid_spec=grid_spec,
        out_shape=[
            jax.ShapeDtypeStruct((rows, WIDE), BF),
            jax.ShapeDtypeStruct((PAIRS_OF_HEADS, 8, rows), F32),
        ],
        compiler_params=params(),
        cost_estimate=cost(23),
        name="attend",
    )(meta, q, k, v)


def attend_back_kernel(n, hb, meta, q_ref, k_ref, v_ref, o_ref, do_ref, lse_ref, dq_ref, dk_ref, dv_ref, kt_ref, dk_acc, dv_acc):
    keys = 2 * hb * n
    for i in range(keys // hb):
        kt_ref[i] = k_ref[pl.ds(i * hb, hb), :].astype(F32).T.astype(BF)
    dk_acc[...] = jnp.zeros_like(dk_acc)
    dv_acc[...] = jnp.zeros_like(dv_acc)
    lane = lax.broadcasted_iota(jnp.int32, (1, LANES), 1)
    plan = chunk_plan(n)
    prods = []
    for i in range(2):
        part = pl.ds(i * hb, hb)
        prods.append((o_ref[part, :].astype(F32) * do_ref[part, :].astype(F32)).T)
    dqs = []
    for head in range(2):
        own_lanes = (lane // HD) == head
        deltas = [jnp.sum(prods[i][head * HD : (head + 1) * HD, :], axis=0, keepdims=True) for i in range(2)]
        lses = [lse_ref[0, pl.ds(head, 1), pl.ds(i * hb, hb)] for i in range(2)]
        accs = [jnp.zeros((HD, hb), F32), jnp.zeros((HD, hb), F32)]
        for p, kind, diagonal in plan:
            q_off, k_off, q_pos, k_pos, low = chunk_offsets(meta, n, hb, p, kind)
            q_at, k_at = pl.ds(q_off, hb), pl.ds(k_off, hb)
            queries = jnp.where(own_lanes, q_ref[q_at, :], 0)
            d_out = jnp.where(own_lanes, do_ref[q_at, :], 0)
            s = chunk_scores(k_ref[k_at, :], queries, meta, diagonal, kind, q_pos, k_pos, hb)
            if low is True or low is False:
                lse, delta = lses[1 - low], deltas[1 - low]
            else:
                lse, delta = jnp.where(low, lses[0], lses[1]), jnp.where(low, deltas[0], deltas[1])
            prob = jnp.exp(s - lse)
            d_prob = dot(v_ref[k_at, :], d_out, NT)
            d_score = (prob * (d_prob - delta)).astype(BF)
            dv_acc[k_at, :] += dot(prob.astype(BF), d_out)
            dk_acc[k_at, :] += dot(d_score, queries)
            got = dot(kt_ref[k_off // hb, pl.ds(head * HD, HD), :], d_score)
            if low is True or low is False:
                accs[1 - low] += got
            else:
                accs[0] += jnp.where(low, got, 0.0)
                accs[1] += jnp.where(low, 0.0, got)
        dqs.append(accs)
    for i in range(2):
        both = jnp.concatenate([dqs[0][i], dqs[1][i]], axis=0) * 0.125
        dq_ref[pl.ds(i * hb, hb), :] = both.T.astype(BF)
    dk_ref[...] = dk_acc[...].astype(BF)
    dv_ref[...] = dv_acc[...].astype(BF)


def attend_back(meta, q, k, v, o, d_o, lse, n):
    rows = q.shape[0]
    keys = k.shape[0]
    row_spec = pl.BlockSpec((rows, LANES), lambda p, *_: (0, p))
    key_spec = pl.BlockSpec((keys, LANES), lambda p, *_: (0, p))
    grid_spec = pltpu.PrefetchScalarGridSpec(
        num_scalar_prefetch=1,
        grid=(PAIRS_OF_HEADS,),
        in_specs=[row_spec, key_spec, key_spec, row_spec, row_spec, pl.BlockSpec((1, 8, rows), lambda p, *_: (p, 0, 0))],
        out_specs=[row_spec, key_spec, key_spec],
        scratch_shapes=[pltpu.VMEM((2 * n, LANES, rows // 2), BF), pltpu.VMEM((keys, LANES), F32), pltpu.VMEM((keys, LANES), F32)],
    )
    return pl.pallas_call(
        functools.partial(attend_back_kernel, n, rows // 2),
        grid_spec=grid_spec,
        out_shape=[
            jax.ShapeDtypeStruct((rows, WIDE), BF),
            jax.ShapeDtypeStruct((keys, WIDE), BF),
            jax.ShapeDtypeStruct((keys, WIDE), BF),
        ],
        compiler_params=params(),
        cost_estimate=cost(46),
        name="attend_back",
    )(meta, q, k, v, o, d_o, lse)


def by_rows(x):
    return with_layout_constraint(x, Layout(major_to_minor=tuple(range(x.ndim))))


def layer_norm(values, gain_vec, bias_vec):
    row_mean = jnp.mean(values, -1, keepdims=True)
    centred = values - row_mean
    variance = jnp.mean(centred * centred, -1, keepdims=True)
    return centred * lax.rsqrt(variance + 1e-05) * gain_vec + bias_vec


def gelu_tanh(values):
    return 0.5 * values * (1.0 + jnp.tanh(0.7978845608 * (values + 0.044715 * values * values * values)))


def softplus(values):
    return jnp.maximum(values, 0.0) + jnp.log1p(jnp.exp(-jnp.abs(values)))


def adam_update(weight, first, second, grad, rate, decay):
    first = 0.9 * first + 0.1 * grad
    second = 0.95 * second + 0.05 * grad * grad
    first_hat = first / (1.0 - 0.9**STEP)
    second_hat = second / (1.0 - 0.95**STEP)
    weight = weight - rate * (first_hat / (jnp.sqrt(second_hat) + 1e-08) + decay * weight)
    return (weight, first, second)


def pieces_by_ctx(x, half):
    got = [x]
    bit = 1
    while bit < half:
        got += [swap(y, "ctx", bit) for y in got]
        bit *= 2
    return got


def pieces_by_section(got):
    own = jnp.concatenate(got)
    return jnp.concatenate([own, swap(own, "section", 1)])


def sum_pieces(x, half):
    rows = x.shape[0] // half
    bit = half // 2
    while bit >= 1:
        keep, send = x[: bit * rows], x[bit * rows : 2 * bit * rows]
        x = keep + swap(send.astype(BF), "ctx", bit).astype(F32)
        bit //= 2
    return x


def layer_weights(units):
    return split_units(units, 0, 3, WIDE), units[U_OUT:U_UP], join_units(units, U_UP, N_UP), units[U_DOWN:]


def layer_forward(values, hidden1, all_hidden1, meta, n, weights, vecs):
    w_qkv, w_out, w_up, w_down = weights
    keys = dot(all_hidden1, w_qkv[1]).astype(BF)
    vals = dot(all_hidden1, w_qkv[2]).astype(BF)
    queries = dot(hidden1, w_qkv[0]).astype(BF) * jnp.asarray(0.125, BF)
    attended, lse = attend(meta, queries, keys, vals, n)
    middle = values + dot(attended[:, :D], w_out)
    hidden2 = layer_norm(middle, vecs[2], vecs[3]).astype(BF)
    ups = dot(hidden2, w_up)
    gated = gelu_tanh(ups).astype(BF)
    result = middle + dot(gated, w_down)
    return result, (values, all_hidden1, queries, keys, vals, attended, lse, middle, hidden2, ups, gated)


def layer_backward(saved, grad_out, meta, n, weights, vecs, factors, fast):
    values, all_hidden1, queries, keys, vals, attended, lse, middle, hidden2, ups, gated = saved
    w_qkv, w_out, w_up, w_down = weights
    grad_ffn = grad_out.astype(BF)
    grad_down = by_rows(dot(gated, grad_ffn, TN).astype(BF))
    if fast:
        mine_down, other_down = core_blocks(grad_down)
        both = beside(factors)
        grad_ffn, other_down, both = lax.optimization_barrier((grad_ffn, other_down, both))
        came_down = swap(other_down, "section", 1)
    _, back = jax.vjp(gelu_tanh, ups)
    grad_ups = by_rows(back(dot(grad_ffn, w_down, NT))[0].astype(BF))
    grad_up, up_starts = dot(hidden2, grad_ups, TN).astype(BF), [(0, j * D) for j in range(N_UP)]
    if fast:
        mine_up, other_up = merge_apart([grad_up], up_starts)
        four = gather_step(both[None], "shard", 1)
        grad_ups, other_up, four = lax.optimization_barrier((grad_ups, other_up, four))
        came_up = swap(other_up, "section", 1)
    grad_hidden2 = dot(grad_ups, w_up, NT)
    _, norm_back2 = jax.vjp(layer_norm, middle, vecs[2], vecs[3])
    grad_norm2, grad_gain2, grad_bias2 = norm_back2(grad_hidden2)
    grad_middle = grad_out + grad_norm2
    grad_branch = grad_middle.astype(BF)
    grad_outw = dot(attended[:, :D], grad_branch, TN).astype(BF)
    grad_att = dot(grad_branch, jnp.pad(w_out, ((0, WIDE - D), (0, 0))), NT).astype(BF)
    if fast:
        rest = jnp.concatenate([fold_cores(grad_outw), add_low(mine_up, came_up), add_low(mine_down, came_down)])
        grad_att, rest = lax.optimization_barrier((grad_att, rest))
        came = rest_first(rest)
    grad_q, part_k, part_v = attend_back(meta, queries, keys, vals, attended, grad_att, lse, n)
    rows, near = grad_q.shape[0], part_k.shape[0] // 2
    if fast:
        grad_q, four = lax.optimization_barrier((grad_q, four))
        factors = gather_step(four, "shard", 2)
    def to_hidden1(at):
        return dot(part_k[at], w_qkv[1], NT) + dot(part_v[at], w_qkv[2], NT)

    far = to_hidden1(slice(near, None)).astype(BF)
    grad_q, part_k, part_v, far = lax.optimization_barrier((grad_q, part_k, part_v, far))
    if fast:
        far, factors, *came = lax.optimization_barrier((far, factors, *came))
    close = to_hidden1(slice(0, near)) + swap(far, "section", 1).astype(F32)
    if fast:
        close, *came = lax.optimization_barrier((close, *came))
    grad_hidden1 = sum_pieces(close, n // 2)
    grad_hidden1 = grad_hidden1 + dot(grad_q, w_qkv[0], NT)
    _, norm_back1 = jax.vjp(layer_norm, values, vecs[0], vecs[1])
    grad_norm1, grad_gain1, grad_bias1 = norm_back1(grad_hidden1)
    grad_input = (grad_middle + grad_norm1).astype(BF)
    grad_input, grad_q, part_k, part_v = lax.optimization_barrier((grad_input, grad_q, part_k, part_v))
    grad_qk = [dot(h, g, TN).astype(BF) for h, g in ((all_hidden1[:rows], grad_q), (all_hidden1, part_k))]

    def grad_qkvw(part_v):
        parts, starts = [*grad_qk, dot(all_hidden1, part_v, TN).astype(BF)], [(j, 0) for j in range(3)]
        if not fast:
            return merge_units(parts, starts)
        mine, other = merge_apart(parts, starts)
        return add_low(mine, swap(other, "section", 1))

    if fast:
        rest = rest_second(rest, came)
        summed = (rest, along_shard_first(rest)), (part_v, grad_qkvw)
    else:
        summed = jnp.concatenate([grad_qkvw(part_v), grad_outw, merge_units([grad_up], up_starts), grad_down])
        factors = gather_axis(beside(factors), "shard")
    return grad_input, summed, [grad_gain1, grad_bias1, grad_gain2, grad_bias2], factors


def head_mask():
    head = lax.broadcasted_iota(jnp.int32, (HEADS, D), 0)
    return lax.broadcasted_iota(jnp.int32, (HEADS, D), 1) // HD == head


def last_forward(values, positions, length, half, weights, vecs):
    (w_q, w_k, w_v), w_out, w_up, w_down = weights
    heads = head_mask()
    hidden1 = layer_norm(values, vecs[0], vecs[1]).astype(BF)
    mine = (positions == length - 1)[:, None]
    row = jnp.sum(jnp.where(mine, values, 0.0), axis=0, keepdims=True)
    row = group_reduce(row, jnp.add, half)
    row_h1 = layer_norm(row, vecs[0], vecs[1]).astype(BF)
    query = dot(row_h1, w_q).astype(BF)
    wq = dot(jnp.where(heads, query, 0), w_k, NT) * 0.125
    scores = dot2(wq, hidden1, NT)
    scores = jnp.where((positions < length)[None, :], scores, -1e30)
    top = jnp.max(scores, axis=1, keepdims=True)
    expo = jnp.exp(scores - top)
    total = jnp.sum(expo, axis=1, keepdims=True)
    mixed = dot(expo.astype(BF), hidden1)
    wide = lambda x: jnp.broadcast_to(x, (HEADS, HD))

    def merge(x, y):
        high = jnp.maximum(x[:, D : D + 1], y[:, D : D + 1])
        x = x * jnp.exp(x[:, D : D + 1] - high)
        y = y * jnp.exp(y[:, D : D + 1] - high)
        return jnp.concatenate([x[:, :D] + y[:, :D], wide(high), x[:, D + HD :] + y[:, D + HD :]], axis=1)

    merged = group_reduce(jnp.concatenate([mixed, wide(top), wide(total)], axis=1), merge, half)
    top, total = merged[:, D : D + 1], merged[:, D + HD : D + HD + 1]
    mixed = merged[:, :D] / total
    probs = jnp.exp(scores - top) / total
    att = jnp.sum(jnp.where(heads, dot2(mixed, w_v), 0.0), axis=0, keepdims=True)
    middle = row + dot(att.astype(BF), w_out)
    hidden2 = layer_norm(middle, vecs[2], vecs[3]).astype(BF)
    ups = dot(hidden2, w_up)
    gated = gelu_tanh(ups).astype(BF)
    result = middle + dot(gated, w_down)
    return result, (values, hidden1, mine, row_h1, query, wq, probs, mixed, att, middle, hidden2, ups, gated)


def last_backward(saved, grad_out, half, weights, vecs):
    values, hidden1, mine, row_h1, query, wq, probs, mixed, att, middle, hidden2, ups, gated = saved
    (w_q, w_k, w_v), w_out, w_up, w_down = weights
    heads = head_mask()
    grad_ffn = grad_out.astype(BF)
    _, back = jax.vjp(gelu_tanh, ups)
    grad_ups = back(dot(grad_ffn, w_down, NT))[0].astype(BF)
    grad_hidden2 = dot(grad_ups, w_up, NT)
    _, norm_back2 = jax.vjp(layer_norm, middle, vecs[2], vecs[3])
    grad_norm2, grad_gain2, grad_bias2 = norm_back2(grad_hidden2)
    grad_middle = grad_out + grad_norm2
    grad_branch = grad_middle.astype(BF)
    grad_att = dot(grad_branch, w_out, NT).astype(BF)
    att_heads = jnp.where(heads, grad_att, 0)
    wv = dot(att_heads, w_v, NT)
    grad_prob = dot2(wv, hidden1, NT)
    delta = jnp.sum(att_heads.astype(F32) * att, axis=1, keepdims=True)
    grad_score = (probs * (grad_prob - delta)).astype(BF)
    summed = group_reduce(dot(grad_score, hidden1), jnp.add, half)
    grad_query = (jnp.sum(jnp.where(heads, dot2(summed, w_k), 0.0), axis=0, keepdims=True) * 0.125).astype(BF)
    low_probs = probs.astype(BF)
    grad_hidden1 = dot(
        jnp.concatenate([grad_score, grad_score, low_probs, low_probs]), jnp.concatenate([split2(wq), split2(wv)]), TN
    )
    grad_hidden1 = grad_hidden1 + jnp.where(mine, dot(grad_query, w_q, NT), 0.0)
    _, norm_back1 = jax.vjp(layer_norm, values, vecs[0], vecs[1])
    grad_norm1, grad_gain1, grad_bias1 = norm_back1(grad_hidden1)
    grad_input = grad_norm1 + jnp.where(mine, grad_middle, 0.0)
    query8 = query * jnp.asarray(0.125, BF)
    factors = [row_h1, grad_query, query8, grad_att, att, grad_branch, hidden2, grad_ffn]
    factors += [grad_ups.reshape(N_UP, D), gated.reshape(N_UP, D), summed, mixed]
    factors = jnp.concatenate([f.astype(BF) for f in factors])
    return grad_input, factors, [grad_gain1, grad_bias1], [grad_gain2, grad_bias2]


def last_gradient(data, chunk_at, n_chunks, size):
    n_seq = data.shape[0]
    heads = head_mask()
    row_h1, grad_query, query8, grad_att, att, grad_branch, hidden2, grad_ffn = [data[:, i] for i in range(8)]
    at = 8
    grad_ups, gated = data[:, at : at + N_UP], data[:, at + N_UP : at + 2 * N_UP]
    at += 2 * N_UP
    summed, mixed = data[:, at : at + HEADS], data[:, at + HEADS : at + 2 * HEADS]

    def by_unit(parts):
        count, width = len(parts), sum(p.shape[0] for p in parts)
        slot = jnp.concatenate([jnp.full((p.shape[0],), j, jnp.int32) for j, p in enumerate(parts)])
        both = jnp.concatenate(parts).T
        spread = jnp.where(slot[None, None, :] == jnp.arange(count)[None, :, None], both[:, None, :], 0)
        return spread.reshape(count * D, width)

    def per_head(x):
        return jnp.where(heads[None], x[:, None, :], 0).reshape(n_seq * HEADS, D)

    left = by_unit([row_h1, summed.reshape(-1, D), mixed.reshape(-1, D)])
    right = jnp.concatenate([grad_query, per_head(query8), per_head(grad_att)])
    first = chunk_at * size
    qkv = dot(lax.dynamic_slice_in_dim(left, jnp.minimum(first, U_OUT - size), size, 0), right)
    lefts = [att.T, by_unit([hidden2] * N_UP), gated.reshape(n_seq, FF).T]
    rights = [grad_branch, grad_ups.transpose(1, 0, 2).reshape(-1, D), grad_ffn]
    width = sum(x.shape[1] for x in lefts)
    columns, before = [], 0
    for x in lefts:
        columns.append(jnp.pad(x, ((0, 0), (before, width - before - x.shape[1]))))
        before += x.shape[1]
    left = jnp.concatenate(columns)
    rest = dot(lax.dynamic_slice_in_dim(left, jnp.maximum(first - U_OUT, 0), size, 0), jnp.concatenate(rights))
    return jnp.where(first < U_OUT, qkv, rest)


def shards(
    tokens,
    lengths,
    end_ids,
    pairs,
    layer_master,
    layer_first,
    layer_second,
    table_master,
    table_first,
    table_second,
    vector_master,
    vector_first,
    vector_second,
):
    rows = tokens.shape[1]
    s_at = lax.axis_index("section")
    c_at = lax.axis_index("ctx")
    z_at = lax.axis_index("shard")
    n_section = lax.axis_size("section")
    n = lax.axis_size("ctx")
    n_shard = lax.axis_size("shard")
    half = n // 2
    hb = rows // 2
    n_dest = n_section * n
    n_seq = MICRO * n_shard
    columns, entries = table_master.shape
    is_first = s_at == 0
    seq_in = c_at // half
    seq_at = z_at * MICRO + seq_in
    group = (c_at % half) * 2 + s_at

    fast = small_block()
    chunk = chunk_rows(layer_master) if fast else layer_master.reshape(-1, D).astype(BF)
    size = chunk.shape[0]
    cut = size // 2
    if fast:
        wide = cut + OVERLAP // 2
        got = swap(jnp.where(is_first, chunk[size - wide :], chunk[:wide]), "section", 1)
        piece0 = jnp.where(is_first, chunk[:wide], got)
        piece1 = jnp.where(is_first, got[:cut], chunk[cut:])
    else:
        got = swap(jnp.where(is_first, chunk[cut:], chunk[:cut]), "section", 1)
        piece0 = jnp.where(is_first, chunk[:cut], got)
        piece1 = jnp.where(is_first, got, chunk[cut:])
    order = ("ctx", "shard", "section")

    own_ids = jnp.concatenate([tokens, end_ids[:, None]], axis=1)
    all_ids = gather_axis(gather_axis(own_ids, "ctx"), "shard")
    natural = all_ids[..., :rows].transpose(0, 2, 1, 3).reshape(n_shard, MICRO, 2 * n, hb)
    zig = jnp.stack([natural[:, :, :n], natural[:, :, n:][:, :, ::-1]], axis=3)
    zig = zig.reshape(n_shard, MICRO, half, 2, rows).transpose(0, 3, 1, 2, 4)
    end_all = all_ids[:, 0, :, rows].reshape(n_seq)
    n_blocks = n_shard * n_dest

    def held(ids):
        ids = ids - z_at * entries
        return jnp.where((ids >= 0) & (ids < entries), ids, entries)

    listed, counts = owned_rows(held(zig.reshape(n_blocks, rows)), entries)
    end_held = held(end_all)
    if fast:
        first = first_moves(piece0)
        listed, piece0, *first = lax.optimization_barrier((listed, piece0, *first))
        second = second_moves(piece0, first[0], first[1])
    else:
        units0 = lax.all_gather(piece0, order, axis=0, tiled=True)
    dest = jnp.arange(n_blocks, dtype=jnp.int32) % n_dest
    groups = (dest % n % half) * 2 + dest // n
    assert VOCAB >= (n_shard - 1) * entries
    meta_emb = jnp.concatenate(
        [
            jnp.stack([(z_at == n_shard - 1).astype(jnp.int32), jnp.int32(n), jnp.int32(VOCAB - (n_shard - 1) * entries), jnp.int32(0)]),
            groups,
        ]
    )
    picked, end_part = lookup(listed, counts, end_held, meta_emb, table_master, n_blocks, rows)
    if fast:
        picked, *second = lax.optimization_barrier((picked, *second))
        halves, piece1 = gather_half(piece0, first, second, piece1)
    column_at = (s_at * n + c_at) * columns
    end_rows = sum_all(lax.dynamic_update_slice(jnp.zeros((n_seq, D), F32), end_part, (0, column_at)))
    summed = lax.psum_scatter(picked.reshape(n_shard, n_dest, columns, rows), "shard", scatter_dimension=0, tiled=True)
    if fast:
        summed, end_rows, *halves = lax.optimization_barrier((summed, end_rows, *halves))
        parts = [part for mine in halves for part in (mine, swap(mine, "section", 1))]
    routed = lax.all_to_all(summed.reshape(n_dest, columns, rows), ("section", "ctx"), split_axis=0, concat_axis=0, tiled=True)
    embedded = routed.reshape(D, rows).T.astype(F32)
    end_row = lax.dynamic_slice_in_dim(end_rows, seq_at, 1, 0)
    units1 = lax.all_gather(piece1, order, axis=0, tiled=True)

    length = lax.dynamic_slice_in_dim(lengths, seq_in, 1, 0)[0]
    others = [group ^ (2 * cb + sb) for sb in range(2) for cb in range(half)]
    meta = jnp.stack([group, length] + others).astype(jnp.int32)
    span = jnp.arange(hb, dtype=jnp.int32)
    positions = jnp.concatenate([group * hb + span, (2 * n - 1 - group) * hb + span])

    vecs0, vecs1 = vector_master[0:4], vector_master[4:8]
    hidden1 = layer_norm(embedded, vecs0[0], vecs0[1]).astype(BF)
    if fast:
        hidden1, *parts = lax.optimization_barrier((hidden1, *parts))
        units0 = place_units(parts)
    weights0 = layer_weights(units0)
    others = pieces_by_ctx(hidden1, half)[1:]
    *others, w_qkv0, w_up0 = lax.optimization_barrier((*others, weights0[0], weights0[2]))
    weights0 = (w_qkv0, weights0[1], w_up0, weights0[3])
    out0, saved0 = layer_forward(embedded, hidden1, pieces_by_section([hidden1, *others]), meta, n, weights0, vecs0)
    x1 = out0.astype(BF).astype(F32)
    x1, units1 = lax.optimization_barrier((x1, units1))
    w_qkv1 = split_units(units1, 0, 3)
    weights1 = ((w_qkv1[0], w_qkv1[1], w_qkv1[2]), units1[U_OUT:U_UP], join_units(units1, U_UP, N_UP), units1[U_DOWN:])
    final, saved1 = last_forward(x1, positions, length, half, weights1, vecs1)

    def score_terms(final_row, end_vals, gain_vec, bias_vec, head_vec):
        normed = layer_norm(final_row, gain_vec, bias_vec)
        return jnp.sum(normed * (end_vals + head_vec)) * D ** (-0.5)

    counted = group == 0
    score, score_back = jax.vjp(score_terms, final, end_row, vector_master[8], vector_master[9], vector_master[10])
    scores = sum_small(jnp.where((jnp.arange(n_seq) == seq_at) & counted, score, 0.0)[None])[0]

    def pair_loss(score_vals):
        return jnp.sum(softplus(score_vals[pairs[:, 1]] - score_vals[pairs[:, 0]]))

    loss_sum, loss_back = jax.vjp(pair_loss, scores)
    grad_scores = loss_back(jnp.ones_like(loss_sum))[0]
    grad_own = lax.dynamic_slice_in_dim(grad_scores, seq_at, 1, 0)[0]
    grad_final, grad_end, *vec_final = score_back(grad_own)

    grad_x1, factors, vec1, vec1_row = last_backward(saved1, grad_final, half, weights1, vecs1)
    factors = jnp.concatenate([factors, grad_end.astype(BF)])
    grad_x1 = grad_x1.astype(BF).astype(F32)
    grad_x0, grads0, vec0, every_factor = layer_backward(saved0, grad_x1, meta, n, weights0, vecs0, factors, fast)
    every_factor = every_factor.reshape(n_seq, -1, D)

    by_owner = grad_x0.T.reshape(n_dest, columns, rows)
    back = lax.all_to_all(by_owner, ("section", "ctx"), split_axis=0, concat_axis=0, tiled=True)
    if fast:
        (rest, passing), (part_v, finish_qkv) = grads0
        every = [back] + [shift(back, "shard", d) for d in (1, 3)]
        every[1], every[2], every_factor, rest, passing = lax.optimization_barrier(
            (every[1], every[2], every_factor, rest, passing)
        )
        every.append(shift(every[1], "shard", 1))
        rest_terms = along_shard(rest, passing)
        qkv_part = qkv_second(*qkv_first(finish_qkv(part_v)))
        every[3], qkv_part = lax.optimization_barrier((every[3], qkv_part))
        every = jnp.concatenate(every)
        near_order = (z_at + 4 - jnp.array((0, 1, 3, 2), jnp.int32)) % 4
        listed = listed.reshape(n_shard, -1)[near_order].reshape(-1)
        counts = counts.reshape(n_shard, -1)[near_order].reshape(-1)
    else:
        every = lax.all_gather(back, "shard", axis=0, tiled=True)
    end_grads = lax.dynamic_slice(every_factor[:, -1].astype(F32), (0, column_at), (n_seq, columns))
    table_grad, table_squares = scatter(listed, counts, end_held, meta_emb, every, end_grads, entries)
    once = [jnp.where(counted, v, 0.0) for v in vec1_row + vec_final]
    vector_part = jnp.stack(vec0 + vec1 + once)

    own1 = last_gradient(every_factor, c_at * n_shard + z_at, n * n_shard, size)
    squares = jnp.sum(table_squares) + jnp.where(is_first, 0.0, jnp.sum(own1 * own1))
    if fast:
        qkv_terms = along_shard(qkv_part, along_shard_first(qkv_part))
        terms = [*rest_terms, *qkv_terms]
        table_grad, own1, squares, vector_part, *terms = lax.optimization_barrier(
            (table_grad, own1, squares, vector_part, *terms)
        )
        rest_terms, qkv_terms = terms[:3], terms[3:]
        mine = sum(t.astype(F32) for t in rest_terms)
        quarter = sum(t.astype(F32) for t in qkv_terms)
        squares = squares + jnp.sum(quarter * quarter) + jnp.where(c_at == 0, 0.0, jnp.sum(mine * mine))
        squares, quarter = lax.optimization_barrier((squares, quarter))
        collected = collect_qkv(quarter)[: mine.shape[0] * BLOCK]
        mine = jnp.where(c_at == 0, collected.reshape(mine.shape), mine)
    else:
        mine = lax.psum_scatter(grads0, order, scatter_dimension=0, tiled=True).astype(F32)
        squares = squares + jnp.sum(mine * mine)
    other = swap(mine.astype(BF), "section", 1).astype(F32)
    own0 = jnp.stack([mine, other], axis=1).reshape(size, D) if fast else jnp.concatenate([mine, other])
    layer_grad = jnp.where(is_first, own0, own1).reshape(-1, LANES)

    n_vec = vector_part.shape[0]
    totals = sum_small(jnp.concatenate([vector_part, jnp.full((1, D), squares)]))
    vector_grad = totals[:n_vec]
    grad_norm = jnp.sqrt(totals[n_vec, 0] + jnp.sum(vector_grad * vector_grad))
    layer_grad, grad_norm = lax.optimization_barrier((layer_grad, grad_norm))
    factor = CLIP_LIMIT / jnp.maximum(grad_norm, CLIP_LIMIT)
    flat = [x.reshape(-1, LANES) for x in (layer_master, layer_first, layer_second)]
    flat_rows = flat[0].shape[0]
    block_rows = max(b for b in range(1, 2313) if flat_rows % b == 0 and (b % 8 == 0 or b == flat_rows))
    table_cols = max(b for b in range(LANES, 1537, LANES) if entries % b == 0)
    layer_new = adam(factor, *flat, layer_grad, 0.4, 0.1, (block_rows, LANES))
    layer_new = [x.reshape(layer_master.shape) for x in layer_new]
    table_new = adam(factor, table_master, table_first, table_second, table_grad, 0.5, 0.1, (columns, table_cols))
    vector_new = adam_update(vector_master, vector_first, vector_second, vector_grad * factor, 0.7, 0.0)
    return (loss_sum, grad_norm, *layer_new, *table_new, *vector_new)


def solution(mesh):
    in_specs = (
        P("shard", "ctx"),
        P("shard"),
        P("shard"),
        P(),
        P("section", ("ctx", "shard")),
        P("section", ("ctx", "shard")),
        P("section", ("ctx", "shard")),
        P(("section", "ctx"), "shard"),
        P(("section", "ctx"), "shard"),
        P(("section", "ctx"), "shard"),
        P(),
        P(),
        P(),
    )
    out_specs = (
        P(),
        P(),
        P("section", ("ctx", "shard")),
        P("section", ("ctx", "shard")),
        P("section", ("ctx", "shard")),
        P(("section", "ctx"), "shard"),
        P(("section", "ctx"), "shard"),
        P(("section", "ctx"), "shard"),
        P(),
        P(),
        P(),
    )
    return jax.shard_map(shards, mesh=mesh, in_specs=in_specs, out_specs=out_specs, check_vma=False)
```
